32 devices in a mesh: groups: 2 (over y), tensor: 4 (over x, core), replica: 4 (over z).
Axes of the slice: x: 2, y: 2, z: 4, core: 2. Of those that a mesh axis runs over, the one named last changes fastest.
Arguments:
- queries: bfloat16 [4, 128, 4096], P(None, ('groups', 'replica'), 'tensor'), parts along dimension 1, may hold values from -15 to 15, as said below
- fresh_token_keys: bfloat16 [4, 128, 1024], P(None, ('groups', 'replica'), 'tensor'), parts along dimension 1, may hold values from -4 to 4
- fresh_token_values: bfloat16 [4, 128, 1024], P(None, ('groups', 'replica'), 'tensor'), parts along dimension 1, may hold values from -16 to 16
- cached_key_rows: bfloat16 [128, 256, 1024], P(('groups', 'replica'), None, 'tensor'), parts along dimension 0, may hold values from -4 to 4
- cached_value_rows: bfloat16 [128, 256, 1024], P(('groups', 'replica'), None, 'tensor'), parts along dimension 0, may hold values from -16 to 16
- cache_live_lengths: int32 [128], P(('groups', 'replica')), parts along dimension 0, may hold values from 2 to 256
- output_projection_weight: bfloat16 [4096, 8192], P('tensor'), may hold values from -0.09375 to 0.09375
- adapter_down_factors: bfloat16 [48, 64, 4096], P(('groups', 'replica'), None, 'tensor'), parts along dimension 0, may hold values from -0.09375 to 0.09375
- adapter_up_factors: bfloat16 [48, 64, 8192], P(('groups', 'replica'), None, 'tensor'), parts along dimension 0, may hold values from -0.75 to 0.75
- adapter_of_row: int32 [128], P(('groups', 'replica')), parts along dimension 0, may hold values from 0 to 23, as said below
- adapter_storage_slot: int32 [48], P('groups'), parts along dimension 0, may hold values from 0 to 23, as said below
Outputs:
- mixed: bfloat16 [4, 128, 8192], P(None, ('groups', 'replica'), 'tensor'), parts along dimension 1
The draws below stay inside these ranges and needn't reach their ends.
There are 2 independent parts, one for each index of `groups`. The reference program is written for one: setup_inputs(seed, part) draws one part's arguments, and reference() takes and returns one part's arrays. A program takes and returns all parts, laid end to end along the dimension named above; an argument that names none is the same for every part. Nothing has to cross between parts.
Inputs may be any that keep to these rules, and one draw needn't show every extreme that they name: queries of a row pair with the keys of that row. `adapter_storage_slot`: a permutation; slot k lies on index k // 6 of replica. `adapter_of_row`: of the 16 rows of one index of replica at most 8 have adapters whose slots lie on one index of replica; one index of replica, the same for all rows of a part, holds the adapters of exactly 8 rows of every index.
All inputs are finite; a program needn't handle non-finite values.
Results may differ from the reference program's by a relative error of at most 0.0063.
Values may be sent and summed in bfloat16 or wider, within the bound.
No kernel may reach another device: no remote copies, remote signals or barrier semaphores. Data moves between devices by JAX's collectives and lax.ppermute only.
A program may use at most 128 MiB of HBM per device.

```python
import math
import jax
import jax.numpy as jnp
from jax import lax

MODEL_WIDTH = 8192
KVH = 8
HEAD_WIDTH = 128
QUERY_HEADS = 32
ADAPTER_RANK = 64
STEPS = 4
ROW_DEV = 16
CACHE = 256
ADP_DEV = 6
ROWS = 64
ADAPTER_TOTAL = 24
CAP = 8


def slot_table(key):
    return jax.random.permutation(jax.random.fold_in(key, 200), ADAPTER_TOTAL).astype(jnp.int32)


def draw_cached_key_rows(key, part):
    key = jax.random.fold_in(key, 1)
    values = jnp.clip(jax.random.normal(key, (ROWS, CACHE, KVH, HEAD_WIDTH), jnp.float32), -4.0, 4.0)
    return values.reshape(ROWS, CACHE, KVH * HEAD_WIDTH).astype(jnp.bfloat16)


def draw_queries(key, part):
    key = jax.random.fold_in(key, 2)
    group_size = QUERY_HEADS // KVH
    values = jnp.clip(jax.random.normal(key, (STEPS, ROWS, KVH, group_size, HEAD_WIDTH), jnp.float32), -4.0, 4.0)
    return values.reshape(STEPS, ROWS, QUERY_HEADS * HEAD_WIDTH).astype(jnp.bfloat16)


def draw_cache_live_lengths(key, part):
    key = jax.random.fold_in(key, 7)
    lengths = jax.random.randint(key, (ROWS,), 2, CACHE + 1)
    longest = jax.random.randint(jax.random.fold_in(key, 1), (), 0, ROWS)
    return jnp.where(jnp.arange(ROWS) == longest, CACHE, lengths).astype(jnp.int32)


def draw_adapter_storage_slot(key, part):
    table = slot_table(key)
    return table


def draw_adapter_of_row(key, part):
    table = slot_table(key)
    holder = jnp.zeros((ADAPTER_TOTAL,), jnp.int32).at[table].set(jnp.arange(ADAPTER_TOTAL, dtype=jnp.int32))
    key = jax.random.fold_in(key, 6)
    blocks = ROWS // ROW_DEV
    owners_all = ADAPTER_TOTAL // ADP_DEV
    hot_owner = jax.random.randint(jax.random.fold_in(key, 1), (), 0, owners_all)
    entries = jnp.arange(owners_all * CAP, dtype=jnp.int32)
    entry_owner = entries // CAP

    def one_block(block_key):
        shuffle = jax.random.permutation(jax.random.fold_in(block_key, 1), owners_all * CAP)
        ranking = jnp.zeros((owners_all * CAP,), jnp.int32).at[shuffle].set(entries)
        scores = jnp.where(entry_owner == hot_owner, entries - owners_all * CAP, ranking)
        chosen = jnp.argsort(scores, stable=True)[:ROW_DEV]
        chosen = chosen[jax.random.permutation(jax.random.fold_in(block_key, 2), ROW_DEV)]
        owner_rows = chosen // CAP
        local_index = jax.random.randint(jax.random.fold_in(block_key, 3), (ROW_DEV,), 0, ADP_DEV)
        return holder[owner_rows * ADP_DEV + local_index]
    return jax.vmap(one_block)(jax.random.split(key, blocks)).reshape(ROWS).astype(jnp.int32)


def block_levels(stream_key, shape, cuts, least, top_value):
    factor_of = 1.0
    for dim, parts in cuts:
        draws = jax.random.uniform(jax.random.fold_in(jax.random.fold_in(stream_key, 6), dim), (parts,), jnp.float32, least / len(cuts), top_value / len(cuts))
        factor_of = factor_of * jnp.repeat(jnp.exp(draws), shape[dim] // parts).reshape((-1,) + (1,) * (len(shape) - 1 - dim))
    return factor_of


def gaussian(rng, extent, spread, most, cuts=(), kind=jnp.bfloat16):
    array = spread * jax.random.normal(rng, extent, jnp.float32)
    if cuts:
        array = array * block_levels(rng, extent, cuts, -0.22, 0.18)
    return jnp.clip(array, -most, most).astype(kind)


def setup_inputs(seed: int = 0, part: int = 0) -> dict:
    seeds = jax.random.split(jax.random.key(seed), 12)
    part_splits = jax.random.split(jax.random.fold_in(seeds[11], part), 12)
    queries = draw_queries(jax.random.fold_in(jax.random.fold_in(seeds[11], part), 71), part)
    fresh_token_keys = gaussian(part_splits[1], (STEPS, ROWS, KVH * HEAD_WIDTH), 1.0, 4.0, ((1, 4), (2, 4)))
    fresh_token_values = gaussian(part_splits[2], (STEPS, ROWS, KVH * HEAD_WIDTH), 4.0, 16.0, ((1, 4), (2, 4)))
    cached_key_rows = draw_cached_key_rows(jax.random.fold_in(jax.random.fold_in(seeds[11], part), 71), part)
    cached_value_rows = gaussian(part_splits[4], (ROWS, CACHE, KVH * HEAD_WIDTH), 4.0, 16.0, ((0, 4), (2, 4)))
    cache_live_lengths = draw_cache_live_lengths(jax.random.fold_in(jax.random.fold_in(seeds[11], part), 71), part)
    output_projection_weight = gaussian(seeds[6], (QUERY_HEADS * HEAD_WIDTH, MODEL_WIDTH), (QUERY_HEADS * HEAD_WIDTH) ** -0.5, 0.09375, ((0, 4),))
    adapter_down_factors = gaussian(part_splits[7], (ADAPTER_TOTAL, ADAPTER_RANK, QUERY_HEADS * HEAD_WIDTH), (QUERY_HEADS * HEAD_WIDTH) ** -0.5, 0.09375, ((0, 4), (2, 4)))
    adapter_up_factors = gaussian(part_splits[8], (ADAPTER_TOTAL, ADAPTER_RANK, MODEL_WIDTH), ADAPTER_RANK ** -0.5, 0.75, ((0, 4), (2, 4)))
    adapter_of_row = draw_adapter_of_row(jax.random.fold_in(jax.random.fold_in(seeds[11], part), 71), part)
    adapter_storage_slot = draw_adapter_storage_slot(jax.random.fold_in(jax.random.fold_in(seeds[11], part), 71), part)
    return {"queries": queries, "fresh_token_keys": fresh_token_keys, "fresh_token_values": fresh_token_values, "cached_key_rows": cached_key_rows, "cached_value_rows": cached_value_rows, "cache_live_lengths": cache_live_lengths, "output_projection_weight": output_projection_weight, "adapter_down_factors": adapter_down_factors, "adapter_up_factors": adapter_up_factors, "adapter_of_row": adapter_of_row, "adapter_storage_slot": adapter_storage_slot}


def reference(queries, fresh_token_keys, fresh_token_values, cached_key_rows, cached_value_rows, cache_live_lengths, output_projection_weight, adapter_down_factors, adapter_up_factors, adapter_of_row, adapter_storage_slot):
    group_size = QUERY_HEADS // KVH
    score_scale = 1.0 / math.sqrt(HEAD_WIDTH)
    query_heads = queries.astype(jnp.float32).reshape(STEPS, ROWS, KVH, group_size, HEAD_WIDTH)
    key_cache = cached_key_rows.astype(jnp.float32).reshape(ROWS, CACHE, KVH, HEAD_WIDTH)
    value_cache = cached_value_rows.astype(jnp.float32).reshape(ROWS, CACHE, KVH, HEAD_WIDTH)
    key_new = fresh_token_keys.astype(jnp.float32).reshape(STEPS, ROWS, KVH, HEAD_WIDTH)
    value_new = fresh_token_values.astype(jnp.float32).reshape(STEPS, ROWS, KVH, HEAD_WIDTH)
    cached = jnp.einsum('srgjd,rcgd->srgjc', query_heads, key_cache) * score_scale
    fresh = jnp.einsum('srgjd,trgd->srgjt', query_heads, key_new) * score_scale
    live_cache = (jnp.arange(CACHE)[None, :] < cache_live_lengths[:, None])[None, :, None, None, :]
    live_fresh = (jnp.arange(STEPS)[None, :] <= jnp.arange(STEPS)[:, None])[:, None, None, None, :]
    cached = jnp.where(live_cache, cached, -jnp.inf)
    fresh = jnp.where(live_fresh, fresh, -jnp.inf)
    row_max = jnp.maximum(lax.optimization_barrier(jnp.max(cached, axis=-1, keepdims=True)), lax.optimization_barrier(jnp.max(fresh, axis=-1, keepdims=True)))
    weight_cache = jnp.exp(cached - row_max)
    weight_fresh = jnp.exp(fresh - row_max)
    denominator = lax.optimization_barrier(jnp.sum(weight_cache, axis=-1, keepdims=True)) + lax.optimization_barrier(jnp.sum(weight_fresh, axis=-1, keepdims=True))
    probs_cache = (weight_cache / denominator).astype(jnp.bfloat16).astype(jnp.float32)
    probs_fresh = (weight_fresh / denominator).astype(jnp.bfloat16).astype(jnp.float32)
    heads_out = jnp.einsum('srgjc,rcgd->srgjd', probs_cache, value_cache) + jnp.einsum('srgjt,trgd->srgjd', probs_fresh, value_new)
    attention_output = heads_out.astype(jnp.bfloat16).reshape(STEPS, ROWS, QUERY_HEADS * HEAD_WIDTH)
    base_projection = jnp.dot(attention_output.reshape(STEPS * ROWS, QUERY_HEADS * HEAD_WIDTH), output_projection_weight, preferred_element_type=jnp.float32).reshape(STEPS, ROWS, MODEL_WIDTH)
    storage_slot = adapter_storage_slot[adapter_of_row].astype(jnp.int32)

    def single_row(pieces):
        row_attn, row_storage_slot = pieces
        down_factor = lax.dynamic_index_in_dim(adapter_down_factors, row_storage_slot, 0, keepdims=False)
        upper_bound = lax.dynamic_index_in_dim(adapter_up_factors, row_storage_slot, 0, keepdims=False)
        low_rank = jnp.dot(row_attn, down_factor.T, preferred_element_type=jnp.float32).astype(jnp.bfloat16)
        return jnp.dot(low_rank, upper_bound, preferred_element_type=jnp.float32).astype(jnp.bfloat16)
    adapter_delta = lax.map(single_row, (jnp.swapaxes(attention_output, 0, 1), storage_slot))
    mixed = base_projection + jnp.swapaxes(adapter_delta, 0, 1).astype(jnp.float32)
    return mixed.astype(jnp.bfloat16)
```

```python
import math

import jax
import jax.numpy as jnp
from jax import lax
from jax.sharding import PartitionSpec as P

HEAD_WIDTH = 128


def attend(
    queries,
    fresh_token_keys,
    fresh_token_values,
    cached_key_rows,
    cached_value_rows,
    cache_live_lengths,
):
    step_count, row_count, shard_width = queries.shape
    kv_here = cached_key_rows.shape[2] // HEAD_WIDTH
    group_size = shard_width // HEAD_WIDTH // kv_here
    cache_len = cached_key_rows.shape[1]
    score_scale = 1.0 / math.sqrt(HEAD_WIDTH)
    query_heads = queries.reshape(step_count, row_count, kv_here, group_size, HEAD_WIDTH)
    key_cache = cached_key_rows.reshape(row_count, cache_len, kv_here, HEAD_WIDTH)
    value_cache = cached_value_rows.reshape(row_count, cache_len, kv_here, HEAD_WIDTH)
    key_new = fresh_token_keys.reshape(step_count, row_count, kv_here, HEAD_WIDTH)
    value_new = fresh_token_values.reshape(step_count, row_count, kv_here, HEAD_WIDTH)
    cached = (
        jnp.einsum("srgjd,rcgd->srgjc", query_heads, key_cache, preferred_element_type=jnp.float32)
        * score_scale
    )
    fresh = (
        jnp.einsum("srgjd,trgd->srgjt", query_heads, key_new, preferred_element_type=jnp.float32)
        * score_scale
    )
    live_cache = (jnp.arange(cache_len)[None, :] < cache_live_lengths[:, None])[
        None, :, None, None, :
    ]
    live_fresh = (jnp.arange(step_count)[None, :] <= jnp.arange(step_count)[:, None])[
        :, None, None, None, :
    ]
    cached = jnp.where(live_cache, cached, -jnp.inf)
    fresh = jnp.where(live_fresh, fresh, -jnp.inf)
    row_max = jnp.maximum(
        jnp.max(cached, axis=-1, keepdims=True), jnp.max(fresh, axis=-1, keepdims=True)
    )
    weight_cache = jnp.exp(cached - row_max)
    weight_fresh = jnp.exp(fresh - row_max)
    denominator = jnp.sum(weight_cache, axis=-1, keepdims=True) + jnp.sum(
        weight_fresh, axis=-1, keepdims=True
    )
    probs_cache = (weight_cache / denominator).astype(jnp.bfloat16)
    probs_fresh = (weight_fresh / denominator).astype(jnp.bfloat16)
    heads_out = jnp.einsum(
        "srgjc,rcgd->srgjd", probs_cache, value_cache, preferred_element_type=jnp.float32
    )
    heads_out = heads_out + jnp.einsum(
        "srgjt,trgd->srgjd", probs_fresh, value_new, preferred_element_type=jnp.float32
    )
    return heads_out.astype(jnp.bfloat16).reshape(step_count, row_count, shard_width)


def xor_exchange(value, axis, distance):
    size = lax.axis_size(axis)
    return lax.ppermute(value, axis, [(i, i ^ distance) for i in range(size)])


def sum_over_tensor(partial_value):
    width = lax.axis_size("tensor")
    sent = partial_value.astype(jnp.bfloat16)
    total = partial_value
    for distance in range(1, width):
        total = total + xor_exchange(sent, "tensor", distance).astype(jnp.float32)
    return total


def scatter_over_tensor(partial_out):
    width = lax.axis_size("tensor")
    chips = width // 2
    rows = partial_out.shape[0]
    me = lax.axis_index("tensor")
    chip, core = me // 2, me % 2
    blocks = partial_out.reshape(rows, chips, 2, -1)
    mine = lax.dynamic_index_in_dim(blocks, core, 2, keepdims=False)
    other = lax.dynamic_index_in_dim(blocks, 1 - core, 2, keepdims=False)
    got = xor_exchange(other.astype(jnp.bfloat16), "tensor", 1)
    half = mine + got.astype(jnp.float32)
    total = lax.dynamic_index_in_dim(half, chip, 1, keepdims=False)
    for distance in range(1, chips):
        block = lax.dynamic_index_in_dim(half, chip ^ distance, 1, keepdims=False)
        total = total + xor_exchange(
            block.astype(jnp.bfloat16), "tensor", 2 * distance
        ).astype(jnp.float32)
    return total


def body(
    queries,
    fresh_token_keys,
    fresh_token_values,
    cached_key_rows,
    cached_value_rows,
    cache_live_lengths,
    output_projection_weight,
    adapter_down_factors,
    adapter_up_factors,
    adapter_of_row,
    adapter_storage_slot,
):
    step_count, row_count, shard_width = queries.shape
    resident, rank, _ = adapter_down_factors.shape
    output_columns = adapter_up_factors.shape[2]
    adapters_all = adapter_storage_slot.shape[0]
    owners = lax.axis_size("replica")
    capacity = max(2, 2 * row_count // owners)
    me = lax.axis_index("replica")

    slot_of_row = jnp.sum(
        jnp.where(
            adapter_of_row[:, None] == jnp.arange(adapters_all)[None, :],
            adapter_storage_slot[None, :],
            0,
        ),
        axis=1,
    )
    partner = jnp.bitwise_xor(slot_of_row // resident, me)
    local_of_row = slot_of_row % resident
    same = partner[:, None] == partner[None, :]
    earlier = jnp.arange(row_count)[None, :] < jnp.arange(row_count)[:, None]
    place = jnp.sum((same & earlier).astype(jnp.int32), axis=1)
    pick = (
        (partner[None, None, :] == jnp.arange(owners)[:, None, None])
        & (place[None, None, :] == jnp.arange(capacity)[None, :, None])
    )
    local_hot = (local_of_row[:, None] == jnp.arange(resident)[None, :]).astype(jnp.bfloat16)
    pick16 = pick.astype(jnp.bfloat16)
    local_pick = jnp.einsum("ocr,ra->oca", pick16, local_hot).astype(jnp.bfloat16)
    local_got = [local_pick[0]] + [
        xor_exchange(local_pick[d], "replica", d) for d in range(1, owners)
    ]

    attention_output = attend(
        queries,
        fresh_token_keys,
        fresh_token_values,
        cached_key_rows,
        cached_value_rows,
        cache_live_lengths,
    )
    sent_rows = jnp.einsum(
        "ocr,srf->ocsf", pick16, attention_output, preferred_element_type=jnp.float32
    ).astype(jnp.bfloat16)
    rows_got = jnp.stack(
        [sent_rows[0]] + [xor_exchange(sent_rows[d], "replica", d) for d in range(1, owners)]
    )
    mask = jnp.stack(local_got).astype(jnp.float32)

    partial_out = jnp.dot(
        attention_output.reshape(step_count * row_count, shard_width),
        output_projection_weight,
        preferred_element_type=jnp.float32,
    )
    base_projection = scatter_over_tensor(partial_out)

    held = owners * capacity * step_count
    low_all = lax.dot_general(
        rows_got.reshape(held, shard_width),
        adapter_down_factors.reshape(resident * rank, shard_width),
        (((1,), (1,)), ((), ())),
        preferred_element_type=jnp.float32,
    ).reshape(owners, capacity, step_count, resident, rank)
    low_partial = jnp.sum(low_all * mask[:, :, None, :, None], axis=3)
    low_rank = sum_over_tensor(low_partial).astype(jnp.bfloat16)
    low_wide = (low_rank[:, :, :, None, :] * mask[:, :, None, :, None].astype(jnp.bfloat16)).reshape(
        held, resident * rank
    )
    delta = (
        jnp.dot(
            low_wide,
            adapter_up_factors.reshape(resident * rank, output_columns),
            preferred_element_type=jnp.float32,
        )
        .astype(jnp.bfloat16)
        .reshape(owners, capacity, step_count, output_columns)
    )
    delta_got = jnp.stack(
        [delta[0]] + [xor_exchange(delta[d], "replica", d) for d in range(1, owners)]
    )
    adapter_delta = jnp.einsum(
        "ocr,ocsd->srd", pick16, delta_got, preferred_element_type=jnp.float32
    )
    mixed = base_projection.reshape(step_count, row_count, output_columns) + adapter_delta
    return mixed.astype(jnp.bfloat16)


def solution(mesh):
    in_specs = (
        P(None, ("groups", "replica"), "tensor"),
        P(None, ("groups", "replica"), "tensor"),
        P(None, ("groups", "replica"), "tensor"),
        P(("groups", "replica"), None, "tensor"),
        P(("groups", "replica"), None, "tensor"),
        P(("groups", "replica")),
        P("tensor", None),
        P(("groups", "replica"), None, "tensor"),
        P(("groups", "replica"), None, "tensor"),
        P(("groups", "replica")),
        P("groups"),
    )
    out_specs = P(None, ("groups", "replica"), "tensor")
    return jax.shard_map(body, mesh=mesh, in_specs=in_specs, out_specs=out_specs, check_vma=False)
```

```python
import functools
import math

import jax
import jax.numpy as jnp
from jax import lax
from jax.experimental import pallas as pl
from jax.experimental.pallas import tpu as pltpu
from jax.sharding import PartitionSpec as P

HEAD_WIDTH = 128
LANES = 128
MIB = 1024 * 1024
VMEM = pl.BlockSpec(memory_space=pltpu.VMEM)
SMEM = pl.BlockSpec(memory_space=pltpu.SMEM)
ANY = pl.BlockSpec(memory_space=pl.ANY)


def iota(shape, dim):
    return lax.broadcasted_iota(jnp.int32, shape, dim)


def xor_exchange(value, axis, distance):
    size = lax.axis_size(axis)
    return lax.ppermute(value, axis, [(i, i ^ distance) for i in range(size)])


def attend_kernel(
    owners,
    capacity,
    resident,
    me_ref,
    lengths_ref,
    adapter_ref,
    slot_ref,
    q_ref,
    kf_ref,
    vf_ref,
    k_hbm,
    v_hbm,
    attn_ref,
    unpick_ref,
    *rest,
):
    send_refs, (k_ref, v_ref, q2_ref, s_ref, p_ref, o_ref, sems) = rest[:owners], rest[owners:]
    steps, rows, width = q_ref.shape
    cache, kv_width = k_ref.shape[1:]
    heads = width // HEAD_WIDTH
    kv_here = kv_width // HEAD_WIDTH
    group = heads // kv_here
    per_row = heads * steps
    total = rows * per_row
    tokens = steps * rows
    chunks = sems.shape[1]
    chunk_rows = rows // chunks
    scale = 1.0 / math.sqrt(HEAD_WIDTH)

    def copies(src, dst, which):
        return [
            pltpu.make_async_copy(
                src.at[pl.ds(c * chunk_rows, chunk_rows)],
                dst.at[pl.ds(c * chunk_rows, chunk_rows)],
                sems.at[which, c],
            )
            for c in range(chunks)
        ]

    k_copies = copies(k_hbm, k_ref, 0)
    v_copies = copies(v_hbm, v_ref, 1)
    for copy in k_copies + v_copies:
        copy.start()

    me = me_ref[0]
    counts = [jnp.int32(0)] * owners
    places, locals_ = [], []
    for r in range(rows):
        slot = slot_ref[adapter_ref[r]]
        owner = lax.div(slot, jnp.int32(resident))
        locals_.append(slot - owner * resident)
        partner = lax.bitwise_xor(owner, me)
        place = jnp.int32(0)
        for d in range(owners):
            hit = partner == d
            place = jnp.where(hit, d * capacity + counts[d], place)
            counts[d] = jnp.where(hit, counts[d] + 1, counts[d])
        places.append(place)

    by_head = jnp.concatenate(
        [
            q_ref[:, :, h * HEAD_WIDTH : (h + 1) * HEAD_WIDTH].reshape(tokens, HEAD_WIDTH)
            for h in range(heads)
        ],
        axis=0,
    )
    to_row = iota((total, total), 0)
    from_head = iota((total, total), 1)
    source = ((to_row // steps) % heads) * tokens + (to_row % steps) * rows + to_row // per_row
    order = (source == from_head).astype(jnp.bfloat16)
    by_row = jnp.dot(order, by_head, preferred_element_type=jnp.float32)
    kv_of = (iota((total, HEAD_WIDTH), 0) // (steps * group)) % kv_here
    for g in range(kv_here):
        q2_ref[:, g * HEAD_WIDTH : (g + 1) * HEAD_WIDTH] = jnp.where(
            kv_of == g, by_row, 0.0
        ).astype(jnp.bfloat16)

    kf = kf_ref[...].reshape(tokens, kv_width)
    vf = vf_ref[...].reshape(tokens, kv_width)
    nt = (((1,), (1,)), ((), ()))
    fresh = (
        lax.dot_general(q2_ref[...], kf, nt, preferred_element_type=jnp.float32) * scale
    )
    at_row, at_token = iota((total, tokens), 0), iota((total, tokens), 1)
    live = (at_token % rows == at_row // per_row) & (at_token // rows <= at_row % steps)
    fresh = jnp.where(live, fresh, -jnp.inf)

    position = iota((per_row, cache), 1)
    for c in range(chunks):
        k_copies[c].wait()
        for r in range(c * chunk_rows, (c + 1) * chunk_rows):
            here = slice(r * per_row, (r + 1) * per_row)
            scores = (
                lax.dot_general(
                    q2_ref[here, :], k_ref[r], nt, preferred_element_type=jnp.float32
                )
                * scale
            )
            s_ref[here, :] = jnp.where(position < lengths_ref[r], scores, -jnp.inf)

    fresh_probs = []
    block = chunk_rows * per_row
    for c in range(chunks):
        here = slice(c * block, (c + 1) * block)
        cached_c, fresh_c = s_ref[here, :], fresh[here, :]
        top = jnp.maximum(
            jnp.max(cached_c, axis=1, keepdims=True), jnp.max(fresh_c, axis=1, keepdims=True)
        )
        wc, wf = jnp.exp(cached_c - top), jnp.exp(fresh_c - top)
        denominator = jnp.sum(wc, axis=1, keepdims=True) + jnp.sum(wf, axis=1, keepdims=True)
        p_ref[here, :] = (wc / denominator).astype(jnp.bfloat16)
        fresh_probs.append((wf / denominator).astype(jnp.bfloat16))
    o_ref[...] = jnp.dot(
        jnp.concatenate(fresh_probs, axis=0), vf, preferred_element_type=jnp.float32
    )
    for c in range(chunks):
        v_copies[c].wait()
        for r in range(c * chunk_rows, (c + 1) * chunk_rows):
            here = slice(r * per_row, (r + 1) * per_row)
            o_ref[here, :] += jnp.dot(
                p_ref[here, :], v_ref[r], preferred_element_type=jnp.float32
            )

    out = o_ref[:, :HEAD_WIDTH]
    for g in range(1, kv_here):
        out = jnp.where(kv_of == g, o_ref[:, g * HEAD_WIDTH : (g + 1) * HEAD_WIDTH], out)
    back = iota((total, total), 0)
    source = (back % rows) * per_row + (back // tokens) * steps + (back // rows) % steps
    order_back = (source == iota((total, total), 1)).astype(jnp.bfloat16)
    out = jnp.dot(
        order_back, out.astype(jnp.bfloat16), preferred_element_type=jnp.float32
    ).astype(jnp.bfloat16)
    attn = jnp.concatenate(
        [out[h * tokens : (h + 1) * tokens, :] for h in range(heads)], axis=1
    )
    attn_ref[...] = attn

    held = owners * capacity * steps
    slot_at = iota((held, tokens), 0)
    token_at = iota((held, tokens), 1)
    place_of = jnp.zeros((held, tokens), jnp.int32)
    slot_at_t = iota((tokens, held), 1)
    token_at_t = iota((tokens, held), 0)
    place_of_t = jnp.zeros((tokens, held), jnp.int32)
    slot_at_l = iota((held, LANES), 0) // steps
    lane = iota((held, LANES), 1)
    meta = jnp.zeros((held, LANES), jnp.float32)
    for r in range(rows):
        place_of = jnp.where(token_at % rows == r, places[r], place_of)
        place_of_t = jnp.where(token_at_t % rows == r, places[r], place_of_t)
        meta = jnp.where((slot_at_l == places[r]) & (lane == locals_[r]), 1.0, meta)
    pick = (
        (slot_at // steps == place_of) & (slot_at % steps == token_at // rows)
    ).astype(jnp.bfloat16)
    unpick_ref[...] = (
        (slot_at_t // steps == place_of_t) & (slot_at_t % steps == token_at_t // rows)
    ).astype(jnp.bfloat16)
    sent = jnp.dot(pick, attn, preferred_element_type=jnp.float32).astype(jnp.bfloat16)
    meta = meta.astype(jnp.bfloat16)
    size = capacity * steps
    for d in range(owners):
        here = slice(d * size, (d + 1) * size)
        send_refs[d][:, :width] = sent[here, :]
        send_refs[d][:, width:] = meta[here, :]


def attend_and_pick(
    me,
    lengths,
    adapter_of_row,
    storage_slot,
    queries,
    fresh_keys,
    fresh_values,
    cached_keys,
    cached_values,
    owners,
    capacity,
    resident,
):
    steps, rows, width = queries.shape
    cache, kv_width = cached_keys.shape[1:]
    heads = width // HEAD_WIDTH
    total = rows * heads * steps
    tokens = steps * rows
    size = capacity * steps
    chunks = 4
    outs = pl.pallas_call(
        functools.partial(attend_kernel, owners, capacity, resident),
        out_shape=[
            jax.ShapeDtypeStruct((tokens, width), jnp.bfloat16),
            jax.ShapeDtypeStruct((tokens, owners * size), jnp.bfloat16),
        ]
        + [jax.ShapeDtypeStruct((size, width + LANES), jnp.bfloat16)] * owners,
        in_specs=[SMEM] * 4 + [VMEM] * 3 + [ANY] * 2,
        out_specs=[VMEM] * (2 + owners),
        scratch_shapes=[
            pltpu.VMEM((rows, cache, kv_width), jnp.bfloat16),
            pltpu.VMEM((rows, cache, kv_width), jnp.bfloat16),
            pltpu.VMEM((total, kv_width), jnp.bfloat16),
            pltpu.VMEM((total, cache), jnp.float32),
            pltpu.VMEM((total, cache), jnp.bfloat16),
            pltpu.VMEM((total, kv_width), jnp.float32),
            pltpu.SemaphoreType.DMA((2, chunks)),
        ],
        compiler_params=pltpu.CompilerParams(vmem_limit_bytes=24 * MIB),
        cost_estimate=pl.CostEstimate(
            flops=8 * total * cache * kv_width,
            bytes_accessed=4 * rows * cache * kv_width,
            transcendentals=total * cache,
        ),
        name="attend",
    )(
        me,
        lengths,
        adapter_of_row,
        storage_slot,
        queries,
        fresh_keys,
        fresh_values,
        cached_keys,
        cached_values,
    )
    return outs[0], outs[1], outs[2:]


def project_kernel(blocks, me_ref, attn_ref, w_hbm, send_ref, keep_ref, w_ref, sems):
    columns = w_hbm.shape[1] // blocks
    me = me_ref[0]

    def copy(n, d):
        at = pl.multiple_of(lax.bitwise_xor(me, jnp.int32(d)) * columns, LANES)
        return pltpu.make_async_copy(w_hbm.at[:, pl.ds(at, columns)], w_ref.at[n], sems.at[n])

    order = list(range(1, blocks, 2)) + list(range(0, blocks, 2))
    copies = [copy(n, d) for n, d in enumerate(order)]
    for c in copies:
        c.start()
    attn = attn_ref[...]
    for n, d in enumerate(order):
        copies[n].wait()
        out = jnp.dot(attn, w_ref[n], preferred_element_type=jnp.float32)
        if d % 2:
            send_ref[d // 2] = out.astype(jnp.bfloat16)
        else:
            keep_ref[d // 2] = out


def project(me, attn, weight, blocks):
    tokens, width = attn.shape
    columns = weight.shape[1] // blocks
    return pl.pallas_call(
        functools.partial(project_kernel, blocks),
        out_shape=[
            jax.ShapeDtypeStruct((blocks // 2, tokens, columns), jnp.bfloat16),
            jax.ShapeDtypeStruct((blocks // 2, tokens, columns), jnp.float32),
        ],
        in_specs=[SMEM, VMEM, ANY],
        out_specs=[VMEM, VMEM],
        scratch_shapes=[
            pltpu.VMEM((blocks, width, columns), jnp.bfloat16),
            pltpu.SemaphoreType.DMA((blocks,)),
        ],
        compiler_params=pltpu.CompilerParams(vmem_limit_bytes=28 * MIB),
        cost_estimate=pl.CostEstimate(
            flops=2 * tokens * width * weight.shape[1],
            bytes_accessed=2 * width * weight.shape[1],
            transcendentals=0,
        ),
        name="project",
    )(me, attn, weight)


def down_kernel(*refs):
    (*got_refs, down_ref, mine_ref, sent_ref, mask_ref) = refs
    resident, rank, width = down_ref.shape
    wide = resident * rank
    got = jnp.concatenate([ref[...] for ref in got_refs], axis=0)
    held = got.shape[0]
    low = lax.dot_general(
        got[:, :width],
        down_ref[...].reshape(wide, width),
        (((1,), (1,)), ((), ())),
        preferred_element_type=jnp.float32,
    )
    spread = (iota((LANES, wide), 1) // rank == iota((LANES, wide), 0)).astype(jnp.bfloat16)
    mask = jnp.dot(got[:, width:], spread, preferred_element_type=jnp.float32)
    mask_ref[...] = mask.astype(jnp.bfloat16)
    low = low * mask
    pair = low[:, :LANES]
    for n in range(1, wide // LANES):
        pair = pair + low[:, n * LANES : (n + 1) * LANES]
    both = pair + pltpu.roll(pair, rank, 1)
    half = held // 2
    packed = jnp.where(iota((half, LANES), 1) < rank, both[:half, :], both[half:, :])
    mine_ref[...] = packed
    sent_ref[...] = packed.astype(jnp.bfloat16)


def down(got, factors):
    resident, rank, width = factors.shape
    held = len(got) * got[0].shape[0]
    return pl.pallas_call(
        down_kernel,
        out_shape=[
            jax.ShapeDtypeStruct((held // 2, LANES), jnp.float32),
            jax.ShapeDtypeStruct((held // 2, LANES), jnp.bfloat16),
            jax.ShapeDtypeStruct((held, resident * rank), jnp.bfloat16),
        ],
        compiler_params=pltpu.CompilerParams(vmem_limit_bytes=12 * MIB),
        cost_estimate=pl.CostEstimate(
            flops=2 * held * resident * rank * width,
            bytes_accessed=2 * resident * rank * width,
            transcendentals=0,
        ),
        name="down",
    )(*got, factors)


def up_kernel(peers, mine_ref, *refs):
    got_refs, (mask_ref, up_ref, *delta_refs) = refs[:peers], refs[peers:]
    resident, rank, columns = up_ref.shape
    wide = resident * rank
    total = mine_ref[...]
    for ref in got_refs:
        total = total + ref[...].astype(jnp.float32)
    other = pltpu.roll(total, rank, 1)
    first = iota(total.shape, 1) < rank
    both = jnp.concatenate(
        [jnp.where(first, total, other), jnp.where(first, other, total)], axis=0
    )
    both = jnp.concatenate([both] * (wide // LANES), axis=1)
    low = jnp.where(mask_ref[...].astype(jnp.float32) > 0.5, both, 0.0).astype(jnp.bfloat16)
    delta = jnp.dot(
        low, up_ref[...].reshape(wide, columns), preferred_element_type=jnp.float32
    ).astype(jnp.bfloat16)
    size = delta.shape[0] // len(delta_refs)
    for d, ref in enumerate(delta_refs):
        ref[...] = delta[d * size : (d + 1) * size, :]


def up(mine, got, mask, factors, owners):
    resident, rank, columns = factors.shape
    held = mask.shape[0]
    return pl.pallas_call(
        functools.partial(up_kernel, len(got)),
        out_shape=[jax.ShapeDtypeStruct((held // owners, columns), jnp.bfloat16)] * owners,
        compiler_params=pltpu.CompilerParams(vmem_limit_bytes=16 * MIB),
        cost_estimate=pl.CostEstimate(
            flops=2 * held * resident * rank * columns,
            bytes_accessed=2 * resident * rank * columns,
            transcendentals=0,
        ),
        name="up",
    )(mine, *got, mask, factors)


def finish_kernel(base_ref, unpick_ref, *refs):
    *delta_refs, out_ref = refs
    delta = jnp.concatenate([ref[...] for ref in delta_refs], axis=0)
    mixed = base_ref[...] + jnp.dot(
        unpick_ref[...], delta, preferred_element_type=jnp.float32
    )
    out_ref[...] = mixed.astype(jnp.bfloat16).reshape(out_ref.shape)


def finish(base, unpick, delta, steps):
    tokens, columns = base.shape
    return pl.pallas_call(
        finish_kernel,
        out_shape=jax.ShapeDtypeStruct((steps, tokens // steps, columns), jnp.bfloat16),
        compiler_params=pltpu.CompilerParams(vmem_limit_bytes=12 * MIB),
        cost_estimate=pl.CostEstimate(
            flops=2 * tokens * unpick.shape[1] * columns,
            bytes_accessed=8 * tokens * columns,
            transcendentals=0,
        ),
        name="finish",
    )(base, unpick, *delta)


def body(
    queries,
    fresh_token_keys,
    fresh_token_values,
    cached_key_rows,
    cached_value_rows,
    cache_live_lengths,
    output_projection_weight,
    adapter_down_factors,
    adapter_up_factors,
    adapter_of_row,
    adapter_storage_slot,
):
    step_count, row_count, _ = queries.shape
    resident = adapter_down_factors.shape[0]
    owners = lax.axis_size("replica")
    tensors = lax.axis_size("tensor")
    capacity = max(2, 2 * row_count // owners)
    my_replica = lax.axis_index("replica").astype(jnp.int32).reshape(1)
    my_tensor = lax.axis_index("tensor").astype(jnp.int32).reshape(1)

    attn, unpick, sent = attend_and_pick(
        my_replica,
        cache_live_lengths,
        adapter_of_row,
        adapter_storage_slot,
        queries,
        fresh_token_keys,
        fresh_token_values,
        cached_key_rows,
        cached_value_rows,
        owners,
        capacity,
        resident,
    )
    got = [sent[0]] + [xor_exchange(sent[d], "replica", d) for d in range(1, owners)]

    send_core, keep = project(my_tensor, attn, output_projection_weight, tensors)
    got_core = xor_exchange(send_core, "tensor", 1)

    mine, low_sent, mask = down(got, adapter_down_factors)
    low_got = [xor_exchange(low_sent, "tensor", d) for d in range(1, tensors)]
    delta = up(mine, low_got, mask, adapter_up_factors, owners)
    delta_got = [delta[0]] + [xor_exchange(delta[d], "replica", d) for d in range(1, owners)]

    got_core, _ = lax.optimization_barrier((got_core, delta[0]))
    base = keep[0] + got_core[0].astype(jnp.float32)
    for n in range(1, tensors // 2):
        half = (keep[n] + got_core[n].astype(jnp.float32)).astype(jnp.bfloat16)
        base = base + xor_exchange(half, "tensor", 2 * n).astype(jnp.float32)
    return finish(base, unpick, delta_got, step_count)


def solution(mesh):
    in_specs = (
        P(None, ("groups", "replica"), "tensor"),
        P(None, ("groups", "replica"), "tensor"),
        P(None, ("groups", "replica"), "tensor"),
        P(("groups", "replica"), None, "tensor"),
        P(("groups", "replica"), None, "tensor"),
        P(("groups", "replica")),
        P("tensor", None),
        P(("groups", "replica"), None, "tensor"),
        P(("groups", "replica"), None, "tensor"),
        P(("groups", "replica")),
        P("groups"),
    )
    out_specs = P(None, ("groups", "replica"), "tensor")
    return jax.shard_map(body, mesh=mesh, in_specs=in_specs, out_specs=out_specs, check_vma=False)
```

```python
import functools
import math

import jax
import jax.numpy as jnp
from jax import lax
from jax.experimental import pallas as pl
from jax.experimental.pallas import tpu as pltpu
from jax.sharding import PartitionSpec as P

HEAD_WIDTH = 128
LANES = 128
MIB = 1024 * 1024
VMEM = pl.BlockSpec(memory_space=pltpu.VMEM)
SMEM = pl.BlockSpec(memory_space=pltpu.SMEM)
ANY = pl.BlockSpec(memory_space=pl.ANY)
HBM = pl.BlockSpec(memory_space=pltpu.HBM)


def iota(shape, dim):
    return lax.broadcasted_iota(jnp.int32, shape, dim)


def in_hbm(*arrays):
    return [pltpu.with_memory_space_constraint(a, pltpu.HBM) for a in arrays]


def xor_exchange(value, axis, distance):
    size = lax.axis_size(axis)
    return lax.ppermute(value, axis, [(i, i ^ distance) for i in range(size)])


def partner_order(size):
    return [0, *range(size // 2, size), *range(1, size // 2)]


def exchange_all(blocks, axis):
    order = partner_order(lax.axis_size(axis))
    return [blocks[0]] + [
        xor_exchange(block, axis, distance)
        for block, distance in zip(blocks[1:], order[1:], strict=True)
    ]


def attend_kernel(
    owners,
    capacity,
    resident,
    me_ref,
    lengths_hbm,
    adapter_hbm,
    slot_hbm,
    q_hbm,
    kf_hbm,
    vf_hbm,
    k_hbm,
    v_hbm,
    attn_ref,
    unpick_ref,
    *rest,
):
    send_refs, rest = rest[:owners], rest[owners:]
    lengths_ref, adapter_ref, slot_ref, q_ref, kf_ref, vf_ref, k_ref, v_ref = rest[:8]
    q2_ref, s_ref, p_ref, o_ref, sems, small_sems = rest[8:]
    steps, rows, width = q_ref.shape
    cache, kv_width = k_ref.shape[1:]
    heads = width // HEAD_WIDTH
    kv_here = kv_width // HEAD_WIDTH
    group = heads // kv_here
    per_row = heads * steps
    total = rows * per_row
    tokens = steps * rows
    chunks = sems.shape[1]
    chunk_rows = rows // chunks
    scale = 1.0 / math.sqrt(HEAD_WIDTH)

    def copies(src, dst, which):
        return [
            pltpu.make_async_copy(
                src.at[pl.ds(c * chunk_rows, chunk_rows)],
                dst.at[pl.ds(c * chunk_rows, chunk_rows)],
                sems.at[which, c],
            )
            for c in range(chunks)
        ]

    k_copies = copies(k_hbm, k_ref, 0)
    v_copies = copies(v_hbm, v_ref, 1)
    small = [
        pltpu.make_async_copy(src, dst, small_sems.at[n])
        for n, (src, dst) in enumerate(
            [
                (q_hbm, q_ref),
                (kf_hbm, kf_ref),
                (lengths_hbm, lengths_ref),
                (vf_hbm, vf_ref),
                (adapter_hbm, adapter_ref),
                (slot_hbm, slot_ref),
            ]
        )
    ]
    q_copy, kf_copy, lengths_copy, vf_copy, adapter_copy, slot_copy = small
    for copy in small + k_copies + v_copies:
        copy.start()

    adapter_copy.wait()
    slot_copy.wait()
    me = me_ref[0]
    counts = [jnp.int32(0)] * owners
    places, locals_ = [], []
    for r in range(rows):
        slot = slot_ref[adapter_ref[r]]
        owner = lax.div(slot, jnp.int32(resident))
        locals_.append(slot - owner * resident)
        partner = lax.bitwise_xor(owner, me)
        place = jnp.int32(0)
        for d, distance in enumerate(partner_order(owners)):
            hit = partner == distance
            place = jnp.where(hit, d * capacity + counts[d], place)
            counts[d] = jnp.where(hit, counts[d] + 1, counts[d])
        places.append(place)

    q_copy.wait()
    by_head = jnp.concatenate(
        [
            q_ref[:, :, h * HEAD_WIDTH : (h + 1) * HEAD_WIDTH].reshape(tokens, HEAD_WIDTH)
            for h in range(heads)
        ],
        axis=0,
    )
    to_row = iota((total, total), 0)
    from_head = iota((total, total), 1)
    source = ((to_row // steps) % heads) * tokens + (to_row % steps) * rows + to_row // per_row
    order = (source == from_head).astype(jnp.bfloat16)
    by_row = jnp.dot(order, by_head, preferred_element_type=jnp.float32)
    kv_of = (iota((total, HEAD_WIDTH), 0) // (steps * group)) % kv_here
    for g in range(kv_here):
        q2_ref[:, g * HEAD_WIDTH : (g + 1) * HEAD_WIDTH] = jnp.where(
            kv_of == g, by_row, 0.0
        ).astype(jnp.bfloat16)

    kf_copy.wait()
    vf_copy.wait()
    lengths_copy.wait()
    kf = kf_ref[...].reshape(tokens, kv_width)
    vf = vf_ref[...].reshape(tokens, kv_width)
    nt = (((1,), (1,)), ((), ()))
    fresh = (
        lax.dot_general(q2_ref[...], kf, nt, preferred_element_type=jnp.float32) * scale
    )
    at_row, at_token = iota((total, tokens), 0), iota((total, tokens), 1)
    live = (at_token % rows == at_row // per_row) & (at_token // rows <= at_row % steps)
    fresh = jnp.where(live, fresh, -jnp.inf)

    position = iota((per_row, cache), 1)
    for c in range(chunks):
        k_copies[c].wait()
        for r in range(c * chunk_rows, (c + 1) * chunk_rows):
            here = slice(r * per_row, (r + 1) * per_row)
            scores = (
                lax.dot_general(
                    q2_ref[here, :], k_ref[r], nt, preferred_element_type=jnp.float32
                )
                * scale
            )
            s_ref[here, :] = jnp.where(position < lengths_ref[r], scores, -jnp.inf)

    fresh_probs = []
    block = chunk_rows * per_row
    for c in range(chunks):
        here = slice(c * block, (c + 1) * block)
        cached_c, fresh_c = s_ref[here, :], fresh[here, :]
        top = jnp.maximum(
            jnp.max(cached_c, axis=1, keepdims=True), jnp.max(fresh_c, axis=1, keepdims=True)
        )
        wc, wf = jnp.exp(cached_c - top), jnp.exp(fresh_c - top)
        denominator = jnp.sum(wc, axis=1, keepdims=True) + jnp.sum(wf, axis=1, keepdims=True)
        p_ref[here, :] = (wc / denominator).astype(jnp.bfloat16)
        fresh_probs.append((wf / denominator).astype(jnp.bfloat16))
    o_ref[...] = jnp.dot(
        jnp.concatenate(fresh_probs, axis=0), vf, preferred_element_type=jnp.float32
    )
    for c in range(chunks):
        v_copies[c].wait()
        for r in range(c * chunk_rows, (c + 1) * chunk_rows):
            here = slice(r * per_row, (r + 1) * per_row)
            o_ref[here, :] += jnp.dot(
                p_ref[here, :], v_ref[r], preferred_element_type=jnp.float32
            )

    out = o_ref[:, :HEAD_WIDTH]
    for g in range(1, kv_here):
        out = jnp.where(kv_of == g, o_ref[:, g * HEAD_WIDTH : (g + 1) * HEAD_WIDTH], out)
    back = iota((total, total), 0)
    source = (back % rows) * per_row + (back // tokens) * steps + (back // rows) % steps
    order_back = (source == iota((total, total), 1)).astype(jnp.bfloat16)
    out = jnp.dot(
        order_back, out.astype(jnp.bfloat16), preferred_element_type=jnp.float32
    ).astype(jnp.bfloat16)
    attn = jnp.concatenate(
        [out[h * tokens : (h + 1) * tokens, :] for h in range(heads)], axis=1
    )
    attn_ref[...] = attn

    held = owners * capacity * steps
    slot_at = iota((held, tokens), 0)
    token_at = iota((held, tokens), 1)
    place_of = jnp.zeros((held, tokens), jnp.int32)
    slot_at_t = iota((tokens, held), 1)
    token_at_t = iota((tokens, held), 0)
    place_of_t = jnp.zeros((tokens, held), jnp.int32)
    slot_at_l = iota((held, LANES), 0) // steps
    lane = iota((held, LANES), 1)
    meta = jnp.zeros((held, LANES), jnp.float32)
    for r in range(rows):
        place_of = jnp.where(token_at % rows == r, places[r], place_of)
        place_of_t = jnp.where(token_at_t % rows == r, places[r], place_of_t)
        meta = jnp.where((slot_at_l == places[r]) & (lane == locals_[r]), 1.0, meta)
    pick = (
        (slot_at // steps == place_of) & (slot_at % steps == token_at // rows)
    ).astype(jnp.bfloat16)
    unpick_ref[...] = (
        (slot_at_t // steps == place_of_t) & (slot_at_t % steps == token_at_t // rows)
    ).astype(jnp.bfloat16)
    sent = jnp.dot(pick, attn, preferred_element_type=jnp.float32).astype(jnp.bfloat16)
    meta = meta.astype(jnp.bfloat16)
    size = capacity * steps
    for d in range(owners):
        here = slice(d * size, (d + 1) * size)
        send_refs[d][:, :width] = sent[here, :]
        send_refs[d][:, width:] = meta[here, :]


def attend_and_pick(
    me,
    lengths,
    adapter_of_row,
    storage_slot,
    queries,
    fresh_keys,
    fresh_values,
    cached_keys,
    cached_values,
    owners,
    capacity,
    resident,
):
    steps, rows, width = queries.shape
    cache, kv_width = cached_keys.shape[1:]
    heads = width // HEAD_WIDTH
    total = rows * heads * steps
    tokens = steps * rows
    size = capacity * steps
    chunks = 4
    outs = pl.pallas_call(
        functools.partial(attend_kernel, owners, capacity, resident),
        out_shape=[
            jax.ShapeDtypeStruct((tokens, width), jnp.bfloat16),
            jax.ShapeDtypeStruct((tokens, owners * size), jnp.bfloat16),
        ]
        + [jax.ShapeDtypeStruct((size, width + LANES), jnp.bfloat16)] * owners,
        in_specs=[SMEM] + [HBM] * 8,
        out_specs=[VMEM] * (2 + owners),
        scratch_shapes=[
            pltpu.SMEM(lengths.shape, jnp.int32),
            pltpu.SMEM(adapter_of_row.shape, jnp.int32),
            pltpu.SMEM(storage_slot.shape, jnp.int32),
            pltpu.VMEM(queries.shape, jnp.bfloat16),
            pltpu.VMEM(fresh_keys.shape, jnp.bfloat16),
            pltpu.VMEM(fresh_values.shape, jnp.bfloat16),
            pltpu.VMEM((rows, cache, kv_width), jnp.bfloat16),
            pltpu.VMEM((rows, cache, kv_width), jnp.bfloat16),
            pltpu.VMEM((total, kv_width), jnp.bfloat16),
            pltpu.VMEM((total, cache), jnp.float32),
            pltpu.VMEM((total, cache), jnp.bfloat16),
            pltpu.VMEM((total, kv_width), jnp.float32),
            pltpu.SemaphoreType.DMA((2, chunks)),
            pltpu.SemaphoreType.DMA((6,)),
        ],
        compiler_params=pltpu.CompilerParams(vmem_limit_bytes=24 * MIB),
        cost_estimate=pl.CostEstimate(
            flops=8 * total * cache * kv_width,
            bytes_accessed=4 * rows * cache * kv_width,
            transcendentals=total * cache,
        ),
        name="attend",
    )(
        me,
        *in_hbm(
            lengths,
            adapter_of_row,
            storage_slot,
            queries,
            fresh_keys,
            fresh_values,
            cached_keys,
            cached_values,
        ),
    )
    return outs[0], outs[1], outs[2:]


def project_kernel(blocks, me_ref, attn_ref, w_hbm, send_ref, keep_ref, w_ref, sems):
    columns = w_hbm.shape[1] // blocks
    me = me_ref[0]

    def copy(n, d):
        at = pl.multiple_of(lax.bitwise_xor(me, jnp.int32(d)) * columns, LANES)
        return pltpu.make_async_copy(w_hbm.at[:, pl.ds(at, columns)], w_ref.at[n], sems.at[n])

    order = list(range(1, blocks, 2)) + list(range(0, blocks, 2))
    copies = [copy(n, d) for n, d in enumerate(order)]
    for c in copies:
        c.start()
    attn = attn_ref[...]
    for n, d in enumerate(order):
        copies[n].wait()
        out = jnp.dot(attn, w_ref[n], preferred_element_type=jnp.float32)
        if d % 2:
            send_ref[d // 2] = out.astype(jnp.bfloat16)
        else:
            keep_ref[d // 2] = out


def project(me, attn, weight, blocks):
    tokens, width = attn.shape
    columns = weight.shape[1] // blocks
    return pl.pallas_call(
        functools.partial(project_kernel, blocks),
        out_shape=[
            jax.ShapeDtypeStruct((blocks // 2, tokens, columns), jnp.bfloat16),
            jax.ShapeDtypeStruct((blocks // 2, tokens, columns), jnp.float32),
        ],
        in_specs=[SMEM, VMEM, HBM],
        out_specs=[VMEM, VMEM],
        scratch_shapes=[
            pltpu.VMEM((blocks, width, columns), jnp.bfloat16),
            pltpu.SemaphoreType.DMA((blocks,)),
        ],
        compiler_params=pltpu.CompilerParams(vmem_limit_bytes=28 * MIB),
        cost_estimate=pl.CostEstimate(
            flops=2 * tokens * width * weight.shape[1],
            bytes_accessed=2 * width * weight.shape[1],
            transcendentals=0,
        ),
        name="project",
    )(me, attn, *in_hbm(weight))


def down_kernel(*refs):
    (*got_refs, down_ref, mine_ref, sent_ref, mask_ref) = refs
    resident, rank, width = down_ref.shape
    wide = resident * rank
    got = jnp.concatenate([ref[...] for ref in got_refs], axis=0)
    held = got.shape[0]
    low = lax.dot_general(
        got[:, :width],
        down_ref[...].reshape(wide, width),
        (((1,), (1,)), ((), ())),
        preferred_element_type=jnp.float32,
    )
    spread = (iota((LANES, wide), 1) // rank == iota((LANES, wide), 0)).astype(jnp.bfloat16)
    mask = jnp.dot(got[:, width:], spread, preferred_element_type=jnp.float32)
    mask_ref[...] = mask.astype(jnp.bfloat16)
    low = low * mask
    pair = low[:, :LANES]
    for n in range(1, wide // LANES):
        pair = pair + low[:, n * LANES : (n + 1) * LANES]
    both = pair + pltpu.roll(pair, rank, 1)
    half = held // 2
    packed = jnp.where(iota((half, LANES), 1) < rank, both[:half, :], both[half:, :])
    mine_ref[...] = packed
    sent_ref[...] = packed.astype(jnp.bfloat16)


def down(got, factors):
    resident, rank, width = factors.shape
    held = len(got) * got[0].shape[0]
    return pl.pallas_call(
        down_kernel,
        out_shape=[
            jax.ShapeDtypeStruct((held // 2, LANES), jnp.float32),
            jax.ShapeDtypeStruct((held // 2, LANES), jnp.bfloat16),
            jax.ShapeDtypeStruct((held, resident * rank), jnp.bfloat16),
        ],
        compiler_params=pltpu.CompilerParams(vmem_limit_bytes=12 * MIB),
        cost_estimate=pl.CostEstimate(
            flops=200 * held * resident * rank * width,
            bytes_accessed=2 * resident * rank * width,
            transcendentals=0,
        ),
        name="down",
    )(*got, factors)


def up_kernel(peers, mine_ref, *refs):
    got_refs, (mask_ref, up_ref, *delta_refs) = refs[:peers], refs[peers:]
    resident, rank, columns = up_ref.shape
    wide = resident * rank
    total = mine_ref[...]
    for ref in got_refs:
        total = total + ref[...].astype(jnp.float32)
    other = pltpu.roll(total, rank, 1)
    first = iota(total.shape, 1) < rank
    both = jnp.concatenate(
        [jnp.where(first, total, other), jnp.where(first, other, total)], axis=0
    )
    both = jnp.concatenate([both] * (wide // LANES), axis=1)
    low = jnp.where(mask_ref[...].astype(jnp.float32) > 0.5, both, 0.0).astype(jnp.bfloat16)
    delta = jnp.dot(
        low, up_ref[...].reshape(wide, columns), preferred_element_type=jnp.float32
    ).astype(jnp.bfloat16)
    size = delta.shape[0] // len(delta_refs)
    for d, ref in enumerate(delta_refs):
        ref[...] = delta[d * size : (d + 1) * size, :]


def up(mine, got, mask, factors, owners):
    resident, rank, columns = factors.shape
    held = mask.shape[0]
    return pl.pallas_call(
        functools.partial(up_kernel, len(got)),
        out_shape=[jax.ShapeDtypeStruct((held // owners, columns), jnp.bfloat16)] * owners,
        compiler_params=pltpu.CompilerParams(vmem_limit_bytes=16 * MIB),
        cost_estimate=pl.CostEstimate(
            flops=200 * held * resident * rank * columns,
            bytes_accessed=2 * resident * rank * columns,
            transcendentals=0,
        ),
        name="up",
    )(mine, *got, mask, factors)


def finish_kernel(owners, unpick_ref, *refs):
    delta_refs, (*other_refs, base_ref, out_ref) = refs[:owners], refs[owners:]
    delta = jnp.concatenate([ref[...] for ref in delta_refs], axis=0)
    base = base_ref[...]
    for ref in other_refs:
        base = base + ref[...].astype(jnp.float32)
    mixed = base + jnp.dot(unpick_ref[...], delta, preferred_element_type=jnp.float32)
    out_ref[...] = mixed.astype(jnp.bfloat16).reshape(out_ref.shape)


def finish(base, unpick, delta, others, steps):
    tokens, columns = base.shape
    return pl.pallas_call(
        functools.partial(finish_kernel, len(delta)),
        out_shape=jax.ShapeDtypeStruct((steps, tokens // steps, columns), jnp.bfloat16),
        compiler_params=pltpu.CompilerParams(vmem_limit_bytes=12 * MIB),
        cost_estimate=pl.CostEstimate(
            flops=2 * tokens * unpick.shape[1] * columns,
            bytes_accessed=8 * tokens * columns,
            transcendentals=0,
        ),
        name="finish",
    )(unpick, *delta, *others, base)


def body(
    queries,
    fresh_token_keys,
    fresh_token_values,
    cached_key_rows,
    cached_value_rows,
    cache_live_lengths,
    output_projection_weight,
    adapter_down_factors,
    adapter_up_factors,
    adapter_of_row,
    adapter_storage_slot,
):
    step_count, row_count, _ = queries.shape
    resident = adapter_down_factors.shape[0]
    owners = lax.axis_size("replica")
    tensors = lax.axis_size("tensor")
    capacity = max(2, 2 * row_count // owners)
    my_replica = lax.axis_index("replica").astype(jnp.int32).reshape(1)
    my_tensor = lax.axis_index("tensor").astype(jnp.int32).reshape(1)

    attn, unpick, sent = attend_and_pick(
        my_replica,
        cache_live_lengths,
        adapter_of_row,
        adapter_storage_slot,
        queries,
        fresh_token_keys,
        fresh_token_values,
        cached_key_rows,
        cached_value_rows,
        owners,
        capacity,
        resident,
    )
    got = exchange_all(sent, "replica")

    send_core, keep = project(my_tensor, attn, output_projection_weight, tensors)
    got_core = xor_exchange(send_core, "tensor", 1)

    mine, low_sent, mask = down(got, adapter_down_factors)
    low_got = [xor_exchange(low_sent, "tensor", d) for d in range(1, tensors)]
    delta = up(mine, low_got, mask, adapter_up_factors, owners)
    delta_got = exchange_all(delta, "replica")

    parts = [keep[n] + got_core[n].astype(jnp.float32) for n in range(tensors // 2)]
    others = [
        xor_exchange(parts[n].astype(jnp.bfloat16), "tensor", 2 * n)
        for n in range(1, tensors // 2)
    ]
    return finish(parts[0], unpick, delta_got, others, step_count)


def solution(mesh):
    in_specs = (
        P(None, ("groups", "replica"), "tensor"),
        P(None, ("groups", "replica"), "tensor"),
        P(None, ("groups", "replica"), "tensor"),
        P(("groups", "replica"), None, "tensor"),
        P(("groups", "replica"), None, "tensor"),
        P(("groups", "replica")),
        P("tensor", None),
        P(("groups", "replica"), None, "tensor"),
        P(("groups", "replica"), None, "tensor"),
        P(("groups", "replica")),
        P("groups"),
    )
    out_specs = P(None, ("groups", "replica"), "tensor")
    return jax.shard_map(body, mesh=mesh, in_specs=in_specs, out_specs=out_specs, check_vma=False)
```

```python
import functools
import math

import jax
import jax.numpy as jnp
from jax import lax
from jax.experimental import pallas as pl
from jax.experimental.pallas import tpu as pltpu
from jax.sharding import PartitionSpec as P

HEAD_WIDTH = 128
LANES = 128
MIB = 1024 * 1024
VMEM = pl.BlockSpec(memory_space=pltpu.VMEM)
SMEM = pl.BlockSpec(memory_space=pltpu.SMEM)
ANY = pl.BlockSpec(memory_space=pl.ANY)
HBM = pl.BlockSpec(memory_space=pltpu.HBM)


def iota(shape, dim):
    return lax.broadcasted_iota(jnp.int32, shape, dim)


def halves(n):
    if n & (n - 1):
        raise ValueError(n)
    return n.bit_length() - 1


def div(x, n):
    return lax.shift_right_logical(x, jnp.int32(halves(n)))


def mod(x, n):
    return x & ((1 << halves(n)) - 1)


def one_hot(source, width):
    lane = iota(source.shape, 1)
    return jnp.concatenate(
        [(source == lane + at).astype(jnp.bfloat16) for at in range(0, width, source.shape[1])],
        axis=1,
    )


def in_hbm(*arrays):
    return [pltpu.with_memory_space_constraint(a, pltpu.HBM) for a in arrays]


def xor_exchange(value, axis, distance):
    size = lax.axis_size(axis)
    return lax.ppermute(value, axis, [(i, i ^ distance) for i in range(size)])


def in_pieces(value, axis, distance, pieces):
    width = value.shape[-1] // pieces
    return [
        xor_exchange(value[..., n * width : (n + 1) * width], axis, distance)
        for n in range(pieces)
    ]


def partner_order(size):
    return [0, *range(size // 2, size), *range(1, size // 2)]


def exchange_all(blocks, axis):
    order = partner_order(lax.axis_size(axis))
    return [blocks[0]] + [
        xor_exchange(block, axis, distance)
        for block, distance in zip(blocks[1:], order[1:], strict=True)
    ]


def attend_kernel(
    owners,
    capacity,
    resident,
    me_ref,
    lengths_hbm,
    adapter_hbm,
    slot_hbm,
    q_hbm,
    kf_hbm,
    vf_hbm,
    k_hbm,
    v_hbm,
    attn_ref,
    pick_ref,
    *rest,
):
    send_refs, rest = rest[:owners], rest[owners:]
    lengths_ref, adapter_ref, slot_ref, q_ref, kf_ref, vf_ref, k_ref, v_ref = rest[:8]
    sems, small_sems = rest[8:]
    steps, rows, width = q_ref.shape
    cache, kv_width = k_ref.shape[1:]
    heads = width // HEAD_WIDTH
    kv_here = kv_width // HEAD_WIDTH
    group = heads // kv_here
    per_row = heads * steps
    total = rows * per_row
    tokens = steps * rows
    chunks = sems.shape[1]
    chunk_rows = rows // chunks
    scale = 1.0 / math.sqrt(HEAD_WIDTH)

    def copies(src, dst, which):
        return [
            pltpu.make_async_copy(
                src.at[pl.ds(c * chunk_rows, chunk_rows)],
                dst.at[pl.ds(c * chunk_rows, chunk_rows)],
                sems.at[which, c],
            )
            for c in range(chunks)
        ]

    k_copies = copies(k_hbm, k_ref, 0)
    v_copies = copies(v_hbm, v_ref, 1)
    small = [
        pltpu.make_async_copy(src, dst, small_sems.at[n])
        for n, (src, dst) in enumerate(
            [
                (adapter_hbm, adapter_ref),
                (slot_hbm, slot_ref),
                (lengths_hbm, lengths_ref),
                (q_hbm, q_ref),
                (kf_hbm, kf_ref),
                (vf_hbm, vf_ref),
            ]
        )
    ]
    for copy in small + k_copies + v_copies:
        copy.start()
    adapter_copy, slot_copy, lengths_copy, q_copy, kf_copy, vf_copy = small

    at = iota((total, LANES), 0)
    order = one_hot(
        mod(at, rows) * per_row + div(at, tokens) * steps + mod(div(at, rows), steps), total
    )

    adapter_copy.wait()
    slot_copy.wait()
    lengths_copy.wait()
    me = me_ref[0]
    positions = partner_order(owners)
    row_at = mod(iota((8, tokens), 1), rows)
    row_down = mod(iota((tokens, LANES), 0), rows)
    first_slot = jnp.zeros((8, tokens), jnp.int32)
    local_of = jnp.zeros((tokens, LANES), jnp.int32)
    firsts = []
    for r in range(rows):
        slot = slot_ref[adapter_ref[r]]
        owner = jnp.int32(0)
        for d in range(1, owners):
            owner = owner + (slot >= d * resident).astype(jnp.int32)
        partner = lax.bitwise_xor(owner, me)
        first = jnp.int32(0)
        for d in range(1, owners):
            first = jnp.where(partner == positions[d], d * capacity, first)
        firsts.append(first)
        first_slot = jnp.where(row_at == r, first, first_slot)
        local_of = jnp.where(row_down == r, slot - owner * resident, local_of)
    place = first_slot
    for r in range(rows - 1):
        place = place + ((first_slot == firsts[r]) & (row_at > r)).astype(jnp.int32)
    held = owners * capacity * steps
    slot_at = iota((held, tokens), 0)
    token_at = iota((held, tokens), 1)
    pick = (
        (jnp.concatenate([place] * (held // 8), axis=0) == div(slot_at, steps))
        & (mod(slot_at, steps) == div(token_at, rows))
    ).astype(jnp.bfloat16)
    pick_ref[...] = pick
    local_hot = (local_of == iota((tokens, LANES), 1)).astype(jnp.bfloat16)
    meta = jnp.dot(pick, local_hot, preferred_element_type=jnp.float32).astype(jnp.bfloat16)

    q_copy.wait()
    by_head = jnp.concatenate(
        [
            q_ref[:, :, h * HEAD_WIDTH : (h + 1) * HEAD_WIDTH].reshape(tokens, HEAD_WIDTH)
            for h in range(heads)
        ],
        axis=0,
    )
    q_cols = jnp.dot(
        by_head.astype(jnp.float32).T.astype(jnp.bfloat16),
        order,
        preferred_element_type=jnp.float32,
    )
    lane = iota((HEAD_WIDTH, LANES), 1)
    row_of = div(lane, per_row)
    kv_of = mod(div(lane, steps * group), kv_here)

    kf_copy.wait()
    vf_copy.wait()
    kf = kf_ref[...].reshape(tokens, kv_width)
    vf = vf_ref[...].reshape(tokens, kv_width)
    token, query = iota((tokens, LANES), 0), iota((tokens, LANES), 1)
    position = iota((cache, LANES), 0)

    def scores(c):
        cols = q_cols[:, c * LANES : (c + 1) * LANES]
        by_kv = [jnp.where(kv_of == g, cols, 0.0) for g in range(kv_here)]
        fresh = jnp.dot(
            kf,
            jnp.concatenate(by_kv, axis=0).astype(jnp.bfloat16),
            preferred_element_type=jnp.float32,
        )
        live = (mod(token, rows) == div(query, per_row) + c * chunk_rows) & (
            div(token, rows) <= mod(query, steps)
        )
        fresh = jnp.where(live, fresh * scale, -jnp.inf)
        weights = jnp.concatenate(
            [jnp.where(row_of == j, q, 0.0) for j in range(chunk_rows) for q in by_kv], axis=0
        ).astype(jnp.bfloat16)
        k_copies[c].wait()
        keys = jnp.concatenate([k_ref[c * chunk_rows + j] for j in range(chunk_rows)], axis=1)
        cached = jnp.dot(keys, weights, preferred_element_type=jnp.float32)
        length = jnp.zeros((1, LANES), jnp.int32)
        for j in range(chunk_rows):
            length = jnp.where(
                div(iota((1, LANES), 1), per_row) == j, lengths_ref[c * chunk_rows + j], length
            )
        return jnp.where(position < length, cached * scale, -jnp.inf), fresh

    def softmax(cached, fresh):
        top = jnp.maximum(
            jnp.max(cached, axis=0, keepdims=True), jnp.max(fresh, axis=0, keepdims=True)
        )
        wc, wf = jnp.exp(cached - top), jnp.exp(fresh - top)
        share = 1.0 / (
            jnp.sum(wc, axis=0, keepdims=True) + jnp.sum(wf, axis=0, keepdims=True)
        )
        return (wc * share).T.astype(jnp.bfloat16), (wf * share).T.astype(jnp.bfloat16)

    kv_down = mod(div(iota((LANES, HEAD_WIDTH), 0), steps * group), kv_here)

    def values(c, cached, fresh):
        v_copies[c].wait()
        out = jnp.concatenate(
            [
                jnp.dot(
                    cached[j * per_row : (j + 1) * per_row, :],
                    v_ref[c * chunk_rows + j],
                    preferred_element_type=jnp.float32,
                )
                for j in range(chunk_rows)
            ],
            axis=0,
        ) + jnp.dot(fresh, vf, preferred_element_type=jnp.float32)
        own = out[:, :HEAD_WIDTH]
        for g in range(1, kv_here):
            own = jnp.where(kv_down == g, out[:, g * HEAD_WIDTH : (g + 1) * HEAD_WIDTH], own)
        return own.astype(jnp.bfloat16)

    scored, probs, outs = {}, {}, {}
    for c in range(chunks + 2):
        if c < chunks:
            scored[c] = scores(c)
        if 1 <= c <= chunks:
            probs[c - 1] = softmax(*scored[c - 1])
        if c >= 2:
            outs[c - 2] = values(c - 2, *probs[c - 2])

    out = jnp.dot(
        order,
        jnp.concatenate([outs[c] for c in range(chunks)], axis=0),
        preferred_element_type=jnp.float32,
    ).astype(jnp.bfloat16)
    attn = jnp.concatenate(
        [out[h * tokens : (h + 1) * tokens, :] for h in range(heads)], axis=1
    )
    attn_ref[...] = attn
    sent = jnp.dot(pick, attn, preferred_element_type=jnp.float32).astype(jnp.bfloat16)
    size = capacity * steps
    for d in range(owners):
        here = slice(d * size, (d + 1) * size)
        send_refs[d][:, :width] = sent[here, :]
        send_refs[d][:, width:] = meta[here, :]


def attend_and_pick(
    me,
    lengths,
    adapter_of_row,
    storage_slot,
    queries,
    fresh_keys,
    fresh_values,
    cached_keys,
    cached_values,
    owners,
    capacity,
    resident,
):
    steps, rows, width = queries.shape
    cache, kv_width = cached_keys.shape[1:]
    heads = width // HEAD_WIDTH
    total = rows * heads * steps
    tokens = steps * rows
    size = capacity * steps
    chunks = total // LANES
    outs = pl.pallas_call(
        functools.partial(attend_kernel, owners, capacity, resident),
        out_shape=[
            jax.ShapeDtypeStruct((tokens, width), jnp.bfloat16),
            jax.ShapeDtypeStruct((owners * size, tokens), jnp.bfloat16),
        ]
        + [jax.ShapeDtypeStruct((size, width + LANES), jnp.bfloat16)] * owners,
        in_specs=[SMEM] + [HBM] * 8,
        out_specs=[VMEM] * (2 + owners),
        scratch_shapes=[
            pltpu.SMEM(lengths.shape, jnp.int32),
            pltpu.SMEM(adapter_of_row.shape, jnp.int32),
            pltpu.SMEM(storage_slot.shape, jnp.int32),
            pltpu.VMEM(queries.shape, jnp.bfloat16),
            pltpu.VMEM(fresh_keys.shape, jnp.bfloat16),
            pltpu.VMEM(fresh_values.shape, jnp.bfloat16),
            pltpu.VMEM((rows, cache, kv_width), jnp.bfloat16),
            pltpu.VMEM((rows, cache, kv_width), jnp.bfloat16),
            pltpu.SemaphoreType.DMA((2, chunks)),
            pltpu.SemaphoreType.DMA((6,)),
        ],
        compiler_params=pltpu.CompilerParams(vmem_limit_bytes=24 * MIB),
        cost_estimate=pl.CostEstimate(
            flops=8 * total * cache * kv_width,
            bytes_accessed=4 * rows * cache * kv_width,
            transcendentals=total * cache,
        ),
        name="attend",
    )(
        me,
        *in_hbm(
            lengths,
            adapter_of_row,
            storage_slot,
            queries,
            fresh_keys,
            fresh_values,
            cached_keys,
            cached_values,
        ),
    )
    return outs[0], outs[1], outs[2:]


def project_kernel(blocks, columns, me_ref, attn_ref, w_hbm, *refs):
    *outs, w_ref, sems = refs
    outs = outs[len(outs) - len(blocks) :]
    me = me_ref[0]

    def copy(n, d):
        at = pl.multiple_of(lax.bitwise_xor(me, jnp.int32(d)) * columns, LANES)
        return pltpu.make_async_copy(w_hbm.at[:, pl.ds(at, columns)], w_ref.at[n], sems.at[n])

    copies = [copy(n, d) for n, d in enumerate(blocks)]
    for c in copies:
        c.start()
    attn = attn_ref[...]
    for n, d in enumerate(blocks):
        copies[n].wait()
        out = jnp.dot(attn, w_ref[n], preferred_element_type=jnp.float32)
        outs[n][...] = out.astype(outs[n].dtype)


def project(me, attn, weight, columns, blocks, after=()):
    tokens, width = attn.shape
    return pl.pallas_call(
        functools.partial(project_kernel, blocks, columns),
        out_shape=[
            jax.ShapeDtypeStruct((tokens, columns), jnp.bfloat16 if d % 2 else jnp.float32)
            for d in blocks
        ],
        in_specs=[SMEM, VMEM, HBM] + [ANY] * len(after),
        out_specs=[VMEM] * len(blocks),
        scratch_shapes=[
            pltpu.VMEM((len(blocks), width, columns), jnp.bfloat16),
            pltpu.SemaphoreType.DMA((len(blocks),)),
        ],
        compiler_params=pltpu.CompilerParams(vmem_limit_bytes=20 * MIB),
        cost_estimate=pl.CostEstimate(
            flops=2 * tokens * width * columns * len(blocks),
            bytes_accessed=2 * width * columns * len(blocks),
            transcendentals=0,
        ),
        name="project",
    )(me, attn, *in_hbm(weight), *after)


def down_kernel(*refs):
    (*got_refs, down_ref, mine_ref, sent_ref, mask_ref) = refs
    resident, rank, width = down_ref.shape
    wide = resident * rank
    got = jnp.concatenate([ref[...] for ref in got_refs], axis=0)
    held = got.shape[0]
    low = lax.dot_general(
        got[:, :width],
        down_ref[...].reshape(wide, width),
        (((1,), (1,)), ((), ())),
        preferred_element_type=jnp.float32,
    )
    spread = (iota((LANES, wide), 1) // rank == iota((LANES, wide), 0)).astype(jnp.bfloat16)
    mask = jnp.dot(got[:, width:], spread, preferred_element_type=jnp.float32)
    mask_ref[...] = mask.astype(jnp.bfloat16)
    low = low * mask
    pair = low[:, :LANES]
    for n in range(1, wide // LANES):
        pair = pair + low[:, n * LANES : (n + 1) * LANES]
    both = pair + pltpu.roll(pair, rank, 1)
    half = held // 2
    packed = jnp.where(iota((half, LANES), 1) < rank, both[:half, :], both[half:, :])
    mine_ref[...] = packed
    sent_ref[...] = packed.astype(jnp.bfloat16)


def down(got, factors):
    resident, rank, width = factors.shape
    held = len(got) * got[0].shape[0]
    return pl.pallas_call(
        down_kernel,
        out_shape=[
            jax.ShapeDtypeStruct((held // 2, LANES), jnp.float32),
            jax.ShapeDtypeStruct((held // 2, LANES), jnp.bfloat16),
            jax.ShapeDtypeStruct((held, resident * rank), jnp.bfloat16),
        ],
        compiler_params=pltpu.CompilerParams(vmem_limit_bytes=12 * MIB),
        cost_estimate=pl.CostEstimate(
            flops=200 * held * resident * rank * width,
            bytes_accessed=2 * resident * rank * width,
            transcendentals=0,
        ),
        name="down",
    )(*got, factors)


def up_kernel(peers, far, mine_ref, *refs):
    got_refs, (mask_ref, up_ref, *rest) = refs[:peers], refs[peers:]
    keep_refs, core_refs, outs = rest[:far], rest[far : 2 * far], rest[2 * far :]
    delta_refs, half_refs = outs[: len(outs) - far], outs[len(outs) - far :]
    resident, rank, columns = up_ref.shape
    wide = resident * rank
    total = mine_ref[...]
    for ref in got_refs:
        total = total + ref[...].astype(jnp.float32)
    other = pltpu.roll(total, rank, 1)
    first = iota(total.shape, 1) < rank
    both = jnp.concatenate(
        [jnp.where(first, total, other), jnp.where(first, other, total)], axis=0
    )
    both = jnp.concatenate([both] * (wide // LANES), axis=1)
    low = jnp.where(mask_ref[...].astype(jnp.float32) > 0.5, both, 0.0).astype(jnp.bfloat16)
    delta = jnp.dot(
        low, up_ref[...].reshape(wide, columns), preferred_element_type=jnp.float32
    ).astype(jnp.bfloat16)
    size = delta.shape[0] // len(delta_refs)
    for d, ref in enumerate(delta_refs):
        ref[...] = delta[d * size : (d + 1) * size, :]
    for ref, keep_ref, core_ref in zip(half_refs, keep_refs, core_refs, strict=True):
        ref[...] = (keep_ref[...] + core_ref[...].astype(jnp.float32)).astype(jnp.bfloat16)


def up(mine, got, mask, factors, owners, keep, got_core):
    resident, rank, columns = factors.shape
    held = mask.shape[0]
    far, tokens = len(keep), keep[0].shape[0]
    outs = pl.pallas_call(
        functools.partial(up_kernel, len(got), far),
        out_shape=[jax.ShapeDtypeStruct((held // owners, columns), jnp.bfloat16)] * owners
        + [jax.ShapeDtypeStruct((tokens, columns), jnp.bfloat16)] * far,
        compiler_params=pltpu.CompilerParams(vmem_limit_bytes=16 * MIB),
        cost_estimate=pl.CostEstimate(
            flops=200 * held * resident * rank * columns,
            bytes_accessed=2 * resident * rank * columns,
            transcendentals=0,
        ),
        name="up",
    )(mine, *got, mask, factors, *keep, *got_core)
    return outs[:owners], outs[owners:]


def finish_kernel(owners, pieces, pick_ref, *refs):
    delta_refs, (*other_refs, core_ref, base_ref, out_ref) = refs[:owners], refs[owners:]
    delta = jnp.concatenate([ref[...] for ref in delta_refs], axis=0)
    base = base_ref[...] + core_ref[...].astype(jnp.float32)
    for n in range(0, len(other_refs), pieces):
        base = base + jnp.concatenate(
            [ref[...] for ref in other_refs[n : n + pieces]], axis=1
        ).astype(jnp.float32)
    mixed = base + lax.dot_general(
        pick_ref[...], delta, (((0,), (0,)), ((), ())), preferred_element_type=jnp.float32
    )
    out_ref[...] = mixed.astype(jnp.bfloat16).reshape(out_ref.shape)


def finish(base, pick, delta, core_got, others, steps):
    tokens, columns = base.shape
    return pl.pallas_call(
        functools.partial(finish_kernel, len(delta), len(others[0])),
        out_shape=jax.ShapeDtypeStruct((steps, tokens // steps, columns), jnp.bfloat16),
        compiler_params=pltpu.CompilerParams(vmem_limit_bytes=12 * MIB),
        cost_estimate=pl.CostEstimate(
            flops=2 * tokens * pick.shape[0] * columns,
            bytes_accessed=10 * tokens * columns,
            transcendentals=0,
        ),
        name="finish",
    )(pick, *delta, *sum(others, []), core_got, base)


def body(
    queries,
    fresh_token_keys,
    fresh_token_values,
    cached_key_rows,
    cached_value_rows,
    cache_live_lengths,
    output_projection_weight,
    adapter_down_factors,
    adapter_up_factors,
    adapter_of_row,
    adapter_storage_slot,
):
    step_count, row_count, _ = queries.shape
    resident = adapter_down_factors.shape[0]
    owners = lax.axis_size("replica")
    tensors = lax.axis_size("tensor")
    capacity = max(2, 2 * row_count // owners)
    my_replica = lax.axis_index("replica").astype(jnp.int32).reshape(1)
    my_tensor = lax.axis_index("tensor").astype(jnp.int32).reshape(1)

    attn, pick, sent = attend_and_pick(
        my_replica,
        cache_live_lengths,
        adapter_of_row,
        adapter_storage_slot,
        queries,
        fresh_token_keys,
        fresh_token_values,
        cached_key_rows,
        cached_value_rows,
        owners,
        capacity,
        resident,
    )
    got = exchange_all(sent, "replica")

    columns = adapter_up_factors.shape[2]
    blocks = [*range(1, tensors, 2), *range(2, tensors, 2)]
    parts = project(my_tensor, attn, output_projection_weight, columns, blocks)
    core_got = [xor_exchange(part, "tensor", 1) for part in parts[: tensors // 2]]

    mine, low_sent, mask = down(got, adapter_down_factors)
    low_got = [xor_exchange(low_sent, "tensor", d) for d in range(1, tensors)]
    delta, halves_sent = up(
        mine,
        low_got,
        mask,
        adapter_up_factors,
        owners,
        parts[tensors // 2 :],
        core_got[1:],
    )
    delta_got = exchange_all(delta, "replica")
    others = [
        in_pieces(half, "tensor", 2 * n, 2) for n, half in enumerate(halves_sent, start=1)
    ]
    (own,) = project(
        my_tensor, attn, output_projection_weight, columns, [0], after=[delta[0]]
    )
    return finish(own, pick, delta_got, core_got[0], others, step_count)


def solution(mesh):
    in_specs = (
        P(None, ("groups", "replica"), "tensor"),
        P(None, ("groups", "replica"), "tensor"),
        P(None, ("groups", "replica"), "tensor"),
        P(("groups", "replica"), None, "tensor"),
        P(("groups", "replica"), None, "tensor"),
        P(("groups", "replica")),
        P("tensor", None),
        P(("groups", "replica"), None, "tensor"),
        P(("groups", "replica"), None, "tensor"),
        P(("groups", "replica")),
        P("groups"),
    )
    out_specs = P(None, ("groups", "replica"), "tensor")
    return jax.shard_map(body, mesh=mesh, in_specs=in_specs, out_specs=out_specs, check_vma=False)
```

```python
import functools
import math

import jax
import jax.numpy as jnp
from jax import lax
from jax.experimental import pallas as pl
from jax.experimental.pallas import tpu as pltpu
from jax.sharding import PartitionSpec as P

HEAD_WIDTH = 128
LANES = 128
META_ROWS = 16
TILE = 512
MIB = 1024 * 1024
VMEM = pl.BlockSpec(memory_space=pltpu.VMEM)
ANY = pl.BlockSpec(memory_space=pl.ANY)
HBM = pl.BlockSpec(memory_space=pltpu.HBM)


def iota(shape, dim):
    return lax.broadcasted_iota(jnp.int32, shape, dim)


def halves(n):
    if n & (n - 1):
        raise ValueError(n)
    return n.bit_length() - 1


def div(x, n):
    return lax.shift_right_logical(x, jnp.int32(halves(n)))


def mod(x, n):
    return x & ((1 << halves(n)) - 1)


def one_hot(source, width):
    lane = iota(source.shape, 1)
    return jnp.concatenate(
        [(source == lane + at).astype(jnp.bfloat16) for at in range(0, width, source.shape[1])],
        axis=1,
    )


def in_hbm(*arrays):
    return [pltpu.with_memory_space_constraint(a, pltpu.HBM) for a in arrays]


def xor_exchange(value, axis, distance):
    size = lax.axis_size(axis)
    return lax.ppermute(value, axis, [(i, i ^ distance) for i in range(size)])


def in_pieces(value, axis, distance, pieces):
    width = value.shape[-1] // pieces
    return [
        xor_exchange(value[..., n * width : (n + 1) * width], axis, distance)
        for n in range(pieces)
    ]


def partner_order(size):
    return [0, *range(size // 2, size), *range(1, size // 2)]


def exchange_all(blocks, axis):
    order = partner_order(lax.axis_size(axis))
    return [blocks[0]] + [
        xor_exchange(block, axis, distance)
        for block, distance in zip(blocks[1:], order[1:], strict=True)
    ]


def block_copy(w_hbm, dst, sem, distance):
    me = lax.axis_index("tensor")
    columns = dst.shape[-1]
    at = pl.multiple_of(lax.bitwise_xor(me, jnp.int32(distance)) * columns, LANES)
    return pltpu.make_async_copy(w_hbm.at[:, pl.ds(at, columns)], dst, sem)


def attend_kernel(
    owners,
    capacity,
    resident,
    ahead,
    lengths_hbm,
    adapter_hbm,
    slot_hbm,
    q_hbm,
    kf_hbm,
    vf_hbm,
    k_hbm,
    v_hbm,
    w_hbm,
    attn_ref,
    pick_ref,
    w_ref,
    *rest,
):
    send_refs, rest = rest[:owners], rest[owners:]
    lengths_ref, adapter_ref, slot_ref, q_ref, kf_ref, vf_ref, k_ref, v_ref = rest[:8]
    sems, small_sems, w_sems = rest[8:]
    steps, rows, width = q_ref.shape
    cache, kv_width = k_ref.shape[1:]
    heads = width // HEAD_WIDTH
    kv_here = kv_width // HEAD_WIDTH
    group = heads // kv_here
    per_row = heads * steps
    total = rows * per_row
    tokens = steps * rows
    chunks = sems.shape[1]
    chunk_rows = rows // chunks
    scale = 1.0 / math.sqrt(HEAD_WIDTH)

    def copies(src, dst, which):
        return [
            pltpu.make_async_copy(
                src.at[pl.ds(c * chunk_rows, chunk_rows)],
                dst.at[pl.ds(c * chunk_rows, chunk_rows)],
                sems.at[which, c],
            )
            for c in range(chunks)
        ]

    k_copies = copies(k_hbm, k_ref, 0)
    v_copies = copies(v_hbm, v_ref, 1)
    small = [
        pltpu.make_async_copy(src, dst, small_sems.at[n])
        for n, (src, dst) in enumerate(
            [
                (adapter_hbm, adapter_ref),
                (slot_hbm, slot_ref),
                (lengths_hbm, lengths_ref),
                (q_hbm, q_ref),
                (kf_hbm, kf_ref),
                (vf_hbm, vf_ref),
            ]
        )
    ]
    w_copies = [
        block_copy(w_hbm, w_ref.at[n], w_sems.at[n], d)
        for n, d in enumerate(ahead)
    ]
    for copy in small + k_copies + v_copies + w_copies:
        copy.start()
    adapter_copy, slot_copy, lengths_copy, q_copy, kf_copy, vf_copy = small

    at = iota((total, LANES), 0)
    order = one_hot(
        mod(at, rows) * per_row + div(at, tokens) * steps + mod(div(at, rows), steps), total
    )

    adapter_copy.wait()
    slot_copy.wait()
    lengths_copy.wait()
    me = lax.axis_index("replica")
    positions = partner_order(owners)
    row_at = mod(iota((8, tokens), 1), rows)
    row_down = mod(iota((tokens, LANES), 0), rows)
    first_slot = jnp.zeros((8, tokens), jnp.int32)
    local_of = jnp.zeros((tokens, LANES), jnp.int32)
    firsts = []
    for r in range(rows):
        slot = slot_ref[adapter_ref[r]]
        owner = jnp.int32(0)
        for d in range(1, owners):
            owner = owner + (slot >= d * resident).astype(jnp.int32)
        partner = lax.bitwise_xor(owner, me)
        first = jnp.int32(0)
        for d in range(1, owners):
            first = jnp.where(partner == positions[d], d * capacity, first)
        firsts.append(first)
        first_slot = jnp.where(row_at == r, first, first_slot)
        local_of = jnp.where(row_down == r, slot - owner * resident, local_of)
    place = first_slot
    for r in range(rows - 1):
        place = place + ((first_slot == firsts[r]) & (row_at > r)).astype(jnp.int32)
    held = owners * capacity * steps
    slot_at = iota((held, tokens), 0)
    token_at = iota((held, tokens), 1)
    pick = (
        (jnp.concatenate([place] * (held // 8), axis=0) == div(slot_at, steps))
        & (mod(slot_at, steps) == div(token_at, rows))
    ).astype(jnp.bfloat16)
    pick_ref[...] = pick
    local_hot = (local_of == iota((tokens, LANES), 1)).astype(jnp.bfloat16)
    entry = iota((owners * META_ROWS, tokens), 0)
    entry_place = mod(entry, META_ROWS)
    entry_slot = div(entry, META_ROWS) * capacity + entry_place
    entry_pick = (
        (jnp.concatenate([place] * (owners * META_ROWS // 8), axis=0) == entry_slot)
        & (entry_place < capacity)
        & (iota(entry.shape, 1) < rows)
    ).astype(jnp.bfloat16)
    meta = jnp.dot(entry_pick, local_hot, preferred_element_type=jnp.float32)

    q_copy.wait()
    by_head = jnp.concatenate(
        [
            q_ref[:, :, h * HEAD_WIDTH : (h + 1) * HEAD_WIDTH].reshape(tokens, HEAD_WIDTH)
            for h in range(heads)
        ],
        axis=0,
    )
    q_cols = jnp.dot(
        by_head.astype(jnp.float32).T.astype(jnp.bfloat16),
        order,
        preferred_element_type=jnp.float32,
    )
    lane = iota((HEAD_WIDTH, LANES), 1)
    row_of = div(lane, per_row)
    kv_of = mod(div(lane, steps * group), kv_here)

    kf_copy.wait()
    vf_copy.wait()
    kf = kf_ref[...].reshape(tokens, kv_width)
    vf = vf_ref[...].reshape(tokens, kv_width)
    token, query = iota((tokens, LANES), 0), iota((tokens, LANES), 1)
    position = iota((cache, LANES), 0)

    def scores(c):
        cols = q_cols[:, c * LANES : (c + 1) * LANES]
        by_kv = [jnp.where(kv_of == g, cols, 0.0) for g in range(kv_here)]
        fresh = jnp.dot(
            kf,
            jnp.concatenate(by_kv, axis=0).astype(jnp.bfloat16),
            preferred_element_type=jnp.float32,
        )
        live = (mod(token, rows) == div(query, per_row) + c * chunk_rows) & (
            div(token, rows) <= mod(query, steps)
        )
        fresh = jnp.where(live, fresh * scale, -jnp.inf)
        weights = jnp.concatenate(
            [jnp.where(row_of == j, q, 0.0) for j in range(chunk_rows) for q in by_kv], axis=0
        ).astype(jnp.bfloat16)
        k_copies[c].wait()
        keys = jnp.concatenate([k_ref[c * chunk_rows + j] for j in range(chunk_rows)], axis=1)
        cached = jnp.dot(keys, weights, preferred_element_type=jnp.float32)
        length = jnp.zeros((1, LANES), jnp.int32)
        for j in range(chunk_rows):
            length = jnp.where(
                div(iota((1, LANES), 1), per_row) == j, lengths_ref[c * chunk_rows + j], length
            )
        return jnp.where(position < length, cached * scale, -jnp.inf), fresh

    def softmax(cached, fresh):
        top = jnp.maximum(
            jnp.max(cached, axis=0, keepdims=True), jnp.max(fresh, axis=0, keepdims=True)
        )
        wc, wf = jnp.exp(cached - top), jnp.exp(fresh - top)
        share = 1.0 / (
            jnp.sum(wc, axis=0, keepdims=True) + jnp.sum(wf, axis=0, keepdims=True)
        )
        return (wc * share).T.astype(jnp.bfloat16), (wf * share).T.astype(jnp.bfloat16)

    kv_down = mod(div(iota((LANES, HEAD_WIDTH), 0), steps * group), kv_here)

    def values(c, cached, fresh):
        v_copies[c].wait()
        out = jnp.concatenate(
            [
                jnp.dot(
                    cached[j * per_row : (j + 1) * per_row, :],
                    v_ref[c * chunk_rows + j],
                    preferred_element_type=jnp.float32,
                )
                for j in range(chunk_rows)
            ],
            axis=0,
        ) + jnp.dot(fresh, vf, preferred_element_type=jnp.float32)
        own = out[:, :HEAD_WIDTH]
        for g in range(1, kv_here):
            own = jnp.where(kv_down == g, out[:, g * HEAD_WIDTH : (g + 1) * HEAD_WIDTH], own)
        return own.astype(jnp.bfloat16)

    scored, probs, outs = {}, {}, {}
    for c in range(chunks + 2):
        if c < chunks:
            scored[c] = scores(c)
        if 1 <= c <= chunks:
            probs[c - 1] = softmax(*scored[c - 1])
        if c >= 2:
            outs[c - 2] = values(c - 2, *probs[c - 2])

    out = jnp.dot(
        order,
        jnp.concatenate([outs[c] for c in range(chunks)], axis=0),
        preferred_element_type=jnp.float32,
    ).astype(jnp.bfloat16)
    attn = jnp.concatenate(
        [out[h * tokens : (h + 1) * tokens, :] for h in range(heads)], axis=1
    )
    attn_ref[...] = attn
    sent = jnp.dot(pick, attn, preferred_element_type=jnp.float32)
    size = capacity * steps
    for d in range(owners):
        mine = sent[d * size : (d + 1) * size, :]
        send_refs[d][...] = jnp.concatenate(
            [mine[:, h * HEAD_WIDTH : (h + 1) * HEAD_WIDTH] for h in range(heads)]
            + [meta[d * META_ROWS : (d + 1) * META_ROWS, :]],
            axis=0,
        ).astype(jnp.bfloat16)
    for copy in w_copies:
        copy.wait()


def attend_and_pick(
    lengths,
    adapter_of_row,
    storage_slot,
    queries,
    fresh_keys,
    fresh_values,
    cached_keys,
    cached_values,
    weight,
    owners,
    capacity,
    resident,
    columns,
    ahead,
):
    steps, rows, width = queries.shape
    cache, kv_width = cached_keys.shape[1:]
    heads = width // HEAD_WIDTH
    total = rows * heads * steps
    tokens = steps * rows
    size = capacity * steps
    chunks = total // LANES
    outs = pl.pallas_call(
        functools.partial(attend_kernel, owners, capacity, resident, ahead),
        out_shape=[
            jax.ShapeDtypeStruct((tokens, width), jnp.bfloat16),
            jax.ShapeDtypeStruct((owners * size, tokens), jnp.bfloat16),
            pltpu.VMEM((len(ahead), width, columns), jnp.bfloat16),
        ]
        + [jax.ShapeDtypeStruct((heads * size + META_ROWS, HEAD_WIDTH), jnp.bfloat16)] * owners,
        in_specs=[HBM] * 9,
        out_specs=[VMEM] * (3 + owners),
        scratch_shapes=[
            pltpu.SMEM(lengths.shape, jnp.int32),
            pltpu.SMEM(adapter_of_row.shape, jnp.int32),
            pltpu.SMEM(storage_slot.shape, jnp.int32),
            pltpu.VMEM(queries.shape, jnp.bfloat16),
            pltpu.VMEM(fresh_keys.shape, jnp.bfloat16),
            pltpu.VMEM(fresh_values.shape, jnp.bfloat16),
            pltpu.VMEM((rows, cache, kv_width), jnp.bfloat16),
            pltpu.VMEM((rows, cache, kv_width), jnp.bfloat16),
            pltpu.SemaphoreType.DMA((2, chunks)),
            pltpu.SemaphoreType.DMA((6,)),
            pltpu.SemaphoreType.DMA((len(ahead),)),
        ],
        compiler_params=pltpu.CompilerParams(vmem_limit_bytes=24 * MIB),
        cost_estimate=pl.CostEstimate(
            flops=8 * total * cache * kv_width,
            bytes_accessed=4 * rows * cache * kv_width,
            transcendentals=total * cache,
        ),
        name="attend",
    )(
        *in_hbm(
            lengths,
            adapter_of_row,
            storage_slot,
            queries,
            fresh_keys,
            fresh_values,
            cached_keys,
            cached_values,
            weight,
        ),
    )
    return outs[0], outs[1], outs[2], outs[3:]


def project_kernel(blocks, ahead, attn_ref, w_hbm, *refs):
    here_ref = refs[0] if ahead else None
    *outs, w_ref, sems = refs
    outs = outs[len(outs) - len(blocks) :]
    columns = w_ref.shape[-1]

    copies = [
        block_copy(w_hbm, w_ref.at[n], sems.at[n], d)
        for n, d in enumerate(blocks[ahead:])
    ]
    for copy in copies:
        copy.start()
    attn = attn_ref[...]
    for n in range(len(blocks)):
        if n >= ahead:
            copies[n - ahead].wait()
        block = here_ref.at[n] if n < ahead else w_ref.at[n - ahead]

        @pl.loop(0, columns // TILE)
        def _(i):
            cols = pl.ds(pl.multiple_of(i * TILE, TILE), TILE)
            out = jnp.dot(attn, block[:, cols], preferred_element_type=jnp.float32)
            outs[n][:, cols] = out.astype(outs[n].dtype)


def project(attn, weight, columns, blocks, here=(), after=()):
    tokens, width = attn.shape
    ahead = here[0].shape[0] if here else 0
    fetched = len(blocks) - ahead
    return pl.pallas_call(
        functools.partial(project_kernel, blocks, ahead),
        out_shape=[
            jax.ShapeDtypeStruct((tokens, columns), jnp.bfloat16 if d % 2 else jnp.float32)
            for d in blocks
        ],
        in_specs=[VMEM, HBM] + [VMEM] * len(here) + [ANY] * len(after),
        out_specs=[VMEM] * len(blocks),
        scratch_shapes=[
            pltpu.VMEM((fetched, width, columns), jnp.bfloat16),
            pltpu.SemaphoreType.DMA((fetched,)),
        ],
        compiler_params=pltpu.CompilerParams(vmem_limit_bytes=20 * MIB),
        cost_estimate=pl.CostEstimate(
            flops=2 * tokens * width * columns * len(blocks),
            bytes_accessed=2 * width * columns * len(blocks),
            transcendentals=0,
        ),
        name="project",
    )(attn, *in_hbm(weight), *here, *after)


def down_kernel(capacity, steps, *refs):
    (*got_refs, down_ref, mine_ref, sent_ref, mask_ref) = refs
    resident, rank, width = down_ref.shape
    wide = resident * rank
    heads = width // HEAD_WIDTH
    size = capacity * steps
    held = size * len(got_refs)
    got = [ref[...].astype(jnp.float32) for ref in got_refs]
    rows = jnp.concatenate(
        [
            jnp.concatenate([part[h * size : (h + 1) * size, :] for part in got], axis=0)
            for h in range(heads)
        ],
        axis=1,
    ).astype(jnp.bfloat16)
    meta = jnp.concatenate([part[heads * size :, :] for part in got], axis=0)
    spread = div(iota((LANES, wide), 1), rank) == iota((LANES, wide), 0)
    entries = meta.shape[0]
    slot, entry = iota((held, entries), 0), iota((held, entries), 1)
    of_slot = entry == div(slot, size) * META_ROWS + div(mod(slot, size), steps)
    local = jnp.dot(
        of_slot.astype(jnp.bfloat16),
        meta.astype(jnp.bfloat16),
        preferred_element_type=jnp.float32,
    )
    mask = jnp.dot(
        local.astype(jnp.bfloat16),
        spread.astype(jnp.bfloat16),
        preferred_element_type=jnp.float32,
    )
    mask_ref[...] = mask.astype(jnp.bfloat16)
    low = lax.dot_general(
        rows,
        down_ref[...].reshape(wide, width),
        (((1,), (1,)), ((), ())),
        preferred_element_type=jnp.float32,
    )
    low = low * mask
    pair = low[:, :LANES]
    for n in range(1, wide // LANES):
        pair = pair + low[:, n * LANES : (n + 1) * LANES]
    both = pair + pltpu.roll(pair, rank, 1)
    half = held // 2
    packed = jnp.where(iota((half, LANES), 1) < rank, both[:half, :], both[half:, :])
    mine_ref[...] = packed
    sent_ref[...] = packed.astype(jnp.bfloat16)


def down(got, factors, capacity, steps):
    resident, rank, width = factors.shape
    held = len(got) * capacity * steps
    return pl.pallas_call(
        functools.partial(down_kernel, capacity, steps),
        out_shape=[
            jax.ShapeDtypeStruct((held // 2, LANES), jnp.float32),
            jax.ShapeDtypeStruct((held // 2, LANES), jnp.bfloat16),
            jax.ShapeDtypeStruct((held, resident * rank), jnp.bfloat16),
        ],
        compiler_params=pltpu.CompilerParams(vmem_limit_bytes=12 * MIB),
        cost_estimate=pl.CostEstimate(
            flops=200 * held * resident * rank * width,
            bytes_accessed=2 * resident * rank * width,
            transcendentals=0,
        ),
        name="down",
    )(*got, factors)


def up_kernel(peers, far, mine_ref, *refs):
    got_refs, (mask_ref, up_ref, *rest) = refs[:peers], refs[peers:]
    keep_refs, core_refs, outs = rest[:far], rest[far : 2 * far], rest[2 * far :]
    delta_refs, half_refs = outs[: len(outs) - far], outs[len(outs) - far :]
    resident, rank, columns = up_ref.shape
    wide = resident * rank
    total = mine_ref[...]
    for ref in got_refs:
        total = total + ref[...].astype(jnp.float32)
    other = pltpu.roll(total, rank, 1)
    first = iota(total.shape, 1) < rank
    both = jnp.concatenate(
        [jnp.where(first, total, other), jnp.where(first, other, total)], axis=0
    )
    both = jnp.concatenate([both] * (wide // LANES), axis=1)
    low = jnp.where(mask_ref[...].astype(jnp.float32) > 0.5, both, 0.0).astype(jnp.bfloat16)
    delta = jnp.dot(
        low, up_ref[...].reshape(wide, columns), preferred_element_type=jnp.float32
    ).astype(jnp.bfloat16)
    size = delta.shape[0] // len(delta_refs)
    for d, ref in enumerate(delta_refs):
        ref[...] = delta[d * size : (d + 1) * size, :]
    for ref, keep_ref, core_ref in zip(half_refs, keep_refs, core_refs, strict=True):
        ref[...] = (keep_ref[...] + core_ref[...].astype(jnp.float32)).astype(jnp.bfloat16)


def up(mine, got, mask, factors, owners, keep, got_core):
    resident, rank, columns = factors.shape
    held = mask.shape[0]
    far, tokens = len(keep), keep[0].shape[0]
    outs = pl.pallas_call(
        functools.partial(up_kernel, len(got), far),
        out_shape=[jax.ShapeDtypeStruct((held // owners, columns), jnp.bfloat16)] * owners
        + [jax.ShapeDtypeStruct((tokens, columns), jnp.bfloat16)] * far,
        compiler_params=pltpu.CompilerParams(vmem_limit_bytes=16 * MIB),
        cost_estimate=pl.CostEstimate(
            flops=200 * held * resident * rank * columns,
            bytes_accessed=2 * resident * rank * columns,
            transcendentals=0,
        ),
        name="up",
    )(mine, *got, mask, factors, *keep, *got_core)
    return outs[:owners], outs[owners:]


def finish_kernel(owners, pieces, pick_ref, *refs):
    delta_refs, (*other_refs, core_ref, base_ref, out_ref) = refs[:owners], refs[owners:]
    delta = jnp.concatenate([ref[...] for ref in delta_refs], axis=0)
    base = base_ref[...] + core_ref[...].astype(jnp.float32)
    for n in range(0, len(other_refs), pieces):
        base = base + jnp.concatenate(
            [ref[...] for ref in other_refs[n : n + pieces]], axis=1
        ).astype(jnp.float32)
    mixed = base + lax.dot_general(
        pick_ref[...], delta, (((0,), (0,)), ((), ())), preferred_element_type=jnp.float32
    )
    out_ref[...] = mixed.astype(jnp.bfloat16).reshape(out_ref.shape)


def finish(base, pick, delta, core_got, others, steps):
    tokens, columns = base.shape
    return pl.pallas_call(
        functools.partial(finish_kernel, len(delta), len(others[0])),
        out_shape=jax.ShapeDtypeStruct((steps, tokens // steps, columns), jnp.bfloat16),
        compiler_params=pltpu.CompilerParams(vmem_limit_bytes=12 * MIB),
        cost_estimate=pl.CostEstimate(
            flops=2 * tokens * pick.shape[0] * columns,
            bytes_accessed=10 * tokens * columns,
            transcendentals=0,
        ),
        name="finish",
    )(pick, *delta, *sum(others, []), core_got, base)


def body(
    queries,
    fresh_token_keys,
    fresh_token_values,
    cached_key_rows,
    cached_value_rows,
    cache_live_lengths,
    output_projection_weight,
    adapter_down_factors,
    adapter_up_factors,
    adapter_of_row,
    adapter_storage_slot,
):
    step_count, row_count, _ = queries.shape
    resident = adapter_down_factors.shape[0]
    owners = lax.axis_size("replica")
    tensors = lax.axis_size("tensor")
    capacity = max(2, 2 * row_count // owners)
    columns = adapter_up_factors.shape[2]
    blocks = [*range(1, tensors, 2), *range(2, tensors, 2)]
    ahead = blocks[:2]

    attn, pick, w_here, sent = attend_and_pick(
        cache_live_lengths,
        adapter_of_row,
        adapter_storage_slot,
        queries,
        fresh_token_keys,
        fresh_token_values,
        cached_key_rows,
        cached_value_rows,
        output_projection_weight,
        owners,
        capacity,
        resident,
        columns,
        ahead,
    )
    got = exchange_all(sent, "replica")

    parts = project(attn, output_projection_weight, columns, blocks, here=[w_here])
    core_got = [xor_exchange(part, "tensor", 1) for part in parts[: tensors // 2]]

    mine, low_sent, mask = down(got, adapter_down_factors, capacity, step_count)
    low_got = [xor_exchange(low_sent, "tensor", d) for d in range(1, tensors)]
    delta, halves_sent = up(
        mine,
        low_got,
        mask,
        adapter_up_factors,
        owners,
        parts[tensors // 2 :],
        core_got[1:],
    )
    delta_got = exchange_all(delta, "replica")
    others = [
        in_pieces(half, "tensor", 2 * n, 2) for n, half in enumerate(halves_sent, start=1)
    ]
    (own,) = project(attn, output_projection_weight, columns, [0], after=[delta[0]])
    return finish(own, pick, delta_got, core_got[0], others, step_count)


def solution(mesh):
    in_specs = (
        P(None, ("groups", "replica"), "tensor"),
        P(None, ("groups", "replica"), "tensor"),
        P(None, ("groups", "replica"), "tensor"),
        P(("groups", "replica"), None, "tensor"),
        P(("groups", "replica"), None, "tensor"),
        P(("groups", "replica")),
        P("tensor", None),
        P(("groups", "replica"), None, "tensor"),
        P(("groups", "replica"), None, "tensor"),
        P(("groups", "replica")),
        P("groups"),
    )
    out_specs = P(None, ("groups", "replica"), "tensor")
    return jax.shard_map(body, mesh=mesh, in_specs=in_specs, out_specs=out_specs, check_vma=False)
```

```python
import functools
import math

import jax
import jax.numpy as jnp
from jax import lax
from jax.experimental import pallas as pl
from jax.experimental.pallas import tpu as pltpu
from jax.sharding import PartitionSpec as P

HEAD_WIDTH = 128
LANES = 128
META_ROWS = 16
TILE = 512
PIECES = 2
MIB = 1024 * 1024
VMEM = pl.BlockSpec(memory_space=pltpu.VMEM)
ANY = pl.BlockSpec(memory_space=pl.ANY)
HBM = pl.BlockSpec(memory_space=pltpu.HBM)


def iota(shape, dim):
    return lax.broadcasted_iota(jnp.int32, shape, dim)


def halves(n):
    if n & (n - 1):
        raise ValueError(n)
    return n.bit_length() - 1


def div(x, n):
    return lax.shift_right_logical(x, jnp.int32(halves(n)))


def mod(x, n):
    return x & ((1 << halves(n)) - 1)


def one_hot(source, width):
    lane = iota(source.shape, 1)
    return jnp.concatenate(
        [(source == lane + at).astype(jnp.bfloat16) for at in range(0, width, source.shape[1])],
        axis=1,
    )


def in_hbm(*arrays):
    return [pltpu.with_memory_space_constraint(a, pltpu.HBM) for a in arrays]


def xor_exchange(value, axis, distance):
    size = lax.axis_size(axis)
    return lax.ppermute(value, axis, [(i, i ^ distance) for i in range(size)])


def in_pieces(value, axis, distance, pieces):
    width = value.shape[-1] // pieces
    return [
        xor_exchange(value[..., n * width : (n + 1) * width], axis, distance)
        for n in range(pieces)
    ]


def partner_order(size):
    return [0, *range(size // 2, size), *range(1, size // 2)]


def exchange_all(blocks, axis):
    order = partner_order(lax.axis_size(axis))
    return [blocks[0]] + [
        xor_exchange(block, axis, distance)
        for block, distance in zip(blocks[1:], order[1:], strict=True)
    ]


def block_copy(w_hbm, dst, sem, distance):
    me = lax.axis_index("tensor")
    columns = dst.shape[-1]
    at = pl.multiple_of(lax.bitwise_xor(me, jnp.int32(distance)) * columns, LANES)
    return pltpu.make_async_copy(w_hbm.at[:, pl.ds(at, columns)], dst, sem)


def attend_kernel(
    owners,
    capacity,
    resident,
    ahead,
    lengths_hbm,
    adapter_hbm,
    slot_hbm,
    q_hbm,
    kf_hbm,
    vf_hbm,
    k_hbm,
    v_hbm,
    w_hbm,
    attn_ref,
    pick_ref,
    w_ref,
    *rest,
):
    send_refs, rest = rest[:owners], rest[owners:]
    lengths_ref, adapter_ref, slot_ref, q_ref, kf_ref, vf_ref, k_ref, v_ref = rest[:8]
    sems, small_sems, w_sems = rest[8:]
    steps, rows, width = q_ref.shape
    cache, kv_width = k_ref.shape[1:]
    heads = width // HEAD_WIDTH
    kv_here = kv_width // HEAD_WIDTH
    group = heads // kv_here
    per_row = heads * steps
    total = rows * per_row
    tokens = steps * rows
    chunks = sems.shape[1]
    chunk_rows = rows // chunks
    scale = 1.0 / math.sqrt(HEAD_WIDTH)

    def copies(src, dst, which):
        return [
            pltpu.make_async_copy(
                src.at[pl.ds(c * chunk_rows, chunk_rows)],
                dst.at[pl.ds(c * chunk_rows, chunk_rows)],
                sems.at[which, c],
            )
            for c in range(chunks)
        ]

    k_copies = copies(k_hbm, k_ref, 0)
    v_copies = copies(v_hbm, v_ref, 1)
    small = [
        pltpu.make_async_copy(src, dst, small_sems.at[n])
        for n, (src, dst) in enumerate(
            [
                (q_hbm, q_ref),
                (kf_hbm, kf_ref),
                (lengths_hbm, lengths_ref),
                (adapter_hbm, adapter_ref),
                (slot_hbm, slot_ref),
                (vf_hbm, vf_ref),
            ]
        )
    ]
    q_copy, kf_copy, lengths_copy, adapter_copy, slot_copy, vf_copy = small
    w_copies = [
        block_copy(w_hbm, w_ref.at[n], w_sems.at[n], d)
        for n, d in enumerate(ahead)
    ]
    for copy in [q_copy, *k_copies, *small[1:], *v_copies, *w_copies]:
        copy.start()

    at = iota((total, LANES), 0)
    order = one_hot(
        mod(at, rows) * per_row + div(at, tokens) * steps + mod(div(at, rows), steps), total
    )

    q_copy.wait()
    by_head = jnp.concatenate(
        [
            q_ref[:, :, h * HEAD_WIDTH : (h + 1) * HEAD_WIDTH].reshape(tokens, HEAD_WIDTH)
            for h in range(heads)
        ],
        axis=0,
    )
    q_cols = jnp.dot(
        by_head.astype(jnp.float32).T.astype(jnp.bfloat16),
        order,
        preferred_element_type=jnp.float32,
    )
    lane = iota((HEAD_WIDTH, LANES), 1)
    row_of = div(lane, per_row)
    kv_of = mod(div(lane, steps * group), kv_here)

    kf_copy.wait()
    kf = kf_ref[...].reshape(tokens, kv_width)
    token, query = iota((tokens, LANES), 0), iota((tokens, LANES), 1)
    position = iota((cache, LANES), 0)

    def scores(c):
        cols = q_cols[:, c * LANES : (c + 1) * LANES]
        by_kv = [jnp.where(kv_of == g, cols, 0.0) for g in range(kv_here)]
        fresh = jnp.dot(
            kf,
            jnp.concatenate(by_kv, axis=0).astype(jnp.bfloat16),
            preferred_element_type=jnp.float32,
        )
        live = (mod(token, rows) == div(query, per_row) + c * chunk_rows) & (
            div(token, rows) <= mod(query, steps)
        )
        fresh = jnp.where(live, fresh * scale, -jnp.inf)
        weights = jnp.concatenate(
            [jnp.where(row_of == j, q, 0.0) for j in range(chunk_rows) for q in by_kv], axis=0
        ).astype(jnp.bfloat16)
        k_copies[c].wait()
        keys = jnp.concatenate([k_ref[c * chunk_rows + j] for j in range(chunk_rows)], axis=1)
        cached = jnp.dot(keys, weights, preferred_element_type=jnp.float32)
        return cached * scale, fresh

    def softmax(c, cached, fresh):
        length = jnp.zeros((1, LANES), jnp.int32)
        for j in range(chunk_rows):
            length = jnp.where(
                div(iota((1, LANES), 1), per_row) == j, lengths_ref[c * chunk_rows + j], length
            )
        cached = jnp.where(position < length, cached, -jnp.inf)
        top = jnp.maximum(
            jnp.max(cached, axis=0, keepdims=True), jnp.max(fresh, axis=0, keepdims=True)
        )
        wc, wf = jnp.exp(cached - top), jnp.exp(fresh - top)
        share = 1.0 / (
            jnp.sum(wc, axis=0, keepdims=True) + jnp.sum(wf, axis=0, keepdims=True)
        )
        return (wc * share).T.astype(jnp.bfloat16), (wf * share).T.astype(jnp.bfloat16)

    kv_down = mod(div(iota((LANES, HEAD_WIDTH), 0), steps * group), kv_here)

    def values(c, cached, fresh):
        v_copies[c].wait()
        out = jnp.concatenate(
            [
                jnp.dot(
                    cached[j * per_row : (j + 1) * per_row, :],
                    v_ref[c * chunk_rows + j],
                    preferred_element_type=jnp.float32,
                )
                for j in range(chunk_rows)
            ],
            axis=0,
        ) + jnp.dot(fresh, vf, preferred_element_type=jnp.float32)
        own = out[:, :HEAD_WIDTH]
        for g in range(1, kv_here):
            own = jnp.where(kv_down == g, out[:, g * HEAD_WIDTH : (g + 1) * HEAD_WIDTH], own)
        return own.astype(jnp.bfloat16)

    scored = [scores(c) for c in range(chunks)]

    adapter_copy.wait()
    slot_copy.wait()
    me = lax.axis_index("replica")
    positions = partner_order(owners)
    row_at = mod(iota((8, tokens), 1), rows)
    row_down = mod(iota((tokens, LANES), 0), rows)
    first_slot = jnp.zeros((8, tokens), jnp.int32)
    local_of = jnp.zeros((tokens, LANES), jnp.int32)
    firsts = []
    for r in range(rows):
        slot = slot_ref[adapter_ref[r]]
        owner = jnp.int32(0)
        for d in range(1, owners):
            owner = owner + (slot >= d * resident).astype(jnp.int32)
        partner = lax.bitwise_xor(owner, me)
        first = jnp.int32(0)
        for d in range(1, owners):
            first = jnp.where(partner == positions[d], d * capacity, first)
        firsts.append(first)
        first_slot = jnp.where(row_at == r, first, first_slot)
        local_of = jnp.where(row_down == r, slot - owner * resident, local_of)
    place = first_slot
    for r in range(rows - 1):
        place = place + ((first_slot == firsts[r]) & (row_at > r)).astype(jnp.int32)
    held = owners * capacity * steps
    slot_at = iota((held, tokens), 0)
    token_at = iota((held, tokens), 1)
    pick = (
        (jnp.concatenate([place] * (held // 8), axis=0) == div(slot_at, steps))
        & (mod(slot_at, steps) == div(token_at, rows))
    ).astype(jnp.bfloat16)
    pick_ref[...] = pick
    local_hot = (local_of == iota((tokens, LANES), 1)).astype(jnp.bfloat16)
    entry = iota((owners * META_ROWS, tokens), 0)
    entry_place = mod(entry, META_ROWS)
    entry_slot = div(entry, META_ROWS) * capacity + entry_place
    entry_pick = (
        (jnp.concatenate([place] * (owners * META_ROWS // 8), axis=0) == entry_slot)
        & (entry_place < capacity)
        & (iota(entry.shape, 1) < rows)
    ).astype(jnp.bfloat16)
    meta = jnp.dot(entry_pick, local_hot, preferred_element_type=jnp.float32)

    lengths_copy.wait()
    vf_copy.wait()
    vf = vf_ref[...].reshape(tokens, kv_width)
    probs = [softmax(0, *scored[0])]
    outs = []
    for c in range(chunks):
        if c + 1 < chunks:
            probs.append(softmax(c + 1, *scored[c + 1]))
        outs.append(values(c, *probs[c]))

    out = jnp.dot(
        order,
        jnp.concatenate(outs, axis=0),
        preferred_element_type=jnp.float32,
    ).astype(jnp.bfloat16)
    attn = jnp.concatenate(
        [out[h * tokens : (h + 1) * tokens, :] for h in range(heads)], axis=1
    )
    attn_ref[...] = attn
    sent = jnp.dot(pick, attn, preferred_element_type=jnp.float32)
    size = capacity * steps
    for d in range(owners):
        mine = sent[d * size : (d + 1) * size, :]
        send_refs[d][...] = jnp.concatenate(
            [mine[:, h * HEAD_WIDTH : (h + 1) * HEAD_WIDTH] for h in range(heads)]
            + [meta[d * META_ROWS : (d + 1) * META_ROWS, :]],
            axis=0,
        ).astype(jnp.bfloat16)
    for copy in w_copies:
        copy.wait()


def attend_and_pick(
    lengths,
    adapter_of_row,
    storage_slot,
    queries,
    fresh_keys,
    fresh_values,
    cached_keys,
    cached_values,
    weight,
    owners,
    capacity,
    resident,
    columns,
    ahead,
):
    steps, rows, width = queries.shape
    cache, kv_width = cached_keys.shape[1:]
    heads = width // HEAD_WIDTH
    total = rows * heads * steps
    tokens = steps * rows
    size = capacity * steps
    chunks = total // LANES
    outs = pl.pallas_call(
        functools.partial(attend_kernel, owners, capacity, resident, ahead),
        out_shape=[
            jax.ShapeDtypeStruct((tokens, width), jnp.bfloat16),
            jax.ShapeDtypeStruct((owners * size, tokens), jnp.bfloat16),
            pltpu.VMEM((len(ahead), width, columns), jnp.bfloat16),
        ]
        + [jax.ShapeDtypeStruct((heads * size + META_ROWS, HEAD_WIDTH), jnp.bfloat16)] * owners,
        in_specs=[HBM] * 9,
        out_specs=[VMEM] * (3 + owners),
        scratch_shapes=[
            pltpu.SMEM(lengths.shape, jnp.int32),
            pltpu.SMEM(adapter_of_row.shape, jnp.int32),
            pltpu.SMEM(storage_slot.shape, jnp.int32),
            pltpu.VMEM(queries.shape, jnp.bfloat16),
            pltpu.VMEM(fresh_keys.shape, jnp.bfloat16),
            pltpu.VMEM(fresh_values.shape, jnp.bfloat16),
            pltpu.VMEM((rows, cache, kv_width), jnp.bfloat16),
            pltpu.VMEM((rows, cache, kv_width), jnp.bfloat16),
            pltpu.SemaphoreType.DMA((2, chunks)),
            pltpu.SemaphoreType.DMA((6,)),
            pltpu.SemaphoreType.DMA((len(ahead),)),
        ],
        compiler_params=pltpu.CompilerParams(vmem_limit_bytes=24 * MIB),
        cost_estimate=pl.CostEstimate(
            flops=8 * total * cache * kv_width,
            bytes_accessed=4 * rows * cache * kv_width,
            transcendentals=total * cache,
        ),
        name="attend",
    )(
        *in_hbm(
            lengths,
            adapter_of_row,
            storage_slot,
            queries,
            fresh_keys,
            fresh_values,
            cached_keys,
            cached_values,
            weight,
        ),
    )
    return outs[0], outs[1], outs[2], outs[3:]


def project_kernel(blocks, ahead, attn_ref, w_hbm, *refs):
    here_ref = refs[0] if ahead else None
    *outs, w_ref, sems = refs
    outs = outs[len(outs) - len(blocks) :]
    columns = w_ref.shape[-1]

    copies = [
        block_copy(w_hbm, w_ref.at[n], sems.at[n], d)
        for n, d in enumerate(blocks[ahead:])
    ]
    for copy in copies:
        copy.start()
    attn = attn_ref[...]
    for n in range(len(blocks)):
        if n >= ahead:
            copies[n - ahead].wait()
        block = here_ref.at[n] if n < ahead else w_ref.at[n - ahead]

        @pl.loop(0, columns // TILE)
        def _(i):
            cols = pl.ds(pl.multiple_of(i * TILE, TILE), TILE)
            out = jnp.dot(attn, block[:, cols], preferred_element_type=jnp.float32)
            outs[n][:, cols] = out.astype(outs[n].dtype)


def project(attn, weight, columns, blocks, here=(), after=()):
    tokens, width = attn.shape
    ahead = here[0].shape[0] if here else 0
    fetched = len(blocks) - ahead
    return pl.pallas_call(
        functools.partial(project_kernel, blocks, ahead),
        out_shape=[
            jax.ShapeDtypeStruct((tokens, columns), jnp.bfloat16 if d % 2 else jnp.float32)
            for d in blocks
        ],
        in_specs=[VMEM, HBM] + [VMEM] * len(here) + [ANY] * len(after),
        out_specs=[VMEM] * len(blocks),
        scratch_shapes=[
            pltpu.VMEM((fetched, width, columns), jnp.bfloat16),
            pltpu.SemaphoreType.DMA((fetched,)),
        ],
        compiler_params=pltpu.CompilerParams(vmem_limit_bytes=20 * MIB),
        cost_estimate=pl.CostEstimate(
            flops=2 * tokens * width * columns * len(blocks),
            bytes_accessed=2 * width * columns * len(blocks),
            transcendentals=0,
        ),
        name="project",
    )(attn, *in_hbm(weight), *here, *after)


def down_kernel(capacity, steps, *refs):
    (*got_refs, down_ref, mine_ref, sent_ref, mask_ref) = refs
    resident, rank, width = down_ref.shape
    wide = resident * rank
    heads = width // HEAD_WIDTH
    size = capacity * steps
    held = size * len(got_refs)
    got = [ref[...].astype(jnp.float32) for ref in got_refs]
    rows = jnp.concatenate(
        [
            jnp.concatenate([part[h * size : (h + 1) * size, :] for part in got], axis=0)
            for h in range(heads)
        ],
        axis=1,
    ).astype(jnp.bfloat16)
    meta = jnp.concatenate([part[heads * size :, :] for part in got], axis=0)
    spread = div(iota((LANES, wide), 1), rank) == iota((LANES, wide), 0)
    entries = meta.shape[0]
    slot, entry = iota((held, entries), 0), iota((held, entries), 1)
    of_slot = entry == div(slot, size) * META_ROWS + div(mod(slot, size), steps)
    local = jnp.dot(
        of_slot.astype(jnp.bfloat16),
        meta.astype(jnp.bfloat16),
        preferred_element_type=jnp.float32,
    )
    mask = jnp.dot(
        local.astype(jnp.bfloat16),
        spread.astype(jnp.bfloat16),
        preferred_element_type=jnp.float32,
    )
    mask_ref[...] = mask.astype(jnp.bfloat16)
    low = lax.dot_general(
        rows,
        down_ref[...].reshape(wide, width),
        (((1,), (1,)), ((), ())),
        preferred_element_type=jnp.float32,
    )
    low = low * mask
    pair = low[:, :LANES]
    for n in range(1, wide // LANES):
        pair = pair + low[:, n * LANES : (n + 1) * LANES]
    both = pair + pltpu.roll(pair, rank, 1)
    half = held // 2
    packed = jnp.where(iota((half, LANES), 1) < rank, both[:half, :], both[half:, :])
    mine_ref[...] = packed
    sent_ref[...] = packed.astype(jnp.bfloat16)


def down(got, factors, capacity, steps):
    resident, rank, width = factors.shape
    held = len(got) * capacity * steps
    return pl.pallas_call(
        functools.partial(down_kernel, capacity, steps),
        out_shape=[
            jax.ShapeDtypeStruct((held // 2, LANES), jnp.float32),
            jax.ShapeDtypeStruct((held // 2, LANES), jnp.bfloat16),
            jax.ShapeDtypeStruct((held, resident * rank), jnp.bfloat16),
        ],
        compiler_params=pltpu.CompilerParams(vmem_limit_bytes=12 * MIB),
        cost_estimate=pl.CostEstimate(
            flops=200 * held * resident * rank * width,
            bytes_accessed=2 * resident * rank * width,
            transcendentals=0,
        ),
        name="down",
    )(*got, factors)


def up_kernel(peers, far, mine_ref, *refs):
    got_refs, (mask_ref, up_ref, *rest) = refs[:peers], refs[peers:]
    keep_refs, core_refs, outs = rest[:far], rest[far : 2 * far], rest[2 * far :]
    delta_refs, half_refs = outs[: len(outs) - far], outs[len(outs) - far :]
    resident, rank, columns = up_ref.shape
    wide = resident * rank
    total = mine_ref[...]
    for ref in got_refs:
        total = total + ref[...].astype(jnp.float32)
    other = pltpu.roll(total, rank, 1)
    first = iota(total.shape, 1) < rank
    both = jnp.concatenate(
        [jnp.where(first, total, other), jnp.where(first, other, total)], axis=0
    )
    both = jnp.concatenate([both] * (wide // LANES), axis=1)
    low = jnp.where(mask_ref[...].astype(jnp.float32) > 0.5, both, 0.0).astype(jnp.bfloat16)
    delta = jnp.dot(
        low, up_ref[...].reshape(wide, columns), preferred_element_type=jnp.float32
    ).astype(jnp.bfloat16)
    size = delta.shape[0] // len(delta_refs)
    for d, ref in enumerate(delta_refs):
        ref[...] = delta[d * size : (d + 1) * size, :]
    for ref, keep_ref, core_ref in zip(half_refs, keep_refs, core_refs, strict=True):
        ref[...] = (keep_ref[...] + core_ref[...].astype(jnp.float32)).astype(jnp.bfloat16)


def up(mine, got, mask, factors, owners, keep, got_core):
    resident, rank, columns = factors.shape
    held = mask.shape[0]
    far, tokens = len(keep), keep[0].shape[0]
    outs = pl.pallas_call(
        functools.partial(up_kernel, len(got), far),
        out_shape=[jax.ShapeDtypeStruct((held // owners, columns), jnp.bfloat16)] * owners
        + [jax.ShapeDtypeStruct((tokens, columns), jnp.bfloat16)] * far,
        compiler_params=pltpu.CompilerParams(vmem_limit_bytes=16 * MIB),
        cost_estimate=pl.CostEstimate(
            flops=200 * held * resident * rank * columns,
            bytes_accessed=2 * resident * rank * columns,
            transcendentals=0,
        ),
        name="up",
    )(mine, *got, mask, factors, *keep, *got_core)
    return outs[:owners], outs[owners:]


def finish_kernel(owners, pieces, pick_ref, *refs):
    delta_refs, (*other_refs, core_ref, base_ref, out_hbm, out_ref, sems) = (
        refs[:owners],
        refs[owners:],
    )
    columns = base_ref.shape[1]
    width = columns // pieces
    pick = pick_ref[...]
    copies = []
    for n in range(pieces):
        cols = slice(n * width, (n + 1) * width)
        mixed = base_ref[:, cols] + core_ref[:, cols].astype(jnp.float32)
        for ref in other_refs[n::pieces]:
            mixed = mixed + ref[...].astype(jnp.float32)
        delta = jnp.concatenate([ref[:, cols] for ref in delta_refs], axis=0)
        mixed = mixed + lax.dot_general(
            pick, delta, (((0,), (0,)), ((), ())), preferred_element_type=jnp.float32
        )
        out_ref[:, :, cols] = mixed.astype(jnp.bfloat16).reshape(*out_ref.shape[:2], width)
        copies.append(
            pltpu.make_async_copy(out_ref.at[:, :, cols], out_hbm.at[:, :, cols], sems.at[n])
        )
        copies[n].start()
    for copy in copies:
        copy.wait()


def finish(base, pick, delta, core_got, others, steps, pieces):
    tokens, columns = base.shape
    shape = (steps, tokens // steps, columns)
    operands = [pick, *delta, *sum(others, []), core_got, base]
    return pl.pallas_call(
        functools.partial(finish_kernel, len(delta), pieces),
        out_shape=jax.ShapeDtypeStruct(shape, jnp.bfloat16),
        in_specs=[VMEM] * len(operands),
        out_specs=HBM,
        scratch_shapes=[
            pltpu.VMEM(shape, jnp.bfloat16),
            pltpu.SemaphoreType.DMA((pieces,)),
        ],
        compiler_params=pltpu.CompilerParams(vmem_limit_bytes=12 * MIB),
        cost_estimate=pl.CostEstimate(
            flops=2 * tokens * pick.shape[0] * columns,
            bytes_accessed=10 * tokens * columns,
            transcendentals=0,
        ),
        name="finish",
    )(*operands)


def body(
    queries,
    fresh_token_keys,
    fresh_token_values,
    cached_key_rows,
    cached_value_rows,
    cache_live_lengths,
    output_projection_weight,
    adapter_down_factors,
    adapter_up_factors,
    adapter_of_row,
    adapter_storage_slot,
):
    step_count, row_count, _ = queries.shape
    resident = adapter_down_factors.shape[0]
    owners = lax.axis_size("replica")
    tensors = lax.axis_size("tensor")
    capacity = max(2, 2 * row_count // owners)
    columns = adapter_up_factors.shape[2]
    blocks = [*range(1, tensors, 2), *range(2, tensors, 2)]
    ahead = blocks[:1]

    attn, pick, w_here, sent = attend_and_pick(
        cache_live_lengths,
        adapter_of_row,
        adapter_storage_slot,
        queries,
        fresh_token_keys,
        fresh_token_values,
        cached_key_rows,
        cached_value_rows,
        output_projection_weight,
        owners,
        capacity,
        resident,
        columns,
        ahead,
    )
    got = exchange_all(sent, "replica")

    parts = project(attn, output_projection_weight, columns, blocks, here=[w_here])
    core_got = [xor_exchange(part, "tensor", 1) for part in parts[: tensors // 2]]

    mine, low_sent, mask = down(got, adapter_down_factors, capacity, step_count)
    low_got = [xor_exchange(low_sent, "tensor", d) for d in range(1, tensors)]
    delta, halves_sent = up(
        mine,
        low_got,
        mask,
        adapter_up_factors,
        owners,
        parts[tensors // 2 :],
        core_got[1:],
    )
    delta_got = exchange_all(delta, "replica")
    others = [
        in_pieces(half, "tensor", 2 * n, PIECES) for n, half in enumerate(halves_sent, start=1)
    ]
    (own,) = project(attn, output_projection_weight, columns, [0], after=[delta[0]])
    return finish(own, pick, delta_got, core_got[0], others, step_count, PIECES)


def solution(mesh):
    in_specs = (
        P(None, ("groups", "replica"), "tensor"),
        P(None, ("groups", "replica"), "tensor"),
        P(None, ("groups", "replica"), "tensor"),
        P(("groups", "replica"), None, "tensor"),
        P(("groups", "replica"), None, "tensor"),
        P(("groups", "replica")),
        P("tensor", None),
        P(("groups", "replica"), None, "tensor"),
        P(("groups", "replica"), None, "tensor"),
        P(("groups", "replica")),
        P("groups"),
    )
    out_specs = P(None, ("groups", "replica"), "tensor")
    return jax.shard_map(body, mesh=mesh, in_specs=in_specs, out_specs=out_specs, check_vma=False)
```

```python
import functools
import math

import jax
import jax.numpy as jnp
from jax import lax
from jax.experimental import pallas as pl
from jax.experimental.pallas import tpu as pltpu
from jax.sharding import PartitionSpec as P

HEAD_WIDTH = 128
LANES = 128
META_ROWS = 16
TILE = 512
PIECES = 2
MIB = 1024 * 1024
VMEM = pl.BlockSpec(memory_space=pltpu.VMEM)
ANY = pl.BlockSpec(memory_space=pl.ANY)
HBM = pl.BlockSpec(memory_space=pltpu.HBM)


def iota(shape, dim):
    return lax.broadcasted_iota(jnp.int32, shape, dim)


def halves(n):
    if n & (n - 1):
        raise ValueError(n)
    return n.bit_length() - 1


def div(x, n):
    return lax.shift_right_logical(x, jnp.int32(halves(n)))


def mod(x, n):
    return x & ((1 << halves(n)) - 1)


def one_hot(source, width):
    lane = iota(source.shape, 1)
    return jnp.concatenate(
        [(source == lane + at).astype(jnp.bfloat16) for at in range(0, width, source.shape[1])],
        axis=1,
    )


def in_hbm(*arrays):
    return [pltpu.with_memory_space_constraint(a, pltpu.HBM) for a in arrays]


def xor_exchange(value, axis, distance):
    size = lax.axis_size(axis)
    return lax.ppermute(value, axis, [(i, i ^ distance) for i in range(size)])


def in_pieces(value, axis, distance, pieces):
    width = value.shape[-1] // pieces
    return [
        xor_exchange(value[..., n * width : (n + 1) * width], axis, distance)
        for n in range(pieces)
    ]


def partner_order(size):
    return [0, *range(size - 1, 0, -1)]


def exchange_all(blocks, axis):
    order = partner_order(lax.axis_size(axis))
    return [blocks[0]] + [
        xor_exchange(block, axis, distance)
        for block, distance in zip(blocks[1:], order[1:], strict=True)
    ]


def block_copy(w_hbm, dst, sem, distance):
    me = lax.axis_index("tensor")
    columns = dst.shape[-1]
    at = pl.multiple_of(lax.bitwise_xor(me, jnp.int32(distance)) * columns, LANES)
    return pltpu.make_async_copy(w_hbm.at[:, pl.ds(at, columns)], dst, sem)


def attend_kernel(
    owners,
    capacity,
    resident,
    ahead,
    lengths_hbm,
    adapter_hbm,
    slot_hbm,
    q_hbm,
    kf_hbm,
    vf_hbm,
    k_hbm,
    v_hbm,
    w_hbm,
    attn_ref,
    pick_ref,
    w_ref,
    *rest,
):
    send_refs, rest = rest[:owners], rest[owners:]
    lengths_ref, adapter_ref, slot_ref, q_ref, kf_ref, vf_ref, k_ref, v_ref = rest[:8]
    sems, small_sems, w_sems = rest[8:]
    steps, rows, width = q_ref.shape
    cache, kv_width = k_ref.shape[1:]
    heads = width // HEAD_WIDTH
    kv_here = kv_width // HEAD_WIDTH
    group = heads // kv_here
    per_row = heads * steps
    total = rows * per_row
    tokens = steps * rows
    chunks = sems.shape[1]
    chunk_rows = rows // chunks
    scale = 1.0 / math.sqrt(HEAD_WIDTH)

    def copies(src, dst, which):
        return [
            pltpu.make_async_copy(
                src.at[pl.ds(c * chunk_rows, chunk_rows)],
                dst.at[pl.ds(c * chunk_rows, chunk_rows)],
                sems.at[which, c],
            )
            for c in range(chunks)
        ]

    k_copies = copies(k_hbm, k_ref, 0)
    v_copies = copies(v_hbm, v_ref, 1)
    small = [
        pltpu.make_async_copy(src, dst, small_sems.at[n])
        for n, (src, dst) in enumerate(
            [
                (q_hbm, q_ref),
                (kf_hbm, kf_ref),
                (lengths_hbm, lengths_ref),
                (adapter_hbm, adapter_ref),
                (slot_hbm, slot_ref),
                (vf_hbm, vf_ref),
            ]
        )
    ]
    q_copy, kf_copy, lengths_copy, adapter_copy, slot_copy, vf_copy = small
    w_copies = [
        block_copy(w_hbm, w_ref.at[n], w_sems.at[n], d)
        for n, d in enumerate(ahead)
    ]
    for copy in [q_copy, *k_copies, *small[1:], *v_copies, *w_copies]:
        copy.start()

    at = iota((total, LANES), 0)
    order = one_hot(
        mod(at, rows) * per_row + div(at, tokens) * steps + mod(div(at, rows), steps), total
    )

    q_copy.wait()
    by_head = jnp.concatenate(
        [
            q_ref[:, :, h * HEAD_WIDTH : (h + 1) * HEAD_WIDTH].reshape(tokens, HEAD_WIDTH)
            for h in range(heads)
        ],
        axis=0,
    )
    q_cols = jnp.dot(
        by_head.astype(jnp.float32).T.astype(jnp.bfloat16),
        order,
        preferred_element_type=jnp.float32,
    )
    lane = iota((HEAD_WIDTH, LANES), 1)
    row_of = div(lane, per_row)
    kv_of = mod(div(lane, steps * group), kv_here)

    kf_copy.wait()
    kf = kf_ref[...].reshape(tokens, kv_width)
    token, query = iota((tokens, LANES), 0), iota((tokens, LANES), 1)
    position = iota((cache, LANES), 0)

    def scores(c):
        cols = q_cols[:, c * LANES : (c + 1) * LANES]
        by_kv = [jnp.where(kv_of == g, cols, 0.0) for g in range(kv_here)]
        fresh = jnp.dot(
            kf,
            jnp.concatenate(by_kv, axis=0).astype(jnp.bfloat16),
            preferred_element_type=jnp.float32,
        )
        live = (mod(token, rows) == div(query, per_row) + c * chunk_rows) & (
            div(token, rows) <= mod(query, steps)
        )
        fresh = jnp.where(live, fresh * scale, -jnp.inf)
        weights = jnp.concatenate(
            [jnp.where(row_of == j, q, 0.0) for j in range(chunk_rows) for q in by_kv], axis=0
        ).astype(jnp.bfloat16)
        k_copies[c].wait()
        keys = jnp.concatenate([k_ref[c * chunk_rows + j] for j in range(chunk_rows)], axis=1)
        cached = jnp.dot(keys, weights, preferred_element_type=jnp.float32)
        return cached * scale, fresh

    def softmax(c, cached, fresh):
        length = jnp.zeros((1, LANES), jnp.int32)
        for j in range(chunk_rows):
            length = jnp.where(
                div(iota((1, LANES), 1), per_row) == j, lengths_ref[c * chunk_rows + j], length
            )
        cached = jnp.where(position < length, cached, -jnp.inf)
        top = jnp.maximum(
            jnp.max(cached, axis=0, keepdims=True), jnp.max(fresh, axis=0, keepdims=True)
        )
        wc, wf = jnp.exp(cached - top), jnp.exp(fresh - top)
        share = 1.0 / (
            jnp.sum(wc, axis=0, keepdims=True) + jnp.sum(wf, axis=0, keepdims=True)
        )
        return (wc * share).T.astype(jnp.bfloat16), (wf * share).T.astype(jnp.bfloat16)

    kv_down = mod(div(iota((LANES, HEAD_WIDTH), 0), steps * group), kv_here)

    def values(c, cached, fresh):
        v_copies[c].wait()
        out = jnp.concatenate(
            [
                jnp.dot(
                    cached[j * per_row : (j + 1) * per_row, :],
                    v_ref[c * chunk_rows + j],
                    preferred_element_type=jnp.float32,
                )
                for j in range(chunk_rows)
            ],
            axis=0,
        ) + jnp.dot(fresh, vf, preferred_element_type=jnp.float32)
        own = out[:, :HEAD_WIDTH]
        for g in range(1, kv_here):
            own = jnp.where(kv_down == g, out[:, g * HEAD_WIDTH : (g + 1) * HEAD_WIDTH], own)
        return own.astype(jnp.bfloat16)

    scored = [scores(c) for c in range(chunks)]

    adapter_copy.wait()
    slot_copy.wait()
    me = lax.axis_index("replica")
    positions = partner_order(owners)
    row_at = mod(iota((8, tokens), 1), rows)
    row_down = mod(iota((tokens, LANES), 0), rows)
    first_slot = jnp.zeros((8, tokens), jnp.int32)
    local_of = jnp.zeros((tokens, LANES), jnp.int32)
    firsts = []
    for r in range(rows):
        slot = slot_ref[adapter_ref[r]]
        owner = jnp.int32(0)
        for d in range(1, owners):
            owner = owner + (slot >= d * resident).astype(jnp.int32)
        partner = lax.bitwise_xor(owner, me)
        first = jnp.int32(0)
        for d in range(1, owners):
            first = jnp.where(partner == positions[d], d * capacity, first)
        firsts.append(first)
        first_slot = jnp.where(row_at == r, first, first_slot)
        local_of = jnp.where(row_down == r, slot - owner * resident, local_of)
    place = first_slot
    for r in range(rows - 1):
        place = place + ((first_slot == firsts[r]) & (row_at > r)).astype(jnp.int32)
    held = owners * capacity * steps
    slot_at = iota((held, tokens), 0)
    token_at = iota((held, tokens), 1)
    pick = (
        (jnp.concatenate([place] * (held // 8), axis=0) == div(slot_at, steps))
        & (mod(slot_at, steps) == div(token_at, rows))
    ).astype(jnp.bfloat16)
    pick_ref[...] = pick
    local_hot = (local_of == iota((tokens, LANES), 1)).astype(jnp.bfloat16)
    entry = iota((owners * META_ROWS, tokens), 0)
    entry_place = mod(entry, META_ROWS)
    entry_slot = div(entry, META_ROWS) * capacity + entry_place
    entry_pick = (
        (jnp.concatenate([place] * (owners * META_ROWS // 8), axis=0) == entry_slot)
        & (entry_place < capacity)
        & (iota(entry.shape, 1) < rows)
    ).astype(jnp.bfloat16)
    meta = jnp.dot(entry_pick, local_hot, preferred_element_type=jnp.float32)

    lengths_copy.wait()
    vf_copy.wait()
    vf = vf_ref[...].reshape(tokens, kv_width)
    probs = [softmax(0, *scored[0])]
    outs = []
    for c in range(chunks):
        if c + 1 < chunks:
            probs.append(softmax(c + 1, *scored[c + 1]))
        outs.append(values(c, *probs[c]))

    out = jnp.dot(
        order,
        jnp.concatenate(outs, axis=0),
        preferred_element_type=jnp.float32,
    ).astype(jnp.bfloat16)
    attn = jnp.concatenate(
        [out[h * tokens : (h + 1) * tokens, :] for h in range(heads)], axis=1
    )
    attn_ref[...] = attn
    sent = jnp.dot(pick, attn, preferred_element_type=jnp.float32)
    size = capacity * steps
    for d in range(owners):
        mine = sent[d * size : (d + 1) * size, :]
        send_refs[d][...] = jnp.concatenate(
            [mine[:, h * HEAD_WIDTH : (h + 1) * HEAD_WIDTH] for h in range(heads)]
            + [meta[d * META_ROWS : (d + 1) * META_ROWS, :]],
            axis=0,
        ).astype(jnp.bfloat16)
    for copy in w_copies:
        copy.wait()


def attend_and_pick(
    lengths,
    adapter_of_row,
    storage_slot,
    queries,
    fresh_keys,
    fresh_values,
    cached_keys,
    cached_values,
    weight,
    owners,
    capacity,
    resident,
    columns,
    ahead,
):
    steps, rows, width = queries.shape
    cache, kv_width = cached_keys.shape[1:]
    heads = width // HEAD_WIDTH
    total = rows * heads * steps
    tokens = steps * rows
    size = capacity * steps
    chunks = total // LANES
    outs = pl.pallas_call(
        functools.partial(attend_kernel, owners, capacity, resident, ahead),
        out_shape=[
            jax.ShapeDtypeStruct((tokens, width), jnp.bfloat16),
            jax.ShapeDtypeStruct((owners * size, tokens), jnp.bfloat16),
            pltpu.VMEM((len(ahead), width, columns), jnp.bfloat16),
        ]
        + [jax.ShapeDtypeStruct((heads * size + META_ROWS, HEAD_WIDTH), jnp.bfloat16)] * owners,
        in_specs=[HBM] * 9,
        out_specs=[VMEM] * (3 + owners),
        scratch_shapes=[
            pltpu.SMEM(lengths.shape, jnp.int32),
            pltpu.SMEM(adapter_of_row.shape, jnp.int32),
            pltpu.SMEM(storage_slot.shape, jnp.int32),
            pltpu.VMEM(queries.shape, jnp.bfloat16),
            pltpu.VMEM(fresh_keys.shape, jnp.bfloat16),
            pltpu.VMEM(fresh_values.shape, jnp.bfloat16),
            pltpu.VMEM((rows, cache, kv_width), jnp.bfloat16),
            pltpu.VMEM((rows, cache, kv_width), jnp.bfloat16),
            pltpu.SemaphoreType.DMA((2, chunks)),
            pltpu.SemaphoreType.DMA((6,)),
            pltpu.SemaphoreType.DMA((len(ahead),)),
        ],
        compiler_params=pltpu.CompilerParams(vmem_limit_bytes=24 * MIB),
        cost_estimate=pl.CostEstimate(
            flops=8 * total * cache * kv_width,
            bytes_accessed=4 * rows * cache * kv_width,
            transcendentals=total * cache,
        ),
        name="attend",
    )(
        *in_hbm(
            lengths,
            adapter_of_row,
            storage_slot,
            queries,
            fresh_keys,
            fresh_values,
            cached_keys,
            cached_values,
            weight,
        ),
    )
    return outs[0], outs[1], outs[2], outs[3:]


def project_kernel(blocks, ahead, attn_ref, w_hbm, *refs):
    here_ref = refs[0] if ahead else None
    *outs, w_ref, sems = refs
    sent = sum(d % 2 for d in blocks)
    outs = outs[len(outs) - (len(blocks) - sent + (sent > 0)) :]
    columns = w_ref.shape[-1]

    copies = [
        block_copy(w_hbm, w_ref.at[n], sems.at[n], d)
        for n, d in enumerate(blocks[ahead:])
    ]
    for copy in copies:
        copy.start()
    attn = attn_ref[...]
    for n in range(len(blocks)):
        if n >= ahead:
            copies[n - ahead].wait()
        block = here_ref.at[n] if n < ahead else w_ref.at[n - ahead]

        out_ref = outs[0].at[n] if n < sent else outs[n - sent + (sent > 0)]

        @pl.loop(0, columns // TILE)
        def _(i, block=block, out_ref=out_ref):
            cols = pl.ds(pl.multiple_of(i * TILE, TILE), TILE)
            out = jnp.dot(attn, block[:, cols], preferred_element_type=jnp.float32)
            out_ref[:, cols] = out.astype(out_ref.dtype)


def project(attn, weight, columns, blocks, here=(), after=()):
    tokens, width = attn.shape
    ahead = here[0].shape[0] if here else 0
    fetched = len(blocks) - ahead
    sent = sum(d % 2 for d in blocks)
    out_shape = [jax.ShapeDtypeStruct((sent, tokens, columns), jnp.bfloat16)] * (sent > 0)
    out_shape += [jax.ShapeDtypeStruct((tokens, columns), jnp.float32)] * (len(blocks) - sent)
    return pl.pallas_call(
        functools.partial(project_kernel, blocks, ahead),
        out_shape=out_shape,
        in_specs=[VMEM, HBM] + [VMEM] * len(here) + [ANY] * len(after),
        out_specs=[VMEM] * len(out_shape),
        scratch_shapes=[
            pltpu.VMEM((fetched, width, columns), jnp.bfloat16),
            pltpu.SemaphoreType.DMA((fetched,)),
        ],
        compiler_params=pltpu.CompilerParams(vmem_limit_bytes=20 * MIB),
        cost_estimate=pl.CostEstimate(
            flops=2 * tokens * width * columns * len(blocks),
            bytes_accessed=2 * width * columns * len(blocks),
            transcendentals=0,
        ),
        name="project",
    )(attn, *in_hbm(weight), *here, *after)


def down_kernel(capacity, steps, *refs):
    (*got_refs, down_ref, mine_ref, sent_ref, mask_ref) = refs
    resident, rank, width = down_ref.shape
    wide = resident * rank
    heads = width // HEAD_WIDTH
    size = capacity * steps
    held = size * len(got_refs)
    got = [ref[...].astype(jnp.float32) for ref in got_refs]
    rows = jnp.concatenate(
        [
            jnp.concatenate([part[h * size : (h + 1) * size, :] for part in got], axis=0)
            for h in range(heads)
        ],
        axis=1,
    ).astype(jnp.bfloat16)
    meta = jnp.concatenate([part[heads * size :, :] for part in got], axis=0)
    spread = div(iota((LANES, wide), 1), rank) == iota((LANES, wide), 0)
    entries = meta.shape[0]
    slot, entry = iota((held, entries), 0), iota((held, entries), 1)
    of_slot = entry == div(slot, size) * META_ROWS + div(mod(slot, size), steps)
    local = jnp.dot(
        of_slot.astype(jnp.bfloat16),
        meta.astype(jnp.bfloat16),
        preferred_element_type=jnp.float32,
    )
    mask = jnp.dot(
        local.astype(jnp.bfloat16),
        spread.astype(jnp.bfloat16),
        preferred_element_type=jnp.float32,
    )
    mask_ref[...] = mask.astype(jnp.bfloat16)
    low = lax.dot_general(
        rows,
        down_ref[...].reshape(wide, width),
        (((1,), (1,)), ((), ())),
        preferred_element_type=jnp.float32,
    )
    low = low * mask
    pair = low[:, :LANES]
    for n in range(1, wide // LANES):
        pair = pair + low[:, n * LANES : (n + 1) * LANES]
    both = pair + pltpu.roll(pair, rank, 1)
    half = held // 2
    packed = jnp.where(iota((half, LANES), 1) < rank, both[:half, :], both[half:, :])
    mine_ref[...] = packed
    sent_ref[...] = packed.astype(jnp.bfloat16)


def down(got, factors, capacity, steps):
    resident, rank, width = factors.shape
    held = len(got) * capacity * steps
    return pl.pallas_call(
        functools.partial(down_kernel, capacity, steps),
        out_shape=[
            jax.ShapeDtypeStruct((held // 2, LANES), jnp.float32),
            jax.ShapeDtypeStruct((held // 2, LANES), jnp.bfloat16),
            jax.ShapeDtypeStruct((held, resident * rank), jnp.bfloat16),
        ],
        compiler_params=pltpu.CompilerParams(vmem_limit_bytes=12 * MIB),
        cost_estimate=pl.CostEstimate(
            flops=200 * held * resident * rank * width,
            bytes_accessed=2 * resident * rank * width,
            transcendentals=0,
        ),
        name="down",
    )(*got, factors)


def up_kernel(peers, far, mine_ref, *refs):
    got_refs, (mask_ref, up_ref, *rest) = refs[:peers], refs[peers:]
    keep_refs, (core_ref, *outs) = rest[:far], rest[far:]
    delta_refs, half_refs = outs[: len(outs) - far], outs[len(outs) - far :]
    resident, rank, columns = up_ref.shape
    wide = resident * rank
    total = mine_ref[...]
    for ref in got_refs:
        total = total + ref[...].astype(jnp.float32)
    other = pltpu.roll(total, rank, 1)
    first = iota(total.shape, 1) < rank
    both = jnp.concatenate(
        [jnp.where(first, total, other), jnp.where(first, other, total)], axis=0
    )
    both = jnp.concatenate([both] * (wide // LANES), axis=1)
    low = jnp.where(mask_ref[...].astype(jnp.float32) > 0.5, both, 0.0).astype(jnp.bfloat16)
    delta = jnp.dot(
        low, up_ref[...].reshape(wide, columns), preferred_element_type=jnp.float32
    ).astype(jnp.bfloat16)
    size = delta.shape[0] // len(delta_refs)
    for d, ref in enumerate(delta_refs):
        ref[...] = delta[d * size : (d + 1) * size, :]
    for n, (ref, keep_ref) in enumerate(zip(half_refs, keep_refs, strict=True), start=1):
        ref[...] = (keep_ref[...] + core_ref[n].astype(jnp.float32)).astype(jnp.bfloat16)


def up(mine, got, mask, factors, owners, keep, got_core):
    resident, rank, columns = factors.shape
    held = mask.shape[0]
    far, tokens = len(keep), keep[0].shape[0]
    outs = pl.pallas_call(
        functools.partial(up_kernel, len(got), far),
        out_shape=[jax.ShapeDtypeStruct((held // owners, columns), jnp.bfloat16)] * owners
        + [jax.ShapeDtypeStruct((tokens, columns), jnp.bfloat16)] * far,
        compiler_params=pltpu.CompilerParams(vmem_limit_bytes=16 * MIB),
        cost_estimate=pl.CostEstimate(
            flops=200 * held * resident * rank * columns,
            bytes_accessed=2 * resident * rank * columns,
            transcendentals=0,
        ),
        name="up",
    )(mine, *got, mask, factors, *keep, got_core)
    return outs[:owners], outs[owners:]


def finish_kernel(owners, pieces, pick_ref, *refs):
    delta_refs, (*other_refs, core_ref, base_ref, out_hbm, out_ref, sems) = (
        refs[:owners],
        refs[owners:],
    )
    columns = base_ref.shape[1]
    width = columns // pieces
    pick = pick_ref[...]
    copies = []
    for n in range(pieces):
        cols = slice(n * width, (n + 1) * width)
        mixed = base_ref[:, cols] + core_ref[0, :, cols].astype(jnp.float32)
        for ref in other_refs[n::pieces]:
            mixed = mixed + ref[...].astype(jnp.float32)
        delta = jnp.concatenate([ref[:, cols] for ref in delta_refs], axis=0)
        mixed = mixed + lax.dot_general(
            pick, delta, (((0,), (0,)), ((), ())), preferred_element_type=jnp.float32
        )
        out_ref[:, :, cols] = mixed.astype(jnp.bfloat16).reshape(*out_ref.shape[:2], width)
        copies.append(
            pltpu.make_async_copy(out_ref.at[:, :, cols], out_hbm.at[:, :, cols], sems.at[n])
        )
        copies[n].start()
    for copy in copies:
        copy.wait()


def finish(base, pick, delta, core_got, others, steps, pieces):
    tokens, columns = base.shape
    shape = (steps, tokens // steps, columns)
    operands = [pick, *delta, *sum(others, []), core_got, base]
    return pl.pallas_call(
        functools.partial(finish_kernel, len(delta), pieces),
        out_shape=jax.ShapeDtypeStruct(shape, jnp.bfloat16),
        in_specs=[VMEM] * len(operands),
        out_specs=HBM,
        scratch_shapes=[
            pltpu.VMEM(shape, jnp.bfloat16),
            pltpu.SemaphoreType.DMA((pieces,)),
        ],
        compiler_params=pltpu.CompilerParams(vmem_limit_bytes=12 * MIB),
        cost_estimate=pl.CostEstimate(
            flops=2 * tokens * pick.shape[0] * columns,
            bytes_accessed=10 * tokens * columns,
            transcendentals=0,
        ),
        name="finish",
    )(*operands)


def body(
    queries,
    fresh_token_keys,
    fresh_token_values,
    cached_key_rows,
    cached_value_rows,
    cache_live_lengths,
    output_projection_weight,
    adapter_down_factors,
    adapter_up_factors,
    adapter_of_row,
    adapter_storage_slot,
):
    step_count, row_count, _ = queries.shape
    resident = adapter_down_factors.shape[0]
    owners = lax.axis_size("replica")
    tensors = lax.axis_size("tensor")
    capacity = max(2, 2 * row_count // owners)
    columns = adapter_up_factors.shape[2]
    blocks = [*range(1, tensors, 2), *range(2, tensors, 2)]
    ahead = blocks[:2]

    attn, pick, w_here, sent = attend_and_pick(
        cache_live_lengths,
        adapter_of_row,
        adapter_storage_slot,
        queries,
        fresh_token_keys,
        fresh_token_values,
        cached_key_rows,
        cached_value_rows,
        output_projection_weight,
        owners,
        capacity,
        resident,
        columns,
        ahead,
    )
    got = exchange_all(sent, "replica")

    odd, *even = project(attn, output_projection_weight, columns, blocks, here=[w_here])
    core_got = xor_exchange(odd, "tensor", 1)

    mine, low_sent, mask = down(got, adapter_down_factors, capacity, step_count)
    low_got = [xor_exchange(low_sent, "tensor", d) for d in range(1, tensors)]
    delta, halves_sent = up(
        mine, low_got, mask, adapter_up_factors, owners, even, core_got
    )
    delta_got = exchange_all(delta, "replica")
    others = [
        in_pieces(half, "tensor", 2 * n, PIECES) for n, half in enumerate(halves_sent, start=1)
    ]
    (own,) = project(attn, output_projection_weight, columns, [0], after=[delta[0]])
    return finish(own, pick, delta_got, core_got, others, step_count, PIECES)


def solution(mesh):
    in_specs = (
        P(None, ("groups", "replica"), "tensor"),
        P(None, ("groups", "replica"), "tensor"),
        P(None, ("groups", "replica"), "tensor"),
        P(("groups", "replica"), None, "tensor"),
        P(("groups", "replica"), None, "tensor"),
        P(("groups", "replica")),
        P("tensor", None),
        P(("groups", "replica"), None, "tensor"),
        P(("groups", "replica"), None, "tensor"),
        P(("groups", "replica")),
        P("groups"),
    )
    out_specs = P(None, ("groups", "replica"), "tensor")
    return jax.shard_map(body, mesh=mesh, in_specs=in_specs, out_specs=out_specs, check_vma=False)
```

```python
import functools
import math

import jax
import jax.numpy as jnp
from jax import lax
from jax.experimental import pallas as pl
from jax.experimental.pallas import tpu as pltpu
from jax.sharding import PartitionSpec as P

HEAD_WIDTH = 128
LANES = 128
META_ROWS = 16
PIECES = 2
MIB = 1024 * 1024
VMEM = pl.BlockSpec(memory_space=pltpu.VMEM)
ANY = pl.BlockSpec(memory_space=pl.ANY)
HBM = pl.BlockSpec(memory_space=pltpu.HBM)


def iota(shape, dim):
    return lax.broadcasted_iota(jnp.int32, shape, dim)


def halves(n):
    if n & (n - 1):
        raise ValueError(n)
    return n.bit_length() - 1


def div(x, n):
    return lax.shift_right_logical(x, jnp.int32(halves(n)))


def mod(x, n):
    return x & ((1 << halves(n)) - 1)


def one_hot(source, width):
    lane = iota(source.shape, 1)
    return jnp.concatenate(
        [(source == lane + at).astype(jnp.bfloat16) for at in range(0, width, source.shape[1])],
        axis=1,
    )


def in_hbm(*arrays):
    return [pltpu.with_memory_space_constraint(a, pltpu.HBM) for a in arrays]


def xor_exchange(value, axis, distance):
    size = lax.axis_size(axis)
    return lax.ppermute(value, axis, [(i, i ^ distance) for i in range(size)])


def in_pieces(value, axis, distance, pieces):
    width = value.shape[-1] // pieces
    return [
        xor_exchange(value[..., n * width : (n + 1) * width], axis, distance)
        for n in range(pieces)
    ]


def partner_order(size):
    return [0, *range(size // 2, size), *range(1, size // 2)]


def exchange_all(blocks, axis):
    order = partner_order(lax.axis_size(axis))
    return [blocks[0]] + [
        xor_exchange(block, axis, distance)
        for block, distance in zip(blocks[1:], order[1:], strict=True)
    ]


def block_copy(w_hbm, dst, sem, distance):
    me = lax.axis_index("tensor")
    columns = dst.shape[-1]
    at = pl.multiple_of(lax.bitwise_xor(me, jnp.int32(distance)) * columns, LANES)
    return pltpu.make_async_copy(w_hbm.at[:, pl.ds(at, columns)], dst, sem)


def attend_kernel(
    owners,
    capacity,
    resident,
    ahead,
    lengths_hbm,
    adapter_hbm,
    slot_hbm,
    q_hbm,
    kf_hbm,
    vf_hbm,
    k_hbm,
    v_hbm,
    w_hbm,
    attn_ref,
    pick_ref,
    w_ref,
    *rest,
):
    send_refs, rest = rest[:owners], rest[owners:]
    lengths_ref, adapter_ref, slot_ref, q_ref, kf_ref, vf_ref, k_ref, v_ref = rest[:8]
    sems, small_sems, w_sems = rest[8:]
    steps, rows, width = q_ref.shape
    cache, kv_width = k_ref.shape[1:]
    heads = width // HEAD_WIDTH
    kv_here = kv_width // HEAD_WIDTH
    group = heads // kv_here
    per_row = heads * steps
    total = rows * per_row
    tokens = steps * rows
    chunks = sems.shape[1]
    chunk_rows = rows // chunks
    scale = 1.0 / math.sqrt(HEAD_WIDTH)

    def copies(src, dst, which):
        return [
            pltpu.make_async_copy(
                src.at[pl.ds(c * chunk_rows, chunk_rows)],
                dst.at[pl.ds(c * chunk_rows, chunk_rows)],
                sems.at[which, c],
            )
            for c in range(chunks)
        ]

    k_copies = copies(k_hbm, k_ref, 0)
    v_copies = copies(v_hbm, v_ref, 1)
    small = [
        pltpu.make_async_copy(src, dst, small_sems.at[n])
        for n, (src, dst) in enumerate(
            [
                (q_hbm, q_ref),
                (kf_hbm, kf_ref),
                (lengths_hbm, lengths_ref),
                (adapter_hbm, adapter_ref),
                (slot_hbm, slot_ref),
                (vf_hbm, vf_ref),
            ]
        )
    ]
    q_copy, kf_copy, lengths_copy, adapter_copy, slot_copy, vf_copy = small
    w_copies = [
        block_copy(w_hbm, w_ref.at[n], w_sems.at[n], d)
        for n, d in enumerate(ahead)
    ]
    for copy in [q_copy, *k_copies, *small[1:], *v_copies, *w_copies]:
        copy.start()

    at = iota((total, LANES), 0)
    order = one_hot(
        mod(at, rows) * per_row + div(at, tokens) * steps + mod(div(at, rows), steps), total
    )

    adapter_copy.wait()
    slot_copy.wait()
    me = lax.axis_index("replica")
    positions = partner_order(owners)
    row_at = mod(iota((8, tokens), 1), rows)
    row_down = mod(iota((tokens, LANES), 0), rows)
    first_slot = jnp.zeros((8, tokens), jnp.int32)
    local_of = jnp.zeros((tokens, LANES), jnp.int32)
    firsts = []
    for r in range(rows):
        slot = slot_ref[adapter_ref[r]]
        owner = jnp.int32(0)
        for d in range(1, owners):
            owner = owner + (slot >= d * resident).astype(jnp.int32)
        partner = lax.bitwise_xor(owner, me)
        first = jnp.int32(0)
        for d in range(1, owners):
            first = jnp.where(partner == positions[d], d * capacity, first)
        firsts.append(first)
        first_slot = jnp.where(row_at == r, first, first_slot)
        local_of = jnp.where(row_down == r, slot - owner * resident, local_of)
    place = first_slot
    for r in range(rows - 1):
        place = place + ((first_slot == firsts[r]) & (row_at > r)).astype(jnp.int32)
    held = owners * capacity * steps
    slot_at = iota((held, tokens), 0)
    token_at = iota((held, tokens), 1)
    pick = (
        (jnp.concatenate([place] * (held // 8), axis=0) == div(slot_at, steps))
        & (mod(slot_at, steps) == div(token_at, rows))
    ).astype(jnp.bfloat16)
    pick_ref[...] = pick
    local_hot = (local_of == iota((tokens, LANES), 1)).astype(jnp.bfloat16)
    entry = iota((owners * META_ROWS, tokens), 0)
    entry_place = mod(entry, META_ROWS)
    entry_slot = div(entry, META_ROWS) * capacity + entry_place
    entry_pick = (
        (jnp.concatenate([place] * (owners * META_ROWS // 8), axis=0) == entry_slot)
        & (entry_place < capacity)
        & (iota(entry.shape, 1) < rows)
    ).astype(jnp.bfloat16)
    meta = jnp.dot(entry_pick, local_hot, preferred_element_type=jnp.float32)

    q_copy.wait()
    by_head = jnp.concatenate(
        [
            q_ref[:, :, h * HEAD_WIDTH : (h + 1) * HEAD_WIDTH].reshape(tokens, HEAD_WIDTH)
            for h in range(heads)
        ],
        axis=0,
    )
    q_cols = jnp.dot(
        by_head.astype(jnp.float32).T.astype(jnp.bfloat16),
        order,
        preferred_element_type=jnp.float32,
    )
    lane = iota((HEAD_WIDTH, LANES), 1)
    row_of = div(lane, per_row)
    kv_of = mod(div(lane, steps * group), kv_here)

    kf_copy.wait()
    kf = kf_ref[...].reshape(tokens, kv_width)
    token, query = iota((tokens, LANES), 0), iota((tokens, LANES), 1)
    position = iota((cache, LANES), 0)

    def scores(c):
        cols = q_cols[:, c * LANES : (c + 1) * LANES]
        by_kv = [jnp.where(kv_of == g, cols, 0.0) for g in range(kv_here)]
        fresh = jnp.dot(
            kf,
            jnp.concatenate(by_kv, axis=0).astype(jnp.bfloat16),
            preferred_element_type=jnp.float32,
        )
        live = (mod(token, rows) == div(query, per_row) + c * chunk_rows) & (
            div(token, rows) <= mod(query, steps)
        )
        fresh = jnp.where(live, fresh * scale, -jnp.inf)
        weights = jnp.concatenate(
            [jnp.where(row_of == j, q, 0.0) for j in range(chunk_rows) for q in by_kv], axis=0
        ).astype(jnp.bfloat16)
        keys = jnp.concatenate([k_ref[c * chunk_rows + j] for j in range(chunk_rows)], axis=1)
        cached = jnp.dot(keys, weights, preferred_element_type=jnp.float32)
        return cached * scale, fresh

    def softmax(c, cached, fresh):
        length = jnp.zeros((1, LANES), jnp.int32)
        for j in range(chunk_rows):
            length = jnp.where(
                div(iota((1, LANES), 1), per_row) == j, lengths_ref[c * chunk_rows + j], length
            )
        cached = jnp.where(position < length, cached, -jnp.inf)
        top = jnp.maximum(
            jnp.max(cached, axis=0, keepdims=True), jnp.max(fresh, axis=0, keepdims=True)
        )
        wc, wf = jnp.exp(cached - top), jnp.exp(fresh - top)
        share = 1.0 / (
            jnp.sum(wc, axis=0, keepdims=True) + jnp.sum(wf, axis=0, keepdims=True)
        )
        return (wc * share).T.astype(jnp.bfloat16), (wf * share).T.astype(jnp.bfloat16)

    kv_down = mod(div(iota((LANES, HEAD_WIDTH), 0), steps * group), kv_here)

    def values(c, cached, fresh):
        out = jnp.concatenate(
            [
                jnp.dot(
                    cached[j * per_row : (j + 1) * per_row, :],
                    v_ref[c * chunk_rows + j],
                    preferred_element_type=jnp.float32,
                )
                for j in range(chunk_rows)
            ],
            axis=0,
        ) + jnp.dot(fresh, vf, preferred_element_type=jnp.float32)
        own = out[:, :HEAD_WIDTH]
        for g in range(1, kv_here):
            own = jnp.where(kv_down == g, out[:, g * HEAD_WIDTH : (g + 1) * HEAD_WIDTH], own)
        return own.astype(jnp.bfloat16)

    for copy in k_copies:
        copy.wait()
    scored = [scores(c) for c in range(chunks)]

    lengths_copy.wait()
    vf_copy.wait()
    for copy in v_copies:
        copy.wait()
    vf = vf_ref[...].reshape(tokens, kv_width)
    outs = [values(c, *softmax(c, *scored[c])) for c in range(chunks)]

    out = jnp.dot(
        order,
        jnp.concatenate(outs, axis=0),
        preferred_element_type=jnp.float32,
    ).astype(jnp.bfloat16)
    attn = jnp.concatenate(
        [out[h * tokens : (h + 1) * tokens, :] for h in range(heads)], axis=1
    )
    attn_ref[...] = attn
    sent = jnp.dot(pick, attn, preferred_element_type=jnp.float32)
    size = capacity * steps
    for d in range(owners):
        mine = sent[d * size : (d + 1) * size, :]
        send_refs[d][...] = jnp.concatenate(
            [mine[:, h * HEAD_WIDTH : (h + 1) * HEAD_WIDTH] for h in range(heads)]
            + [meta[d * META_ROWS : (d + 1) * META_ROWS, :]],
            axis=0,
        ).astype(jnp.bfloat16)
    for copy in w_copies:
        copy.wait()


def attend_and_pick(
    lengths,
    adapter_of_row,
    storage_slot,
    queries,
    fresh_keys,
    fresh_values,
    cached_keys,
    cached_values,
    weight,
    owners,
    capacity,
    resident,
    columns,
    ahead,
):
    steps, rows, width = queries.shape
    cache, kv_width = cached_keys.shape[1:]
    heads = width // HEAD_WIDTH
    total = rows * heads * steps
    tokens = steps * rows
    size = capacity * steps
    chunks = total // LANES
    outs = pl.pallas_call(
        functools.partial(attend_kernel, owners, capacity, resident, ahead),
        out_shape=[
            jax.ShapeDtypeStruct((tokens, width), jnp.bfloat16),
            jax.ShapeDtypeStruct((owners * size, tokens), jnp.bfloat16),
            pltpu.VMEM((len(ahead), width, columns), jnp.bfloat16),
        ]
        + [jax.ShapeDtypeStruct((heads * size + META_ROWS, HEAD_WIDTH), jnp.bfloat16)] * owners,
        in_specs=[HBM] * 9,
        out_specs=[VMEM] * (3 + owners),
        scratch_shapes=[
            pltpu.SMEM(lengths.shape, jnp.int32),
            pltpu.SMEM(adapter_of_row.shape, jnp.int32),
            pltpu.SMEM(storage_slot.shape, jnp.int32),
            pltpu.VMEM(queries.shape, jnp.bfloat16),
            pltpu.VMEM(fresh_keys.shape, jnp.bfloat16),
            pltpu.VMEM(fresh_values.shape, jnp.bfloat16),
            pltpu.VMEM((rows, cache, kv_width), jnp.bfloat16),
            pltpu.VMEM((rows, cache, kv_width), jnp.bfloat16),
            pltpu.SemaphoreType.DMA((2, chunks)),
            pltpu.SemaphoreType.DMA((6,)),
            pltpu.SemaphoreType.DMA((len(ahead),)),
        ],
        compiler_params=pltpu.CompilerParams(vmem_limit_bytes=24 * MIB),
        cost_estimate=pl.CostEstimate(
            flops=8 * total * cache * kv_width,
            bytes_accessed=4 * rows * cache * kv_width,
            transcendentals=total * cache,
        ),
        name="attend",
    )(
        *in_hbm(
            lengths,
            adapter_of_row,
            storage_slot,
            queries,
            fresh_keys,
            fresh_values,
            cached_keys,
            cached_values,
            weight,
        ),
    )
    return outs[0], outs[1], outs[2], outs[3:]


def project_kernel(blocks, ahead, attn_ref, w_hbm, *refs):
    here_ref = refs[0] if ahead else None
    *outs, w_ref, sems = refs
    sent = sum(d % 2 for d in blocks)
    outs = outs[len(outs) - (len(blocks) - sent + (sent > 0)) :]
    copies = [
        block_copy(w_hbm, w_ref.at[n], sems.at[n], d)
        for n, d in enumerate(blocks[ahead:])
    ]
    for copy in copies:
        copy.start()
    attn = attn_ref[...]
    for n in range(len(blocks)):
        if n >= ahead:
            copies[n - ahead].wait()
        block = here_ref.at[n] if n < ahead else w_ref.at[n - ahead]

        out_ref = outs[0].at[n] if n < sent else outs[n - sent + (sent > 0)]

        out = jnp.dot(attn, block[...], preferred_element_type=jnp.float32)
        out_ref[...] = out.astype(out_ref.dtype)


def project(attn, weight, columns, blocks, here=(), after=()):
    tokens, width = attn.shape
    ahead = here[0].shape[0] if here else 0
    fetched = len(blocks) - ahead
    sent = sum(d % 2 for d in blocks)
    out_shape = [jax.ShapeDtypeStruct((sent, tokens, columns), jnp.bfloat16)] * (sent > 0)
    out_shape += [jax.ShapeDtypeStruct((tokens, columns), jnp.float32)] * (len(blocks) - sent)
    return pl.pallas_call(
        functools.partial(project_kernel, blocks, ahead),
        out_shape=out_shape,
        in_specs=[VMEM, HBM] + [VMEM] * len(here) + [ANY] * len(after),
        out_specs=[VMEM] * len(out_shape),
        scratch_shapes=[
            pltpu.VMEM((fetched, width, columns), jnp.bfloat16),
            pltpu.SemaphoreType.DMA((fetched,)),
        ],
        compiler_params=pltpu.CompilerParams(vmem_limit_bytes=20 * MIB),
        cost_estimate=pl.CostEstimate(
            flops=2 * tokens * width * columns * len(blocks),
            bytes_accessed=2 * width * columns * len(blocks),
            transcendentals=0,
        ),
        name="project",
    )(attn, *in_hbm(weight), *here, *after)


def down_kernel(capacity, steps, *refs):
    (*got_refs, down_ref, mine_ref, sent_ref, mask_ref) = refs
    resident, rank, width = down_ref.shape
    wide = resident * rank
    heads = width // HEAD_WIDTH
    size = capacity * steps
    held = size * len(got_refs)
    got = [ref[...].astype(jnp.float32) for ref in got_refs]
    rows = jnp.concatenate(
        [
            jnp.concatenate([part[h * size : (h + 1) * size, :] for part in got], axis=0)
            for h in range(heads)
        ],
        axis=1,
    ).astype(jnp.bfloat16)
    meta = jnp.concatenate([part[heads * size :, :] for part in got], axis=0)
    spread = div(iota((LANES, wide), 1), rank) == iota((LANES, wide), 0)
    entries = meta.shape[0]
    slot, entry = iota((held, entries), 0), iota((held, entries), 1)
    of_slot = entry == div(slot, size) * META_ROWS + div(mod(slot, size), steps)
    local = jnp.dot(
        of_slot.astype(jnp.bfloat16),
        meta.astype(jnp.bfloat16),
        preferred_element_type=jnp.float32,
    )
    mask = jnp.dot(
        local.astype(jnp.bfloat16),
        spread.astype(jnp.bfloat16),
        preferred_element_type=jnp.float32,
    )
    mask_ref[...] = mask.astype(jnp.bfloat16)
    low = lax.dot_general(
        rows,
        down_ref[...].reshape(wide, width),
        (((1,), (1,)), ((), ())),
        preferred_element_type=jnp.float32,
    )
    low = low * mask
    pair = low[:, :LANES]
    for n in range(1, wide // LANES):
        pair = pair + low[:, n * LANES : (n + 1) * LANES]
    both = pair + pltpu.roll(pair, rank, 1)
    half = held // 2
    packed = jnp.where(iota((half, LANES), 1) < rank, both[:half, :], both[half:, :])
    mine_ref[...] = packed
    sent_ref[...] = packed.astype(jnp.bfloat16)


def down(got, factors, capacity, steps):
    resident, rank, width = factors.shape
    held = len(got) * capacity * steps
    return pl.pallas_call(
        functools.partial(down_kernel, capacity, steps),
        out_shape=[
            jax.ShapeDtypeStruct((held // 2, LANES), jnp.float32),
            jax.ShapeDtypeStruct((held // 2, LANES), jnp.bfloat16),
            jax.ShapeDtypeStruct((held, resident * rank), jnp.bfloat16),
        ],
        compiler_params=pltpu.CompilerParams(vmem_limit_bytes=12 * MIB),
        cost_estimate=pl.CostEstimate(
            flops=200 * held * resident * rank * width,
            bytes_accessed=2 * resident * rank * width,
            transcendentals=0,
        ),
        name="down",
    )(*got, factors)


def up_kernel(peers, far, mine_ref, *refs):
    got_refs, (mask_ref, up_ref, *rest) = refs[:peers], refs[peers:]
    keep_refs, (core_ref, *outs) = rest[:far], rest[far:]
    delta_refs, half_refs = outs[: len(outs) - far], outs[len(outs) - far :]
    resident, rank, columns = up_ref.shape
    wide = resident * rank
    total = mine_ref[...]
    for ref in got_refs:
        total = total + ref[...].astype(jnp.float32)
    other = pltpu.roll(total, rank, 1)
    first = iota(total.shape, 1) < rank
    both = jnp.concatenate(
        [jnp.where(first, total, other), jnp.where(first, other, total)], axis=0
    )
    both = jnp.concatenate([both] * (wide // LANES), axis=1)
    low = jnp.where(mask_ref[...].astype(jnp.float32) > 0.5, both, 0.0).astype(jnp.bfloat16)
    delta = jnp.dot(
        low, up_ref[...].reshape(wide, columns), preferred_element_type=jnp.float32
    ).astype(jnp.bfloat16)
    size = delta.shape[0] // len(delta_refs)
    for d, ref in enumerate(delta_refs):
        ref[...] = delta[d * size : (d + 1) * size, :]
    for n, (ref, keep_ref) in enumerate(zip(half_refs, keep_refs, strict=True), start=1):
        ref[...] = (keep_ref[...] + core_ref[n].astype(jnp.float32)).astype(jnp.bfloat16)


def up(mine, got, mask, factors, owners, keep, got_core):
    resident, rank, columns = factors.shape
    held = mask.shape[0]
    far, tokens = len(keep), keep[0].shape[0]
    outs = pl.pallas_call(
        functools.partial(up_kernel, len(got), far),
        out_shape=[jax.ShapeDtypeStruct((held // owners, columns), jnp.bfloat16)] * owners
        + [jax.ShapeDtypeStruct((tokens, columns), jnp.bfloat16)] * far,
        compiler_params=pltpu.CompilerParams(vmem_limit_bytes=16 * MIB),
        cost_estimate=pl.CostEstimate(
            flops=200 * held * resident * rank * columns,
            bytes_accessed=2 * resident * rank * columns,
            transcendentals=0,
        ),
        name="up",
    )(mine, *got, mask, factors, *keep, got_core)
    return outs[:owners], outs[owners:]


def finish_kernel(owners, pieces, pick_ref, *refs):
    delta_refs, (*other_refs, core_ref, base_ref, out_hbm, out_ref, sems) = (
        refs[:owners],
        refs[owners:],
    )
    columns = base_ref.shape[1]
    width = columns // pieces
    pick = pick_ref[...]
    copies = []
    for n in range(pieces):
        cols = slice(n * width, (n + 1) * width)
        mixed = base_ref[:, cols] + core_ref[0, :, cols].astype(jnp.float32)
        for ref in other_refs[n::pieces]:
            mixed = mixed + ref[...].astype(jnp.float32)
        delta = jnp.concatenate([ref[:, cols] for ref in delta_refs], axis=0)
        mixed = mixed + lax.dot_general(
            pick, delta, (((0,), (0,)), ((), ())), preferred_element_type=jnp.float32
        )
        out_ref[:, :, cols] = mixed.astype(jnp.bfloat16).reshape(*out_ref.shape[:2], width)
        copies.append(
            pltpu.make_async_copy(out_ref.at[:, :, cols], out_hbm.at[:, :, cols], sems.at[n])
        )
        copies[n].start()
    for copy in copies:
        copy.wait()


def finish(base, pick, delta, core_got, others, steps, pieces):
    tokens, columns = base.shape
    shape = (steps, tokens // steps, columns)
    operands = [pick, *delta, *sum(others, []), core_got, base]
    return pl.pallas_call(
        functools.partial(finish_kernel, len(delta), pieces),
        out_shape=jax.ShapeDtypeStruct(shape, jnp.bfloat16),
        in_specs=[VMEM] * len(operands),
        out_specs=HBM,
        scratch_shapes=[
            pltpu.VMEM(shape, jnp.bfloat16),
            pltpu.SemaphoreType.DMA((pieces,)),
        ],
        compiler_params=pltpu.CompilerParams(vmem_limit_bytes=12 * MIB),
        cost_estimate=pl.CostEstimate(
            flops=2 * tokens * pick.shape[0] * columns,
            bytes_accessed=10 * tokens * columns,
            transcendentals=0,
        ),
        name="finish",
    )(*operands)


def body(
    queries,
    fresh_token_keys,
    fresh_token_values,
    cached_key_rows,
    cached_value_rows,
    cache_live_lengths,
    output_projection_weight,
    adapter_down_factors,
    adapter_up_factors,
    adapter_of_row,
    adapter_storage_slot,
):
    step_count, row_count, _ = queries.shape
    resident = adapter_down_factors.shape[0]
    owners = lax.axis_size("replica")
    tensors = lax.axis_size("tensor")
    capacity = max(2, 2 * row_count // owners)
    columns = adapter_up_factors.shape[2]
    blocks = [*range(1, tensors, 2), *range(2, tensors, 2)]
    ahead = blocks[:2]

    attn, pick, w_here, sent = attend_and_pick(
        cache_live_lengths,
        adapter_of_row,
        adapter_storage_slot,
        queries,
        fresh_token_keys,
        fresh_token_values,
        cached_key_rows,
        cached_value_rows,
        output_projection_weight,
        owners,
        capacity,
        resident,
        columns,
        ahead,
    )
    got = exchange_all(sent, "replica")

    odd, *even = project(attn, output_projection_weight, columns, blocks, here=[w_here])
    core_got = xor_exchange(odd, "tensor", 1)

    mine, low_sent, mask = down(got, adapter_down_factors, capacity, step_count)
    low_got = [xor_exchange(low_sent, "tensor", d) for d in range(1, tensors)]
    delta, halves_sent = up(
        mine, low_got, mask, adapter_up_factors, owners, even, core_got
    )
    delta_got = exchange_all(delta, "replica")
    others = [
        in_pieces(half, "tensor", 2 * n, PIECES) for n, half in enumerate(halves_sent, start=1)
    ]
    (own,) = project(attn, output_projection_weight, columns, [0], after=[delta[0]])
    return finish(own, pick, delta_got, core_got, others, step_count, PIECES)


def solution(mesh):
    in_specs = (
        P(None, ("groups", "replica"), "tensor"),
        P(None, ("groups", "replica"), "tensor"),
        P(None, ("groups", "replica"), "tensor"),
        P(("groups", "replica"), None, "tensor"),
        P(("groups", "replica"), None, "tensor"),
        P(("groups", "replica")),
        P("tensor", None),
        P(("groups", "replica"), None, "tensor"),
        P(("groups", "replica"), None, "tensor"),
        P(("groups", "replica")),
        P("groups"),
    )
    out_specs = P(None, ("groups", "replica"), "tensor")
    return jax.shard_map(body, mesh=mesh, in_specs=in_specs, out_specs=out_specs, check_vma=False)
```

```python
import functools
import math

import jax
import jax.numpy as jnp
from jax import lax
from jax.experimental import pallas as pl
from jax.experimental.pallas import tpu as pltpu
from jax.sharding import PartitionSpec as P

HEAD_WIDTH = 128
LANES = 128
META_ROWS = 16
TILE = 512
TOGETHER = 2
ORDER_ROWS = 32
PIECES = 2
MIB = 1024 * 1024
VMEM = pl.BlockSpec(memory_space=pltpu.VMEM)
ANY = pl.BlockSpec(memory_space=pl.ANY)
HBM = pl.BlockSpec(memory_space=pltpu.HBM)


def iota(shape, dim):
    return lax.broadcasted_iota(jnp.int32, shape, dim)


def halves(n):
    if n & (n - 1):
        raise ValueError(n)
    return n.bit_length() - 1


def div(x, n):
    return lax.shift_right_logical(x, jnp.int32(halves(n)))


def mod(x, n):
    return x & ((1 << halves(n)) - 1)


def one_hot(source, width):
    lane = iota(source.shape, 1)
    return jnp.concatenate(
        [(source == lane + at).astype(jnp.bfloat16) for at in range(0, width, source.shape[1])],
        axis=1,
    )


def in_hbm(*arrays):
    return [pltpu.with_memory_space_constraint(a, pltpu.HBM) for a in arrays]


def xor_exchange(value, axis, distance):
    size = lax.axis_size(axis)
    return lax.ppermute(value, axis, [(i, i ^ distance) for i in range(size)])


def in_pieces(value, axis, distance, pieces):
    width = value.shape[-1] // pieces
    return [
        xor_exchange(value[..., n * width : (n + 1) * width], axis, distance)
        for n in range(pieces)
    ]


def partner_order(size):
    return [0, *range(size // 2, size), *range(1, size // 2)]


def exchange_all(blocks, axis):
    order = partner_order(lax.axis_size(axis))
    return [blocks[0]] + [
        xor_exchange(block, axis, distance)
        for block, distance in zip(blocks[1:], order[1:], strict=True)
    ]


def block_copy(w_hbm, dst, sem, distance):
    me = lax.axis_index("tensor")
    columns = dst.shape[-1]
    at = pl.multiple_of(lax.bitwise_xor(me, jnp.int32(distance)) * columns, LANES)
    return pltpu.make_async_copy(w_hbm.at[:, pl.ds(at, columns)], dst, sem)


def attend_kernel(
    owners,
    capacity,
    resident,
    ahead,
    lengths_hbm,
    adapter_hbm,
    slot_hbm,
    q_hbm,
    kf_hbm,
    vf_hbm,
    k_hbm,
    v_hbm,
    w_hbm,
    attn_ref,
    pick_ref,
    w_ref,
    *rest,
):
    send_refs, rest = rest[:owners], rest[owners:]
    lengths_ref, adapter_ref, slot_ref, q_ref, kf_ref, vf_ref, k_ref, v_ref = rest[:8]
    order_ref, q_cols_ref, o_ref, sems, small_sems, w_sems = rest[8:]
    steps, rows, width = q_ref.shape
    cache, kv_width = k_ref.shape[1:]
    heads = width // HEAD_WIDTH
    kv_here = kv_width // HEAD_WIDTH
    group = heads // kv_here
    per_row = heads * steps
    total = rows * per_row
    tokens = steps * rows
    chunks = sems.shape[1]
    chunk_rows = rows // chunks
    scale = 1.0 / math.sqrt(HEAD_WIDTH)

    def copies(src, dst, which):
        return [
            pltpu.make_async_copy(
                src.at[pl.ds(c * chunk_rows, chunk_rows)],
                dst.at[pl.ds(c * chunk_rows, chunk_rows)],
                sems.at[which, c],
            )
            for c in range(chunks)
        ]

    k_copies = copies(k_hbm, k_ref, 0)
    v_copies = copies(v_hbm, v_ref, 1)
    small = [
        pltpu.make_async_copy(src, dst, small_sems.at[n])
        for n, (src, dst) in enumerate(
            [
                (q_hbm, q_ref),
                (kf_hbm, kf_ref),
                (lengths_hbm, lengths_ref),
                (adapter_hbm, adapter_ref),
                (slot_hbm, slot_ref),
                (vf_hbm, vf_ref),
            ]
        )
    ]
    q_copy, kf_copy, lengths_copy, adapter_copy, slot_copy, vf_copy = small
    w_copies = [
        block_copy(w_hbm, w_ref.at[n], w_sems.at[n], d)
        for n, d in enumerate(ahead)
    ]
    for copy in [q_copy, *k_copies, *small[1:], *v_copies, *w_copies]:
        copy.start()

    @pl.loop(0, total // ORDER_ROWS)
    def _(i):
        at = iota((ORDER_ROWS, LANES), 0) + i * ORDER_ROWS
        source = mod(at, rows) * per_row + div(at, tokens) * steps + mod(div(at, rows), steps)
        here = pl.ds(pl.multiple_of(i * ORDER_ROWS, ORDER_ROWS), ORDER_ROWS)
        order_ref[here, :] = one_hot(source, total)

    adapter_copy.wait()
    slot_copy.wait()
    me = lax.axis_index("replica")
    positions = partner_order(owners)
    row_at = mod(iota((8, tokens), 1), rows)
    row_down = iota((rows, LANES), 0)
    first_slot = jnp.zeros((8, tokens), jnp.int32)
    local_of = jnp.zeros((rows, LANES), jnp.int32)
    firsts = []
    for r in range(rows):
        slot = slot_ref[adapter_ref[r]]
        owner = jnp.int32(0)
        for d in range(1, owners):
            owner = owner + (slot >= d * resident).astype(jnp.int32)
        partner = lax.bitwise_xor(owner, me)
        first = jnp.int32(0)
        for d in range(1, owners):
            first = jnp.where(partner == positions[d], d * capacity, first)
        firsts.append(first)
        first_slot = jnp.where(row_at == r, first, first_slot)
        local_of = jnp.where(row_down == r, slot - owner * resident, local_of)
    place = first_slot
    for r in range(rows - 1):
        place = place + ((first_slot == firsts[r]) & (row_at > r)).astype(jnp.int32)
    held = owners * capacity * steps
    slot_at = iota((held, tokens), 0)
    token_at = iota((held, tokens), 1)
    pick = (
        (jnp.concatenate([place] * (held // 8), axis=0) == div(slot_at, steps))
        & (mod(slot_at, steps) == div(token_at, rows))
    ).astype(jnp.bfloat16)
    pick_ref[...] = pick
    local_hot = (local_of == iota((rows, LANES), 1)).astype(jnp.bfloat16)
    entry = iota((owners * META_ROWS, rows), 0)
    entry_place = mod(entry, META_ROWS)
    entry_slot = div(entry, META_ROWS) * capacity + entry_place
    entry_pick = (
        (jnp.concatenate([place[:, :rows]] * (owners * META_ROWS // 8), axis=0) == entry_slot)
        & (entry_place < capacity)
    ).astype(jnp.bfloat16)
    meta = jnp.dot(entry_pick, local_hot, preferred_element_type=jnp.float32)

    q_copy.wait()
    by_head = jnp.concatenate(
        [
            q_ref[:, :, h * HEAD_WIDTH : (h + 1) * HEAD_WIDTH].reshape(tokens, HEAD_WIDTH)
            for h in range(heads)
        ],
        axis=0,
    )
    q_cols_ref[...] = jnp.dot(
        by_head.astype(jnp.float32).T.astype(jnp.bfloat16),
        order_ref[...],
        preferred_element_type=jnp.float32,
    )
    lane = iota((HEAD_WIDTH, LANES), 1)
    row_of = div(lane, per_row)
    kv_of = mod(div(lane, steps * group), kv_here)

    kf_copy.wait()
    kf = kf_ref[...].reshape(tokens, kv_width)
    token, query = iota((tokens, LANES), 0), iota((tokens, LANES), 1)
    position = iota((cache, LANES), 0)

    def scores(c):
        cols = q_cols_ref[:, pl.ds(pl.multiple_of(c * LANES, LANES), LANES)]
        by_kv = [jnp.where(kv_of == g, cols, 0.0) for g in range(kv_here)]
        fresh = jnp.dot(
            kf,
            jnp.concatenate(by_kv, axis=0).astype(jnp.bfloat16),
            preferred_element_type=jnp.float32,
        )
        live = (mod(token, rows) == div(query, per_row) + c * chunk_rows) & (
            div(token, rows) <= mod(query, steps)
        )
        fresh = jnp.where(live, fresh * scale, -jnp.inf)
        weights = jnp.concatenate(
            [jnp.where(row_of == j, q, 0.0) for j in range(chunk_rows) for q in by_kv], axis=0
        ).astype(jnp.bfloat16)
        keys = jnp.concatenate([k_ref[c * chunk_rows + j] for j in range(chunk_rows)], axis=1)
        cached = jnp.dot(keys, weights, preferred_element_type=jnp.float32)
        return cached * scale, fresh

    def softmax(c, cached, fresh):
        length = jnp.zeros((1, LANES), jnp.int32)
        for j in range(chunk_rows):
            length = jnp.where(
                div(iota((1, LANES), 1), per_row) == j, lengths_ref[c * chunk_rows + j], length
            )
        cached = jnp.where(position < length, cached, -jnp.inf)
        top = jnp.maximum(
            jnp.max(cached, axis=0, keepdims=True), jnp.max(fresh, axis=0, keepdims=True)
        )
        wc, wf = jnp.exp(cached - top), jnp.exp(fresh - top)
        share = 1.0 / (
            jnp.sum(wc, axis=0, keepdims=True) + jnp.sum(wf, axis=0, keepdims=True)
        )
        return (wc * share).T.astype(jnp.bfloat16), (wf * share).T.astype(jnp.bfloat16)

    kv_down = mod(div(iota((LANES, HEAD_WIDTH), 0), steps * group), kv_here)

    def values(c, cached, fresh):
        out = jnp.concatenate(
            [
                jnp.dot(
                    cached[j * per_row : (j + 1) * per_row, :],
                    v_ref[c * chunk_rows + j],
                    preferred_element_type=jnp.float32,
                )
                for j in range(chunk_rows)
            ],
            axis=0,
        ) + jnp.dot(fresh, vf, preferred_element_type=jnp.float32)
        own = out[:, :HEAD_WIDTH]
        for g in range(1, kv_here):
            own = jnp.where(kv_down == g, out[:, g * HEAD_WIDTH : (g + 1) * HEAD_WIDTH], own)
        return own.astype(jnp.bfloat16)

    lengths_copy.wait()
    vf_copy.wait()
    vf = vf_ref[...].reshape(tokens, kv_width)
    for copy in k_copies + v_copies:
        copy.wait()

    @pl.loop(0, chunks // TOGETHER)
    def _(i):
        groups = [i * TOGETHER + n for n in range(TOGETHER)]
        scored = [scores(c) for c in groups]
        probs = [softmax(c, *part) for c, part in zip(groups, scored, strict=True)]
        for c, part in zip(groups, probs, strict=True):
            o_ref[pl.ds(pl.multiple_of(c * LANES, LANES), LANES), :] = values(c, *part)

    out = jnp.dot(
        order_ref[...], o_ref[...], preferred_element_type=jnp.float32
    ).astype(jnp.bfloat16)
    attn = jnp.concatenate(
        [out[h * tokens : (h + 1) * tokens, :] for h in range(heads)], axis=1
    )
    attn_ref[...] = attn
    sent = jnp.dot(pick, attn, preferred_element_type=jnp.float32)
    size = capacity * steps
    for d in range(owners):
        mine = sent[d * size : (d + 1) * size, :]
        send_refs[d][...] = jnp.concatenate(
            [mine[:, h * HEAD_WIDTH : (h + 1) * HEAD_WIDTH] for h in range(heads)]
            + [meta[d * META_ROWS : (d + 1) * META_ROWS, :]],
            axis=0,
        ).astype(jnp.bfloat16)
    for copy in w_copies:
        copy.wait()


def attend_and_pick(
    lengths,
    adapter_of_row,
    storage_slot,
    queries,
    fresh_keys,
    fresh_values,
    cached_keys,
    cached_values,
    weight,
    owners,
    capacity,
    resident,
    columns,
    ahead,
):
    steps, rows, width = queries.shape
    cache, kv_width = cached_keys.shape[1:]
    heads = width // HEAD_WIDTH
    total = rows * heads * steps
    tokens = steps * rows
    size = capacity * steps
    chunks = total // LANES
    outs = pl.pallas_call(
        functools.partial(attend_kernel, owners, capacity, resident, ahead),
        out_shape=[
            jax.ShapeDtypeStruct((tokens, width), jnp.bfloat16),
            jax.ShapeDtypeStruct((owners * size, tokens), jnp.bfloat16),
            pltpu.VMEM((len(ahead), width, columns), jnp.bfloat16),
        ]
        + [jax.ShapeDtypeStruct((heads * size + META_ROWS, HEAD_WIDTH), jnp.bfloat16)] * owners,
        in_specs=[HBM] * 9,
        out_specs=[VMEM] * (3 + owners),
        scratch_shapes=[
            pltpu.SMEM(lengths.shape, jnp.int32),
            pltpu.SMEM(adapter_of_row.shape, jnp.int32),
            pltpu.SMEM(storage_slot.shape, jnp.int32),
            pltpu.VMEM(queries.shape, jnp.bfloat16),
            pltpu.VMEM(fresh_keys.shape, jnp.bfloat16),
            pltpu.VMEM(fresh_values.shape, jnp.bfloat16),
            pltpu.VMEM((rows, cache, kv_width), jnp.bfloat16),
            pltpu.VMEM((rows, cache, kv_width), jnp.bfloat16),
            pltpu.VMEM((total, total), jnp.bfloat16),
            pltpu.VMEM((HEAD_WIDTH, total), jnp.float32),
            pltpu.VMEM((total, HEAD_WIDTH), jnp.bfloat16),
            pltpu.SemaphoreType.DMA((2, chunks)),
            pltpu.SemaphoreType.DMA((6,)),
            pltpu.SemaphoreType.DMA((len(ahead),)),
        ],
        compiler_params=pltpu.CompilerParams(vmem_limit_bytes=24 * MIB),
        cost_estimate=pl.CostEstimate(
            flops=8 * total * cache * kv_width,
            bytes_accessed=4 * rows * cache * kv_width,
            transcendentals=total * cache,
        ),
        name="attend",
    )(
        *in_hbm(
            lengths,
            adapter_of_row,
            storage_slot,
            queries,
            fresh_keys,
            fresh_values,
            cached_keys,
            cached_values,
            weight,
        ),
    )
    return outs[0], outs[1], outs[2], outs[3:]


def project_kernel(blocks, ahead, attn_ref, w_hbm, *refs):
    here_ref = refs[0] if ahead else None
    *outs, w_ref, sems = refs
    sent = sum(d % 2 for d in blocks)
    outs = outs[len(outs) - (len(blocks) - sent + (sent > 0)) :]
    copies = [
        block_copy(w_hbm, w_ref.at[n], sems.at[n], d)
        for n, d in enumerate(blocks[ahead:])
    ]
    for copy in copies:
        copy.start()
    attn = attn_ref[...]
    for n in range(len(blocks)):
        if n >= ahead:
            copies[n - ahead].wait()
        block = here_ref.at[n] if n < ahead else w_ref.at[n - ahead]

        out_ref = outs[0].at[n] if n < sent else outs[n - sent + (sent > 0)]

        @pl.loop(0, block.shape[-1] // TILE)
        def _(i, block=block, out_ref=out_ref):
            cols = pl.ds(pl.multiple_of(i * TILE, TILE), TILE)
            out = jnp.dot(attn, block[:, cols], preferred_element_type=jnp.float32)
            out_ref[:, cols] = out.astype(out_ref.dtype)


def project(attn, weight, columns, blocks, here=(), after=()):
    tokens, width = attn.shape
    ahead = here[0].shape[0] if here else 0
    fetched = len(blocks) - ahead
    sent = sum(d % 2 for d in blocks)
    out_shape = [jax.ShapeDtypeStruct((sent, tokens, columns), jnp.bfloat16)] * (sent > 0)
    out_shape += [jax.ShapeDtypeStruct((tokens, columns), jnp.float32)] * (len(blocks) - sent)
    return pl.pallas_call(
        functools.partial(project_kernel, blocks, ahead),
        out_shape=out_shape,
        in_specs=[VMEM, HBM] + [VMEM] * len(here) + [ANY] * len(after),
        out_specs=[VMEM] * len(out_shape),
        scratch_shapes=[
            pltpu.VMEM((fetched, width, columns), jnp.bfloat16),
            pltpu.SemaphoreType.DMA((fetched,)),
        ],
        compiler_params=pltpu.CompilerParams(vmem_limit_bytes=20 * MIB),
        cost_estimate=pl.CostEstimate(
            flops=2 * tokens * width * columns * len(blocks),
            bytes_accessed=2 * width * columns * len(blocks),
            transcendentals=0,
        ),
        name="project",
    )(attn, *in_hbm(weight), *here, *after)


def down_kernel(capacity, steps, *refs):
    (*got_refs, down_ref, mine_ref, sent_ref, mask_ref) = refs
    resident, rank, width = down_ref.shape
    wide = resident * rank
    heads = width // HEAD_WIDTH
    size = capacity * steps
    held = size * len(got_refs)
    got = [ref[...].astype(jnp.float32) for ref in got_refs]
    rows = jnp.concatenate(
        [
            jnp.concatenate([part[h * size : (h + 1) * size, :] for part in got], axis=0)
            for h in range(heads)
        ],
        axis=1,
    ).astype(jnp.bfloat16)
    meta = jnp.concatenate([part[heads * size :, :] for part in got], axis=0)
    spread = div(iota((LANES, wide), 1), rank) == iota((LANES, wide), 0)
    entries = meta.shape[0]
    slot, entry = iota((held, entries), 0), iota((held, entries), 1)
    of_slot = entry == div(slot, size) * META_ROWS + div(mod(slot, size), steps)
    local = jnp.dot(
        of_slot.astype(jnp.bfloat16),
        meta.astype(jnp.bfloat16),
        preferred_element_type=jnp.float32,
    )
    mask = jnp.dot(
        local.astype(jnp.bfloat16),
        spread.astype(jnp.bfloat16),
        preferred_element_type=jnp.float32,
    )
    mask_ref[...] = mask.astype(jnp.bfloat16)
    low = lax.dot_general(
        rows,
        down_ref[...].reshape(wide, width),
        (((1,), (1,)), ((), ())),
        preferred_element_type=jnp.float32,
    )
    low = low * mask
    pair = low[:, :LANES]
    for n in range(1, wide // LANES):
        pair = pair + low[:, n * LANES : (n + 1) * LANES]
    both = pair + pltpu.roll(pair, rank, 1)
    half = held // 2
    packed = jnp.where(iota((half, LANES), 1) < rank, both[:half, :], both[half:, :])
    mine_ref[...] = packed
    sent_ref[...] = packed.astype(jnp.bfloat16)


def down(got, factors, capacity, steps):
    resident, rank, width = factors.shape
    held = len(got) * capacity * steps
    return pl.pallas_call(
        functools.partial(down_kernel, capacity, steps),
        out_shape=[
            jax.ShapeDtypeStruct((held // 2, LANES), jnp.float32),
            jax.ShapeDtypeStruct((held // 2, LANES), jnp.bfloat16),
            jax.ShapeDtypeStruct((held, resident * rank), jnp.bfloat16),
        ],
        compiler_params=pltpu.CompilerParams(vmem_limit_bytes=12 * MIB),
        cost_estimate=pl.CostEstimate(
            flops=200 * held * resident * rank * width,
            bytes_accessed=2 * resident * rank * width,
            transcendentals=0,
        ),
        name="down",
    )(*got, factors)


def up_kernel(peers, far, mine_ref, *refs):
    got_refs, (mask_ref, up_ref, *rest) = refs[:peers], refs[peers:]
    keep_refs, (core_ref, *outs) = rest[:far], rest[far:]
    delta_refs, half_refs = outs[: len(outs) - far], outs[len(outs) - far :]
    resident, rank, columns = up_ref.shape
    wide = resident * rank
    total = mine_ref[...]
    for ref in got_refs:
        total = total + ref[...].astype(jnp.float32)
    other = pltpu.roll(total, rank, 1)
    first = iota(total.shape, 1) < rank
    both = jnp.concatenate(
        [jnp.where(first, total, other), jnp.where(first, other, total)], axis=0
    )
    both = jnp.concatenate([both] * (wide // LANES), axis=1)
    low = jnp.where(mask_ref[...].astype(jnp.float32) > 0.5, both, 0.0).astype(jnp.bfloat16)
    delta = jnp.dot(
        low, up_ref[...].reshape(wide, columns), preferred_element_type=jnp.float32
    ).astype(jnp.bfloat16)
    size = delta.shape[0] // len(delta_refs)
    for d, ref in enumerate(delta_refs):
        ref[...] = delta[d * size : (d + 1) * size, :]
    for n, (ref, keep_ref) in enumerate(zip(half_refs, keep_refs, strict=True), start=1):
        ref[...] = (keep_ref[...] + core_ref[n].astype(jnp.float32)).astype(jnp.bfloat16)


def up(mine, got, mask, factors, owners, keep, got_core):
    resident, rank, columns = factors.shape
    held = mask.shape[0]
    far, tokens = len(keep), keep[0].shape[0]
    outs = pl.pallas_call(
        functools.partial(up_kernel, len(got), far),
        out_shape=[jax.ShapeDtypeStruct((held // owners, columns), jnp.bfloat16)] * owners
        + [jax.ShapeDtypeStruct((tokens, columns), jnp.bfloat16)] * far,
        compiler_params=pltpu.CompilerParams(vmem_limit_bytes=16 * MIB),
        cost_estimate=pl.CostEstimate(
            flops=200 * held * resident * rank * columns,
            bytes_accessed=2 * resident * rank * columns,
            transcendentals=0,
        ),
        name="up",
    )(mine, *got, mask, factors, *keep, got_core)
    return outs[:owners], outs[owners:]


def finish_kernel(owners, pieces, pick_ref, *refs):
    delta_refs, (*other_refs, core_ref, base_ref, out_hbm, out_ref, sems) = (
        refs[:owners],
        refs[owners:],
    )
    columns = base_ref.shape[1]
    width = columns // pieces
    pick = pick_ref[...]
    copies = []
    for n in range(pieces):
        cols = slice(n * width, (n + 1) * width)
        mixed = base_ref[:, cols] + core_ref[0, :, cols].astype(jnp.float32)
        for ref in other_refs[n::pieces]:
            mixed = mixed + ref[...].astype(jnp.float32)
        delta = jnp.concatenate([ref[:, cols] for ref in delta_refs], axis=0)
        mixed = mixed + lax.dot_general(
            pick, delta, (((0,), (0,)), ((), ())), preferred_element_type=jnp.float32
        )
        out_ref[:, :, cols] = mixed.astype(jnp.bfloat16).reshape(*out_ref.shape[:2], width)
        copies.append(
            pltpu.make_async_copy(out_ref.at[:, :, cols], out_hbm.at[:, :, cols], sems.at[n])
        )
        copies[n].start()
    for copy in copies:
        copy.wait()


def finish(base, pick, delta, core_got, others, steps, pieces):
    tokens, columns = base.shape
    shape = (steps, tokens // steps, columns)
    operands = [pick, *delta, *sum(others, []), core_got, base]
    return pl.pallas_call(
        functools.partial(finish_kernel, len(delta), pieces),
        out_shape=jax.ShapeDtypeStruct(shape, jnp.bfloat16),
        in_specs=[VMEM] * len(operands),
        out_specs=HBM,
        scratch_shapes=[
            pltpu.VMEM(shape, jnp.bfloat16),
            pltpu.SemaphoreType.DMA((pieces,)),
        ],
        compiler_params=pltpu.CompilerParams(vmem_limit_bytes=12 * MIB),
        cost_estimate=pl.CostEstimate(
            flops=2 * tokens * pick.shape[0] * columns,
            bytes_accessed=10 * tokens * columns,
            transcendentals=0,
        ),
        name="finish",
    )(*operands)


def body(
    queries,
    fresh_token_keys,
    fresh_token_values,
    cached_key_rows,
    cached_value_rows,
    cache_live_lengths,
    output_projection_weight,
    adapter_down_factors,
    adapter_up_factors,
    adapter_of_row,
    adapter_storage_slot,
):
    step_count, row_count, _ = queries.shape
    resident = adapter_down_factors.shape[0]
    owners = lax.axis_size("replica")
    tensors = lax.axis_size("tensor")
    capacity = max(2, 2 * row_count // owners)
    columns = adapter_up_factors.shape[2]
    blocks = [*range(1, tensors, 2), *range(2, tensors, 2)]
    ahead = blocks[:2]

    attn, pick, w_here, sent = attend_and_pick(
        cache_live_lengths,
        adapter_of_row,
        adapter_storage_slot,
        queries,
        fresh_token_keys,
        fresh_token_values,
        cached_key_rows,
        cached_value_rows,
        output_projection_weight,
        owners,
        capacity,
        resident,
        columns,
        ahead,
    )
    got = exchange_all(sent, "replica")

    odd, *even = project(attn, output_projection_weight, columns, blocks, here=[w_here])
    core_got = xor_exchange(odd, "tensor", 1)

    mine, low_sent, mask = down(got, adapter_down_factors, capacity, step_count)
    low_got = [xor_exchange(low_sent, "tensor", d) for d in range(1, tensors)]
    delta, halves_sent = up(
        mine, low_got, mask, adapter_up_factors, owners, even, core_got
    )
    delta_got = exchange_all(delta, "replica")
    others = [
        in_pieces(half, "tensor", 2 * n, PIECES) for n, half in enumerate(halves_sent, start=1)
    ]
    (own,) = project(attn, output_projection_weight, columns, [0], after=[delta[0]])
    return finish(own, pick, delta_got, core_got, others, step_count, PIECES)


def solution(mesh):
    in_specs = (
        P(None, ("groups", "replica"), "tensor"),
        P(None, ("groups", "replica"), "tensor"),
        P(None, ("groups", "replica"), "tensor"),
        P(("groups", "replica"), None, "tensor"),
        P(("groups", "replica"), None, "tensor"),
        P(("groups", "replica")),
        P("tensor", None),
        P(("groups", "replica"), None, "tensor"),
        P(("groups", "replica"), None, "tensor"),
        P(("groups", "replica")),
        P("groups"),
    )
    out_specs = P(None, ("groups", "replica"), "tensor")
    return jax.shard_map(body, mesh=mesh, in_specs=in_specs, out_specs=out_specs, check_vma=False)
```

```python
import functools
import math

import jax
import jax.numpy as jnp
from jax import lax
from jax.experimental import pallas as pl
from jax.experimental.pallas import tpu as pltpu
from jax.sharding import PartitionSpec as P

HEAD_WIDTH = 128
LANES = 128
META_ROWS = 16
TILE = 512
TOGETHER = 2
ORDER_ROWS = 32
PIECES = 2
MIB = 1024 * 1024
VMEM = pl.BlockSpec(memory_space=pltpu.VMEM)
ANY = pl.BlockSpec(memory_space=pl.ANY)
HBM = pl.BlockSpec(memory_space=pltpu.HBM)


def iota(shape, dim):
    return lax.broadcasted_iota(jnp.int32, shape, dim)


def halves(n):
    if n & (n - 1):
        raise ValueError(n)
    return n.bit_length() - 1


def div(x, n):
    return lax.shift_right_logical(x, jnp.int32(halves(n)))


def mod(x, n):
    return x & ((1 << halves(n)) - 1)


def one_hot(source, width):
    lane = iota(source.shape, 1)
    return jnp.concatenate(
        [(source == lane + at).astype(jnp.bfloat16) for at in range(0, width, source.shape[1])],
        axis=1,
    )


def in_hbm(*arrays):
    return [pltpu.with_memory_space_constraint(a, pltpu.HBM) for a in arrays]


def xor_exchange(value, axis, distance):
    size = lax.axis_size(axis)
    return lax.ppermute(value, axis, [(i, i ^ distance) for i in range(size)])


def in_pieces(value, axis, distance, pieces):
    width = value.shape[-1] // pieces
    return [
        xor_exchange(value[..., n * width : (n + 1) * width], axis, distance)
        for n in range(pieces)
    ]


def partner_order(size):
    return [0, *range(size // 2, size), *range(1, size // 2)]


def exchange_all(blocks, axis):
    order = partner_order(lax.axis_size(axis))
    return [blocks[0]] + [
        xor_exchange(block, axis, distance)
        for block, distance in zip(blocks[1:], order[1:], strict=True)
    ]


def block_copy(w_hbm, dst, sem, distance):
    me = lax.axis_index("tensor")
    columns = dst.shape[-1]
    at = pl.multiple_of(lax.bitwise_xor(me, jnp.int32(distance)) * columns, LANES)
    return pltpu.make_async_copy(w_hbm.at[:, pl.ds(at, columns)], dst, sem)


def attend_kernel(
    owners,
    capacity,
    resident,
    ahead,
    lengths_hbm,
    adapter_hbm,
    slot_hbm,
    q_hbm,
    kf_hbm,
    vf_hbm,
    k_hbm,
    v_hbm,
    w_hbm,
    attn_ref,
    pick_ref,
    w_ref,
    *rest,
):
    send_refs, rest = rest[:owners], rest[owners:]
    lengths_ref, adapter_ref, slot_ref, q_ref, kf_ref, vf_ref, k_ref, v_ref = rest[:8]
    order_ref, q_cols_ref, o_ref, sems, small_sems, w_sems = rest[8:]
    steps, rows, width = q_ref.shape
    cache, kv_width = k_ref.shape[1:]
    heads = width // HEAD_WIDTH
    kv_here = kv_width // HEAD_WIDTH
    group = heads // kv_here
    per_row = heads * steps
    total = rows * per_row
    tokens = steps * rows
    chunks = sems.shape[1]
    chunk_rows = rows // chunks
    scale = 1.0 / math.sqrt(HEAD_WIDTH)

    def copies(src, dst, which):
        return [
            pltpu.make_async_copy(
                src.at[pl.ds(c * chunk_rows, chunk_rows)],
                dst.at[pl.ds(c * chunk_rows, chunk_rows)],
                sems.at[which, c],
            )
            for c in range(chunks)
        ]

    k_copies = copies(k_hbm, k_ref, 0)
    v_copies = copies(v_hbm, v_ref, 1)
    small = [
        pltpu.make_async_copy(src, dst, small_sems.at[n])
        for n, (src, dst) in enumerate(
            [
                (q_hbm, q_ref),
                (kf_hbm, kf_ref),
                (lengths_hbm, lengths_ref),
                (adapter_hbm, adapter_ref),
                (slot_hbm, slot_ref),
                (vf_hbm, vf_ref),
            ]
        )
    ]
    q_copy, kf_copy, lengths_copy, adapter_copy, slot_copy, vf_copy = small
    w_copies = [
        block_copy(w_hbm, w_ref.at[n], w_sems.at[n], d)
        for n, d in enumerate(ahead)
    ]
    for copy in [q_copy, *k_copies, *small[1:], *v_copies]:
        copy.start()

    @pl.loop(0, total // ORDER_ROWS)
    def _(i):
        at = iota((ORDER_ROWS, LANES), 0) + i * ORDER_ROWS
        source = mod(at, rows) * per_row + div(at, tokens) * steps + mod(div(at, rows), steps)
        here = pl.ds(pl.multiple_of(i * ORDER_ROWS, ORDER_ROWS), ORDER_ROWS)
        order_ref[here, :] = one_hot(source, total)

    adapter_copy.wait()
    slot_copy.wait()
    me = lax.axis_index("replica")
    positions = partner_order(owners)
    row_at = mod(iota((8, tokens), 1), rows)
    row_down = iota((rows, LANES), 0)
    first_slot = jnp.zeros((8, tokens), jnp.int32)
    local_of = jnp.zeros((rows, LANES), jnp.int32)
    firsts = []
    for r in range(rows):
        slot = slot_ref[adapter_ref[r]]
        owner = jnp.int32(0)
        for d in range(1, owners):
            owner = owner + (slot >= d * resident).astype(jnp.int32)
        partner = lax.bitwise_xor(owner, me)
        first = jnp.int32(0)
        for d in range(1, owners):
            first = jnp.where(partner == positions[d], d * capacity, first)
        firsts.append(first)
        first_slot = jnp.where(row_at == r, first, first_slot)
        local_of = jnp.where(row_down == r, slot - owner * resident, local_of)
    place = first_slot
    for r in range(rows - 1):
        place = place + ((first_slot == firsts[r]) & (row_at > r)).astype(jnp.int32)
    held = owners * capacity * steps
    slot_at = iota((held, tokens), 0)
    token_at = iota((held, tokens), 1)
    pick = (
        (jnp.concatenate([place] * (held // 8), axis=0) == div(slot_at, steps))
        & (mod(slot_at, steps) == div(token_at, rows))
    ).astype(jnp.bfloat16)
    pick_ref[...] = pick
    local_hot = (local_of == iota((rows, LANES), 1)).astype(jnp.bfloat16)
    entry = iota((owners * META_ROWS, rows), 0)
    entry_place = mod(entry, META_ROWS)
    entry_slot = div(entry, META_ROWS) * capacity + entry_place
    entry_pick = (
        (jnp.concatenate([place[:, :rows]] * (owners * META_ROWS // 8), axis=0) == entry_slot)
        & (entry_place < capacity)
    ).astype(jnp.bfloat16)
    meta = jnp.dot(entry_pick, local_hot, preferred_element_type=jnp.float32)

    q_copy.wait()
    by_head = jnp.concatenate(
        [
            q_ref[:, :, h * HEAD_WIDTH : (h + 1) * HEAD_WIDTH].reshape(tokens, HEAD_WIDTH)
            for h in range(heads)
        ],
        axis=0,
    )
    q_cols_ref[...] = jnp.dot(
        by_head.astype(jnp.float32).T.astype(jnp.bfloat16),
        order_ref[...],
        preferred_element_type=jnp.float32,
    )
    lane = iota((HEAD_WIDTH, LANES), 1)
    row_of = div(lane, per_row)
    kv_of = mod(div(lane, steps * group), kv_here)

    kf_copy.wait()
    kf = kf_ref[...].reshape(tokens, kv_width)
    token, query = iota((tokens, LANES), 0), iota((tokens, LANES), 1)
    position = iota((cache, LANES), 0)

    def scores(c):
        cols = q_cols_ref[:, pl.ds(pl.multiple_of(c * LANES, LANES), LANES)]
        by_kv = [jnp.where(kv_of == g, cols, 0.0) for g in range(kv_here)]
        fresh = jnp.dot(
            kf,
            jnp.concatenate(by_kv, axis=0).astype(jnp.bfloat16),
            preferred_element_type=jnp.float32,
        )
        live = (mod(token, rows) == div(query, per_row) + c * chunk_rows) & (
            div(token, rows) <= mod(query, steps)
        )
        fresh = jnp.where(live, fresh * scale, -jnp.inf)
        weights = jnp.concatenate(
            [jnp.where(row_of == j, q, 0.0) for j in range(chunk_rows) for q in by_kv], axis=0
        ).astype(jnp.bfloat16)
        keys = jnp.concatenate([k_ref[c * chunk_rows + j] for j in range(chunk_rows)], axis=1)
        cached = jnp.dot(keys, weights, preferred_element_type=jnp.float32)
        return cached * scale, fresh

    def softmax(c, cached, fresh):
        length = jnp.zeros((1, LANES), jnp.int32)
        for j in range(chunk_rows):
            length = jnp.where(
                div(iota((1, LANES), 1), per_row) == j, lengths_ref[c * chunk_rows + j], length
            )
        cached = jnp.where(position < length, cached, -jnp.inf)
        top = jnp.maximum(
            jnp.max(cached, axis=0, keepdims=True), jnp.max(fresh, axis=0, keepdims=True)
        )
        wc, wf = jnp.exp(cached - top), jnp.exp(fresh - top)
        share = 1.0 / (
            jnp.sum(wc, axis=0, keepdims=True) + jnp.sum(wf, axis=0, keepdims=True)
        )
        return (wc * share).T.astype(jnp.bfloat16), (wf * share).T.astype(jnp.bfloat16)

    kv_down = mod(div(iota((LANES, HEAD_WIDTH), 0), steps * group), kv_here)

    def values(c, cached, fresh):
        out = jnp.concatenate(
            [
                jnp.dot(
                    cached[j * per_row : (j + 1) * per_row, :],
                    v_ref[c * chunk_rows + j],
                    preferred_element_type=jnp.float32,
                )
                for j in range(chunk_rows)
            ],
            axis=0,
        ) + jnp.dot(fresh, vf, preferred_element_type=jnp.float32)
        own = out[:, :HEAD_WIDTH]
        for g in range(1, kv_here):
            own = jnp.where(kv_down == g, out[:, g * HEAD_WIDTH : (g + 1) * HEAD_WIDTH], own)
        return own.astype(jnp.bfloat16)

    lengths_copy.wait()
    vf_copy.wait()
    vf = vf_ref[...].reshape(tokens, kv_width)
    for copy in k_copies + v_copies:
        copy.wait()
    for copy in w_copies:
        copy.start()

    @pl.loop(0, chunks // TOGETHER)
    def _(i):
        groups = [i * TOGETHER + n for n in range(TOGETHER)]
        scored = [scores(c) for c in groups]
        probs = [softmax(c, *part) for c, part in zip(groups, scored, strict=True)]
        for c, part in zip(groups, probs, strict=True):
            o_ref[pl.ds(pl.multiple_of(c * LANES, LANES), LANES), :] = values(c, *part)

    out = jnp.dot(
        order_ref[...], o_ref[...], preferred_element_type=jnp.float32
    ).astype(jnp.bfloat16)
    attn = jnp.concatenate(
        [out[h * tokens : (h + 1) * tokens, :] for h in range(heads)], axis=1
    )
    attn_ref[...] = attn
    sent = jnp.dot(pick, attn, preferred_element_type=jnp.float32)
    size = capacity * steps
    for d in range(owners):
        mine = sent[d * size : (d + 1) * size, :]
        send_refs[d][...] = jnp.concatenate(
            [mine[:, h * HEAD_WIDTH : (h + 1) * HEAD_WIDTH] for h in range(heads)]
            + [meta[d * META_ROWS : (d + 1) * META_ROWS, :]],
            axis=0,
        ).astype(jnp.bfloat16)
    for copy in w_copies:
        copy.wait()


def attend_and_pick(
    lengths,
    adapter_of_row,
    storage_slot,
    queries,
    fresh_keys,
    fresh_values,
    cached_keys,
    cached_values,
    weight,
    owners,
    capacity,
    resident,
    columns,
    ahead,
):
    steps, rows, width = queries.shape
    cache, kv_width = cached_keys.shape[1:]
    heads = width // HEAD_WIDTH
    total = rows * heads * steps
    tokens = steps * rows
    size = capacity * steps
    chunks = total // LANES
    outs = pl.pallas_call(
        functools.partial(attend_kernel, owners, capacity, resident, ahead),
        out_shape=[
            jax.ShapeDtypeStruct((tokens, width), jnp.bfloat16),
            jax.ShapeDtypeStruct((owners * size, tokens), jnp.bfloat16),
            pltpu.VMEM((len(ahead), width, columns), jnp.bfloat16),
        ]
        + [jax.ShapeDtypeStruct((heads * size + META_ROWS, HEAD_WIDTH), jnp.bfloat16)] * owners,
        in_specs=[HBM] * 9,
        out_specs=[VMEM] * (3 + owners),
        scratch_shapes=[
            pltpu.SMEM(lengths.shape, jnp.int32),
            pltpu.SMEM(adapter_of_row.shape, jnp.int32),
            pltpu.SMEM(storage_slot.shape, jnp.int32),
            pltpu.VMEM(queries.shape, jnp.bfloat16),
            pltpu.VMEM(fresh_keys.shape, jnp.bfloat16),
            pltpu.VMEM(fresh_values.shape, jnp.bfloat16),
            pltpu.VMEM((rows, cache, kv_width), jnp.bfloat16),
            pltpu.VMEM((rows, cache, kv_width), jnp.bfloat16),
            pltpu.VMEM((total, total), jnp.bfloat16),
            pltpu.VMEM((HEAD_WIDTH, total), jnp.float32),
            pltpu.VMEM((total, HEAD_WIDTH), jnp.bfloat16),
            pltpu.SemaphoreType.DMA((2, chunks)),
            pltpu.SemaphoreType.DMA((6,)),
            pltpu.SemaphoreType.DMA((len(ahead),)),
        ],
        compiler_params=pltpu.CompilerParams(vmem_limit_bytes=24 * MIB),
        cost_estimate=pl.CostEstimate(
            flops=8 * total * cache * kv_width,
            bytes_accessed=4 * rows * cache * kv_width,
            transcendentals=total * cache,
        ),
        name="attend",
    )(
        *in_hbm(
            lengths,
            adapter_of_row,
            storage_slot,
            queries,
            fresh_keys,
            fresh_values,
            cached_keys,
            cached_values,
            weight,
        ),
    )
    return outs[0], outs[1], outs[2], outs[3:]


def project_kernel(blocks, ahead, attn_ref, w_hbm, *refs):
    here_ref = refs[0] if ahead else None
    *outs, w_ref, sems = refs
    sent = sum(d % 2 for d in blocks)
    outs = outs[len(outs) - (len(blocks) - sent + (sent > 0)) :]
    copies = [
        block_copy(w_hbm, w_ref.at[n], sems.at[n], d)
        for n, d in enumerate(blocks[ahead:])
    ]
    for copy in copies:
        copy.start()
    attn = attn_ref[...]
    for n in range(len(blocks)):
        if n >= ahead:
            copies[n - ahead].wait()
        block = here_ref.at[n] if n < ahead else w_ref.at[n - ahead]

        out_ref = outs[0].at[n] if n < sent else outs[n - sent + (sent > 0)]

        @pl.loop(0, block.shape[-1] // TILE)
        def _(i, block=block, out_ref=out_ref):
            cols = pl.ds(pl.multiple_of(i * TILE, TILE), TILE)
            out = jnp.dot(attn, block[:, cols], preferred_element_type=jnp.float32)
            out_ref[:, cols] = out.astype(out_ref.dtype)


def project(attn, weight, columns, blocks, here=(), after=()):
    tokens, width = attn.shape
    ahead = here[0].shape[0] if here else 0
    fetched = len(blocks) - ahead
    sent = sum(d % 2 for d in blocks)
    out_shape = [jax.ShapeDtypeStruct((sent, tokens, columns), jnp.bfloat16)] * (sent > 0)
    out_shape += [jax.ShapeDtypeStruct((tokens, columns), jnp.float32)] * (len(blocks) - sent)
    return pl.pallas_call(
        functools.partial(project_kernel, blocks, ahead),
        out_shape=out_shape,
        in_specs=[VMEM, HBM] + [VMEM] * len(here) + [ANY] * len(after),
        out_specs=[VMEM] * len(out_shape),
        scratch_shapes=[
            pltpu.VMEM((fetched, width, columns), jnp.bfloat16),
            pltpu.SemaphoreType.DMA((fetched,)),
        ],
        compiler_params=pltpu.CompilerParams(vmem_limit_bytes=20 * MIB),
        cost_estimate=pl.CostEstimate(
            flops=2 * tokens * width * columns * len(blocks),
            bytes_accessed=2 * width * columns * len(blocks),
            transcendentals=0,
        ),
        name="project",
    )(attn, *in_hbm(weight), *here, *after)


def down_kernel(capacity, steps, *refs):
    (*got_refs, down_ref, mine_ref, sent_ref, mask_ref) = refs
    resident, rank, width = down_ref.shape
    wide = resident * rank
    heads = width // HEAD_WIDTH
    size = capacity * steps
    held = size * len(got_refs)
    got = [ref[...].astype(jnp.float32) for ref in got_refs]
    rows = jnp.concatenate(
        [
            jnp.concatenate([part[h * size : (h + 1) * size, :] for part in got], axis=0)
            for h in range(heads)
        ],
        axis=1,
    ).astype(jnp.bfloat16)
    meta = jnp.concatenate([part[heads * size :, :] for part in got], axis=0)
    spread = div(iota((LANES, wide), 1), rank) == iota((LANES, wide), 0)
    entries = meta.shape[0]
    slot, entry = iota((held, entries), 0), iota((held, entries), 1)
    of_slot = entry == div(slot, size) * META_ROWS + div(mod(slot, size), steps)
    local = jnp.dot(
        of_slot.astype(jnp.bfloat16),
        meta.astype(jnp.bfloat16),
        preferred_element_type=jnp.float32,
    )
    mask = jnp.dot(
        local.astype(jnp.bfloat16),
        spread.astype(jnp.bfloat16),
        preferred_element_type=jnp.float32,
    )
    mask_ref[...] = mask.astype(jnp.bfloat16)
    low = lax.dot_general(
        rows,
        down_ref[...].reshape(wide, width),
        (((1,), (1,)), ((), ())),
        preferred_element_type=jnp.float32,
    )
    low = low * mask
    pair = low[:, :LANES]
    for n in range(1, wide // LANES):
        pair = pair + low[:, n * LANES : (n + 1) * LANES]
    both = pair + pltpu.roll(pair, rank, 1)
    half = held // 2
    packed = jnp.where(iota((half, LANES), 1) < rank, both[:half, :], both[half:, :])
    mine_ref[...] = packed
    sent_ref[...] = packed.astype(jnp.bfloat16)


def down(got, factors, capacity, steps):
    resident, rank, width = factors.shape
    held = len(got) * capacity * steps
    return pl.pallas_call(
        functools.partial(down_kernel, capacity, steps),
        out_shape=[
            jax.ShapeDtypeStruct((held // 2, LANES), jnp.float32),
            jax.ShapeDtypeStruct((held // 2, LANES), jnp.bfloat16),
            jax.ShapeDtypeStruct((held, resident * rank), jnp.bfloat16),
        ],
        compiler_params=pltpu.CompilerParams(vmem_limit_bytes=12 * MIB),
        cost_estimate=pl.CostEstimate(
            flops=200 * held * resident * rank * width,
            bytes_accessed=2 * resident * rank * width,
            transcendentals=0,
        ),
        name="down",
    )(*got, factors)


def up_kernel(peers, far, mine_ref, *refs):
    got_refs, (mask_ref, up_ref, *rest) = refs[:peers], refs[peers:]
    keep_refs, (core_ref, *outs) = rest[:far], rest[far:]
    delta_refs, half_refs = outs[: len(outs) - far], outs[len(outs) - far :]
    resident, rank, columns = up_ref.shape
    wide = resident * rank
    total = mine_ref[...]
    for ref in got_refs:
        total = total + ref[...].astype(jnp.float32)
    other = pltpu.roll(total, rank, 1)
    first = iota(total.shape, 1) < rank
    both = jnp.concatenate(
        [jnp.where(first, total, other), jnp.where(first, other, total)], axis=0
    )
    both = jnp.concatenate([both] * (wide // LANES), axis=1)
    low = jnp.where(mask_ref[...].astype(jnp.float32) > 0.5, both, 0.0).astype(jnp.bfloat16)
    delta = jnp.dot(
        low, up_ref[...].reshape(wide, columns), preferred_element_type=jnp.float32
    ).astype(jnp.bfloat16)
    size = delta.shape[0] // len(delta_refs)
    for d, ref in enumerate(delta_refs):
        ref[...] = delta[d * size : (d + 1) * size, :]
    for n, (ref, keep_ref) in enumerate(zip(half_refs, keep_refs, strict=True), start=1):
        ref[...] = (keep_ref[...] + core_ref[n].astype(jnp.float32)).astype(jnp.bfloat16)


def up(mine, got, mask, factors, owners, keep, got_core):
    resident, rank, columns = factors.shape
    held = mask.shape[0]
    far, tokens = len(keep), keep[0].shape[0]
    outs = pl.pallas_call(
        functools.partial(up_kernel, len(got), far),
        out_shape=[jax.ShapeDtypeStruct((held // owners, columns), jnp.bfloat16)] * owners
        + [jax.ShapeDtypeStruct((tokens, columns), jnp.bfloat16)] * far,
        compiler_params=pltpu.CompilerParams(vmem_limit_bytes=16 * MIB),
        cost_estimate=pl.CostEstimate(
            flops=200 * held * resident * rank * columns,
            bytes_accessed=2 * resident * rank * columns,
            transcendentals=0,
        ),
        name="up",
    )(mine, *got, mask, factors, *keep, got_core)
    return outs[:owners], outs[owners:]


def finish_kernel(owners, pieces, pick_ref, *refs):
    delta_refs, (*other_refs, core_ref, base_ref, out_hbm, out_ref, sems) = (
        refs[:owners],
        refs[owners:],
    )
    columns = base_ref.shape[1]
    width = columns // pieces
    pick = pick_ref[...]
    copies = []
    for n in range(pieces):
        cols = slice(n * width, (n + 1) * width)
        mixed = base_ref[:, cols] + core_ref[0, :, cols].astype(jnp.float32)
        for ref in other_refs[n::pieces]:
            mixed = mixed + ref[...].astype(jnp.float32)
        delta = jnp.concatenate([ref[:, cols] for ref in delta_refs], axis=0)
        mixed = mixed + lax.dot_general(
            pick, delta, (((0,), (0,)), ((), ())), preferred_element_type=jnp.float32
        )
        out_ref[:, :, cols] = mixed.astype(jnp.bfloat16).reshape(*out_ref.shape[:2], width)
        copies.append(
            pltpu.make_async_copy(out_ref.at[:, :, cols], out_hbm.at[:, :, cols], sems.at[n])
        )
        copies[n].start()
    for copy in copies:
        copy.wait()


def finish(base, pick, delta, core_got, others, steps, pieces):
    tokens, columns = base.shape
    shape = (steps, tokens // steps, columns)
    operands = [pick, *delta, *sum(others, []), core_got, base]
    return pl.pallas_call(
        functools.partial(finish_kernel, len(delta), pieces),
        out_shape=jax.ShapeDtypeStruct(shape, jnp.bfloat16),
        in_specs=[VMEM] * len(operands),
        out_specs=HBM,
        scratch_shapes=[
            pltpu.VMEM(shape, jnp.bfloat16),
            pltpu.SemaphoreType.DMA((pieces,)),
        ],
        compiler_params=pltpu.CompilerParams(vmem_limit_bytes=12 * MIB),
        cost_estimate=pl.CostEstimate(
            flops=2 * tokens * pick.shape[0] * columns,
            bytes_accessed=10 * tokens * columns,
            transcendentals=0,
        ),
        name="finish",
    )(*operands)


def body(
    queries,
    fresh_token_keys,
    fresh_token_values,
    cached_key_rows,
    cached_value_rows,
    cache_live_lengths,
    output_projection_weight,
    adapter_down_factors,
    adapter_up_factors,
    adapter_of_row,
    adapter_storage_slot,
):
    step_count, row_count, _ = queries.shape
    resident = adapter_down_factors.shape[0]
    owners = lax.axis_size("replica")
    tensors = lax.axis_size("tensor")
    capacity = max(2, 2 * row_count // owners)
    columns = adapter_up_factors.shape[2]
    blocks = [*range(1, tensors, 2), *range(2, tensors, 2)]
    ahead = blocks[:1]

    attn, pick, w_here, sent = attend_and_pick(
        cache_live_lengths,
        adapter_of_row,
        adapter_storage_slot,
        queries,
        fresh_token_keys,
        fresh_token_values,
        cached_key_rows,
        cached_value_rows,
        output_projection_weight,
        owners,
        capacity,
        resident,
        columns,
        ahead,
    )
    got = exchange_all(sent, "replica")

    odd, *even = project(attn, output_projection_weight, columns, blocks, here=[w_here])
    core_got = xor_exchange(odd, "tensor", 1)

    mine, low_sent, mask = down(got, adapter_down_factors, capacity, step_count)
    low_got = [xor_exchange(low_sent, "tensor", d) for d in range(1, tensors)]
    delta, halves_sent = up(
        mine, low_got, mask, adapter_up_factors, owners, even, core_got
    )
    delta_got = exchange_all(delta, "replica")
    others = [
        in_pieces(half, "tensor", 2 * n, PIECES) for n, half in enumerate(halves_sent, start=1)
    ]
    (own,) = project(attn, output_projection_weight, columns, [0], after=[delta[0]])
    return finish(own, pick, delta_got, core_got, others, step_count, PIECES)


def solution(mesh):
    in_specs = (
        P(None, ("groups", "replica"), "tensor"),
        P(None, ("groups", "replica"), "tensor"),
        P(None, ("groups", "replica"), "tensor"),
        P(("groups", "replica"), None, "tensor"),
        P(("groups", "replica"), None, "tensor"),
        P(("groups", "replica")),
        P("tensor", None),
        P(("groups", "replica"), None, "tensor"),
        P(("groups", "replica"), None, "tensor"),
        P(("groups", "replica")),
        P("groups"),
    )
    out_specs = P(None, ("groups", "replica"), "tensor")
    return jax.shard_map(body, mesh=mesh, in_specs=in_specs, out_specs=out_specs, check_vma=False)
```

```python
import functools
import math

import jax
import jax.numpy as jnp
from jax import lax
from jax.experimental import pallas as pl
from jax.experimental.pallas import tpu as pltpu
from jax.sharding import PartitionSpec as P

HEAD_WIDTH = 128
LANES = 128
META_ROWS = 16
TILE = 512
TOGETHER = 2
ORDER_ROWS = 32
PIECES = 2
MIB = 1024 * 1024
VMEM = pl.BlockSpec(memory_space=pltpu.VMEM)
ANY = pl.BlockSpec(memory_space=pl.ANY)
HBM = pl.BlockSpec(memory_space=pltpu.HBM)


def iota(shape, dim):
    return lax.broadcasted_iota(jnp.int32, shape, dim)


def halves(n):
    if n & (n - 1):
        raise ValueError(n)
    return n.bit_length() - 1


def div(x, n):
    return lax.shift_right_logical(x, jnp.int32(halves(n)))


def mod(x, n):
    return x & ((1 << halves(n)) - 1)


def one_hot(source, width):
    lane = iota(source.shape, 1)
    return jnp.concatenate(
        [(source == lane + at).astype(jnp.bfloat16) for at in range(0, width, source.shape[1])],
        axis=1,
    )


def in_hbm(*arrays):
    return [pltpu.with_memory_space_constraint(a, pltpu.HBM) for a in arrays]


def xor_exchange(value, axis, distance):
    size = lax.axis_size(axis)
    return lax.ppermute(value, axis, [(i, i ^ distance) for i in range(size)])


def partner_order(size):
    return [0, *range(size // 2, size), *range(1, size // 2)]


def exchange_all(blocks, axis):
    order = partner_order(lax.axis_size(axis))
    return [blocks[0]] + [
        xor_exchange(block, axis, distance)
        for block, distance in zip(blocks[1:], order[1:], strict=True)
    ]


def block_copy(w_hbm, dst, sem, distance):
    me = lax.axis_index("tensor")
    columns = dst.shape[-1]
    at = pl.multiple_of(lax.bitwise_xor(me, jnp.int32(distance)) * columns, LANES)
    return pltpu.make_async_copy(w_hbm.at[:, pl.ds(at, columns)], dst, sem)


def attend_kernel(
    owners,
    capacity,
    resident,
    ahead,
    lengths_hbm,
    adapter_hbm,
    slot_hbm,
    q_hbm,
    kf_hbm,
    vf_hbm,
    k_hbm,
    v_hbm,
    w_hbm,
    attn_ref,
    pick_ref,
    w_ref,
    *rest,
):
    send_refs, rest = rest[:owners], rest[owners:]
    lengths_ref, adapter_ref, slot_ref, q_ref, kf_ref, vf_ref, k_ref, v_ref = rest[:8]
    order_ref, q_cols_ref, o_ref, sems, small_sems, w_sems = rest[8:]
    steps, rows, width = q_ref.shape
    cache, kv_width = k_ref.shape[1:]
    heads = width // HEAD_WIDTH
    kv_here = kv_width // HEAD_WIDTH
    group = heads // kv_here
    per_row = heads * steps
    total = rows * per_row
    tokens = steps * rows
    chunks = sems.shape[1]
    chunk_rows = rows // chunks
    scale = 1.0 / math.sqrt(HEAD_WIDTH)

    def copies(src, dst, which):
        return [
            pltpu.make_async_copy(
                src.at[pl.ds(c * chunk_rows, chunk_rows)],
                dst.at[pl.ds(c * chunk_rows, chunk_rows)],
                sems.at[which, c],
            )
            for c in range(chunks)
        ]

    k_copies = copies(k_hbm, k_ref, 0)
    v_copies = copies(v_hbm, v_ref, 1)
    small = [
        pltpu.make_async_copy(src, dst, small_sems.at[n])
        for n, (src, dst) in enumerate(
            [
                (q_hbm, q_ref),
                (kf_hbm, kf_ref),
                (lengths_hbm, lengths_ref),
                (adapter_hbm, adapter_ref),
                (slot_hbm, slot_ref),
                (vf_hbm, vf_ref),
            ]
        )
    ]
    q_copy, kf_copy, lengths_copy, adapter_copy, slot_copy, vf_copy = small
    w_copies = [
        block_copy(w_hbm, w_ref.at[n], w_sems.at[n], d)
        for n, d in enumerate(ahead)
    ]
    for copy in [q_copy, *k_copies, *small[1:], *v_copies]:
        copy.start()

    @pl.loop(0, total // ORDER_ROWS)
    def _(i):
        at = iota((ORDER_ROWS, LANES), 0) + i * ORDER_ROWS
        source = mod(at, rows) * per_row + div(at, tokens) * steps + mod(div(at, rows), steps)
        here = pl.ds(pl.multiple_of(i * ORDER_ROWS, ORDER_ROWS), ORDER_ROWS)
        order_ref[here, :] = one_hot(source, total)

    adapter_copy.wait()
    slot_copy.wait()
    me = lax.axis_index("replica")
    positions = partner_order(owners)
    row_at = mod(iota((8, tokens), 1), rows)
    row_down = iota((rows, LANES), 0)
    first_slot = jnp.zeros((8, tokens), jnp.int32)
    local_of = jnp.zeros((rows, LANES), jnp.int32)
    firsts = []
    for r in range(rows):
        slot = slot_ref[adapter_ref[r]]
        owner = jnp.int32(0)
        for d in range(1, owners):
            owner = owner + (slot >= d * resident).astype(jnp.int32)
        partner = lax.bitwise_xor(owner, me)
        first = jnp.int32(0)
        for d in range(1, owners):
            first = jnp.where(partner == positions[d], d * capacity, first)
        firsts.append(first)
        first_slot = jnp.where(row_at == r, first, first_slot)
        local_of = jnp.where(row_down == r, slot - owner * resident, local_of)
    place = first_slot
    for r in range(rows - 1):
        place = place + ((first_slot == firsts[r]) & (row_at > r)).astype(jnp.int32)
    held = owners * capacity * steps
    slot_at = iota((held, tokens), 0)
    token_at = iota((held, tokens), 1)
    pick = (
        (jnp.concatenate([place] * (held // 8), axis=0) == div(slot_at, steps))
        & (mod(slot_at, steps) == div(token_at, rows))
    ).astype(jnp.bfloat16)
    pick_ref[...] = pick
    local_hot = (local_of == iota((rows, LANES), 1)).astype(jnp.bfloat16)
    entry = iota((owners * META_ROWS, rows), 0)
    entry_place = mod(entry, META_ROWS)
    entry_slot = div(entry, META_ROWS) * capacity + entry_place
    entry_pick = (
        (jnp.concatenate([place[:, :rows]] * (owners * META_ROWS // 8), axis=0) == entry_slot)
        & (entry_place < capacity)
    ).astype(jnp.bfloat16)
    meta = jnp.dot(entry_pick, local_hot, preferred_element_type=jnp.float32)

    q_copy.wait()
    by_head = jnp.concatenate(
        [
            q_ref[:, :, h * HEAD_WIDTH : (h + 1) * HEAD_WIDTH].reshape(tokens, HEAD_WIDTH)
            for h in range(heads)
        ],
        axis=0,
    )
    q_cols_ref[...] = jnp.dot(
        by_head.astype(jnp.float32).T.astype(jnp.bfloat16),
        order_ref[...],
        preferred_element_type=jnp.float32,
    )
    lane = iota((HEAD_WIDTH, LANES), 1)
    row_of = div(lane, per_row)
    kv_of = mod(div(lane, steps * group), kv_here)

    kf_copy.wait()
    kf = kf_ref[...].reshape(tokens, kv_width)
    token, query = iota((tokens, LANES), 0), iota((tokens, LANES), 1)
    position = iota((cache, LANES), 0)

    def scores(c):
        cols = q_cols_ref[:, pl.ds(pl.multiple_of(c * LANES, LANES), LANES)]
        by_kv = [jnp.where(kv_of == g, cols, 0.0) for g in range(kv_here)]
        fresh = jnp.dot(
            kf,
            jnp.concatenate(by_kv, axis=0).astype(jnp.bfloat16),
            preferred_element_type=jnp.float32,
        )
        live = (mod(token, rows) == div(query, per_row) + c * chunk_rows) & (
            div(token, rows) <= mod(query, steps)
        )
        fresh = jnp.where(live, fresh * scale, -jnp.inf)
        weights = jnp.concatenate(
            [jnp.where(row_of == j, q, 0.0) for j in range(chunk_rows) for q in by_kv], axis=0
        ).astype(jnp.bfloat16)
        keys = jnp.concatenate([k_ref[c * chunk_rows + j] for j in range(chunk_rows)], axis=1)
        cached = jnp.dot(keys, weights, preferred_element_type=jnp.float32)
        return cached * scale, fresh

    def softmax(c, cached, fresh):
        length = jnp.zeros((1, LANES), jnp.int32)
        for j in range(chunk_rows):
            length = jnp.where(
                div(iota((1, LANES), 1), per_row) == j, lengths_ref[c * chunk_rows + j], length
            )
        cached = jnp.where(position < length, cached, -jnp.inf)
        top = jnp.maximum(
            jnp.max(cached, axis=0, keepdims=True), jnp.max(fresh, axis=0, keepdims=True)
        )
        wc, wf = jnp.exp(cached - top), jnp.exp(fresh - top)
        share = 1.0 / (
            jnp.sum(wc, axis=0, keepdims=True) + jnp.sum(wf, axis=0, keepdims=True)
        )
        return (wc * share).T.astype(jnp.bfloat16), (wf * share).T.astype(jnp.bfloat16)

    kv_down = mod(div(iota((LANES, HEAD_WIDTH), 0), steps * group), kv_here)

    def values(c, cached, fresh):
        out = jnp.concatenate(
            [
                jnp.dot(
                    cached[j * per_row : (j + 1) * per_row, :],
                    v_ref[c * chunk_rows + j],
                    preferred_element_type=jnp.float32,
                )
                for j in range(chunk_rows)
            ],
            axis=0,
        ) + jnp.dot(fresh, vf, preferred_element_type=jnp.float32)
        own = out[:, :HEAD_WIDTH]
        for g in range(1, kv_here):
            own = jnp.where(kv_down == g, out[:, g * HEAD_WIDTH : (g + 1) * HEAD_WIDTH], own)
        return own.astype(jnp.bfloat16)

    lengths_copy.wait()
    vf_copy.wait()
    vf = vf_ref[...].reshape(tokens, kv_width)
    for copy in k_copies + v_copies:
        copy.wait()
    for copy in w_copies:
        copy.start()

    @pl.loop(0, chunks // TOGETHER)
    def _(i):
        groups = [i * TOGETHER + n for n in range(TOGETHER)]
        scored = [scores(c) for c in groups]
        probs = [softmax(c, *part) for c, part in zip(groups, scored, strict=True)]
        for c, part in zip(groups, probs, strict=True):
            o_ref[pl.ds(pl.multiple_of(c * LANES, LANES), LANES), :] = values(c, *part)

    out = jnp.dot(
        order_ref[...], o_ref[...], preferred_element_type=jnp.float32
    ).astype(jnp.bfloat16)
    attn = jnp.concatenate(
        [out[h * tokens : (h + 1) * tokens, :] for h in range(heads)], axis=1
    )
    attn_ref[...] = attn
    sent = jnp.dot(pick, attn, preferred_element_type=jnp.float32)
    size = capacity * steps
    for d in range(owners):
        mine = sent[d * size : (d + 1) * size, :]
        send_refs[d][...] = jnp.concatenate(
            [mine[:, h * HEAD_WIDTH : (h + 1) * HEAD_WIDTH] for h in range(heads)]
            + [meta[d * META_ROWS : (d + 1) * META_ROWS, :]],
            axis=0,
        ).astype(jnp.bfloat16)
    for copy in w_copies:
        copy.wait()


def attend_and_pick(
    lengths,
    adapter_of_row,
    storage_slot,
    queries,
    fresh_keys,
    fresh_values,
    cached_keys,
    cached_values,
    weight,
    owners,
    capacity,
    resident,
    columns,
    ahead,
):
    steps, rows, width = queries.shape
    cache, kv_width = cached_keys.shape[1:]
    heads = width // HEAD_WIDTH
    total = rows * heads * steps
    tokens = steps * rows
    size = capacity * steps
    chunks = total // LANES
    outs = pl.pallas_call(
        functools.partial(attend_kernel, owners, capacity, resident, ahead),
        out_shape=[
            jax.ShapeDtypeStruct((tokens, width), jnp.bfloat16),
            jax.ShapeDtypeStruct((owners * size, tokens), jnp.bfloat16),
            pltpu.VMEM((len(ahead), width, columns), jnp.bfloat16),
        ]
        + [jax.ShapeDtypeStruct((heads * size + META_ROWS, HEAD_WIDTH), jnp.bfloat16)] * owners,
        in_specs=[HBM] * 9,
        out_specs=[VMEM] * (3 + owners),
        scratch_shapes=[
            pltpu.SMEM(lengths.shape, jnp.int32),
            pltpu.SMEM(adapter_of_row.shape, jnp.int32),
            pltpu.SMEM(storage_slot.shape, jnp.int32),
            pltpu.VMEM(queries.shape, jnp.bfloat16),
            pltpu.VMEM(fresh_keys.shape, jnp.bfloat16),
            pltpu.VMEM(fresh_values.shape, jnp.bfloat16),
            pltpu.VMEM((rows, cache, kv_width), jnp.bfloat16),
            pltpu.VMEM((rows, cache, kv_width), jnp.bfloat16),
            pltpu.VMEM((total, total), jnp.bfloat16),
            pltpu.VMEM((HEAD_WIDTH, total), jnp.float32),
            pltpu.VMEM((total, HEAD_WIDTH), jnp.bfloat16),
            pltpu.SemaphoreType.DMA((2, chunks)),
            pltpu.SemaphoreType.DMA((6,)),
            pltpu.SemaphoreType.DMA((len(ahead),)),
        ],
        compiler_params=pltpu.CompilerParams(vmem_limit_bytes=24 * MIB),
        cost_estimate=pl.CostEstimate(
            flops=8 * total * cache * kv_width,
            bytes_accessed=4 * rows * cache * kv_width,
            transcendentals=total * cache,
        ),
        name="attend",
    )(
        *in_hbm(
            lengths,
            adapter_of_row,
            storage_slot,
            queries,
            fresh_keys,
            fresh_values,
            cached_keys,
            cached_values,
            weight,
        ),
    )
    return outs[0], outs[1], outs[2], outs[3:]


def project_kernel(blocks, here, bring, added, attn_ref, w_hbm, *refs):
    here_ref = refs[0] if here else None
    add_refs = refs[bool(here) :][:added]
    refs = refs[len(refs) - len(blocks) - bool(bring) - 2 :]
    outs, w_ref, sems = refs[: len(blocks)], refs[-2], refs[-1]
    fetched = blocks[here:]
    copies = [
        block_copy(w_hbm, w_ref.at[n], sems.at[n], d) for n, d in enumerate(fetched)
    ] + [
        block_copy(w_hbm, refs[len(blocks)].at[n], sems.at[len(fetched) + n], d)
        for n, d in enumerate(bring)
    ]
    for copy in copies:
        copy.start()
    attn = attn_ref[...]
    for n in range(len(blocks)):
        if n >= here:
            copies[n - here].wait()
        block = here_ref.at[n] if n < here else w_ref.at[n - here]

        @pl.loop(0, block.shape[-1] // TILE)
        def _(i, n=n, block=block, out_ref=outs[n]):
            cols = pl.ds(pl.multiple_of(i * TILE, TILE), TILE)
            out = jnp.dot(attn, block[:, cols], preferred_element_type=jnp.float32)
            for add_ref in add_refs[n :: len(blocks)]:
                out = out + add_ref[:, cols].astype(jnp.float32)
            out_ref[:, cols] = out.astype(out_ref.dtype)

    for copy in copies[len(fetched) :]:
        copy.wait()


def project(attn, weight, columns, blocks, here=None, bring=(), add=(), dtype=jnp.bfloat16, after=()):
    tokens, width = attn.shape
    held = 0 if here is None else here.shape[0]
    fetched = len(blocks) - held
    extra = [*([here] if held else []), *add]
    outs = [jax.ShapeDtypeStruct((tokens, columns), dtype)] * len(blocks)
    if bring:
        outs.append(pltpu.VMEM((len(bring), width, columns), jnp.bfloat16))
    return pl.pallas_call(
        functools.partial(project_kernel, blocks, held, bring, len(add)),
        out_shape=outs,
        in_specs=[VMEM, HBM] + [VMEM] * len(extra) + [ANY] * len(after),
        out_specs=[VMEM] * len(outs),
        scratch_shapes=[
            pltpu.VMEM((max(fetched, 1), width if fetched else 16, columns), jnp.bfloat16),
            pltpu.SemaphoreType.DMA((fetched + len(bring),)),
        ],
        compiler_params=pltpu.CompilerParams(vmem_limit_bytes=16 * MIB),
        cost_estimate=pl.CostEstimate(
            flops=2 * tokens * width * columns * len(blocks),
            bytes_accessed=2 * width * columns * len(blocks),
            transcendentals=0,
        ),
        name="project",
    )(attn, *in_hbm(weight), *extra, *after)


def down_kernel(capacity, steps, *refs):
    (*got_refs, down_ref, _, mine_ref, sent_ref, mask_ref) = refs
    resident, rank, width = down_ref.shape
    wide = resident * rank
    heads = width // HEAD_WIDTH
    size = capacity * steps
    held = size * len(got_refs)
    got = [ref[...].astype(jnp.float32) for ref in got_refs]
    rows = jnp.concatenate(
        [
            jnp.concatenate([part[h * size : (h + 1) * size, :] for part in got], axis=0)
            for h in range(heads)
        ],
        axis=1,
    ).astype(jnp.bfloat16)
    meta = jnp.concatenate([part[heads * size :, :] for part in got], axis=0)
    spread = div(iota((LANES, wide), 1), rank) == iota((LANES, wide), 0)
    entries = meta.shape[0]
    slot, entry = iota((held, entries), 0), iota((held, entries), 1)
    of_slot = entry == div(slot, size) * META_ROWS + div(mod(slot, size), steps)
    local = jnp.dot(
        of_slot.astype(jnp.bfloat16),
        meta.astype(jnp.bfloat16),
        preferred_element_type=jnp.float32,
    )
    mask = jnp.dot(
        local.astype(jnp.bfloat16),
        spread.astype(jnp.bfloat16),
        preferred_element_type=jnp.float32,
    )
    mask_ref[...] = mask.astype(jnp.bfloat16)
    low = lax.dot_general(
        rows,
        down_ref[...].reshape(wide, width),
        (((1,), (1,)), ((), ())),
        preferred_element_type=jnp.float32,
    )
    low = low * mask
    pair = low[:, :LANES]
    for n in range(1, wide // LANES):
        pair = pair + low[:, n * LANES : (n + 1) * LANES]
    both = pair + pltpu.roll(pair, rank, 1)
    half = held // 2
    packed = jnp.where(iota((half, LANES), 1) < rank, both[:half, :], both[half:, :])
    mine_ref[...] = packed
    sent_ref[...] = packed.astype(jnp.bfloat16)


def down(got, factors, capacity, steps, after):
    resident, rank, width = factors.shape
    held = len(got) * capacity * steps
    return pl.pallas_call(
        functools.partial(down_kernel, capacity, steps),
        out_shape=[
            jax.ShapeDtypeStruct((held // 2, LANES), jnp.float32),
            jax.ShapeDtypeStruct((held // 2, LANES), jnp.bfloat16),
            jax.ShapeDtypeStruct((held, resident * rank), jnp.bfloat16),
        ],
        in_specs=[VMEM] * (len(got) + 1) + [ANY],
        out_specs=[VMEM] * 3,
        compiler_params=pltpu.CompilerParams(vmem_limit_bytes=12 * MIB),
        cost_estimate=pl.CostEstimate(
            flops=200 * held * resident * rank * width,
            bytes_accessed=2 * resident * rank * width,
            transcendentals=0,
        ),
        name="down",
    )(*got, factors, after)


def up_kernel(peers, mine_ref, *refs):
    got_refs, (mask_ref, up_ref, _, *delta_refs) = refs[:peers], refs[peers:]
    resident, rank, columns = up_ref.shape
    wide = resident * rank
    total = mine_ref[...]
    for ref in got_refs:
        total = total + ref[...].astype(jnp.float32)
    other = pltpu.roll(total, rank, 1)
    first = iota(total.shape, 1) < rank
    both = jnp.concatenate(
        [jnp.where(first, total, other), jnp.where(first, other, total)], axis=0
    )
    both = jnp.concatenate([both] * (wide // LANES), axis=1)
    low = jnp.where(mask_ref[...].astype(jnp.float32) > 0.5, both, 0.0).astype(jnp.bfloat16)
    delta = jnp.dot(
        low, up_ref[...].reshape(wide, columns), preferred_element_type=jnp.float32
    ).astype(jnp.bfloat16)
    size = delta.shape[0] // len(delta_refs)
    for d, ref in enumerate(delta_refs):
        ref[...] = delta[d * size : (d + 1) * size, :]


def up(mine, got, mask, factors, owners, after):
    resident, rank, columns = factors.shape
    held = mask.shape[0]
    return pl.pallas_call(
        functools.partial(up_kernel, len(got)),
        out_shape=[jax.ShapeDtypeStruct((held // owners, columns), jnp.bfloat16)] * owners,
        in_specs=[VMEM] * (len(got) + 3) + [ANY],
        out_specs=[VMEM] * owners,
        compiler_params=pltpu.CompilerParams(vmem_limit_bytes=16 * MIB),
        cost_estimate=pl.CostEstimate(
            flops=200 * held * resident * rank * columns,
            bytes_accessed=2 * resident * rank * columns,
            transcendentals=0,
        ),
        name="up",
    )(mine, *got, mask, factors, after)


def finish_kernel(owners, pick_ref, *refs):
    delta_refs, (*near_refs, base_ref, out_hbm, out_ref, sems) = refs[:owners], refs[owners:]
    width = near_refs[0].shape[1]
    pick = pick_ref[...]
    copies = []
    for n, near_ref in enumerate(near_refs):
        cols = slice(n * width, (n + 1) * width)
        mixed = base_ref[:, cols] + near_ref[...].astype(jnp.float32)
        delta = jnp.concatenate([ref[:, cols] for ref in delta_refs], axis=0)
        mixed = mixed + lax.dot_general(
            pick, delta, (((0,), (0,)), ((), ())), preferred_element_type=jnp.float32
        )
        out_ref[:, :, cols] = mixed.astype(jnp.bfloat16).reshape(*out_ref.shape[:2], width)
        copies.append(
            pltpu.make_async_copy(out_ref.at[:, :, cols], out_hbm.at[:, :, cols], sems.at[n])
        )
        copies[n].start()
    for copy in copies:
        copy.wait()


def finish(base, pick, delta, near, steps):
    tokens, columns = base.shape
    shape = (steps, tokens // steps, columns)
    operands = [pick, *delta, *near, base]
    return pl.pallas_call(
        functools.partial(finish_kernel, len(delta)),
        out_shape=jax.ShapeDtypeStruct(shape, jnp.bfloat16),
        in_specs=[VMEM] * len(operands),
        out_specs=HBM,
        scratch_shapes=[
            pltpu.VMEM(shape, jnp.bfloat16),
            pltpu.SemaphoreType.DMA((len(near),)),
        ],
        compiler_params=pltpu.CompilerParams(vmem_limit_bytes=12 * MIB),
        cost_estimate=pl.CostEstimate(
            flops=2 * tokens * pick.shape[0] * columns,
            bytes_accessed=10 * tokens * columns,
            transcendentals=0,
        ),
        name="finish",
    )(*operands)


def body(
    queries,
    fresh_token_keys,
    fresh_token_values,
    cached_key_rows,
    cached_value_rows,
    cache_live_lengths,
    output_projection_weight,
    adapter_down_factors,
    adapter_up_factors,
    adapter_of_row,
    adapter_storage_slot,
):
    step_count, row_count, _ = queries.shape
    resident = adapter_down_factors.shape[0]
    owners = lax.axis_size("replica")
    tensors = lax.axis_size("tensor")
    capacity = max(2, 2 * row_count // owners)
    columns = adapter_up_factors.shape[2]
    far_sent, far_kept = list(range(3, tensors, 2)), list(range(2, tensors, 2))

    attn, pick, w_here, sent = attend_and_pick(
        cache_live_lengths,
        adapter_of_row,
        adapter_storage_slot,
        queries,
        fresh_token_keys,
        fresh_token_values,
        cached_key_rows,
        cached_value_rows,
        output_projection_weight,
        owners,
        capacity,
        resident,
        columns,
        far_sent,
    )
    got = exchange_all(sent, "replica")

    weight = output_projection_weight
    *parts, w_here = project(attn, weight, columns, far_sent, here=w_here, bring=far_kept)
    far_got = [xor_exchange(part, "tensor", 1) for part in parts]

    mine, low_sent, mask = down(got, adapter_down_factors, capacity, step_count, parts[0])
    low_got = [xor_exchange(low_sent, "tensor", d) for d in range(1, tensors)]
    halves_sent = project(
        attn, weight, columns, far_kept, here=w_here, add=far_got, after=[low_sent]
    )
    others = [xor_exchange(half, "tensor", d) for half, d in zip(halves_sent, far_kept, strict=True)]
    delta = up(mine, low_got, mask, adapter_up_factors, owners, halves_sent[0])
    delta_got = exchange_all(delta, "replica")

    (near,) = project(attn, weight, columns, [1], after=[delta[0]])
    width = columns // PIECES
    near_got = [
        xor_exchange(near[:, n * width : (n + 1) * width], "tensor", 1) for n in range(PIECES)
    ]
    (own,) = project(
        attn, weight, columns, [0], add=others, dtype=jnp.float32, after=[near]
    )
    return finish(own, pick, delta_got, near_got, step_count)


def solution(mesh):
    in_specs = (
        P(None, ("groups", "replica"), "tensor"),
        P(None, ("groups", "replica"), "tensor"),
        P(None, ("groups", "replica"), "tensor"),
        P(("groups", "replica"), None, "tensor"),
        P(("groups", "replica"), None, "tensor"),
        P(("groups", "replica")),
        P("tensor", None),
        P(("groups", "replica"), None, "tensor"),
        P(("groups", "replica"), None, "tensor"),
        P(("groups", "replica")),
        P("groups"),
    )
    out_specs = P(None, ("groups", "replica"), "tensor")
    return jax.shard_map(body, mesh=mesh, in_specs=in_specs, out_specs=out_specs, check_vma=False)
```

```python
import functools
import math

import jax
import jax.numpy as jnp
from jax import lax
from jax.experimental import pallas as pl
from jax.experimental.pallas import tpu as pltpu
from jax.sharding import PartitionSpec as P

HEAD_WIDTH = 128
LANES = 128
META_ROWS = 16
TILE = 512
TOGETHER = 2
ORDER_ROWS = 32
PIECES = 2
MIB = 1024 * 1024
VMEM = pl.BlockSpec(memory_space=pltpu.VMEM)
ANY = pl.BlockSpec(memory_space=pl.ANY)
HBM = pl.BlockSpec(memory_space=pltpu.HBM)


def iota(shape, dim):
    return lax.broadcasted_iota(jnp.int32, shape, dim)


def halves(n):
    if n & (n - 1):
        raise ValueError(n)
    return n.bit_length() - 1


def div(x, n):
    return lax.shift_right_logical(x, jnp.int32(halves(n)))


def mod(x, n):
    return x & ((1 << halves(n)) - 1)


def one_hot(source, width):
    lane = iota(source.shape, 1)
    return jnp.concatenate(
        [(source == lane + at).astype(jnp.bfloat16) for at in range(0, width, source.shape[1])],
        axis=1,
    )


def in_hbm(*arrays):
    return [pltpu.with_memory_space_constraint(a, pltpu.HBM) for a in arrays]


def xor_exchange(value, axis, distance):
    size = lax.axis_size(axis)
    return lax.ppermute(value, axis, [(i, i ^ distance) for i in range(size)])


def partner_order(size):
    return [0, *range(size // 2, size), *range(1, size // 2)]


def exchange_all(blocks, axis):
    order = partner_order(lax.axis_size(axis))
    return [blocks[0]] + [
        xor_exchange(block, axis, distance)
        for block, distance in zip(blocks[1:], order[1:], strict=True)
    ]


def block_copy(w_hbm, dst, sem, distance):
    me = lax.axis_index("tensor")
    columns = dst.shape[-1]
    at = pl.multiple_of(lax.bitwise_xor(me, jnp.int32(distance)) * columns, LANES)
    return pltpu.make_async_copy(w_hbm.at[:, pl.ds(at, columns)], dst, sem)


def attend_kernel(
    owners,
    capacity,
    resident,
    ahead,
    lengths_hbm,
    adapter_hbm,
    slot_hbm,
    q_hbm,
    kf_hbm,
    vf_hbm,
    k_hbm,
    v_hbm,
    w_hbm,
    attn_ref,
    pick_ref,
    w_ref,
    *rest,
):
    send_refs, rest = rest[:owners], rest[owners:]
    lengths_ref, adapter_ref, slot_ref, q_ref, kf_ref, vf_ref, k_ref, v_ref = rest[:8]
    order_ref, q_cols_ref, o_ref, sems, small_sems, w_sems = rest[8:]
    steps, rows, width = q_ref.shape
    cache, kv_width = k_ref.shape[1:]
    heads = width // HEAD_WIDTH
    kv_here = kv_width // HEAD_WIDTH
    group = heads // kv_here
    per_row = heads * steps
    total = rows * per_row
    tokens = steps * rows
    chunks = sems.shape[1]
    chunk_rows = rows // chunks
    scale = 1.0 / math.sqrt(HEAD_WIDTH)

    def copies(src, dst, which):
        return [
            pltpu.make_async_copy(
                src.at[pl.ds(c * chunk_rows, chunk_rows)],
                dst.at[pl.ds(c * chunk_rows, chunk_rows)],
                sems.at[which, c],
            )
            for c in range(chunks)
        ]

    k_copies = copies(k_hbm, k_ref, 0)
    v_copies = copies(v_hbm, v_ref, 1)
    small = [
        pltpu.make_async_copy(src, dst, small_sems.at[n])
        for n, (src, dst) in enumerate(
            [
                (q_hbm, q_ref),
                (kf_hbm, kf_ref),
                (lengths_hbm, lengths_ref),
                (adapter_hbm, adapter_ref),
                (slot_hbm, slot_ref),
                (vf_hbm, vf_ref),
            ]
        )
    ]
    q_copy, kf_copy, lengths_copy, adapter_copy, slot_copy, vf_copy = small
    w_copies = [
        block_copy(w_hbm, w_ref.at[n], w_sems.at[n], d)
        for n, d in enumerate(ahead)
    ]
    for copy in [q_copy, *k_copies, *small[1:], *v_copies]:
        copy.start()

    @pl.loop(0, total // ORDER_ROWS)
    def _(i):
        at = iota((ORDER_ROWS, LANES), 0) + i * ORDER_ROWS
        source = mod(at, rows) * per_row + div(at, tokens) * steps + mod(div(at, rows), steps)
        here = pl.ds(pl.multiple_of(i * ORDER_ROWS, ORDER_ROWS), ORDER_ROWS)
        order_ref[here, :] = one_hot(source, total)

    adapter_copy.wait()
    slot_copy.wait()
    me = lax.axis_index("replica")
    positions = partner_order(owners)
    row_at = mod(iota((8, tokens), 1), rows)
    row_down = iota((rows, LANES), 0)
    first_slot = jnp.zeros((8, tokens), jnp.int32)
    local_of = jnp.zeros((rows, LANES), jnp.int32)
    firsts = []
    for r in range(rows):
        slot = slot_ref[adapter_ref[r]]
        owner = jnp.int32(0)
        for d in range(1, owners):
            owner = owner + (slot >= d * resident).astype(jnp.int32)
        partner = lax.bitwise_xor(owner, me)
        first = jnp.int32(0)
        for d in range(1, owners):
            first = jnp.where(partner == positions[d], d * capacity, first)
        firsts.append(first)
        first_slot = jnp.where(row_at == r, first, first_slot)
        local_of = jnp.where(row_down == r, slot - owner * resident, local_of)
    place = first_slot
    for r in range(rows - 1):
        place = place + ((first_slot == firsts[r]) & (row_at > r)).astype(jnp.int32)
    held = owners * capacity * steps
    slot_at = iota((held, tokens), 0)
    token_at = iota((held, tokens), 1)
    pick = (
        (jnp.concatenate([place] * (held // 8), axis=0) == div(slot_at, steps))
        & (mod(slot_at, steps) == div(token_at, rows))
    ).astype(jnp.bfloat16)
    pick_ref[...] = pick
    local_hot = (local_of == iota((rows, LANES), 1)).astype(jnp.bfloat16)
    entry = iota((owners * META_ROWS, rows), 0)
    entry_place = mod(entry, META_ROWS)
    entry_slot = div(entry, META_ROWS) * capacity + entry_place
    entry_pick = (
        (jnp.concatenate([place[:, :rows]] * (owners * META_ROWS // 8), axis=0) == entry_slot)
        & (entry_place < capacity)
    ).astype(jnp.bfloat16)
    meta = jnp.dot(entry_pick, local_hot, preferred_element_type=jnp.float32)

    q_copy.wait()
    by_head = jnp.concatenate(
        [
            q_ref[:, :, h * HEAD_WIDTH : (h + 1) * HEAD_WIDTH].reshape(tokens, HEAD_WIDTH)
            for h in range(heads)
        ],
        axis=0,
    )
    q_cols_ref[...] = jnp.dot(
        by_head.astype(jnp.float32).T.astype(jnp.bfloat16),
        order_ref[...],
        preferred_element_type=jnp.float32,
    )
    lane = iota((HEAD_WIDTH, LANES), 1)
    row_of = div(lane, per_row)
    kv_of = mod(div(lane, steps * group), kv_here)

    kf_copy.wait()
    kf = kf_ref[...].reshape(tokens, kv_width)
    token, query = iota((tokens, LANES), 0), iota((tokens, LANES), 1)
    position = iota((cache, LANES), 0)

    def scores(c):
        cols = q_cols_ref[:, pl.ds(pl.multiple_of(c * LANES, LANES), LANES)]
        by_kv = [jnp.where(kv_of == g, cols, 0.0) for g in range(kv_here)]
        fresh = jnp.dot(
            kf,
            jnp.concatenate(by_kv, axis=0).astype(jnp.bfloat16),
            preferred_element_type=jnp.float32,
        )
        live = (mod(token, rows) == div(query, per_row) + c * chunk_rows) & (
            div(token, rows) <= mod(query, steps)
        )
        fresh = jnp.where(live, fresh * scale, -jnp.inf)
        weights = jnp.concatenate(
            [jnp.where(row_of == j, q, 0.0) for j in range(chunk_rows) for q in by_kv], axis=0
        ).astype(jnp.bfloat16)
        keys = jnp.concatenate([k_ref[c * chunk_rows + j] for j in range(chunk_rows)], axis=1)
        cached = jnp.dot(keys, weights, preferred_element_type=jnp.float32)
        return cached * scale, fresh

    def softmax(c, cached, fresh):
        length = jnp.zeros((1, LANES), jnp.int32)
        for j in range(chunk_rows):
            length = jnp.where(
                div(iota((1, LANES), 1), per_row) == j, lengths_ref[c * chunk_rows + j], length
            )
        cached = jnp.where(position < length, cached, -jnp.inf)
        top = jnp.maximum(
            jnp.max(cached, axis=0, keepdims=True), jnp.max(fresh, axis=0, keepdims=True)
        )
        wc, wf = jnp.exp(cached - top), jnp.exp(fresh - top)
        share = 1.0 / (
            jnp.sum(wc, axis=0, keepdims=True) + jnp.sum(wf, axis=0, keepdims=True)
        )
        return (wc * share).T.astype(jnp.bfloat16), (wf * share).T.astype(jnp.bfloat16)

    kv_down = mod(div(iota((LANES, HEAD_WIDTH), 0), steps * group), kv_here)

    def values(c, cached, fresh):
        out = jnp.concatenate(
            [
                jnp.dot(
                    cached[j * per_row : (j + 1) * per_row, :],
                    v_ref[c * chunk_rows + j],
                    preferred_element_type=jnp.float32,
                )
                for j in range(chunk_rows)
            ],
            axis=0,
        ) + jnp.dot(fresh, vf, preferred_element_type=jnp.float32)
        own = out[:, :HEAD_WIDTH]
        for g in range(1, kv_here):
            own = jnp.where(kv_down == g, out[:, g * HEAD_WIDTH : (g + 1) * HEAD_WIDTH], own)
        return own.astype(jnp.bfloat16)

    lengths_copy.wait()
    vf_copy.wait()
    vf = vf_ref[...].reshape(tokens, kv_width)
    for copy in k_copies + v_copies:
        copy.wait()
    for copy in w_copies:
        copy.start()

    @pl.loop(0, chunks // TOGETHER)
    def _(i):
        groups = [i * TOGETHER + n for n in range(TOGETHER)]
        scored = [scores(c) for c in groups]
        probs = [softmax(c, *part) for c, part in zip(groups, scored, strict=True)]
        for c, part in zip(groups, probs, strict=True):
            o_ref[pl.ds(pl.multiple_of(c * LANES, LANES), LANES), :] = values(c, *part)

    out = jnp.dot(
        order_ref[...], o_ref[...], preferred_element_type=jnp.float32
    ).astype(jnp.bfloat16)
    attn = jnp.concatenate(
        [out[h * tokens : (h + 1) * tokens, :] for h in range(heads)], axis=1
    )
    attn_ref[...] = attn
    sent = jnp.dot(pick, attn, preferred_element_type=jnp.float32)
    size = capacity * steps
    for d in range(owners):
        mine = sent[d * size : (d + 1) * size, :]
        send_refs[d][...] = jnp.concatenate(
            [mine[:, h * HEAD_WIDTH : (h + 1) * HEAD_WIDTH] for h in range(heads)]
            + [meta[d * META_ROWS : (d + 1) * META_ROWS, :]],
            axis=0,
        ).astype(jnp.bfloat16)
    for copy in w_copies:
        copy.wait()


def attend_and_pick(
    lengths,
    adapter_of_row,
    storage_slot,
    queries,
    fresh_keys,
    fresh_values,
    cached_keys,
    cached_values,
    weight,
    owners,
    capacity,
    resident,
    columns,
    ahead,
):
    steps, rows, width = queries.shape
    cache, kv_width = cached_keys.shape[1:]
    heads = width // HEAD_WIDTH
    total = rows * heads * steps
    tokens = steps * rows
    size = capacity * steps
    chunks = total // LANES
    outs = pl.pallas_call(
        functools.partial(attend_kernel, owners, capacity, resident, ahead),
        out_shape=[
            jax.ShapeDtypeStruct((tokens, width), jnp.bfloat16),
            jax.ShapeDtypeStruct((owners * size, tokens), jnp.bfloat16),
            pltpu.VMEM((len(ahead), width, columns), jnp.bfloat16),
        ]
        + [jax.ShapeDtypeStruct((heads * size + META_ROWS, HEAD_WIDTH), jnp.bfloat16)] * owners,
        in_specs=[HBM] * 9,
        out_specs=[VMEM] * (3 + owners),
        scratch_shapes=[
            pltpu.SMEM(lengths.shape, jnp.int32),
            pltpu.SMEM(adapter_of_row.shape, jnp.int32),
            pltpu.SMEM(storage_slot.shape, jnp.int32),
            pltpu.VMEM(queries.shape, jnp.bfloat16),
            pltpu.VMEM(fresh_keys.shape, jnp.bfloat16),
            pltpu.VMEM(fresh_values.shape, jnp.bfloat16),
            pltpu.VMEM((rows, cache, kv_width), jnp.bfloat16),
            pltpu.VMEM((rows, cache, kv_width), jnp.bfloat16),
            pltpu.VMEM((total, total), jnp.bfloat16),
            pltpu.VMEM((HEAD_WIDTH, total), jnp.float32),
            pltpu.VMEM((total, HEAD_WIDTH), jnp.bfloat16),
            pltpu.SemaphoreType.DMA((2, chunks)),
            pltpu.SemaphoreType.DMA((6,)),
            pltpu.SemaphoreType.DMA((len(ahead),)),
        ],
        compiler_params=pltpu.CompilerParams(vmem_limit_bytes=24 * MIB),
        cost_estimate=pl.CostEstimate(
            flops=8 * total * cache * kv_width,
            bytes_accessed=4 * rows * cache * kv_width,
            transcendentals=total * cache,
        ),
        name="attend",
    )(
        *in_hbm(
            lengths,
            adapter_of_row,
            storage_slot,
            queries,
            fresh_keys,
            fresh_values,
            cached_keys,
            cached_values,
            weight,
        ),
    )
    return outs[0], outs[1], outs[2], outs[3:]


def project_kernel(blocks, here, bring, added, attn_ref, w_hbm, *refs):
    here_ref = refs[0] if here else None
    add_refs = refs[bool(here) :][:added]
    refs = refs[len(refs) - len(blocks) - bool(bring) - 2 :]
    outs, w_ref, sems = refs[: len(blocks)], refs[-2], refs[-1]
    fetched = blocks[here:]
    copies = [
        block_copy(w_hbm, w_ref.at[n], sems.at[n], d) for n, d in enumerate(fetched)
    ] + [
        block_copy(w_hbm, refs[len(blocks)].at[n], sems.at[len(fetched) + n], d)
        for n, d in enumerate(bring)
    ]
    for copy in copies:
        copy.start()
    attn = attn_ref[...]
    for n in range(len(blocks)):
        if n >= here:
            copies[n - here].wait()
        block = here_ref.at[n] if n < here else w_ref.at[n - here]

        @pl.loop(0, block.shape[-1] // TILE)
        def _(i, n=n, block=block, out_ref=outs[n]):
            cols = pl.ds(pl.multiple_of(i * TILE, TILE), TILE)
            out = jnp.dot(attn, block[:, cols], preferred_element_type=jnp.float32)
            for add_ref in add_refs[n :: len(blocks)]:
                out = out + add_ref[:, cols].astype(jnp.float32)
            out_ref[:, cols] = out.astype(out_ref.dtype)

    for copy in copies[len(fetched) :]:
        copy.wait()


def project(attn, weight, columns, blocks, here=None, bring=(), add=(), dtype=jnp.bfloat16, after=()):
    tokens, width = attn.shape
    held = 0 if here is None else here.shape[0]
    fetched = len(blocks) - held
    extra = [*([here] if held else []), *add]
    outs = [jax.ShapeDtypeStruct((tokens, columns), dtype)] * len(blocks)
    if bring:
        outs.append(pltpu.VMEM((len(bring), width, columns), jnp.bfloat16))
    return pl.pallas_call(
        functools.partial(project_kernel, blocks, held, bring, len(add)),
        out_shape=outs,
        in_specs=[VMEM, HBM] + [VMEM] * len(extra) + [ANY] * len(after),
        out_specs=[VMEM] * len(outs),
        scratch_shapes=[
            pltpu.VMEM((max(fetched, 1), width if fetched else 16, columns), jnp.bfloat16),
            pltpu.SemaphoreType.DMA((fetched + len(bring),)),
        ],
        compiler_params=pltpu.CompilerParams(vmem_limit_bytes=16 * MIB),
        cost_estimate=pl.CostEstimate(
            flops=2 * tokens * width * columns * len(blocks),
            bytes_accessed=2 * width * columns * len(blocks),
            transcendentals=0,
        ),
        name="project",
    )(attn, *in_hbm(weight), *extra, *after)


def merge_kernel(mine_ref, got_ref, _, out_ref):
    out_ref[...] = (mine_ref[...] + got_ref[...].astype(jnp.float32)).astype(jnp.bfloat16)


def merge(mine, got, after):
    return pl.pallas_call(
        merge_kernel,
        out_shape=jax.ShapeDtypeStruct(mine.shape, jnp.bfloat16),
        in_specs=[VMEM, VMEM, ANY],
        out_specs=VMEM,
        compiler_params=pltpu.CompilerParams(vmem_limit_bytes=4 * MIB),
        name="merge",
    )(mine, got, after)


def down_kernel(capacity, steps, *refs):
    (*got_refs, down_ref, _, mine_ref, sent_ref, mask_ref) = refs
    resident, rank, width = down_ref.shape
    wide = resident * rank
    heads = width // HEAD_WIDTH
    size = capacity * steps
    held = size * len(got_refs)
    got = [ref[...].astype(jnp.float32) for ref in got_refs]
    rows = jnp.concatenate(
        [
            jnp.concatenate([part[h * size : (h + 1) * size, :] for part in got], axis=0)
            for h in range(heads)
        ],
        axis=1,
    ).astype(jnp.bfloat16)
    meta = jnp.concatenate([part[heads * size :, :] for part in got], axis=0)
    spread = div(iota((LANES, wide), 1), rank) == iota((LANES, wide), 0)
    entries = meta.shape[0]
    slot, entry = iota((held, entries), 0), iota((held, entries), 1)
    of_slot = entry == div(slot, size) * META_ROWS + div(mod(slot, size), steps)
    local = jnp.dot(
        of_slot.astype(jnp.bfloat16),
        meta.astype(jnp.bfloat16),
        preferred_element_type=jnp.float32,
    )
    mask = jnp.dot(
        local.astype(jnp.bfloat16),
        spread.astype(jnp.bfloat16),
        preferred_element_type=jnp.float32,
    )
    mask_ref[...] = mask.astype(jnp.bfloat16)
    low = lax.dot_general(
        rows,
        down_ref[...].reshape(wide, width),
        (((1,), (1,)), ((), ())),
        preferred_element_type=jnp.float32,
    )
    low = low * mask
    pair = low[:, :LANES]
    for n in range(1, wide // LANES):
        pair = pair + low[:, n * LANES : (n + 1) * LANES]
    both = pair + pltpu.roll(pair, rank, 1)
    half = held // 2
    packed = jnp.where(iota((half, LANES), 1) < rank, both[:half, :], both[half:, :])
    mine_ref[...] = packed
    sent_ref[...] = packed.astype(jnp.bfloat16)


def down(got, factors, capacity, steps, after):
    resident, rank, width = factors.shape
    held = len(got) * capacity * steps
    return pl.pallas_call(
        functools.partial(down_kernel, capacity, steps),
        out_shape=[
            jax.ShapeDtypeStruct((held // 2, LANES), jnp.float32),
            jax.ShapeDtypeStruct((held // 2, LANES), jnp.bfloat16),
            jax.ShapeDtypeStruct((held, resident * rank), jnp.bfloat16),
        ],
        in_specs=[VMEM] * (len(got) + 1) + [ANY],
        out_specs=[VMEM] * 3,
        compiler_params=pltpu.CompilerParams(vmem_limit_bytes=12 * MIB),
        cost_estimate=pl.CostEstimate(
            flops=200 * held * resident * rank * width,
            bytes_accessed=2 * resident * rank * width,
            transcendentals=0,
        ),
        name="down",
    )(*got, factors, after)


def up_kernel(peers, mine_ref, *refs):
    got_refs, (mask_ref, up_ref, _, *delta_refs) = refs[:peers], refs[peers:]
    resident, rank, columns = up_ref.shape
    wide = resident * rank
    total = mine_ref[...]
    for ref in got_refs:
        total = total + ref[...].astype(jnp.float32)
    other = pltpu.roll(total, rank, 1)
    first = iota(total.shape, 1) < rank
    both = jnp.concatenate(
        [jnp.where(first, total, other), jnp.where(first, other, total)], axis=0
    )
    both = jnp.concatenate([both] * (wide // LANES), axis=1)
    low = jnp.where(mask_ref[...].astype(jnp.float32) > 0.5, both, 0.0).astype(jnp.bfloat16)
    delta = jnp.dot(
        low, up_ref[...].reshape(wide, columns), preferred_element_type=jnp.float32
    ).astype(jnp.bfloat16)
    size = delta.shape[0] // len(delta_refs)
    for d, ref in enumerate(delta_refs):
        ref[...] = delta[d * size : (d + 1) * size, :]


def up(mine, got, mask, factors, owners, after):
    resident, rank, columns = factors.shape
    held = mask.shape[0]
    return pl.pallas_call(
        functools.partial(up_kernel, len(got)),
        out_shape=[jax.ShapeDtypeStruct((held // owners, columns), jnp.bfloat16)] * owners,
        in_specs=[VMEM] * (len(got) + 3) + [ANY],
        out_specs=[VMEM] * owners,
        compiler_params=pltpu.CompilerParams(vmem_limit_bytes=16 * MIB),
        cost_estimate=pl.CostEstimate(
            flops=200 * held * resident * rank * columns,
            bytes_accessed=2 * resident * rank * columns,
            transcendentals=0,
        ),
        name="up",
    )(mine, *got, mask, factors, after)


def finish_kernel(owners, pick_ref, *refs):
    delta_refs, (*near_refs, base_ref, out_hbm, out_ref, sems) = refs[:owners], refs[owners:]
    width = near_refs[0].shape[1]
    pick = pick_ref[...]
    copies = []
    for n, near_ref in enumerate(near_refs):
        cols = slice(n * width, (n + 1) * width)
        mixed = base_ref[:, cols] + near_ref[...].astype(jnp.float32)
        delta = jnp.concatenate([ref[:, cols] for ref in delta_refs], axis=0)
        mixed = mixed + lax.dot_general(
            pick, delta, (((0,), (0,)), ((), ())), preferred_element_type=jnp.float32
        )
        out_ref[:, :, cols] = mixed.astype(jnp.bfloat16).reshape(*out_ref.shape[:2], width)
        copies.append(
            pltpu.make_async_copy(out_ref.at[:, :, cols], out_hbm.at[:, :, cols], sems.at[n])
        )
        copies[n].start()
    for copy in copies:
        copy.wait()


def finish(base, pick, delta, near, steps):
    tokens, columns = base.shape
    shape = (steps, tokens // steps, columns)
    operands = [pick, *delta, *near, base]
    return pl.pallas_call(
        functools.partial(finish_kernel, len(delta)),
        out_shape=jax.ShapeDtypeStruct(shape, jnp.bfloat16),
        in_specs=[VMEM] * len(operands),
        out_specs=HBM,
        scratch_shapes=[
            pltpu.VMEM(shape, jnp.bfloat16),
            pltpu.SemaphoreType.DMA((len(near),)),
        ],
        compiler_params=pltpu.CompilerParams(vmem_limit_bytes=12 * MIB),
        cost_estimate=pl.CostEstimate(
            flops=2 * tokens * pick.shape[0] * columns,
            bytes_accessed=10 * tokens * columns,
            transcendentals=0,
        ),
        name="finish",
    )(*operands)


def body(
    queries,
    fresh_token_keys,
    fresh_token_values,
    cached_key_rows,
    cached_value_rows,
    cache_live_lengths,
    output_projection_weight,
    adapter_down_factors,
    adapter_up_factors,
    adapter_of_row,
    adapter_storage_slot,
):
    step_count, row_count, _ = queries.shape
    resident = adapter_down_factors.shape[0]
    owners = lax.axis_size("replica")
    tensors = lax.axis_size("tensor")
    capacity = max(2, 2 * row_count // owners)
    columns = adapter_up_factors.shape[2]
    far_sent, far_kept = list(range(3, tensors, 2)), list(range(2, tensors, 2))

    attn, pick, w_here, sent = attend_and_pick(
        cache_live_lengths,
        adapter_of_row,
        adapter_storage_slot,
        queries,
        fresh_token_keys,
        fresh_token_values,
        cached_key_rows,
        cached_value_rows,
        output_projection_weight,
        owners,
        capacity,
        resident,
        columns,
        far_sent,
    )
    got = exchange_all(sent, "replica")

    weight = output_projection_weight
    *parts, w_here = project(attn, weight, columns, far_sent, here=w_here, bring=far_kept)
    far_got = [xor_exchange(part, "tensor", 1) for part in parts]

    kept = project(
        attn, weight, columns, far_kept, here=w_here, dtype=jnp.float32, after=[parts[0]]
    )
    mine, low_sent, mask = down(got, adapter_down_factors, capacity, step_count, kept[0])
    low_got = [xor_exchange(low_sent, "tensor", d) for d in range(1, tensors)]
    halves_sent = [merge(*pair, low_sent) for pair in zip(kept, far_got, strict=True)]
    others = [xor_exchange(half, "tensor", d) for half, d in zip(halves_sent, far_kept, strict=True)]
    delta = up(mine, low_got, mask, adapter_up_factors, owners, halves_sent[0])
    delta_got = exchange_all(delta, "replica")

    (near,) = project(attn, weight, columns, [1], after=[delta[0]])
    width = columns // PIECES
    near_got = [
        xor_exchange(near[:, n * width : (n + 1) * width], "tensor", 1) for n in range(PIECES)
    ]
    (own,) = project(
        attn, weight, columns, [0], add=others, dtype=jnp.float32, after=[near]
    )
    return finish(own, pick, delta_got, near_got, step_count)


def solution(mesh):
    in_specs = (
        P(None, ("groups", "replica"), "tensor"),
        P(None, ("groups", "replica"), "tensor"),
        P(None, ("groups", "replica"), "tensor"),
        P(("groups", "replica"), None, "tensor"),
        P(("groups", "replica"), None, "tensor"),
        P(("groups", "replica")),
        P("tensor", None),
        P(("groups", "replica"), None, "tensor"),
        P(("groups", "replica"), None, "tensor"),
        P(("groups", "replica")),
        P("groups"),
    )
    out_specs = P(None, ("groups", "replica"), "tensor")
    return jax.shard_map(body, mesh=mesh, in_specs=in_specs, out_specs=out_specs, check_vma=False)
```

```python
import functools
import math

import jax
import jax.numpy as jnp
from jax import lax
from jax.experimental import pallas as pl
from jax.experimental.pallas import tpu as pltpu
from jax.sharding import PartitionSpec as P

HEAD_WIDTH = 128
LANES = 128
META_ROWS = 16
TILE = 512
TOGETHER = 2
ORDER_ROWS = 32
PIECES = 2
MIB = 1024 * 1024
VMEM = pl.BlockSpec(memory_space=pltpu.VMEM)
ANY = pl.BlockSpec(memory_space=pl.ANY)
HBM = pl.BlockSpec(memory_space=pltpu.HBM)


def iota(shape, dim):
    return lax.broadcasted_iota(jnp.int32, shape, dim)


def halves(n):
    if n & (n - 1):
        raise ValueError(n)
    return n.bit_length() - 1


def div(x, n):
    return lax.shift_right_logical(x, jnp.int32(halves(n)))


def mod(x, n):
    return x & ((1 << halves(n)) - 1)


def one_hot(source, width):
    lane = iota(source.shape, 1)
    return jnp.concatenate(
        [(source == lane + at).astype(jnp.bfloat16) for at in range(0, width, source.shape[1])],
        axis=1,
    )


def in_hbm(*arrays):
    return [pltpu.with_memory_space_constraint(a, pltpu.HBM) for a in arrays]


def xor_exchange(value, axis, distance):
    size = lax.axis_size(axis)
    return lax.ppermute(value, axis, [(i, i ^ distance) for i in range(size)])


def partner_order(size):
    return [0, *range(size // 2, size), *range(1, size // 2)]


def exchange_all(blocks, axis):
    order = partner_order(lax.axis_size(axis))
    return [blocks[0]] + [
        xor_exchange(block, axis, distance)
        for block, distance in zip(blocks[1:], order[1:], strict=True)
    ]


def block_copy(w_hbm, dst, sem, distance):
    me = lax.axis_index("tensor")
    columns = dst.shape[-1]
    at = pl.multiple_of(lax.bitwise_xor(me, jnp.int32(distance)) * columns, LANES)
    return pltpu.make_async_copy(w_hbm.at[:, pl.ds(at, columns)], dst, sem)


def attend_kernel(
    owners,
    capacity,
    resident,
    ahead,
    lengths_hbm,
    adapter_hbm,
    slot_hbm,
    q_hbm,
    kf_hbm,
    vf_hbm,
    k_hbm,
    v_hbm,
    w_hbm,
    attn_ref,
    pick_ref,
    w_ref,
    *rest,
):
    send_refs, rest = rest[:owners], rest[owners:]
    lengths_ref, adapter_ref, slot_ref, q_ref, kf_ref, vf_ref, k_ref, v_ref = rest[:8]
    order_ref, q_cols_ref, o_ref, sems, small_sems, w_sems = rest[8:]
    steps, rows, width = q_ref.shape
    cache, kv_width = k_ref.shape[1:]
    heads = width // HEAD_WIDTH
    kv_here = kv_width // HEAD_WIDTH
    group = heads // kv_here
    per_row = heads * steps
    total = rows * per_row
    tokens = steps * rows
    chunks = sems.shape[1]
    chunk_rows = rows // chunks
    scale = 1.0 / math.sqrt(HEAD_WIDTH)

    def kv_copies(c):
        at = pl.ds(c * chunk_rows, chunk_rows)
        return [
            pltpu.make_async_copy(src.at[at], dst.at[at], sems.at[which, c])
            for which, (src, dst) in enumerate([(k_hbm, k_ref), (v_hbm, v_ref)])
        ]

    small = [
        pltpu.make_async_copy(src, dst, small_sems.at[n])
        for n, (src, dst) in enumerate(
            [
                (q_hbm, q_ref),
                (kf_hbm, kf_ref),
                (lengths_hbm, lengths_ref),
                (adapter_hbm, adapter_ref),
                (slot_hbm, slot_ref),
                (vf_hbm, vf_ref),
            ]
        )
    ]
    q_copy, kf_copy, lengths_copy, adapter_copy, slot_copy, vf_copy = small
    w_copies = [
        block_copy(w_hbm, w_ref.at[n], w_sems.at[n], d)
        for n, d in enumerate(ahead)
    ]
    first, *others = [kv_copies(c) for c in range(chunks)]
    for copy in [q_copy, *first, *small[1:], *sum(others, [])]:
        copy.start()

    @pl.loop(0, total // ORDER_ROWS)
    def _(i):
        at = iota((ORDER_ROWS, LANES), 0) + i * ORDER_ROWS
        source = mod(at, rows) * per_row + div(at, tokens) * steps + mod(div(at, rows), steps)
        here = pl.ds(pl.multiple_of(i * ORDER_ROWS, ORDER_ROWS), ORDER_ROWS)
        order_ref[here, :] = one_hot(source, total)

    adapter_copy.wait()
    slot_copy.wait()
    me = lax.axis_index("replica")
    positions = partner_order(owners)
    row_at = mod(iota((8, tokens), 1), rows)
    row_down = iota((rows, LANES), 0)
    first_slot = jnp.zeros((8, tokens), jnp.int32)
    local_of = jnp.zeros((rows, LANES), jnp.int32)
    firsts = []
    for r in range(rows):
        slot = slot_ref[adapter_ref[r]]
        owner = jnp.int32(0)
        for d in range(1, owners):
            owner = owner + (slot >= d * resident).astype(jnp.int32)
        partner = lax.bitwise_xor(owner, me)
        first = jnp.int32(0)
        for d in range(1, owners):
            first = jnp.where(partner == positions[d], d * capacity, first)
        firsts.append(first)
        first_slot = jnp.where(row_at == r, first, first_slot)
        local_of = jnp.where(row_down == r, slot - owner * resident, local_of)
    place = first_slot
    for r in range(rows - 1):
        place = place + ((first_slot == firsts[r]) & (row_at > r)).astype(jnp.int32)
    held = owners * capacity * steps
    slot_at = iota((held, tokens), 0)
    token_at = iota((held, tokens), 1)
    pick = (
        (jnp.concatenate([place] * (held // 8), axis=0) == div(slot_at, steps))
        & (mod(slot_at, steps) == div(token_at, rows))
    ).astype(jnp.bfloat16)
    pick_ref[...] = pick
    local_hot = (local_of == iota((rows, LANES), 1)).astype(jnp.bfloat16)
    entry = iota((owners * META_ROWS, rows), 0)
    entry_place = mod(entry, META_ROWS)
    entry_slot = div(entry, META_ROWS) * capacity + entry_place
    entry_pick = (
        (jnp.concatenate([place[:, :rows]] * (owners * META_ROWS // 8), axis=0) == entry_slot)
        & (entry_place < capacity)
    ).astype(jnp.bfloat16)
    meta = jnp.dot(entry_pick, local_hot, preferred_element_type=jnp.float32)

    q_copy.wait()
    by_head = jnp.concatenate(
        [
            q_ref[:, :, h * HEAD_WIDTH : (h + 1) * HEAD_WIDTH].reshape(tokens, HEAD_WIDTH)
            for h in range(heads)
        ],
        axis=0,
    )
    q_cols_ref[...] = jnp.dot(
        by_head.astype(jnp.float32).T.astype(jnp.bfloat16),
        order_ref[...],
        preferred_element_type=jnp.float32,
    )
    lane = iota((HEAD_WIDTH, LANES), 1)
    row_of = div(lane, per_row)
    kv_of = mod(div(lane, steps * group), kv_here)

    kf_copy.wait()
    kf = kf_ref[...].reshape(tokens, kv_width)
    token, query = iota((tokens, LANES), 0), iota((tokens, LANES), 1)
    position = iota((cache, LANES), 0)

    def scores(c):
        cols = q_cols_ref[:, pl.ds(pl.multiple_of(c * LANES, LANES), LANES)]
        by_kv = [jnp.where(kv_of == g, cols, 0.0) for g in range(kv_here)]
        fresh = jnp.dot(
            kf,
            jnp.concatenate(by_kv, axis=0).astype(jnp.bfloat16),
            preferred_element_type=jnp.float32,
        )
        live = (mod(token, rows) == div(query, per_row) + c * chunk_rows) & (
            div(token, rows) <= mod(query, steps)
        )
        fresh = jnp.where(live, fresh * scale, -jnp.inf)
        weights = jnp.concatenate(
            [jnp.where(row_of == j, q, 0.0) for j in range(chunk_rows) for q in by_kv], axis=0
        ).astype(jnp.bfloat16)
        keys = jnp.concatenate([k_ref[c * chunk_rows + j] for j in range(chunk_rows)], axis=1)
        cached = jnp.dot(keys, weights, preferred_element_type=jnp.float32)
        return cached * scale, fresh

    def softmax(c, cached, fresh):
        length = jnp.zeros((1, LANES), jnp.int32)
        for j in range(chunk_rows):
            length = jnp.where(
                div(iota((1, LANES), 1), per_row) == j, lengths_ref[c * chunk_rows + j], length
            )
        cached = jnp.where(position < length, cached, -jnp.inf)
        top = jnp.maximum(
            jnp.max(cached, axis=0, keepdims=True), jnp.max(fresh, axis=0, keepdims=True)
        )
        wc, wf = jnp.exp(cached - top), jnp.exp(fresh - top)
        share = 1.0 / (
            jnp.sum(wc, axis=0, keepdims=True) + jnp.sum(wf, axis=0, keepdims=True)
        )
        return (wc * share).T.astype(jnp.bfloat16), (wf * share).T.astype(jnp.bfloat16)

    kv_down = mod(div(iota((LANES, HEAD_WIDTH), 0), steps * group), kv_here)

    def values(c, cached, fresh):
        out = jnp.concatenate(
            [
                jnp.dot(
                    cached[j * per_row : (j + 1) * per_row, :],
                    v_ref[c * chunk_rows + j],
                    preferred_element_type=jnp.float32,
                )
                for j in range(chunk_rows)
            ],
            axis=0,
        ) + jnp.dot(fresh, vf, preferred_element_type=jnp.float32)
        own = out[:, :HEAD_WIDTH]
        for g in range(1, kv_here):
            own = jnp.where(kv_down == g, out[:, g * HEAD_WIDTH : (g + 1) * HEAD_WIDTH], own)
        return own.astype(jnp.bfloat16)

    lengths_copy.wait()
    vf_copy.wait()
    vf = vf_ref[...].reshape(tokens, kv_width)

    @pl.loop(0, chunks // TOGETHER)
    def _(i):
        groups = [i * TOGETHER + n for n in range(TOGETHER)]
        for c in groups:
            for copy in kv_copies(c):
                copy.wait()

        @pl.when(i == chunks // TOGETHER - 1)
        def _():
            for copy in w_copies:
                copy.start()

        scored = [scores(c) for c in groups]
        probs = [softmax(c, *part) for c, part in zip(groups, scored, strict=True)]
        for c, part in zip(groups, probs, strict=True):
            o_ref[pl.ds(pl.multiple_of(c * LANES, LANES), LANES), :] = values(c, *part)

    out = jnp.dot(
        order_ref[...], o_ref[...], preferred_element_type=jnp.float32
    ).astype(jnp.bfloat16)
    attn = jnp.concatenate(
        [out[h * tokens : (h + 1) * tokens, :] for h in range(heads)], axis=1
    )
    attn_ref[...] = attn
    sent = jnp.dot(pick, attn, preferred_element_type=jnp.float32)
    size = capacity * steps
    for d in range(owners):
        mine = sent[d * size : (d + 1) * size, :]
        send_refs[d][...] = jnp.concatenate(
            [mine[:, h * HEAD_WIDTH : (h + 1) * HEAD_WIDTH] for h in range(heads)]
            + [meta[d * META_ROWS : (d + 1) * META_ROWS, :]],
            axis=0,
        ).astype(jnp.bfloat16)
    for copy in w_copies:
        copy.wait()


def attend_and_pick(
    lengths,
    adapter_of_row,
    storage_slot,
    queries,
    fresh_keys,
    fresh_values,
    cached_keys,
    cached_values,
    weight,
    owners,
    capacity,
    resident,
    columns,
    ahead,
):
    steps, rows, width = queries.shape
    cache, kv_width = cached_keys.shape[1:]
    heads = width // HEAD_WIDTH
    total = rows * heads * steps
    tokens = steps * rows
    size = capacity * steps
    chunks = total // LANES
    outs = pl.pallas_call(
        functools.partial(attend_kernel, owners, capacity, resident, ahead),
        out_shape=[
            jax.ShapeDtypeStruct((tokens, width), jnp.bfloat16),
            jax.ShapeDtypeStruct((owners * size, tokens), jnp.bfloat16),
            pltpu.VMEM((len(ahead), width, columns), jnp.bfloat16),
        ]
        + [jax.ShapeDtypeStruct((heads * size + META_ROWS, HEAD_WIDTH), jnp.bfloat16)] * owners,
        in_specs=[HBM] * 9,
        out_specs=[VMEM] * (3 + owners),
        scratch_shapes=[
            pltpu.SMEM(lengths.shape, jnp.int32),
            pltpu.SMEM(adapter_of_row.shape, jnp.int32),
            pltpu.SMEM(storage_slot.shape, jnp.int32),
            pltpu.VMEM(queries.shape, jnp.bfloat16),
            pltpu.VMEM(fresh_keys.shape, jnp.bfloat16),
            pltpu.VMEM(fresh_values.shape, jnp.bfloat16),
            pltpu.VMEM((rows, cache, kv_width), jnp.bfloat16),
            pltpu.VMEM((rows, cache, kv_width), jnp.bfloat16),
            pltpu.VMEM((total, total), jnp.bfloat16),
            pltpu.VMEM((HEAD_WIDTH, total), jnp.float32),
            pltpu.VMEM((total, HEAD_WIDTH), jnp.bfloat16),
            pltpu.SemaphoreType.DMA((2, chunks)),
            pltpu.SemaphoreType.DMA((6,)),
            pltpu.SemaphoreType.DMA((len(ahead),)),
        ],
        compiler_params=pltpu.CompilerParams(vmem_limit_bytes=24 * MIB),
        cost_estimate=pl.CostEstimate(
            flops=8 * total * cache * kv_width,
            bytes_accessed=4 * rows * cache * kv_width,
            transcendentals=total * cache,
        ),
        name="attend",
    )(
        *in_hbm(
            lengths,
            adapter_of_row,
            storage_slot,
            queries,
            fresh_keys,
            fresh_values,
            cached_keys,
            cached_values,
            weight,
        ),
    )
    return outs[0], outs[1], outs[2], outs[3:]


def project_kernel(blocks, here, bring, added, attn_ref, w_hbm, *refs):
    here_ref = refs[0] if here else None
    add_refs = refs[bool(here) :][:added]
    refs = refs[len(refs) - len(blocks) - bool(bring) - 2 :]
    outs, w_ref, sems = refs[: len(blocks)], refs[-2], refs[-1]
    fetched = blocks[here:]
    copies = [
        block_copy(w_hbm, w_ref.at[n], sems.at[n], d) for n, d in enumerate(fetched)
    ] + [
        block_copy(w_hbm, refs[len(blocks)].at[n], sems.at[len(fetched) + n], d)
        for n, d in enumerate(bring)
    ]
    for copy in copies:
        copy.start()
    attn = attn_ref[...]
    for n in range(len(blocks)):
        if n >= here:
            copies[n - here].wait()
        block = here_ref.at[n] if n < here else w_ref.at[n - here]

        @pl.loop(0, block.shape[-1] // TILE)
        def _(i, n=n, block=block, out_ref=outs[n]):
            cols = pl.ds(pl.multiple_of(i * TILE, TILE), TILE)
            out = jnp.dot(attn, block[:, cols], preferred_element_type=jnp.float32)
            for add_ref in add_refs[n :: len(blocks)]:
                out = out + add_ref[:, cols].astype(jnp.float32)
            out_ref[:, cols] = out.astype(out_ref.dtype)

    for copy in copies[len(fetched) :]:
        copy.wait()


def project(attn, weight, columns, blocks, here=None, bring=(), add=(), dtype=jnp.bfloat16, after=()):
    tokens, width = attn.shape
    held = 0 if here is None else here.shape[0]
    fetched = len(blocks) - held
    extra = [*([here] if held else []), *add]
    outs = [jax.ShapeDtypeStruct((tokens, columns), dtype)] * len(blocks)
    if bring:
        outs.append(pltpu.VMEM((len(bring), width, columns), jnp.bfloat16))
    return pl.pallas_call(
        functools.partial(project_kernel, blocks, held, bring, len(add)),
        out_shape=outs,
        in_specs=[VMEM, HBM] + [VMEM] * len(extra) + [ANY] * len(after),
        out_specs=[VMEM] * len(outs),
        scratch_shapes=[
            pltpu.VMEM((max(fetched, 1), width if fetched else 16, columns), jnp.bfloat16),
            pltpu.SemaphoreType.DMA((fetched + len(bring),)),
        ],
        compiler_params=pltpu.CompilerParams(vmem_limit_bytes=16 * MIB),
        cost_estimate=pl.CostEstimate(
            flops=2 * tokens * width * columns * len(blocks),
            bytes_accessed=2 * width * columns * len(blocks),
            transcendentals=0,
        ),
        name="project",
    )(attn, *in_hbm(weight), *extra, *after)


def merge_kernel(mine_ref, got_ref, _, out_ref):
    out_ref[...] = (mine_ref[...] + got_ref[...].astype(jnp.float32)).astype(jnp.bfloat16)


def merge(mine, got, after):
    return pl.pallas_call(
        merge_kernel,
        out_shape=jax.ShapeDtypeStruct(mine.shape, jnp.bfloat16),
        in_specs=[VMEM, VMEM, ANY],
        out_specs=VMEM,
        compiler_params=pltpu.CompilerParams(vmem_limit_bytes=4 * MIB),
        name="merge",
    )(mine, got, after)


def down_kernel(capacity, steps, order, *refs):
    (*got_refs, down_ref, _, mine_ref, sent_ref, mask_ref) = refs
    resident, rank, width = down_ref.shape
    wide = resident * rank
    heads = width // HEAD_WIDTH
    size = capacity * steps
    held = size * len(got_refs)
    got = [got_refs[order.index(n)][...].astype(jnp.float32) for n in range(len(order))]
    rows = jnp.concatenate(
        [
            jnp.concatenate([part[h * size : (h + 1) * size, :] for part in got], axis=0)
            for h in range(heads)
        ],
        axis=1,
    ).astype(jnp.bfloat16)
    meta = jnp.concatenate([part[heads * size :, :] for part in got], axis=0)
    spread = div(iota((LANES, wide), 1), rank) == iota((LANES, wide), 0)
    entries = meta.shape[0]
    slot, entry = iota((held, entries), 0), iota((held, entries), 1)
    of_slot = entry == div(slot, size) * META_ROWS + div(mod(slot, size), steps)
    local = jnp.dot(
        of_slot.astype(jnp.bfloat16),
        meta.astype(jnp.bfloat16),
        preferred_element_type=jnp.float32,
    )
    mask = jnp.dot(
        local.astype(jnp.bfloat16),
        spread.astype(jnp.bfloat16),
        preferred_element_type=jnp.float32,
    )
    mask_ref[...] = mask.astype(jnp.bfloat16)
    low = lax.dot_general(
        rows,
        down_ref[...].reshape(wide, width),
        (((1,), (1,)), ((), ())),
        preferred_element_type=jnp.float32,
    )
    low = low * mask
    pair = low[:, :LANES]
    for n in range(1, wide // LANES):
        pair = pair + low[:, n * LANES : (n + 1) * LANES]
    both = pair + pltpu.roll(pair, rank, 1)
    half = held // 2
    packed = jnp.where(iota((half, LANES), 1) < rank, both[:half, :], both[half:, :])
    mine_ref[...] = packed
    sent_ref[...] = packed.astype(jnp.bfloat16)


def down(got, factors, capacity, steps, after):
    resident, rank, width = factors.shape
    held = len(got) * capacity * steps
    partners = partner_order(len(got))
    order = sorted(range(len(got)), key=lambda n: -partners[n])
    return pl.pallas_call(
        functools.partial(down_kernel, capacity, steps, order),
        out_shape=[
            jax.ShapeDtypeStruct((held // 2, LANES), jnp.float32),
            jax.ShapeDtypeStruct((held // 2, LANES), jnp.bfloat16),
            jax.ShapeDtypeStruct((held, resident * rank), jnp.bfloat16),
        ],
        in_specs=[VMEM] * (len(got) + 1) + [ANY],
        out_specs=[VMEM] * 3,
        compiler_params=pltpu.CompilerParams(vmem_limit_bytes=12 * MIB),
        cost_estimate=pl.CostEstimate(
            flops=200 * held * resident * rank * width,
            bytes_accessed=2 * resident * rank * width,
            transcendentals=0,
        ),
        name="down",
    )(*[got[n] for n in order], factors, after)


def up_kernel(peers, mine_ref, *refs):
    got_refs, (mask_ref, up_ref, _, *delta_refs) = refs[:peers], refs[peers:]
    resident, rank, columns = up_ref.shape
    wide = resident * rank
    total = mine_ref[...]
    for ref in got_refs:
        total = total + ref[...].astype(jnp.float32)
    other = pltpu.roll(total, rank, 1)
    first = iota(total.shape, 1) < rank
    both = jnp.concatenate(
        [jnp.where(first, total, other), jnp.where(first, other, total)], axis=0
    )
    both = jnp.concatenate([both] * (wide // LANES), axis=1)
    low = jnp.where(mask_ref[...].astype(jnp.float32) > 0.5, both, 0.0).astype(jnp.bfloat16)
    delta = jnp.dot(
        low, up_ref[...].reshape(wide, columns), preferred_element_type=jnp.float32
    ).astype(jnp.bfloat16)
    size = delta.shape[0] // len(delta_refs)
    for d, ref in enumerate(delta_refs):
        ref[...] = delta[d * size : (d + 1) * size, :]


def up(mine, got, mask, factors, owners, after):
    resident, rank, columns = factors.shape
    held = mask.shape[0]
    return pl.pallas_call(
        functools.partial(up_kernel, len(got)),
        out_shape=[jax.ShapeDtypeStruct((held // owners, columns), jnp.bfloat16)] * owners,
        in_specs=[VMEM] * (len(got) + 3) + [ANY],
        out_specs=[VMEM] * owners,
        compiler_params=pltpu.CompilerParams(vmem_limit_bytes=16 * MIB),
        cost_estimate=pl.CostEstimate(
            flops=200 * held * resident * rank * columns,
            bytes_accessed=2 * resident * rank * columns,
            transcendentals=0,
        ),
        name="up",
    )(mine, *got, mask, factors, after)


def finish_kernel(owners, pick_ref, *refs):
    delta_refs, (*near_refs, base_ref, out_hbm, out_ref, sems) = refs[:owners], refs[owners:]
    width = near_refs[0].shape[1]
    pick = pick_ref[...]
    copies = []
    for n, near_ref in enumerate(near_refs):
        cols = slice(n * width, (n + 1) * width)
        mixed = base_ref[:, cols] + near_ref[...].astype(jnp.float32)
        delta = jnp.concatenate([ref[:, cols] for ref in delta_refs], axis=0)
        mixed = mixed + lax.dot_general(
            pick, delta, (((0,), (0,)), ((), ())), preferred_element_type=jnp.float32
        )
        out_ref[:, :, cols] = mixed.astype(jnp.bfloat16).reshape(*out_ref.shape[:2], width)
        copies.append(
            pltpu.make_async_copy(out_ref.at[:, :, cols], out_hbm.at[:, :, cols], sems.at[n])
        )
        copies[n].start()
    for copy in copies:
        copy.wait()


def finish(base, pick, delta, near, steps):
    tokens, columns = base.shape
    shape = (steps, tokens // steps, columns)
    operands = [pick, *delta, *near, base]
    return pl.pallas_call(
        functools.partial(finish_kernel, len(delta)),
        out_shape=jax.ShapeDtypeStruct(shape, jnp.bfloat16),
        in_specs=[VMEM] * len(operands),
        out_specs=HBM,
        scratch_shapes=[
            pltpu.VMEM(shape, jnp.bfloat16),
            pltpu.SemaphoreType.DMA((len(near),)),
        ],
        compiler_params=pltpu.CompilerParams(vmem_limit_bytes=12 * MIB),
        cost_estimate=pl.CostEstimate(
            flops=2 * tokens * pick.shape[0] * columns,
            bytes_accessed=10 * tokens * columns,
            transcendentals=0,
        ),
        name="finish",
    )(*operands)


def body(
    queries,
    fresh_token_keys,
    fresh_token_values,
    cached_key_rows,
    cached_value_rows,
    cache_live_lengths,
    output_projection_weight,
    adapter_down_factors,
    adapter_up_factors,
    adapter_of_row,
    adapter_storage_slot,
):
    step_count, row_count, _ = queries.shape
    resident = adapter_down_factors.shape[0]
    owners = lax.axis_size("replica")
    tensors = lax.axis_size("tensor")
    capacity = max(2, 2 * row_count // owners)
    columns = adapter_up_factors.shape[2]
    far_sent, far_kept = list(range(3, tensors, 2)), list(range(2, tensors, 2))

    attn, pick, w_here, sent = attend_and_pick(
        cache_live_lengths,
        adapter_of_row,
        adapter_storage_slot,
        queries,
        fresh_token_keys,
        fresh_token_values,
        cached_key_rows,
        cached_value_rows,
        output_projection_weight,
        owners,
        capacity,
        resident,
        columns,
        far_sent,
    )
    got = exchange_all(sent, "replica")

    weight = output_projection_weight
    *parts, w_here = project(attn, weight, columns, far_sent, here=w_here, bring=far_kept)
    far_got = [xor_exchange(part, "tensor", 1) for part in parts]

    kept = project(
        attn, weight, columns, far_kept, here=w_here, dtype=jnp.float32, after=[parts[0]]
    )
    mine, low_sent, mask = down(got, adapter_down_factors, capacity, step_count, kept[0])
    low_got = [xor_exchange(low_sent, "tensor", d) for d in range(1, tensors)]
    halves_sent = [merge(*pair, low_sent) for pair in zip(kept, far_got, strict=True)]
    others = [xor_exchange(half, "tensor", d) for half, d in zip(halves_sent, far_kept, strict=True)]
    delta = up(mine, low_got, mask, adapter_up_factors, owners, halves_sent[0])
    delta_got = exchange_all(delta, "replica")

    (near,) = project(attn, weight, columns, [1], after=[delta[0]])
    width = columns // PIECES
    near_got = [
        xor_exchange(near[:, n * width : (n + 1) * width], "tensor", 1) for n in range(PIECES)
    ]
    (own,) = project(
        attn, weight, columns, [0], add=others, dtype=jnp.float32, after=[near]
    )
    return finish(own, pick, delta_got, near_got, step_count)


def solution(mesh):
    in_specs = (
        P(None, ("groups", "replica"), "tensor"),
        P(None, ("groups", "replica"), "tensor"),
        P(None, ("groups", "replica"), "tensor"),
        P(("groups", "replica"), None, "tensor"),
        P(("groups", "replica"), None, "tensor"),
        P(("groups", "replica")),
        P("tensor", None),
        P(("groups", "replica"), None, "tensor"),
        P(("groups", "replica"), None, "tensor"),
        P(("groups", "replica")),
        P("groups"),
    )
    out_specs = P(None, ("groups", "replica"), "tensor")
    return jax.shard_map(body, mesh=mesh, in_specs=in_specs, out_specs=out_specs, check_vma=False)
```

```python
import functools
import math

import jax
import jax.numpy as jnp
from jax import lax
from jax.experimental import pallas as pl
from jax.experimental.pallas import tpu as pltpu
from jax.sharding import PartitionSpec as P

HEAD_WIDTH = 128
LANES = 128
META_ROWS = 16
TILE = 512
TOGETHER = 2
ORDER_ROWS = 32
PIECES = 2
MIB = 1024 * 1024
VMEM = pl.BlockSpec(memory_space=pltpu.VMEM)
ANY = pl.BlockSpec(memory_space=pl.ANY)
HBM = pl.BlockSpec(memory_space=pltpu.HBM)


def iota(shape, dim):
    return lax.broadcasted_iota(jnp.int32, shape, dim)


def halves(n):
    if n & (n - 1):
        raise ValueError(n)
    return n.bit_length() - 1


def div(x, n):
    return lax.shift_right_logical(x, jnp.int32(halves(n)))


def mod(x, n):
    return x & ((1 << halves(n)) - 1)


def one_hot(source, width):
    lane = iota(source.shape, 1)
    return jnp.concatenate(
        [(source == lane + at).astype(jnp.bfloat16) for at in range(0, width, source.shape[1])],
        axis=1,
    )


def in_hbm(*arrays):
    return [pltpu.with_memory_space_constraint(a, pltpu.HBM) for a in arrays]


def xor_exchange(value, axis, distance):
    size = lax.axis_size(axis)
    return lax.ppermute(value, axis, [(i, i ^ distance) for i in range(size)])


def partner_order(size):
    return [0, *range(size // 2, size), *range(1, size // 2)]


def exchange_all(blocks, axis):
    order = partner_order(lax.axis_size(axis))
    return [blocks[0]] + [
        xor_exchange(block, axis, distance)
        for block, distance in zip(blocks[1:], order[1:], strict=True)
    ]


def block_copy(w_hbm, dst, sem, distance):
    me = lax.axis_index("tensor")
    columns = dst.shape[-1]
    at = pl.multiple_of(lax.bitwise_xor(me, jnp.int32(distance)) * columns, LANES)
    return pltpu.make_async_copy(w_hbm.at[:, pl.ds(at, columns)], dst, sem)


def attend_kernel(
    owners,
    capacity,
    resident,
    lengths_hbm,
    adapter_hbm,
    slot_hbm,
    q_hbm,
    kf_hbm,
    vf_hbm,
    k_hbm,
    v_hbm,
    attn_ref,
    pick_ref,
    *rest,
):
    send_refs, rest = rest[:owners], rest[owners:]
    lengths_ref, adapter_ref, slot_ref, q_ref, kf_ref, vf_ref, k_ref, v_ref = rest[:8]
    order_ref, q_cols_ref, o_ref, sems, small_sems = rest[8:]
    steps, rows, width = q_ref.shape
    cache, kv_width = k_ref.shape[1:]
    heads = width // HEAD_WIDTH
    kv_here = kv_width // HEAD_WIDTH
    group = heads // kv_here
    per_row = heads * steps
    total = rows * per_row
    tokens = steps * rows
    chunks = sems.shape[1]
    chunk_rows = rows // chunks
    scale = 1.0 / math.sqrt(HEAD_WIDTH)

    def kv_copies(c):
        at = pl.ds(c * chunk_rows, chunk_rows)
        return [
            pltpu.make_async_copy(src.at[at], dst.at[at], sems.at[which, c])
            for which, (src, dst) in enumerate([(k_hbm, k_ref), (v_hbm, v_ref)])
        ]

    small = [
        pltpu.make_async_copy(src, dst, small_sems.at[n])
        for n, (src, dst) in enumerate(
            [
                (q_hbm, q_ref),
                (kf_hbm, kf_ref),
                (lengths_hbm, lengths_ref),
                (adapter_hbm, adapter_ref),
                (slot_hbm, slot_ref),
                (vf_hbm, vf_ref),
            ]
        )
    ]
    q_copy, kf_copy, lengths_copy, adapter_copy, slot_copy, vf_copy = small
    first, *others = [kv_copies(c) for c in range(chunks)]
    for copy in [q_copy, *first, *small[1:], *sum(others, [])]:
        copy.start()

    @pl.loop(0, total // ORDER_ROWS)
    def _(i):
        at = iota((ORDER_ROWS, LANES), 0) + i * ORDER_ROWS
        source = mod(at, rows) * per_row + div(at, tokens) * steps + mod(div(at, rows), steps)
        here = pl.ds(pl.multiple_of(i * ORDER_ROWS, ORDER_ROWS), ORDER_ROWS)
        order_ref[here, :] = one_hot(source, total)

    adapter_copy.wait()
    slot_copy.wait()
    me = lax.axis_index("replica")
    positions = partner_order(owners)
    row_at = mod(iota((8, tokens), 1), rows)
    row_down = iota((rows, LANES), 0)
    first_slot = jnp.zeros((8, tokens), jnp.int32)
    local_of = jnp.zeros((rows, LANES), jnp.int32)
    firsts = []
    for r in range(rows):
        slot = slot_ref[adapter_ref[r]]
        owner = jnp.int32(0)
        for d in range(1, owners):
            owner = owner + (slot >= d * resident).astype(jnp.int32)
        partner = lax.bitwise_xor(owner, me)
        first = jnp.int32(0)
        for d in range(1, owners):
            first = jnp.where(partner == positions[d], d * capacity, first)
        firsts.append(first)
        first_slot = jnp.where(row_at == r, first, first_slot)
        local_of = jnp.where(row_down == r, slot - owner * resident, local_of)
    place = first_slot
    for r in range(rows - 1):
        place = place + ((first_slot == firsts[r]) & (row_at > r)).astype(jnp.int32)
    held = owners * capacity * steps
    slot_at = iota((held, tokens), 0)
    token_at = iota((held, tokens), 1)
    pick = (
        (jnp.concatenate([place] * (held // 8), axis=0) == div(slot_at, steps))
        & (mod(slot_at, steps) == div(token_at, rows))
    ).astype(jnp.bfloat16)
    pick_ref[...] = pick
    local_hot = (local_of == iota((rows, LANES), 1)).astype(jnp.bfloat16)
    entry = iota((owners * META_ROWS, rows), 0)
    entry_place = mod(entry, META_ROWS)
    entry_slot = div(entry, META_ROWS) * capacity + entry_place
    entry_pick = (
        (jnp.concatenate([place[:, :rows]] * (owners * META_ROWS // 8), axis=0) == entry_slot)
        & (entry_place < capacity)
    ).astype(jnp.bfloat16)
    meta = jnp.dot(entry_pick, local_hot, preferred_element_type=jnp.float32)

    q_copy.wait()
    by_head = jnp.concatenate(
        [
            q_ref[:, :, h * HEAD_WIDTH : (h + 1) * HEAD_WIDTH].reshape(tokens, HEAD_WIDTH)
            for h in range(heads)
        ],
        axis=0,
    )
    q_cols_ref[...] = jnp.dot(
        by_head.astype(jnp.float32).T.astype(jnp.bfloat16),
        order_ref[...],
        preferred_element_type=jnp.float32,
    )
    lane = iota((HEAD_WIDTH, LANES), 1)
    row_of = div(lane, per_row)
    kv_of = mod(div(lane, steps * group), kv_here)

    kf_copy.wait()
    kf = kf_ref[...].reshape(tokens, kv_width)
    token, query = iota((tokens, LANES), 0), iota((tokens, LANES), 1)
    position = iota((cache, LANES), 0)

    def scores(c):
        cols = q_cols_ref[:, pl.ds(pl.multiple_of(c * LANES, LANES), LANES)]
        by_kv = [jnp.where(kv_of == g, cols, 0.0) for g in range(kv_here)]
        fresh = jnp.dot(
            kf,
            jnp.concatenate(by_kv, axis=0).astype(jnp.bfloat16),
            preferred_element_type=jnp.float32,
        )
        live = (mod(token, rows) == div(query, per_row) + c * chunk_rows) & (
            div(token, rows) <= mod(query, steps)
        )
        fresh = jnp.where(live, fresh * scale, -jnp.inf)
        weights = jnp.concatenate(
            [jnp.where(row_of == j, q, 0.0) for j in range(chunk_rows) for q in by_kv], axis=0
        ).astype(jnp.bfloat16)
        keys = jnp.concatenate([k_ref[c * chunk_rows + j] for j in range(chunk_rows)], axis=1)
        cached = jnp.dot(keys, weights, preferred_element_type=jnp.float32)
        return cached * scale, fresh

    def softmax(c, cached, fresh):
        length = jnp.zeros((1, LANES), jnp.int32)
        for j in range(chunk_rows):
            length = jnp.where(
                div(iota((1, LANES), 1), per_row) == j, lengths_ref[c * chunk_rows + j], length
            )
        cached = jnp.where(position < length, cached, -jnp.inf)
        top = jnp.maximum(
            jnp.max(cached, axis=0, keepdims=True), jnp.max(fresh, axis=0, keepdims=True)
        )
        wc, wf = jnp.exp(cached - top), jnp.exp(fresh - top)
        share = 1.0 / (
            jnp.sum(wc, axis=0, keepdims=True) + jnp.sum(wf, axis=0, keepdims=True)
        )
        return (wc * share).T.astype(jnp.bfloat16), (wf * share).T.astype(jnp.bfloat16)

    kv_down = mod(div(iota((LANES, HEAD_WIDTH), 0), steps * group), kv_here)

    def values(c, cached, fresh):
        out = jnp.concatenate(
            [
                jnp.dot(
                    cached[j * per_row : (j + 1) * per_row, :],
                    v_ref[c * chunk_rows + j],
                    preferred_element_type=jnp.float32,
                )
                for j in range(chunk_rows)
            ],
            axis=0,
        ) + jnp.dot(fresh, vf, preferred_element_type=jnp.float32)
        own = out[:, :HEAD_WIDTH]
        for g in range(1, kv_here):
            own = jnp.where(kv_down == g, out[:, g * HEAD_WIDTH : (g + 1) * HEAD_WIDTH], own)
        return own.astype(jnp.bfloat16)

    lengths_copy.wait()
    vf_copy.wait()
    vf = vf_ref[...].reshape(tokens, kv_width)

    @pl.loop(0, chunks // TOGETHER)
    def _(i):
        groups = [i * TOGETHER + n for n in range(TOGETHER)]
        for c in groups:
            for copy in kv_copies(c):
                copy.wait()

        scored = [scores(c) for c in groups]
        probs = [softmax(c, *part) for c, part in zip(groups, scored, strict=True)]
        for c, part in zip(groups, probs, strict=True):
            o_ref[pl.ds(pl.multiple_of(c * LANES, LANES), LANES), :] = values(c, *part)

    out = jnp.dot(
        order_ref[...], o_ref[...], preferred_element_type=jnp.float32
    ).astype(jnp.bfloat16)
    attn = jnp.concatenate(
        [out[h * tokens : (h + 1) * tokens, :] for h in range(heads)], axis=1
    )
    attn_ref[...] = attn
    sent = jnp.dot(pick, attn, preferred_element_type=jnp.float32)
    size = capacity * steps
    for d in range(owners):
        mine = sent[d * size : (d + 1) * size, :]
        send_refs[d][...] = jnp.concatenate(
            [mine[:, h * HEAD_WIDTH : (h + 1) * HEAD_WIDTH] for h in range(heads)]
            + [meta[d * META_ROWS : (d + 1) * META_ROWS, :]],
            axis=0,
        ).astype(jnp.bfloat16)


def attend_and_pick(
    lengths,
    adapter_of_row,
    storage_slot,
    queries,
    fresh_keys,
    fresh_values,
    cached_keys,
    cached_values,
    owners,
    capacity,
    resident,
):
    steps, rows, width = queries.shape
    cache, kv_width = cached_keys.shape[1:]
    heads = width // HEAD_WIDTH
    total = rows * heads * steps
    tokens = steps * rows
    size = capacity * steps
    chunks = total // LANES
    outs = pl.pallas_call(
        functools.partial(attend_kernel, owners, capacity, resident),
        out_shape=[
            jax.ShapeDtypeStruct((tokens, width), jnp.bfloat16),
            jax.ShapeDtypeStruct((owners * size, tokens), jnp.bfloat16),
        ]
        + [jax.ShapeDtypeStruct((heads * size + META_ROWS, HEAD_WIDTH), jnp.bfloat16)] * owners,
        in_specs=[HBM] * 8,
        out_specs=[VMEM] * (2 + owners),
        scratch_shapes=[
            pltpu.SMEM(lengths.shape, jnp.int32),
            pltpu.SMEM(adapter_of_row.shape, jnp.int32),
            pltpu.SMEM(storage_slot.shape, jnp.int32),
            pltpu.VMEM(queries.shape, jnp.bfloat16),
            pltpu.VMEM(fresh_keys.shape, jnp.bfloat16),
            pltpu.VMEM(fresh_values.shape, jnp.bfloat16),
            pltpu.VMEM((rows, cache, kv_width), jnp.bfloat16),
            pltpu.VMEM((rows, cache, kv_width), jnp.bfloat16),
            pltpu.VMEM((total, total), jnp.bfloat16),
            pltpu.VMEM((HEAD_WIDTH, total), jnp.float32),
            pltpu.VMEM((total, HEAD_WIDTH), jnp.bfloat16),
            pltpu.SemaphoreType.DMA((2, chunks)),
            pltpu.SemaphoreType.DMA((6,)),
        ],
        compiler_params=pltpu.CompilerParams(vmem_limit_bytes=24 * MIB),
        cost_estimate=pl.CostEstimate(
            flops=8 * total * cache * kv_width,
            bytes_accessed=4 * rows * cache * kv_width,
            transcendentals=total * cache,
        ),
        name="attend",
    )(
        *in_hbm(
            lengths,
            adapter_of_row,
            storage_slot,
            queries,
            fresh_keys,
            fresh_values,
            cached_keys,
            cached_values,
        ),
    )
    return outs[0], outs[1], outs[2:]


def project_kernel(blocks, here, bring, added, attn_ref, w_hbm, *refs):
    here_ref = refs[0] if here else None
    add_refs = refs[bool(here) :][:added]
    refs = refs[len(refs) - len(blocks) - bool(bring) - 2 :]
    outs, w_ref, sems = refs[: len(blocks)], refs[-2], refs[-1]
    fetched = blocks[here:]
    copies = [
        block_copy(w_hbm, w_ref.at[n], sems.at[n], d) for n, d in enumerate(fetched)
    ] + [
        block_copy(w_hbm, refs[len(blocks)].at[n], sems.at[len(fetched) + n], d)
        for n, d in enumerate(bring)
    ]
    for copy in copies:
        copy.start()
    attn = attn_ref[...]
    for n in range(len(blocks)):
        if n >= here:
            copies[n - here].wait()
        block = here_ref.at[n] if n < here else w_ref.at[n - here]

        @pl.loop(0, block.shape[-1] // TILE)
        def _(i, n=n, block=block, out_ref=outs[n]):
            cols = pl.ds(pl.multiple_of(i * TILE, TILE), TILE)
            out = jnp.dot(attn, block[:, cols], preferred_element_type=jnp.float32)
            for add_ref in add_refs[n :: len(blocks)]:
                out = out + add_ref[:, cols].astype(jnp.float32)
            out_ref[:, cols] = out.astype(out_ref.dtype)

    for copy in copies[len(fetched) :]:
        copy.wait()


def project(attn, weight, columns, blocks, here=None, bring=(), add=(), dtype=jnp.bfloat16, after=()):
    tokens, width = attn.shape
    held = 0 if here is None else here.shape[0]
    fetched = len(blocks) - held
    extra = [*([here] if held else []), *add]
    outs = [jax.ShapeDtypeStruct((tokens, columns), dtype)] * len(blocks)
    if bring:
        outs.append(pltpu.VMEM((len(bring), width, columns), jnp.bfloat16))
    return pl.pallas_call(
        functools.partial(project_kernel, blocks, held, bring, len(add)),
        out_shape=outs,
        in_specs=[VMEM, HBM] + [VMEM] * len(extra) + [ANY] * len(after),
        out_specs=[VMEM] * len(outs),
        scratch_shapes=[
            pltpu.VMEM((max(fetched, 1), width if fetched else 16, columns), jnp.bfloat16),
            pltpu.SemaphoreType.DMA((fetched + len(bring),)),
        ],
        compiler_params=pltpu.CompilerParams(vmem_limit_bytes=16 * MIB),
        cost_estimate=pl.CostEstimate(
            flops=2 * tokens * width * columns * len(blocks),
            bytes_accessed=2 * width * columns * len(blocks),
            transcendentals=0,
        ),
        name="project",
    )(attn, *in_hbm(weight), *extra, *after)


def merge_kernel(mine_ref, got_ref, _, out_ref):
    out_ref[...] = (mine_ref[...] + got_ref[...].astype(jnp.float32)).astype(jnp.bfloat16)


def merge(mine, got, after):
    return pl.pallas_call(
        merge_kernel,
        out_shape=jax.ShapeDtypeStruct(mine.shape, jnp.bfloat16),
        in_specs=[VMEM, VMEM, ANY],
        out_specs=VMEM,
        compiler_params=pltpu.CompilerParams(vmem_limit_bytes=4 * MIB),
        name="merge",
    )(mine, got, after)


def down_kernel(capacity, steps, *refs):
    (*got_refs, down_ref, _, mine_ref, sent_ref, mask_ref) = refs
    resident, rank, width = down_ref.shape
    wide = resident * rank
    heads = width // HEAD_WIDTH
    size = capacity * steps
    held = size * len(got_refs)
    got = [ref[...].astype(jnp.float32) for ref in got_refs]
    rows = jnp.concatenate(
        [
            jnp.concatenate([part[h * size : (h + 1) * size, :] for part in got], axis=0)
            for h in range(heads)
        ],
        axis=1,
    ).astype(jnp.bfloat16)
    meta = jnp.concatenate([part[heads * size :, :] for part in got], axis=0)
    spread = div(iota((LANES, wide), 1), rank) == iota((LANES, wide), 0)
    entries = meta.shape[0]
    slot, entry = iota((held, entries), 0), iota((held, entries), 1)
    of_slot = entry == div(slot, size) * META_ROWS + div(mod(slot, size), steps)
    local = jnp.dot(
        of_slot.astype(jnp.bfloat16),
        meta.astype(jnp.bfloat16),
        preferred_element_type=jnp.float32,
    )
    mask = jnp.dot(
        local.astype(jnp.bfloat16),
        spread.astype(jnp.bfloat16),
        preferred_element_type=jnp.float32,
    )
    mask_ref[...] = mask.astype(jnp.bfloat16)
    low = lax.dot_general(
        rows,
        down_ref[...].reshape(wide, width),
        (((1,), (1,)), ((), ())),
        preferred_element_type=jnp.float32,
    )
    low = low * mask
    pair = low[:, :LANES]
    for n in range(1, wide // LANES):
        pair = pair + low[:, n * LANES : (n + 1) * LANES]
    both = pair + pltpu.roll(pair, rank, 1)
    half = held // 2
    packed = jnp.where(iota((half, LANES), 1) < rank, both[:half, :], both[half:, :])
    mine_ref[...] = packed
    sent_ref[...] = packed.astype(jnp.bfloat16)


def down(got, factors, capacity, steps, after):
    resident, rank, width = factors.shape
    held = len(got) * capacity * steps
    return pl.pallas_call(
        functools.partial(down_kernel, capacity, steps),
        out_shape=[
            jax.ShapeDtypeStruct((held // 2, LANES), jnp.float32),
            jax.ShapeDtypeStruct((held // 2, LANES), jnp.bfloat16),
            jax.ShapeDtypeStruct((held, resident * rank), jnp.bfloat16),
        ],
        in_specs=[VMEM] * (len(got) + 1) + [ANY],
        out_specs=[VMEM] * 3,
        compiler_params=pltpu.CompilerParams(vmem_limit_bytes=12 * MIB),
        cost_estimate=pl.CostEstimate(
            flops=200 * held * resident * rank * width,
            bytes_accessed=2 * resident * rank * width,
            transcendentals=0,
        ),
        name="down",
    )(*got, factors, after)


def up_kernel(peers, mine_ref, *refs):
    got_refs, (mask_ref, up_ref, _, *delta_refs) = refs[:peers], refs[peers:]
    resident, rank, columns = up_ref.shape
    wide = resident * rank
    total = mine_ref[...]
    for ref in got_refs:
        total = total + ref[...].astype(jnp.float32)
    other = pltpu.roll(total, rank, 1)
    first = iota(total.shape, 1) < rank
    both = jnp.concatenate(
        [jnp.where(first, total, other), jnp.where(first, other, total)], axis=0
    )
    both = jnp.concatenate([both] * (wide // LANES), axis=1)
    low = jnp.where(mask_ref[...].astype(jnp.float32) > 0.5, both, 0.0).astype(jnp.bfloat16)
    delta = jnp.dot(
        low, up_ref[...].reshape(wide, columns), preferred_element_type=jnp.float32
    ).astype(jnp.bfloat16)
    size = delta.shape[0] // len(delta_refs)
    for d, ref in enumerate(delta_refs):
        ref[...] = delta[d * size : (d + 1) * size, :]


def up(mine, got, mask, factors, owners, after):
    resident, rank, columns = factors.shape
    held = mask.shape[0]
    return pl.pallas_call(
        functools.partial(up_kernel, len(got)),
        out_shape=[jax.ShapeDtypeStruct((held // owners, columns), jnp.bfloat16)] * owners,
        in_specs=[VMEM] * (len(got) + 3) + [ANY],
        out_specs=[VMEM] * owners,
        compiler_params=pltpu.CompilerParams(vmem_limit_bytes=16 * MIB),
        cost_estimate=pl.CostEstimate(
            flops=200 * held * resident * rank * columns,
            bytes_accessed=2 * resident * rank * columns,
            transcendentals=0,
        ),
        name="up",
    )(mine, *got, mask, factors, after)


def finish_kernel(owners, pick_ref, *refs):
    delta_refs, (*near_refs, base_ref, out_hbm, out_ref, sems) = refs[:owners], refs[owners:]
    width = near_refs[0].shape[1]
    pick = pick_ref[...]
    copies = []
    for n, near_ref in enumerate(near_refs):
        cols = slice(n * width, (n + 1) * width)
        mixed = base_ref[:, cols] + near_ref[...].astype(jnp.float32)
        delta = jnp.concatenate([ref[:, cols] for ref in delta_refs], axis=0)
        mixed = mixed + lax.dot_general(
            pick, delta, (((0,), (0,)), ((), ())), preferred_element_type=jnp.float32
        )
        out_ref[:, :, cols] = mixed.astype(jnp.bfloat16).reshape(*out_ref.shape[:2], width)
        copies.append(
            pltpu.make_async_copy(out_ref.at[:, :, cols], out_hbm.at[:, :, cols], sems.at[n])
        )
        copies[n].start()
    for copy in copies:
        copy.wait()


def finish(base, pick, delta, near, steps):
    tokens, columns = base.shape
    shape = (steps, tokens // steps, columns)
    operands = [pick, *delta, *near, base]
    return pl.pallas_call(
        functools.partial(finish_kernel, len(delta)),
        out_shape=jax.ShapeDtypeStruct(shape, jnp.bfloat16),
        in_specs=[VMEM] * len(operands),
        out_specs=HBM,
        scratch_shapes=[
            pltpu.VMEM(shape, jnp.bfloat16),
            pltpu.SemaphoreType.DMA((len(near),)),
        ],
        compiler_params=pltpu.CompilerParams(vmem_limit_bytes=12 * MIB),
        cost_estimate=pl.CostEstimate(
            flops=2 * tokens * pick.shape[0] * columns,
            bytes_accessed=10 * tokens * columns,
            transcendentals=0,
        ),
        name="finish",
    )(*operands)


def body(
    queries,
    fresh_token_keys,
    fresh_token_values,
    cached_key_rows,
    cached_value_rows,
    cache_live_lengths,
    output_projection_weight,
    adapter_down_factors,
    adapter_up_factors,
    adapter_of_row,
    adapter_storage_slot,
):
    step_count, row_count, _ = queries.shape
    resident = adapter_down_factors.shape[0]
    owners = lax.axis_size("replica")
    tensors = lax.axis_size("tensor")
    capacity = max(2, 2 * row_count // owners)
    columns = adapter_up_factors.shape[2]
    far_sent, far_kept = list(range(3, tensors, 2)), list(range(2, tensors, 2))

    attn, pick, sent = attend_and_pick(
        cache_live_lengths,
        adapter_of_row,
        adapter_storage_slot,
        queries,
        fresh_token_keys,
        fresh_token_values,
        cached_key_rows,
        cached_value_rows,
        owners,
        capacity,
        resident,
    )
    got = exchange_all(sent, "replica")

    weight = output_projection_weight
    *parts, w_here = project(attn, weight, columns, far_sent, bring=far_kept)
    far_got = [xor_exchange(part, "tensor", 1) for part in parts]

    kept = project(
        attn, weight, columns, far_kept, here=w_here, dtype=jnp.float32, after=[parts[0]]
    )
    mine, low_sent, mask = down(got, adapter_down_factors, capacity, step_count, kept[0])
    low_got = [xor_exchange(low_sent, "tensor", d) for d in range(1, tensors)]
    halves_sent = [merge(*pair, low_sent) for pair in zip(kept, far_got, strict=True)]
    others = [xor_exchange(half, "tensor", d) for half, d in zip(halves_sent, far_kept, strict=True)]
    delta = up(mine, low_got, mask, adapter_up_factors, owners, halves_sent[0])
    delta_got = exchange_all(delta, "replica")

    (near,) = project(attn, weight, columns, [1], after=[delta[0]])
    width = columns // PIECES
    near_got = [
        xor_exchange(near[:, n * width : (n + 1) * width], "tensor", 1) for n in range(PIECES)
    ]
    (own,) = project(
        attn, weight, columns, [0], add=others, dtype=jnp.float32, after=[near]
    )
    return finish(own, pick, delta_got, near_got, step_count)


def solution(mesh):
    in_specs = (
        P(None, ("groups", "replica"), "tensor"),
        P(None, ("groups", "replica"), "tensor"),
        P(None, ("groups", "replica"), "tensor"),
        P(("groups", "replica"), None, "tensor"),
        P(("groups", "replica"), None, "tensor"),
        P(("groups", "replica")),
        P("tensor", None),
        P(("groups", "replica"), None, "tensor"),
        P(("groups", "replica"), None, "tensor"),
        P(("groups", "replica")),
        P("groups"),
    )
    out_specs = P(None, ("groups", "replica"), "tensor")
    return jax.shard_map(body, mesh=mesh, in_specs=in_specs, out_specs=out_specs, check_vma=False)
```

```python
import functools
import math

import jax
import jax.numpy as jnp
from jax import lax
from jax.experimental import pallas as pl
from jax.experimental.pallas import tpu as pltpu
from jax.sharding import PartitionSpec as P

HEAD_WIDTH = 128
LANES = 128
META_ROWS = 16
TILE = 512
TOGETHER = 2
ORDER_ROWS = 32
PIECES = 2
MIB = 1024 * 1024
VMEM = pl.BlockSpec(memory_space=pltpu.VMEM)
ANY = pl.BlockSpec(memory_space=pl.ANY)
HBM = pl.BlockSpec(memory_space=pltpu.HBM)


def iota(shape, dim):
    return lax.broadcasted_iota(jnp.int32, shape, dim)


def halves(n):
    if n & (n - 1):
        raise ValueError(n)
    return n.bit_length() - 1


def div(x, n):
    return lax.shift_right_logical(x, jnp.int32(halves(n)))


def mod(x, n):
    return x & ((1 << halves(n)) - 1)


def one_hot(source, width):
    lane = iota(source.shape, 1)
    return jnp.concatenate(
        [(source == lane + at).astype(jnp.bfloat16) for at in range(0, width, source.shape[1])],
        axis=1,
    )


def in_hbm(*arrays):
    return [pltpu.with_memory_space_constraint(a, pltpu.HBM) for a in arrays]


def xor_exchange(value, axis, distance):
    size = lax.axis_size(axis)
    return lax.ppermute(value, axis, [(i, i ^ distance) for i in range(size)])


def partner_order(size):
    return [0, *range(size // 2, size), *range(1, size // 2)]


def exchange_all(blocks, axis):
    order = partner_order(lax.axis_size(axis))
    return [blocks[0]] + [
        xor_exchange(block, axis, distance)
        for block, distance in zip(blocks[1:], order[1:], strict=True)
    ]


def block_copy(w_hbm, dst, sem, distance):
    me = lax.axis_index("tensor")
    columns = dst.shape[-1]
    at = pl.multiple_of(lax.bitwise_xor(me, jnp.int32(distance)) * columns, LANES)
    return pltpu.make_async_copy(w_hbm.at[:, pl.ds(at, columns)], dst, sem)


def attend_kernel(
    owners,
    capacity,
    resident,
    ahead,
    lengths_hbm,
    adapter_hbm,
    slot_hbm,
    q_hbm,
    kf_hbm,
    vf_hbm,
    k_hbm,
    v_hbm,
    w_hbm,
    attn_ref,
    pick_ref,
    w_ref,
    *rest,
):
    send_refs, rest = rest[:owners], rest[owners:]
    lengths_ref, adapter_ref, slot_ref, q_ref, kf_ref, vf_ref, k_ref, v_ref = rest[:8]
    order_ref, q_cols_ref, o_ref, sems, small_sems, w_sems = rest[8:]
    steps, rows, width = q_ref.shape
    cache, kv_width = k_ref.shape[1:]
    heads = width // HEAD_WIDTH
    kv_here = kv_width // HEAD_WIDTH
    group = heads // kv_here
    per_row = heads * steps
    total = rows * per_row
    tokens = steps * rows
    chunks = sems.shape[1]
    chunk_rows = rows // chunks
    scale = 1.0 / math.sqrt(HEAD_WIDTH)

    def kv_copies(c):
        at = pl.ds(c * chunk_rows, chunk_rows)
        return [
            pltpu.make_async_copy(src.at[at], dst.at[at], sems.at[which, c])
            for which, (src, dst) in enumerate([(k_hbm, k_ref), (v_hbm, v_ref)])
        ]

    small = [
        pltpu.make_async_copy(src, dst, small_sems.at[n])
        for n, (src, dst) in enumerate(
            [
                (q_hbm, q_ref),
                (kf_hbm, kf_ref),
                (lengths_hbm, lengths_ref),
                (adapter_hbm, adapter_ref),
                (slot_hbm, slot_ref),
                (vf_hbm, vf_ref),
            ]
        )
    ]
    q_copy, kf_copy, lengths_copy, adapter_copy, slot_copy, vf_copy = small
    first, *others = [kv_copies(c) for c in range(chunks)]
    for copy in [q_copy, *first, *small[1:], *sum(others, [])]:
        copy.start()

    @pl.loop(0, total // ORDER_ROWS)
    def _(i):
        at = iota((ORDER_ROWS, LANES), 0) + i * ORDER_ROWS
        source = mod(at, rows) * per_row + div(at, tokens) * steps + mod(div(at, rows), steps)
        here = pl.ds(pl.multiple_of(i * ORDER_ROWS, ORDER_ROWS), ORDER_ROWS)
        order_ref[here, :] = one_hot(source, total)

    adapter_copy.wait()
    slot_copy.wait()
    me = lax.axis_index("replica")
    positions = partner_order(owners)
    row_at = mod(iota((8, tokens), 1), rows)
    row_down = iota((rows, LANES), 0)
    first_slot = jnp.zeros((8, tokens), jnp.int32)
    local_of = jnp.zeros((rows, LANES), jnp.int32)
    firsts = []
    for r in range(rows):
        slot = slot_ref[adapter_ref[r]]
        owner = jnp.int32(0)
        for d in range(1, owners):
            owner = owner + (slot >= d * resident).astype(jnp.int32)
        partner = lax.bitwise_xor(owner, me)
        first = jnp.int32(0)
        for d in range(1, owners):
            first = jnp.where(partner == positions[d], d * capacity, first)
        firsts.append(first)
        first_slot = jnp.where(row_at == r, first, first_slot)
        local_of = jnp.where(row_down == r, slot - owner * resident, local_of)
    place = first_slot
    for r in range(rows - 1):
        place = place + ((first_slot == firsts[r]) & (row_at > r)).astype(jnp.int32)
    held = owners * capacity * steps
    slot_at = iota((held, tokens), 0)
    token_at = iota((held, tokens), 1)
    pick = (
        (jnp.concatenate([place] * (held // 8), axis=0) == div(slot_at, steps))
        & (mod(slot_at, steps) == div(token_at, rows))
    ).astype(jnp.bfloat16)
    pick_ref[...] = pick
    local_hot = (local_of == iota((rows, LANES), 1)).astype(jnp.bfloat16)
    entry = iota((owners * META_ROWS, rows), 0)
    entry_place = mod(entry, META_ROWS)
    entry_slot = div(entry, META_ROWS) * capacity + entry_place
    entry_pick = (
        (jnp.concatenate([place[:, :rows]] * (owners * META_ROWS // 8), axis=0) == entry_slot)
        & (entry_place < capacity)
    ).astype(jnp.bfloat16)
    meta = jnp.dot(entry_pick, local_hot, preferred_element_type=jnp.float32)

    q_copy.wait()
    by_head = jnp.concatenate(
        [
            q_ref[:, :, h * HEAD_WIDTH : (h + 1) * HEAD_WIDTH].reshape(tokens, HEAD_WIDTH)
            for h in range(heads)
        ],
        axis=0,
    )
    q_cols_ref[...] = jnp.dot(
        by_head.astype(jnp.float32).T.astype(jnp.bfloat16),
        order_ref[...],
        preferred_element_type=jnp.float32,
    )
    lane = iota((HEAD_WIDTH, LANES), 1)
    row_of = div(lane, per_row)
    kv_of = mod(div(lane, steps * group), kv_here)

    kf_copy.wait()
    kf = kf_ref[...].reshape(tokens, kv_width)
    token, query = iota((tokens, LANES), 0), iota((tokens, LANES), 1)
    position = iota((cache, LANES), 0)

    def scores(c):
        cols = q_cols_ref[:, pl.ds(pl.multiple_of(c * LANES, LANES), LANES)]
        by_kv = [jnp.where(kv_of == g, cols, 0.0) for g in range(kv_here)]
        fresh = jnp.dot(
            kf,
            jnp.concatenate(by_kv, axis=0).astype(jnp.bfloat16),
            preferred_element_type=jnp.float32,
        )
        live = (mod(token, rows) == div(query, per_row) + c * chunk_rows) & (
            div(token, rows) <= mod(query, steps)
        )
        fresh = jnp.where(live, fresh * scale, -jnp.inf)
        weights = jnp.concatenate(
            [jnp.where(row_of == j, q, 0.0) for j in range(chunk_rows) for q in by_kv], axis=0
        ).astype(jnp.bfloat16)
        keys = jnp.concatenate([k_ref[c * chunk_rows + j] for j in range(chunk_rows)], axis=1)
        cached = jnp.dot(keys, weights, preferred_element_type=jnp.float32)
        return cached * scale, fresh

    def softmax(c, cached, fresh):
        length = jnp.zeros((1, LANES), jnp.int32)
        for j in range(chunk_rows):
            length = jnp.where(
                div(iota((1, LANES), 1), per_row) == j, lengths_ref[c * chunk_rows + j], length
            )
        cached = jnp.where(position < length, cached, -jnp.inf)
        top = jnp.maximum(
            jnp.max(cached, axis=0, keepdims=True), jnp.max(fresh, axis=0, keepdims=True)
        )
        wc, wf = jnp.exp(cached - top), jnp.exp(fresh - top)
        share = 1.0 / (
            jnp.sum(wc, axis=0, keepdims=True) + jnp.sum(wf, axis=0, keepdims=True)
        )
        return (wc * share).T.astype(jnp.bfloat16), (wf * share).T.astype(jnp.bfloat16)

    kv_down = mod(div(iota((LANES, HEAD_WIDTH), 0), steps * group), kv_here)

    def values(c, cached, fresh):
        out = jnp.concatenate(
            [
                jnp.dot(
                    cached[j * per_row : (j + 1) * per_row, :],
                    v_ref[c * chunk_rows + j],
                    preferred_element_type=jnp.float32,
                )
                for j in range(chunk_rows)
            ],
            axis=0,
        ) + jnp.dot(fresh, vf, preferred_element_type=jnp.float32)
        own = out[:, :HEAD_WIDTH]
        for g in range(1, kv_here):
            own = jnp.where(kv_down == g, out[:, g * HEAD_WIDTH : (g + 1) * HEAD_WIDTH], own)
        return own.astype(jnp.bfloat16)

    lengths_copy.wait()
    vf_copy.wait()
    vf = vf_ref[...].reshape(tokens, kv_width)

    w_copies = [block_copy(w_hbm, w_ref.at[n], w_sems.at[n], d) for n, d in enumerate(ahead)]
    for copy in w_copies:
        copy.start()

    @pl.loop(0, chunks // TOGETHER)
    def _(i):
        groups = [i * TOGETHER + n for n in range(TOGETHER)]
        for c in groups:
            for copy in kv_copies(c):
                copy.wait()

        scored = [scores(c) for c in groups]
        probs = [softmax(c, *part) for c, part in zip(groups, scored, strict=True)]
        for c, part in zip(groups, probs, strict=True):
            o_ref[pl.ds(pl.multiple_of(c * LANES, LANES), LANES), :] = values(c, *part)

    out = jnp.dot(
        order_ref[...], o_ref[...], preferred_element_type=jnp.float32
    ).astype(jnp.bfloat16)
    attn = jnp.concatenate(
        [out[h * tokens : (h + 1) * tokens, :] for h in range(heads)], axis=1
    )
    attn_ref[...] = attn
    sent = jnp.dot(pick, attn, preferred_element_type=jnp.float32)
    size = capacity * steps
    for d in range(owners):
        mine = sent[d * size : (d + 1) * size, :]
        send_refs[d][...] = jnp.concatenate(
            [mine[:, h * HEAD_WIDTH : (h + 1) * HEAD_WIDTH] for h in range(heads)]
            + [meta[d * META_ROWS : (d + 1) * META_ROWS, :]],
            axis=0,
        ).astype(jnp.bfloat16)
    for copy in w_copies:
        copy.wait()


def attend_and_pick(
    lengths,
    adapter_of_row,
    storage_slot,
    queries,
    fresh_keys,
    fresh_values,
    cached_keys,
    cached_values,
    weight,
    owners,
    capacity,
    resident,
    columns,
    ahead,
):
    steps, rows, width = queries.shape
    cache, kv_width = cached_keys.shape[1:]
    heads = width // HEAD_WIDTH
    total = rows * heads * steps
    tokens = steps * rows
    size = capacity * steps
    chunks = total // LANES
    outs = pl.pallas_call(
        functools.partial(attend_kernel, owners, capacity, resident, ahead),
        out_shape=[
            jax.ShapeDtypeStruct((tokens, width), jnp.bfloat16),
            jax.ShapeDtypeStruct((owners * size, tokens), jnp.bfloat16),
            pltpu.VMEM((len(ahead), width, columns), jnp.bfloat16),
        ]
        + [jax.ShapeDtypeStruct((heads * size + META_ROWS, HEAD_WIDTH), jnp.bfloat16)] * owners,
        in_specs=[HBM] * 9,
        out_specs=[VMEM] * (3 + owners),
        scratch_shapes=[
            pltpu.SMEM(lengths.shape, jnp.int32),
            pltpu.SMEM(adapter_of_row.shape, jnp.int32),
            pltpu.SMEM(storage_slot.shape, jnp.int32),
            pltpu.VMEM(queries.shape, jnp.bfloat16),
            pltpu.VMEM(fresh_keys.shape, jnp.bfloat16),
            pltpu.VMEM(fresh_values.shape, jnp.bfloat16),
            pltpu.VMEM((rows, cache, kv_width), jnp.bfloat16),
            pltpu.VMEM((rows, cache, kv_width), jnp.bfloat16),
            pltpu.VMEM((total, total), jnp.bfloat16),
            pltpu.VMEM((HEAD_WIDTH, total), jnp.float32),
            pltpu.VMEM((total, HEAD_WIDTH), jnp.bfloat16),
            pltpu.SemaphoreType.DMA((2, chunks)),
            pltpu.SemaphoreType.DMA((6,)),
            pltpu.SemaphoreType.DMA((len(ahead),)),
        ],
        compiler_params=pltpu.CompilerParams(vmem_limit_bytes=24 * MIB),
        cost_estimate=pl.CostEstimate(
            flops=8 * total * cache * kv_width,
            bytes_accessed=4 * rows * cache * kv_width,
            transcendentals=total * cache,
        ),
        name="attend",
    )(
        *in_hbm(
            lengths,
            adapter_of_row,
            storage_slot,
            queries,
            fresh_keys,
            fresh_values,
            cached_keys,
            cached_values,
            weight,
        ),
    )
    return outs[0], outs[1], outs[2], outs[3:]


def project_kernel(blocks, here, bring, added, attn_ref, w_hbm, *refs):
    here_ref = refs[0] if here else None
    add_refs = refs[bool(here) :][:added]
    refs = refs[len(refs) - len(blocks) - bool(bring) - 2 :]
    outs, w_ref, sems = refs[: len(blocks)], refs[-2], refs[-1]
    fetched = blocks[here:]
    copies = [
        block_copy(w_hbm, w_ref.at[n], sems.at[n], d) for n, d in enumerate(fetched)
    ] + [
        block_copy(w_hbm, refs[len(blocks)].at[n], sems.at[len(fetched) + n], d)
        for n, d in enumerate(bring)
    ]
    for copy in copies:
        copy.start()
    attn = attn_ref[...]
    for n in range(len(blocks)):
        if n >= here:
            copies[n - here].wait()
        block = here_ref.at[n] if n < here else w_ref.at[n - here]

        @pl.loop(0, block.shape[-1] // TILE)
        def _(i, n=n, block=block, out_ref=outs[n]):
            cols = pl.ds(pl.multiple_of(i * TILE, TILE), TILE)
            out = jnp.dot(attn, block[:, cols], preferred_element_type=jnp.float32)
            for add_ref in add_refs[n :: len(blocks)]:
                out = out + add_ref[:, cols].astype(jnp.float32)
            out_ref[:, cols] = out.astype(out_ref.dtype)

    for copy in copies[len(fetched) :]:
        copy.wait()


def project(attn, weight, columns, blocks, here=None, bring=(), add=(), dtype=jnp.bfloat16, after=()):
    tokens, width = attn.shape
    held = 0 if here is None else here.shape[0]
    fetched = len(blocks) - held
    extra = [*([here] if held else []), *add]
    outs = [jax.ShapeDtypeStruct((tokens, columns), dtype)] * len(blocks)
    if bring:
        outs.append(pltpu.VMEM((len(bring), width, columns), jnp.bfloat16))
    return pl.pallas_call(
        functools.partial(project_kernel, blocks, held, bring, len(add)),
        out_shape=outs,
        in_specs=[VMEM, HBM] + [VMEM] * len(extra) + [ANY] * len(after),
        out_specs=[VMEM] * len(outs),
        scratch_shapes=[
            pltpu.VMEM((max(fetched, 1), width if fetched else 16, columns), jnp.bfloat16),
            pltpu.SemaphoreType.DMA((fetched + len(bring),)),
        ],
        compiler_params=pltpu.CompilerParams(vmem_limit_bytes=16 * MIB),
        cost_estimate=pl.CostEstimate(
            flops=2 * tokens * width * columns * len(blocks),
            bytes_accessed=2 * width * columns * len(blocks),
            transcendentals=0,
        ),
        name="project",
    )(attn, *in_hbm(weight), *extra, *after)


def merge_kernel(mine_ref, got_ref, _, out_ref):
    out_ref[...] = (mine_ref[...] + got_ref[...].astype(jnp.float32)).astype(jnp.bfloat16)


def merge(mine, got, after):
    return pl.pallas_call(
        merge_kernel,
        out_shape=jax.ShapeDtypeStruct(mine.shape, jnp.bfloat16),
        in_specs=[VMEM, VMEM, ANY],
        out_specs=VMEM,
        compiler_params=pltpu.CompilerParams(vmem_limit_bytes=4 * MIB),
        name="merge",
    )(mine, got, after)


def down_kernel(capacity, steps, *refs):
    (*got_refs, down_ref, _, mine_ref, sent_ref, mask_ref) = refs
    resident, rank, width = down_ref.shape
    wide = resident * rank
    heads = width // HEAD_WIDTH
    size = capacity * steps
    held = size * len(got_refs)
    got = [ref[...].astype(jnp.float32) for ref in got_refs]
    rows = jnp.concatenate(
        [
            jnp.concatenate([part[h * size : (h + 1) * size, :] for part in got], axis=0)
            for h in range(heads)
        ],
        axis=1,
    ).astype(jnp.bfloat16)
    meta = jnp.concatenate([part[heads * size :, :] for part in got], axis=0)
    spread = div(iota((LANES, wide), 1), rank) == iota((LANES, wide), 0)
    entries = meta.shape[0]
    slot, entry = iota((held, entries), 0), iota((held, entries), 1)
    of_slot = entry == div(slot, size) * META_ROWS + div(mod(slot, size), steps)
    local = jnp.dot(
        of_slot.astype(jnp.bfloat16),
        meta.astype(jnp.bfloat16),
        preferred_element_type=jnp.float32,
    )
    mask = jnp.dot(
        local.astype(jnp.bfloat16),
        spread.astype(jnp.bfloat16),
        preferred_element_type=jnp.float32,
    )
    mask_ref[...] = mask.astype(jnp.bfloat16)
    low = lax.dot_general(
        rows,
        down_ref[...].reshape(wide, width),
        (((1,), (1,)), ((), ())),
        preferred_element_type=jnp.float32,
    )
    low = low * mask
    pair = low[:, :LANES]
    for n in range(1, wide // LANES):
        pair = pair + low[:, n * LANES : (n + 1) * LANES]
    both = pair + pltpu.roll(pair, rank, 1)
    half = held // 2
    packed = jnp.where(iota((half, LANES), 1) < rank, both[:half, :], both[half:, :])
    mine_ref[...] = packed
    sent_ref[...] = packed.astype(jnp.bfloat16)


def down(got, factors, capacity, steps, after):
    resident, rank, width = factors.shape
    held = len(got) * capacity * steps
    return pl.pallas_call(
        functools.partial(down_kernel, capacity, steps),
        out_shape=[
            jax.ShapeDtypeStruct((held // 2, LANES), jnp.float32),
            jax.ShapeDtypeStruct((held // 2, LANES), jnp.bfloat16),
            jax.ShapeDtypeStruct((held, resident * rank), jnp.bfloat16),
        ],
        in_specs=[VMEM] * (len(got) + 1) + [ANY],
        out_specs=[VMEM] * 3,
        compiler_params=pltpu.CompilerParams(vmem_limit_bytes=12 * MIB),
        cost_estimate=pl.CostEstimate(
            flops=200 * held * resident * rank * width,
            bytes_accessed=2 * resident * rank * width,
            transcendentals=0,
        ),
        name="down",
    )(*got, factors, after)


def up_kernel(peers, mine_ref, *refs):
    got_refs, (mask_ref, up_ref, _, *delta_refs) = refs[:peers], refs[peers:]
    resident, rank, columns = up_ref.shape
    wide = resident * rank
    total = mine_ref[...]
    for ref in got_refs:
        total = total + ref[...].astype(jnp.float32)
    other = pltpu.roll(total, rank, 1)
    first = iota(total.shape, 1) < rank
    both = jnp.concatenate(
        [jnp.where(first, total, other), jnp.where(first, other, total)], axis=0
    )
    both = jnp.concatenate([both] * (wide // LANES), axis=1)
    low = jnp.where(mask_ref[...].astype(jnp.float32) > 0.5, both, 0.0).astype(jnp.bfloat16)
    delta = jnp.dot(
        low, up_ref[...].reshape(wide, columns), preferred_element_type=jnp.float32
    ).astype(jnp.bfloat16)
    size = delta.shape[0] // len(delta_refs)
    for d, ref in enumerate(delta_refs):
        ref[...] = delta[d * size : (d + 1) * size, :]


def up(mine, got, mask, factors, owners, after):
    resident, rank, columns = factors.shape
    held = mask.shape[0]
    return pl.pallas_call(
        functools.partial(up_kernel, len(got)),
        out_shape=[jax.ShapeDtypeStruct((held // owners, columns), jnp.bfloat16)] * owners,
        in_specs=[VMEM] * (len(got) + 3) + [ANY],
        out_specs=[VMEM] * owners,
        compiler_params=pltpu.CompilerParams(vmem_limit_bytes=16 * MIB),
        cost_estimate=pl.CostEstimate(
            flops=200 * held * resident * rank * columns,
            bytes_accessed=2 * resident * rank * columns,
            transcendentals=0,
        ),
        name="up",
    )(mine, *got, mask, factors, after)


def finish_kernel(owners, pick_ref, *refs):
    delta_refs, (*near_refs, base_ref, out_hbm, out_ref, sems) = refs[:owners], refs[owners:]
    width = near_refs[0].shape[1]
    pick = pick_ref[...]
    copies = []
    for n, near_ref in enumerate(near_refs):
        cols = slice(n * width, (n + 1) * width)
        mixed = base_ref[:, cols] + near_ref[...].astype(jnp.float32)
        delta = jnp.concatenate([ref[:, cols] for ref in delta_refs], axis=0)
        mixed = mixed + lax.dot_general(
            pick, delta, (((0,), (0,)), ((), ())), preferred_element_type=jnp.float32
        )
        out_ref[:, :, cols] = mixed.astype(jnp.bfloat16).reshape(*out_ref.shape[:2], width)
        copies.append(
            pltpu.make_async_copy(out_ref.at[:, :, cols], out_hbm.at[:, :, cols], sems.at[n])
        )
        copies[n].start()
    for copy in copies:
        copy.wait()


def finish(base, pick, delta, near, steps):
    tokens, columns = base.shape
    shape = (steps, tokens // steps, columns)
    operands = [pick, *delta, *near, base]
    return pl.pallas_call(
        functools.partial(finish_kernel, len(delta)),
        out_shape=jax.ShapeDtypeStruct(shape, jnp.bfloat16),
        in_specs=[VMEM] * len(operands),
        out_specs=HBM,
        scratch_shapes=[
            pltpu.VMEM(shape, jnp.bfloat16),
            pltpu.SemaphoreType.DMA((len(near),)),
        ],
        compiler_params=pltpu.CompilerParams(vmem_limit_bytes=12 * MIB),
        cost_estimate=pl.CostEstimate(
            flops=2 * tokens * pick.shape[0] * columns,
            bytes_accessed=10 * tokens * columns,
            transcendentals=0,
        ),
        name="finish",
    )(*operands)


def body(
    queries,
    fresh_token_keys,
    fresh_token_values,
    cached_key_rows,
    cached_value_rows,
    cache_live_lengths,
    output_projection_weight,
    adapter_down_factors,
    adapter_up_factors,
    adapter_of_row,
    adapter_storage_slot,
):
    step_count, row_count, _ = queries.shape
    resident = adapter_down_factors.shape[0]
    owners = lax.axis_size("replica")
    tensors = lax.axis_size("tensor")
    capacity = max(2, 2 * row_count // owners)
    columns = adapter_up_factors.shape[2]
    far_sent, far_kept = list(range(3, tensors, 2)), list(range(2, tensors, 2))

    attn, pick, w_here, sent = attend_and_pick(
        cache_live_lengths,
        adapter_of_row,
        adapter_storage_slot,
        queries,
        fresh_token_keys,
        fresh_token_values,
        cached_key_rows,
        cached_value_rows,
        output_projection_weight,
        owners,
        capacity,
        resident,
        columns,
        far_sent,
    )
    got = exchange_all(sent, "replica")

    weight = output_projection_weight
    *parts, w_here = project(attn, weight, columns, far_sent, here=w_here, bring=far_kept)
    far_got = [xor_exchange(part, "tensor", 1) for part in parts]

    kept = project(
        attn, weight, columns, far_kept, here=w_here, dtype=jnp.float32, after=[parts[0]]
    )
    mine, low_sent, mask = down(got, adapter_down_factors, capacity, step_count, kept[0])
    low_got = [xor_exchange(low_sent, "tensor", d) for d in range(1, tensors)]
    halves_sent = [merge(*pair, low_sent) for pair in zip(kept, far_got, strict=True)]
    others = [xor_exchange(half, "tensor", d) for half, d in zip(halves_sent, far_kept, strict=True)]
    delta = up(mine, low_got, mask, adapter_up_factors, owners, halves_sent[0])
    delta_got = exchange_all(delta, "replica")

    (near,) = project(attn, weight, columns, [1], after=[delta[0]])
    width = columns // PIECES
    near_got = [
        xor_exchange(near[:, n * width : (n + 1) * width], "tensor", 1) for n in range(PIECES)
    ]
    (own,) = project(
        attn, weight, columns, [0], add=others, dtype=jnp.float32, after=[near]
    )
    return finish(own, pick, delta_got, near_got, step_count)


def solution(mesh):
    in_specs = (
        P(None, ("groups", "replica"), "tensor"),
        P(None, ("groups", "replica"), "tensor"),
        P(None, ("groups", "replica"), "tensor"),
        P(("groups", "replica"), None, "tensor"),
        P(("groups", "replica"), None, "tensor"),
        P(("groups", "replica")),
        P("tensor", None),
        P(("groups", "replica"), None, "tensor"),
        P(("groups", "replica"), None, "tensor"),
        P(("groups", "replica")),
        P("groups"),
    )
    out_specs = P(None, ("groups", "replica"), "tensor")
    return jax.shard_map(body, mesh=mesh, in_specs=in_specs, out_specs=out_specs, check_vma=False)
```

```python
import functools
import math

import jax
import jax.numpy as jnp
from jax import lax
from jax.experimental import pallas as pl
from jax.experimental.pallas import tpu as pltpu
from jax.sharding import PartitionSpec as P

HEAD_WIDTH = 128
LANES = 128
META_ROWS = 16
TILE = 512
TOGETHER = 2
ORDER_ROWS = 32
PIECES = 2
MIB = 1024 * 1024
VMEM = pl.BlockSpec(memory_space=pltpu.VMEM)
ANY = pl.BlockSpec(memory_space=pl.ANY)
HBM = pl.BlockSpec(memory_space=pltpu.HBM)


def iota(shape, dim):
    return lax.broadcasted_iota(jnp.int32, shape, dim)


def halves(n):
    if n & (n - 1):
        raise ValueError(n)
    return n.bit_length() - 1


def div(x, n):
    return lax.shift_right_logical(x, jnp.int32(halves(n)))


def mod(x, n):
    return x & ((1 << halves(n)) - 1)


def one_hot(source, width):
    lane = iota(source.shape, 1)
    return jnp.concatenate(
        [(source == lane + at).astype(jnp.bfloat16) for at in range(0, width, source.shape[1])],
        axis=1,
    )


def in_hbm(*arrays):
    return [pltpu.with_memory_space_constraint(a, pltpu.HBM) for a in arrays]


def xor_exchange(value, axis, distance):
    size = lax.axis_size(axis)
    return lax.ppermute(value, axis, [(i, i ^ distance) for i in range(size)])


def partner_order(size):
    far = list(range(size // 2, size))
    split = (len(far) + 1) // 2
    return [0, *far[:split], *range(1, size // 2)], far[split:]


def exchange_all(blocks, distances, axis):
    return [
        xor_exchange(block, axis, distance) if distance else block
        for block, distance in zip(blocks, distances, strict=True)
    ]


def block_copy(w_hbm, dst, sem, distance):
    me = lax.axis_index("tensor")
    columns = dst.shape[-1]
    at = pl.multiple_of(lax.bitwise_xor(me, jnp.int32(distance)) * columns, LANES)
    return pltpu.make_async_copy(w_hbm.at[:, pl.ds(at, columns)], dst, sem)


def attend_kernel(
    owners,
    capacity,
    resident,
    ahead,
    lengths_hbm,
    adapter_hbm,
    slot_hbm,
    q_hbm,
    kf_hbm,
    vf_hbm,
    k_hbm,
    v_hbm,
    w_hbm,
    attn_ref,
    pick_ref,
    w_ref,
    *rest,
):
    send_refs, rest = rest[:owners], rest[owners:]
    lengths_ref, adapter_ref, slot_ref, q_ref, kf_ref, vf_ref, k_ref, v_ref = rest[:8]
    order_ref, q_cols_ref, o_ref, sems, small_sems, w_sems = rest[8:]
    steps, rows, width = q_ref.shape
    cache, kv_width = k_ref.shape[1:]
    heads = width // HEAD_WIDTH
    kv_here = kv_width // HEAD_WIDTH
    group = heads // kv_here
    per_row = heads * steps
    total = rows * per_row
    tokens = steps * rows
    chunks = sems.shape[1]
    chunk_rows = rows // chunks
    scale = 1.0 / math.sqrt(HEAD_WIDTH)

    def kv_copies(c):
        at = pl.ds(c * chunk_rows, chunk_rows)
        return [
            pltpu.make_async_copy(src.at[at], dst.at[at], sems.at[which, c])
            for which, (src, dst) in enumerate([(k_hbm, k_ref), (v_hbm, v_ref)])
        ]

    small = [
        pltpu.make_async_copy(src, dst, small_sems.at[n])
        for n, (src, dst) in enumerate(
            [
                (q_hbm, q_ref),
                (kf_hbm, kf_ref),
                (lengths_hbm, lengths_ref),
                (adapter_hbm, adapter_ref),
                (slot_hbm, slot_ref),
                (vf_hbm, vf_ref),
            ]
        )
    ]
    q_copy, kf_copy, lengths_copy, adapter_copy, slot_copy, vf_copy = small
    first, *others = [kv_copies(c) for c in range(chunks)]
    for copy in [q_copy, *first, *small[1:], *sum(others, [])]:
        copy.start()

    @pl.loop(0, total // ORDER_ROWS)
    def _(i):
        at = iota((ORDER_ROWS, LANES), 0) + i * ORDER_ROWS
        source = mod(at, rows) * per_row + div(at, tokens) * steps + mod(div(at, rows), steps)
        here = pl.ds(pl.multiple_of(i * ORDER_ROWS, ORDER_ROWS), ORDER_ROWS)
        order_ref[here, :] = one_hot(source, total)

    adapter_copy.wait()
    slot_copy.wait()
    me = lax.axis_index("replica")
    positions = sum(partner_order(owners), [])
    row_at = mod(iota((8, tokens), 1), rows)
    row_down = iota((rows, LANES), 0)
    first_slot = jnp.zeros((8, tokens), jnp.int32)
    local_of = jnp.zeros((rows, LANES), jnp.int32)
    firsts = []
    for r in range(rows):
        slot = slot_ref[adapter_ref[r]]
        owner = jnp.int32(0)
        for d in range(1, owners):
            owner = owner + (slot >= d * resident).astype(jnp.int32)
        partner = lax.bitwise_xor(owner, me)
        first = jnp.int32(0)
        for d in range(1, owners):
            first = jnp.where(partner == positions[d], d * capacity, first)
        firsts.append(first)
        first_slot = jnp.where(row_at == r, first, first_slot)
        local_of = jnp.where(row_down == r, slot - owner * resident, local_of)
    place = first_slot
    for r in range(rows - 1):
        place = place + ((first_slot == firsts[r]) & (row_at > r)).astype(jnp.int32)
    held = owners * capacity * steps
    slot_at = iota((held, tokens), 0)
    token_at = iota((held, tokens), 1)
    pick = (
        (jnp.concatenate([place] * (held // 8), axis=0) == div(slot_at, steps))
        & (mod(slot_at, steps) == div(token_at, rows))
    ).astype(jnp.bfloat16)
    pick_ref[...] = pick
    local_hot = (local_of == iota((rows, LANES), 1)).astype(jnp.bfloat16)
    entry = iota((owners * META_ROWS, rows), 0)
    entry_place = mod(entry, META_ROWS)
    entry_slot = div(entry, META_ROWS) * capacity + entry_place
    entry_pick = (
        (jnp.concatenate([place[:, :rows]] * (owners * META_ROWS // 8), axis=0) == entry_slot)
        & (entry_place < capacity)
    ).astype(jnp.bfloat16)
    meta = jnp.dot(entry_pick, local_hot, preferred_element_type=jnp.float32)

    q_copy.wait()
    by_head = jnp.concatenate(
        [
            q_ref[:, :, h * HEAD_WIDTH : (h + 1) * HEAD_WIDTH].reshape(tokens, HEAD_WIDTH)
            for h in range(heads)
        ],
        axis=0,
    )
    q_cols_ref[...] = jnp.dot(
        by_head.astype(jnp.float32).T.astype(jnp.bfloat16),
        order_ref[...],
        preferred_element_type=jnp.float32,
    )
    lane = iota((HEAD_WIDTH, LANES), 1)
    row_of = div(lane, per_row)
    kv_of = mod(div(lane, steps * group), kv_here)

    kf_copy.wait()
    kf = kf_ref[...].reshape(tokens, kv_width)
    token, query = iota((tokens, LANES), 0), iota((tokens, LANES), 1)
    position = iota((cache, LANES), 0)

    def scores(c):
        cols = q_cols_ref[:, pl.ds(pl.multiple_of(c * LANES, LANES), LANES)]
        by_kv = [jnp.where(kv_of == g, cols, 0.0) for g in range(kv_here)]
        fresh = jnp.dot(
            kf,
            jnp.concatenate(by_kv, axis=0).astype(jnp.bfloat16),
            preferred_element_type=jnp.float32,
        )
        live = (mod(token, rows) == div(query, per_row) + c * chunk_rows) & (
            div(token, rows) <= mod(query, steps)
        )
        fresh = jnp.where(live, fresh * scale, -jnp.inf)
        weights = jnp.concatenate(
            [jnp.where(row_of == j, q, 0.0) for j in range(chunk_rows) for q in by_kv], axis=0
        ).astype(jnp.bfloat16)
        keys = jnp.concatenate([k_ref[c * chunk_rows + j] for j in range(chunk_rows)], axis=1)
        cached = jnp.dot(keys, weights, preferred_element_type=jnp.float32)
        return cached * scale, fresh

    def softmax(c, cached, fresh):
        length = jnp.zeros((1, LANES), jnp.int32)
        for j in range(chunk_rows):
            length = jnp.where(
                div(iota((1, LANES), 1), per_row) == j, lengths_ref[c * chunk_rows + j], length
            )
        cached = jnp.where(position < length, cached, -jnp.inf)
        top = jnp.maximum(
            jnp.max(cached, axis=0, keepdims=True), jnp.max(fresh, axis=0, keepdims=True)
        )
        wc, wf = jnp.exp(cached - top), jnp.exp(fresh - top)
        share = 1.0 / (
            jnp.sum(wc, axis=0, keepdims=True) + jnp.sum(wf, axis=0, keepdims=True)
        )
        return (wc * share).T.astype(jnp.bfloat16), (wf * share).T.astype(jnp.bfloat16)

    kv_down = mod(div(iota((LANES, HEAD_WIDTH), 0), steps * group), kv_here)

    def values(c, cached, fresh):
        out = jnp.concatenate(
            [
                jnp.dot(
                    cached[j * per_row : (j + 1) * per_row, :],
                    v_ref[c * chunk_rows + j],
                    preferred_element_type=jnp.float32,
                )
                for j in range(chunk_rows)
            ],
            axis=0,
        ) + jnp.dot(fresh, vf, preferred_element_type=jnp.float32)
        own = out[:, :HEAD_WIDTH]
        for g in range(1, kv_here):
            own = jnp.where(kv_down == g, out[:, g * HEAD_WIDTH : (g + 1) * HEAD_WIDTH], own)
        return own.astype(jnp.bfloat16)

    lengths_copy.wait()
    vf_copy.wait()
    vf = vf_ref[...].reshape(tokens, kv_width)

    w_copies = [block_copy(w_hbm, w_ref.at[n], w_sems.at[n], d) for n, d in enumerate(ahead)]
    for copy in w_copies:
        copy.start()

    @pl.loop(0, chunks // TOGETHER)
    def _(i):
        groups = [i * TOGETHER + n for n in range(TOGETHER)]
        for c in groups:
            for copy in kv_copies(c):
                copy.wait()

        scored = [scores(c) for c in groups]
        probs = [softmax(c, *part) for c, part in zip(groups, scored, strict=True)]
        for c, part in zip(groups, probs, strict=True):
            o_ref[pl.ds(pl.multiple_of(c * LANES, LANES), LANES), :] = values(c, *part)

    out = jnp.dot(
        order_ref[...], o_ref[...], preferred_element_type=jnp.float32
    ).astype(jnp.bfloat16)
    attn = jnp.concatenate(
        [out[h * tokens : (h + 1) * tokens, :] for h in range(heads)], axis=1
    )
    attn_ref[...] = attn
    sent = jnp.dot(pick, attn, preferred_element_type=jnp.float32)
    size = capacity * steps
    for d in range(owners):
        mine = sent[d * size : (d + 1) * size, :]
        send_refs[d][...] = jnp.concatenate(
            [mine[:, h * HEAD_WIDTH : (h + 1) * HEAD_WIDTH] for h in range(heads)]
            + [meta[d * META_ROWS : (d + 1) * META_ROWS, :]],
            axis=0,
        ).astype(jnp.bfloat16)
    for copy in w_copies:
        copy.wait()


def attend_and_pick(
    lengths,
    adapter_of_row,
    storage_slot,
    queries,
    fresh_keys,
    fresh_values,
    cached_keys,
    cached_values,
    weight,
    owners,
    capacity,
    resident,
    columns,
    ahead,
):
    steps, rows, width = queries.shape
    cache, kv_width = cached_keys.shape[1:]
    heads = width // HEAD_WIDTH
    total = rows * heads * steps
    tokens = steps * rows
    size = capacity * steps
    chunks = total // LANES
    outs = pl.pallas_call(
        functools.partial(attend_kernel, owners, capacity, resident, ahead),
        out_shape=[
            jax.ShapeDtypeStruct((tokens, width), jnp.bfloat16),
            jax.ShapeDtypeStruct((owners * size, tokens), jnp.bfloat16),
            pltpu.VMEM((len(ahead), width, columns), jnp.bfloat16),
        ]
        + [jax.ShapeDtypeStruct((heads * size + META_ROWS, HEAD_WIDTH), jnp.bfloat16)] * owners,
        in_specs=[HBM] * 9,
        out_specs=[VMEM] * (3 + owners),
        scratch_shapes=[
            pltpu.SMEM(lengths.shape, jnp.int32),
            pltpu.SMEM(adapter_of_row.shape, jnp.int32),
            pltpu.SMEM(storage_slot.shape, jnp.int32),
            pltpu.VMEM(queries.shape, jnp.bfloat16),
            pltpu.VMEM(fresh_keys.shape, jnp.bfloat16),
            pltpu.VMEM(fresh_values.shape, jnp.bfloat16),
            pltpu.VMEM((rows, cache, kv_width), jnp.bfloat16),
            pltpu.VMEM((rows, cache, kv_width), jnp.bfloat16),
            pltpu.VMEM((total, total), jnp.bfloat16),
            pltpu.VMEM((HEAD_WIDTH, total), jnp.float32),
            pltpu.VMEM((total, HEAD_WIDTH), jnp.bfloat16),
            pltpu.SemaphoreType.DMA((2, chunks)),
            pltpu.SemaphoreType.DMA((6,)),
            pltpu.SemaphoreType.DMA((len(ahead),)),
        ],
        compiler_params=pltpu.CompilerParams(vmem_limit_bytes=24 * MIB),
        cost_estimate=pl.CostEstimate(
            flops=8 * total * cache * kv_width,
            bytes_accessed=4 * rows * cache * kv_width,
            transcendentals=total * cache,
        ),
        name="attend",
    )(
        *in_hbm(
            lengths,
            adapter_of_row,
            storage_slot,
            queries,
            fresh_keys,
            fresh_values,
            cached_keys,
            cached_values,
            weight,
        ),
    )
    return outs[0], outs[1], outs[2], outs[3:]


def project_kernel(blocks, here, bring, added, attn_ref, w_hbm, *refs):
    here_ref = refs[0] if here else None
    add_refs = refs[bool(here) :][:added]
    refs = refs[len(refs) - len(blocks) - bool(bring) - 2 :]
    outs, w_ref, sems = refs[: len(blocks)], refs[-2], refs[-1]
    fetched = blocks[here:]
    copies = [
        block_copy(w_hbm, w_ref.at[n], sems.at[n], d) for n, d in enumerate(fetched)
    ] + [
        block_copy(w_hbm, refs[len(blocks)].at[n], sems.at[len(fetched) + n], d)
        for n, d in enumerate(bring)
    ]
    for copy in copies:
        copy.start()
    attn = attn_ref[...]
    for n in range(len(blocks)):
        if n >= here:
            copies[n - here].wait()
        block = here_ref.at[n] if n < here else w_ref.at[n - here]

        @pl.loop(0, block.shape[-1] // TILE)
        def _(i, n=n, block=block, out_ref=outs[n]):
            cols = pl.ds(pl.multiple_of(i * TILE, TILE), TILE)
            out = jnp.dot(attn, block[:, cols], preferred_element_type=jnp.float32)
            for add_ref in add_refs[n :: len(blocks)]:
                out = out + add_ref[:, cols].astype(jnp.float32)
            out_ref[:, cols] = out.astype(out_ref.dtype)

    for copy in copies[len(fetched) :]:
        copy.wait()


def project(attn, weight, columns, blocks, here=None, bring=(), add=(), dtype=jnp.bfloat16, after=()):
    tokens, width = attn.shape
    held = 0 if here is None else here.shape[0]
    fetched = len(blocks) - held
    extra = [*([here] if held else []), *add]
    outs = [jax.ShapeDtypeStruct((tokens, columns), dtype)] * len(blocks)
    if bring:
        outs.append(pltpu.VMEM((len(bring), width, columns), jnp.bfloat16))
    return pl.pallas_call(
        functools.partial(project_kernel, blocks, held, bring, len(add)),
        out_shape=outs,
        in_specs=[VMEM, HBM] + [VMEM] * len(extra) + [ANY] * len(after),
        out_specs=[VMEM] * len(outs),
        scratch_shapes=[
            pltpu.VMEM((max(fetched, 1), width if fetched else 16, columns), jnp.bfloat16),
            pltpu.SemaphoreType.DMA((fetched + len(bring),)),
        ],
        compiler_params=pltpu.CompilerParams(vmem_limit_bytes=16 * MIB),
        cost_estimate=pl.CostEstimate(
            flops=2 * tokens * width * columns * len(blocks),
            bytes_accessed=2 * width * columns * len(blocks),
            transcendentals=0,
        ),
        name="project",
    )(attn, *in_hbm(weight), *extra, *after)


def merge_kernel(mine_ref, got_ref, _, out_ref):
    out_ref[...] = (mine_ref[...] + got_ref[...].astype(jnp.float32)).astype(jnp.bfloat16)


def merge(mine, got, after):
    return pl.pallas_call(
        merge_kernel,
        out_shape=jax.ShapeDtypeStruct(mine.shape, jnp.bfloat16),
        in_specs=[VMEM, VMEM, ANY],
        out_specs=VMEM,
        compiler_params=pltpu.CompilerParams(vmem_limit_bytes=4 * MIB),
        name="merge",
    )(mine, got, after)


def down_kernel(capacity, steps, *refs):
    (*got_refs, down_ref, _, mine_ref, sent_ref, mask_ref) = refs
    resident, rank, width = down_ref.shape
    wide = resident * rank
    heads = width // HEAD_WIDTH
    size = capacity * steps
    held = size * len(got_refs)
    got = [ref[...].astype(jnp.float32) for ref in got_refs]
    rows = jnp.concatenate(
        [
            jnp.concatenate([part[h * size : (h + 1) * size, :] for part in got], axis=0)
            for h in range(heads)
        ],
        axis=1,
    ).astype(jnp.bfloat16)
    meta = jnp.concatenate([part[heads * size :, :] for part in got], axis=0)
    spread = div(iota((LANES, wide), 1), rank) == iota((LANES, wide), 0)
    entries = meta.shape[0]
    slot, entry = iota((held, entries), 0), iota((held, entries), 1)
    of_slot = entry == div(slot, size) * META_ROWS + div(mod(slot, size), steps)
    local = jnp.dot(
        of_slot.astype(jnp.bfloat16),
        meta.astype(jnp.bfloat16),
        preferred_element_type=jnp.float32,
    )
    mask = jnp.dot(
        local.astype(jnp.bfloat16),
        spread.astype(jnp.bfloat16),
        preferred_element_type=jnp.float32,
    )
    mask_ref[...] = mask.astype(jnp.bfloat16)
    low = lax.dot_general(
        rows,
        down_ref[...].reshape(wide, width),
        (((1,), (1,)), ((), ())),
        preferred_element_type=jnp.float32,
    )
    low = low * mask
    pair = low[:, :LANES]
    for n in range(1, wide // LANES):
        pair = pair + low[:, n * LANES : (n + 1) * LANES]
    both = pair + pltpu.roll(pair, rank, 1)
    half = held // 2
    packed = jnp.where(iota((half, LANES), 1) < rank, both[:half, :], both[half:, :])
    mine_ref[...] = packed
    sent_ref[...] = packed.astype(jnp.bfloat16)


def down(got, factors, capacity, steps, after):
    resident, rank, width = factors.shape
    held = len(got) * capacity * steps
    return pl.pallas_call(
        functools.partial(down_kernel, capacity, steps),
        out_shape=[
            jax.ShapeDtypeStruct((held // 2, LANES), jnp.float32),
            jax.ShapeDtypeStruct((held // 2, LANES), jnp.bfloat16),
            jax.ShapeDtypeStruct((held, resident * rank), jnp.bfloat16),
        ],
        in_specs=[VMEM] * (len(got) + 1) + [ANY],
        out_specs=[VMEM] * 3,
        compiler_params=pltpu.CompilerParams(vmem_limit_bytes=12 * MIB),
        cost_estimate=pl.CostEstimate(
            flops=200 * held * resident * rank * width,
            bytes_accessed=2 * resident * rank * width,
            transcendentals=0,
        ),
        name="down",
    )(*got, factors, after)


def up_kernel(peers, mine_ref, *refs):
    got_refs, (mask_ref, up_ref, _, *delta_refs) = refs[:peers], refs[peers:]
    resident, rank, columns = up_ref.shape
    wide = resident * rank
    total = mine_ref[...]
    for ref in got_refs:
        total = total + ref[...].astype(jnp.float32)
    other = pltpu.roll(total, rank, 1)
    first = iota(total.shape, 1) < rank
    both = jnp.concatenate(
        [jnp.where(first, total, other), jnp.where(first, other, total)], axis=0
    )
    both = jnp.concatenate([both] * (wide // LANES), axis=1)
    low = jnp.where(mask_ref[...].astype(jnp.float32) > 0.5, both, 0.0).astype(jnp.bfloat16)
    delta = jnp.dot(
        low, up_ref[...].reshape(wide, columns), preferred_element_type=jnp.float32
    ).astype(jnp.bfloat16)
    size = delta.shape[0] // len(delta_refs)
    for d, ref in enumerate(delta_refs):
        ref[...] = delta[d * size : (d + 1) * size, :]


def up(mine, got, mask, factors, owners, after):
    resident, rank, columns = factors.shape
    held = mask.shape[0]
    return pl.pallas_call(
        functools.partial(up_kernel, len(got)),
        out_shape=[jax.ShapeDtypeStruct((held // owners, columns), jnp.bfloat16)] * owners,
        in_specs=[VMEM] * (len(got) + 3) + [ANY],
        out_specs=[VMEM] * owners,
        compiler_params=pltpu.CompilerParams(vmem_limit_bytes=16 * MIB),
        cost_estimate=pl.CostEstimate(
            flops=200 * held * resident * rank * columns,
            bytes_accessed=2 * resident * rank * columns,
            transcendentals=0,
        ),
        name="up",
    )(mine, *got, mask, factors, after)


def finish_kernel(owners, pick_ref, *refs):
    delta_refs, (*near_refs, base_ref, out_hbm, out_ref, sems) = refs[:owners], refs[owners:]
    width = near_refs[0].shape[1]
    pick = pick_ref[...]
    copies = []
    for n, near_ref in enumerate(near_refs):
        cols = slice(n * width, (n + 1) * width)
        mixed = base_ref[:, cols] + near_ref[...].astype(jnp.float32)
        delta = jnp.concatenate([ref[:, cols] for ref in delta_refs], axis=0)
        mixed = mixed + lax.dot_general(
            pick, delta, (((0,), (0,)), ((), ())), preferred_element_type=jnp.float32
        )
        out_ref[:, :, cols] = mixed.astype(jnp.bfloat16).reshape(*out_ref.shape[:2], width)
        copies.append(
            pltpu.make_async_copy(out_ref.at[:, :, cols], out_hbm.at[:, :, cols], sems.at[n])
        )
        copies[n].start()
    for copy in copies:
        copy.wait()


def finish(base, pick, delta, near, steps):
    tokens, columns = base.shape
    shape = (steps, tokens // steps, columns)
    operands = [pick, *delta, *near, base]
    return pl.pallas_call(
        functools.partial(finish_kernel, len(delta)),
        out_shape=jax.ShapeDtypeStruct(shape, jnp.bfloat16),
        in_specs=[VMEM] * len(operands),
        out_specs=HBM,
        scratch_shapes=[
            pltpu.VMEM(shape, jnp.bfloat16),
            pltpu.SemaphoreType.DMA((len(near),)),
        ],
        compiler_params=pltpu.CompilerParams(vmem_limit_bytes=12 * MIB),
        cost_estimate=pl.CostEstimate(
            flops=2 * tokens * pick.shape[0] * columns,
            bytes_accessed=10 * tokens * columns,
            transcendentals=0,
        ),
        name="finish",
    )(*operands)


def body(
    queries,
    fresh_token_keys,
    fresh_token_values,
    cached_key_rows,
    cached_value_rows,
    cache_live_lengths,
    output_projection_weight,
    adapter_down_factors,
    adapter_up_factors,
    adapter_of_row,
    adapter_storage_slot,
):
    step_count, row_count, _ = queries.shape
    resident = adapter_down_factors.shape[0]
    owners = lax.axis_size("replica")
    tensors = lax.axis_size("tensor")
    capacity = max(2, 2 * row_count // owners)
    columns = adapter_up_factors.shape[2]
    far_sent, far_kept = list(range(3, tensors, 2)), list(range(2, tensors, 2))

    attn, pick, w_here, sent = attend_and_pick(
        cache_live_lengths,
        adapter_of_row,
        adapter_storage_slot,
        queries,
        fresh_token_keys,
        fresh_token_values,
        cached_key_rows,
        cached_value_rows,
        output_projection_weight,
        owners,
        capacity,
        resident,
        columns,
        far_sent,
    )
    early, late = partner_order(owners)
    got_early = exchange_all(sent[: len(early)], early, "replica")
    got_late = exchange_all(sent[len(early) :], late, "replica")

    weight = output_projection_weight
    *parts, w_here = project(attn, weight, columns, far_sent, here=w_here, bring=far_kept)
    far_got = [xor_exchange(part, "tensor", 1) for part in parts]
    kept = project(
        attn, weight, columns, far_kept, here=w_here, dtype=jnp.float32, after=[parts[0]]
    )

    def low_rank(got, after):
        mine, sent_low, mask = down(got, adapter_down_factors, capacity, step_count, after)
        others = [xor_exchange(sent_low, "tensor", d) for d in range(1, tensors)]
        return mine, others, mask, sent_low

    *low_early, sent_early = low_rank(got_early, kept[0])
    *low_late, sent_late = low_rank(got_late, sent_early)
    delta_early = up(*low_early, adapter_up_factors, len(early), sent_late)
    back_early = exchange_all(delta_early, early, "replica")
    halves_sent = [merge(*pair, delta_early[0]) for pair in zip(kept, far_got, strict=True)]
    others = [xor_exchange(half, "tensor", d) for half, d in zip(halves_sent, far_kept, strict=True)]
    delta_late = up(*low_late, adapter_up_factors, len(late), halves_sent[0])
    back_late = exchange_all(delta_late, late, "replica")

    near, w_here = project(attn, weight, columns, [1], bring=[0], after=[delta_late[0]])
    width = columns // PIECES
    near_got = [
        xor_exchange(near[:, n * width : (n + 1) * width], "tensor", 1) for n in range(PIECES)
    ]
    (own,) = project(
        attn, weight, columns, [0], here=w_here, add=others, dtype=jnp.float32, after=[near]
    )
    return finish(own, pick, [*back_early, *back_late], near_got, step_count)


def solution(mesh):
    in_specs = (
        P(None, ("groups", "replica"), "tensor"),
        P(None, ("groups", "replica"), "tensor"),
        P(None, ("groups", "replica"), "tensor"),
        P(("groups", "replica"), None, "tensor"),
        P(("groups", "replica"), None, "tensor"),
        P(("groups", "replica")),
        P("tensor", None),
        P(("groups", "replica"), None, "tensor"),
        P(("groups", "replica"), None, "tensor"),
        P(("groups", "replica")),
        P("groups"),
    )
    out_specs = P(None, ("groups", "replica"), "tensor")
    return jax.shard_map(body, mesh=mesh, in_specs=in_specs, out_specs=out_specs, check_vma=False)
```

```python
import functools
import math

import jax
import jax.numpy as jnp
from jax import lax
from jax.experimental import pallas as pl
from jax.experimental.pallas import tpu as pltpu
from jax.sharding import PartitionSpec as P

HEAD_WIDTH = 128
LANES = 128
META_ROWS = 16
TILE = 512
TOGETHER = 2
ORDER_ROWS = 32
PIECES = 2
MIB = 1024 * 1024
VMEM = pl.BlockSpec(memory_space=pltpu.VMEM)
ANY = pl.BlockSpec(memory_space=pl.ANY)
HBM = pl.BlockSpec(memory_space=pltpu.HBM)


def iota(shape, dim):
    return lax.broadcasted_iota(jnp.int32, shape, dim)


def halves(n):
    if n & (n - 1):
        raise ValueError(n)
    return n.bit_length() - 1


def div(x, n):
    return lax.shift_right_logical(x, jnp.int32(halves(n)))


def mod(x, n):
    return x & ((1 << halves(n)) - 1)


def one_hot(source, width):
    lane = iota(source.shape, 1)
    return jnp.concatenate(
        [(source == lane + at).astype(jnp.bfloat16) for at in range(0, width, source.shape[1])],
        axis=1,
    )


def in_hbm(*arrays):
    return [pltpu.with_memory_space_constraint(a, pltpu.HBM) for a in arrays]


def xor_exchange(value, axis, distance):
    size = lax.axis_size(axis)
    return lax.ppermute(value, axis, [(i, i ^ distance) for i in range(size)])


def partner_order(size):
    far = list(range(size // 2, size))
    split = (len(far) + 1) // 2
    return [0, *far[:split]], [*range(1, size // 2), *far[split:]]


def exchange_all(blocks, distances, axis):
    return [
        xor_exchange(block, axis, distance) if distance else block
        for block, distance in zip(blocks, distances, strict=True)
    ]


def block_copy(w_hbm, dst, sem, distance):
    me = lax.axis_index("tensor")
    columns = dst.shape[-1]
    at = pl.multiple_of(lax.bitwise_xor(me, jnp.int32(distance)) * columns, LANES)
    return pltpu.make_async_copy(w_hbm.at[:, pl.ds(at, columns)], dst, sem)


def attend_kernel(
    owners,
    capacity,
    resident,
    ahead,
    lengths_hbm,
    adapter_hbm,
    slot_hbm,
    q_hbm,
    kf_hbm,
    vf_hbm,
    k_hbm,
    v_hbm,
    w_hbm,
    attn_ref,
    pick_ref,
    w_ref,
    *rest,
):
    send_refs, rest = rest[:owners], rest[owners:]
    lengths_ref, adapter_ref, slot_ref, q_ref, kf_ref, vf_ref, k_ref, v_ref = rest[:8]
    order_ref, q_cols_ref, o_ref, sems, small_sems, w_sems = rest[8:]
    steps, rows, width = q_ref.shape
    cache, kv_width = k_ref.shape[1:]
    heads = width // HEAD_WIDTH
    kv_here = kv_width // HEAD_WIDTH
    group = heads // kv_here
    per_row = heads * steps
    total = rows * per_row
    tokens = steps * rows
    chunks = sems.shape[1]
    chunk_rows = rows // chunks
    scale = 1.0 / math.sqrt(HEAD_WIDTH)

    def kv_copies(c):
        at = pl.ds(c * chunk_rows, chunk_rows)
        return [
            pltpu.make_async_copy(src.at[at], dst.at[at], sems.at[which, c])
            for which, (src, dst) in enumerate([(k_hbm, k_ref), (v_hbm, v_ref)])
        ]

    small = [
        pltpu.make_async_copy(src, dst, small_sems.at[n])
        for n, (src, dst) in enumerate(
            [
                (q_hbm, q_ref),
                (kf_hbm, kf_ref),
                (lengths_hbm, lengths_ref),
                (adapter_hbm, adapter_ref),
                (slot_hbm, slot_ref),
                (vf_hbm, vf_ref),
            ]
        )
    ]
    q_copy, kf_copy, lengths_copy, adapter_copy, slot_copy, vf_copy = small
    first, *others = [kv_copies(c) for c in range(chunks)]
    for copy in [q_copy, *first, *small[1:], *sum(others, [])]:
        copy.start()

    @pl.loop(0, total // ORDER_ROWS)
    def _(i):
        at = iota((ORDER_ROWS, LANES), 0) + i * ORDER_ROWS
        source = mod(at, rows) * per_row + div(at, tokens) * steps + mod(div(at, rows), steps)
        here = pl.ds(pl.multiple_of(i * ORDER_ROWS, ORDER_ROWS), ORDER_ROWS)
        order_ref[here, :] = one_hot(source, total)

    adapter_copy.wait()
    slot_copy.wait()
    me = lax.axis_index("replica")
    positions = sum(partner_order(owners), [])
    row_at = mod(iota((8, tokens), 1), rows)
    row_down = iota((rows, LANES), 0)
    first_slot = jnp.zeros((8, tokens), jnp.int32)
    local_of = jnp.zeros((rows, LANES), jnp.int32)
    firsts = []
    for r in range(rows):
        slot = slot_ref[adapter_ref[r]]
        owner = jnp.int32(0)
        for d in range(1, owners):
            owner = owner + (slot >= d * resident).astype(jnp.int32)
        partner = lax.bitwise_xor(owner, me)
        first = jnp.int32(0)
        for d in range(1, owners):
            first = jnp.where(partner == positions[d], d * capacity, first)
        firsts.append(first)
        first_slot = jnp.where(row_at == r, first, first_slot)
        local_of = jnp.where(row_down == r, slot - owner * resident, local_of)
    place = first_slot
    for r in range(rows - 1):
        place = place + ((first_slot == firsts[r]) & (row_at > r)).astype(jnp.int32)
    held = owners * capacity * steps
    slot_at = iota((held, tokens), 0)
    token_at = iota((held, tokens), 1)
    pick = (
        (jnp.concatenate([place] * (held // 8), axis=0) == div(slot_at, steps))
        & (mod(slot_at, steps) == div(token_at, rows))
    ).astype(jnp.bfloat16)
    pick_ref[...] = pick
    local_hot = (local_of == iota((rows, LANES), 1)).astype(jnp.bfloat16)
    entry = iota((owners * META_ROWS, rows), 0)
    entry_place = mod(entry, META_ROWS)
    entry_slot = div(entry, META_ROWS) * capacity + entry_place
    entry_pick = (
        (jnp.concatenate([place[:, :rows]] * (owners * META_ROWS // 8), axis=0) == entry_slot)
        & (entry_place < capacity)
    ).astype(jnp.bfloat16)
    meta = jnp.dot(entry_pick, local_hot, preferred_element_type=jnp.float32)

    q_copy.wait()
    by_head = jnp.concatenate(
        [
            q_ref[:, :, h * HEAD_WIDTH : (h + 1) * HEAD_WIDTH].reshape(tokens, HEAD_WIDTH)
            for h in range(heads)
        ],
        axis=0,
    )
    q_cols_ref[...] = jnp.dot(
        by_head.astype(jnp.float32).T.astype(jnp.bfloat16),
        order_ref[...],
        preferred_element_type=jnp.float32,
    )
    lane = iota((HEAD_WIDTH, LANES), 1)
    row_of = div(lane, per_row)
    kv_of = mod(div(lane, steps * group), kv_here)

    kf_copy.wait()
    kf = kf_ref[...].reshape(tokens, kv_width)
    token, query = iota((tokens, LANES), 0), iota((tokens, LANES), 1)
    position = iota((cache, LANES), 0)

    def scores(c):
        cols = q_cols_ref[:, pl.ds(pl.multiple_of(c * LANES, LANES), LANES)]
        by_kv = [jnp.where(kv_of == g, cols, 0.0) for g in range(kv_here)]
        fresh = jnp.dot(
            kf,
            jnp.concatenate(by_kv, axis=0).astype(jnp.bfloat16),
            preferred_element_type=jnp.float32,
        )
        live = (mod(token, rows) == div(query, per_row) + c * chunk_rows) & (
            div(token, rows) <= mod(query, steps)
        )
        fresh = jnp.where(live, fresh * scale, -jnp.inf)
        weights = jnp.concatenate(
            [jnp.where(row_of == j, q, 0.0) for j in range(chunk_rows) for q in by_kv], axis=0
        ).astype(jnp.bfloat16)
        keys = jnp.concatenate([k_ref[c * chunk_rows + j] for j in range(chunk_rows)], axis=1)
        cached = jnp.dot(keys, weights, preferred_element_type=jnp.float32)
        return cached * scale, fresh

    def softmax(c, cached, fresh):
        length = jnp.zeros((1, LANES), jnp.int32)
        for j in range(chunk_rows):
            length = jnp.where(
                div(iota((1, LANES), 1), per_row) == j, lengths_ref[c * chunk_rows + j], length
            )
        cached = jnp.where(position < length, cached, -jnp.inf)
        top = jnp.maximum(
            jnp.max(cached, axis=0, keepdims=True), jnp.max(fresh, axis=0, keepdims=True)
        )
        wc, wf = jnp.exp(cached - top), jnp.exp(fresh - top)
        share = 1.0 / (
            jnp.sum(wc, axis=0, keepdims=True) + jnp.sum(wf, axis=0, keepdims=True)
        )
        return (wc * share).T.astype(jnp.bfloat16), (wf * share).T.astype(jnp.bfloat16)

    kv_down = mod(div(iota((LANES, HEAD_WIDTH), 0), steps * group), kv_here)

    def values(c, cached, fresh):
        out = jnp.concatenate(
            [
                jnp.dot(
                    cached[j * per_row : (j + 1) * per_row, :],
                    v_ref[c * chunk_rows + j],
                    preferred_element_type=jnp.float32,
                )
                for j in range(chunk_rows)
            ],
            axis=0,
        ) + jnp.dot(fresh, vf, preferred_element_type=jnp.float32)
        own = out[:, :HEAD_WIDTH]
        for g in range(1, kv_here):
            own = jnp.where(kv_down == g, out[:, g * HEAD_WIDTH : (g + 1) * HEAD_WIDTH], own)
        return own.astype(jnp.bfloat16)

    lengths_copy.wait()
    vf_copy.wait()
    vf = vf_ref[...].reshape(tokens, kv_width)

    w_copies = [block_copy(w_hbm, w_ref.at[n], w_sems.at[n], d) for n, d in enumerate(ahead)]
    for copy in w_copies:
        copy.start()

    @pl.loop(0, chunks // TOGETHER)
    def _(i):
        groups = [i * TOGETHER + n for n in range(TOGETHER)]
        for c in groups:
            for copy in kv_copies(c):
                copy.wait()

        scored = [scores(c) for c in groups]
        probs = [softmax(c, *part) for c, part in zip(groups, scored, strict=True)]
        for c, part in zip(groups, probs, strict=True):
            o_ref[pl.ds(pl.multiple_of(c * LANES, LANES), LANES), :] = values(c, *part)

    out = jnp.dot(
        order_ref[...], o_ref[...], preferred_element_type=jnp.float32
    ).astype(jnp.bfloat16)
    attn = jnp.concatenate(
        [out[h * tokens : (h + 1) * tokens, :] for h in range(heads)], axis=1
    )
    attn_ref[...] = attn
    sent = jnp.dot(pick, attn, preferred_element_type=jnp.float32)
    size = capacity * steps
    for d in range(owners):
        mine = sent[d * size : (d + 1) * size, :]
        send_refs[d][...] = jnp.concatenate(
            [mine[:, h * HEAD_WIDTH : (h + 1) * HEAD_WIDTH] for h in range(heads)]
            + [meta[d * META_ROWS : (d + 1) * META_ROWS, :]],
            axis=0,
        ).astype(jnp.bfloat16)
    for copy in w_copies:
        copy.wait()


def attend_and_pick(
    lengths,
    adapter_of_row,
    storage_slot,
    queries,
    fresh_keys,
    fresh_values,
    cached_keys,
    cached_values,
    weight,
    owners,
    capacity,
    resident,
    columns,
    ahead,
):
    steps, rows, width = queries.shape
    cache, kv_width = cached_keys.shape[1:]
    heads = width // HEAD_WIDTH
    total = rows * heads * steps
    tokens = steps * rows
    size = capacity * steps
    chunks = total // LANES
    outs = pl.pallas_call(
        functools.partial(attend_kernel, owners, capacity, resident, ahead),
        out_shape=[
            jax.ShapeDtypeStruct((tokens, width), jnp.bfloat16),
            jax.ShapeDtypeStruct((owners * size, tokens), jnp.bfloat16),
            pltpu.VMEM((len(ahead), width, columns), jnp.bfloat16),
        ]
        + [jax.ShapeDtypeStruct((heads * size + META_ROWS, HEAD_WIDTH), jnp.bfloat16)] * owners,
        in_specs=[HBM] * 9,
        out_specs=[VMEM] * (3 + owners),
        scratch_shapes=[
            pltpu.SMEM(lengths.shape, jnp.int32),
            pltpu.SMEM(adapter_of_row.shape, jnp.int32),
            pltpu.SMEM(storage_slot.shape, jnp.int32),
            pltpu.VMEM(queries.shape, jnp.bfloat16),
            pltpu.VMEM(fresh_keys.shape, jnp.bfloat16),
            pltpu.VMEM(fresh_values.shape, jnp.bfloat16),
            pltpu.VMEM((rows, cache, kv_width), jnp.bfloat16),
            pltpu.VMEM((rows, cache, kv_width), jnp.bfloat16),
            pltpu.VMEM((total, total), jnp.bfloat16),
            pltpu.VMEM((HEAD_WIDTH, total), jnp.float32),
            pltpu.VMEM((total, HEAD_WIDTH), jnp.bfloat16),
            pltpu.SemaphoreType.DMA((2, chunks)),
            pltpu.SemaphoreType.DMA((6,)),
            pltpu.SemaphoreType.DMA((len(ahead),)),
        ],
        compiler_params=pltpu.CompilerParams(vmem_limit_bytes=24 * MIB),
        cost_estimate=pl.CostEstimate(
            flops=8 * total * cache * kv_width,
            bytes_accessed=4 * rows * cache * kv_width,
            transcendentals=total * cache,
        ),
        name="attend",
    )(
        *in_hbm(
            lengths,
            adapter_of_row,
            storage_slot,
            queries,
            fresh_keys,
            fresh_values,
            cached_keys,
            cached_values,
            weight,
        ),
    )
    return outs[0], outs[1], outs[2], outs[3:]


def project_kernel(blocks, here, bring, added, attn_ref, w_hbm, *refs):
    here_ref = refs[0] if here else None
    add_refs = refs[bool(here) :][:added]
    refs = refs[len(refs) - len(blocks) - bool(bring) - 2 :]
    outs, w_ref, sems = refs[: len(blocks)], refs[-2], refs[-1]
    fetched = blocks[here:]
    copies = [
        block_copy(w_hbm, w_ref.at[n], sems.at[n], d) for n, d in enumerate(fetched)
    ] + [
        block_copy(w_hbm, refs[len(blocks)].at[n], sems.at[len(fetched) + n], d)
        for n, d in enumerate(bring)
    ]
    for copy in copies:
        copy.start()
    attn = attn_ref[...]
    for n in range(len(blocks)):
        if n >= here:
            copies[n - here].wait()
        block = here_ref.at[n] if n < here else w_ref.at[n - here]

        @pl.loop(0, block.shape[-1] // TILE)
        def _(i, n=n, block=block, out_ref=outs[n]):
            cols = pl.ds(pl.multiple_of(i * TILE, TILE), TILE)
            out = jnp.dot(attn, block[:, cols], preferred_element_type=jnp.float32)
            for add_ref in add_refs[n :: len(blocks)]:
                out = out + add_ref[:, cols].astype(jnp.float32)
            out_ref[:, cols] = out.astype(out_ref.dtype)

    for copy in copies[len(fetched) :]:
        copy.wait()


def project(attn, weight, columns, blocks, here=None, bring=(), add=(), dtype=jnp.bfloat16, after=()):
    tokens, width = attn.shape
    held = 0 if here is None else here.shape[0]
    fetched = len(blocks) - held
    extra = [*([here] if held else []), *add]
    outs = [jax.ShapeDtypeStruct((tokens, columns), dtype)] * len(blocks)
    if bring:
        outs.append(pltpu.VMEM((len(bring), width, columns), jnp.bfloat16))
    return pl.pallas_call(
        functools.partial(project_kernel, blocks, held, bring, len(add)),
        out_shape=outs,
        in_specs=[VMEM, HBM] + [VMEM] * len(extra) + [ANY] * len(after),
        out_specs=[VMEM] * len(outs),
        scratch_shapes=[
            pltpu.VMEM((max(fetched, 1), width if fetched else 16, columns), jnp.bfloat16),
            pltpu.SemaphoreType.DMA((fetched + len(bring),)),
        ],
        compiler_params=pltpu.CompilerParams(vmem_limit_bytes=16 * MIB),
        cost_estimate=pl.CostEstimate(
            flops=2 * tokens * width * columns * len(blocks),
            bytes_accessed=2 * width * columns * len(blocks),
            transcendentals=0,
        ),
        name="project",
    )(attn, *in_hbm(weight), *extra, *after)


def merge_kernel(mine_ref, got_ref, _, out_ref):
    out_ref[...] = (mine_ref[...] + got_ref[...].astype(jnp.float32)).astype(jnp.bfloat16)


def merge(mine, got, after):
    return pl.pallas_call(
        merge_kernel,
        out_shape=jax.ShapeDtypeStruct(mine.shape, jnp.bfloat16),
        in_specs=[VMEM, VMEM, ANY],
        out_specs=VMEM,
        compiler_params=pltpu.CompilerParams(vmem_limit_bytes=4 * MIB),
        name="merge",
    )(mine, got, after)


def down_kernel(capacity, steps, *refs):
    (*got_refs, down_ref, _, mine_ref, sent_ref, mask_ref) = refs
    resident, rank, width = down_ref.shape
    wide = resident * rank
    heads = width // HEAD_WIDTH
    size = capacity * steps
    held = size * len(got_refs)
    got = [ref[...].astype(jnp.float32) for ref in got_refs]
    rows = jnp.concatenate(
        [
            jnp.concatenate([part[h * size : (h + 1) * size, :] for part in got], axis=0)
            for h in range(heads)
        ],
        axis=1,
    ).astype(jnp.bfloat16)
    meta = jnp.concatenate([part[heads * size :, :] for part in got], axis=0)
    spread = div(iota((LANES, wide), 1), rank) == iota((LANES, wide), 0)
    entries = meta.shape[0]
    slot, entry = iota((held, entries), 0), iota((held, entries), 1)
    of_slot = entry == div(slot, size) * META_ROWS + div(mod(slot, size), steps)
    local = jnp.dot(
        of_slot.astype(jnp.bfloat16),
        meta.astype(jnp.bfloat16),
        preferred_element_type=jnp.float32,
    )
    mask = jnp.dot(
        local.astype(jnp.bfloat16),
        spread.astype(jnp.bfloat16),
        preferred_element_type=jnp.float32,
    )
    mask_ref[...] = mask.astype(jnp.bfloat16)
    low = lax.dot_general(
        rows,
        down_ref[...].reshape(wide, width),
        (((1,), (1,)), ((), ())),
        preferred_element_type=jnp.float32,
    )
    low = low * mask
    pair = low[:, :LANES]
    for n in range(1, wide // LANES):
        pair = pair + low[:, n * LANES : (n + 1) * LANES]
    both = pair + pltpu.roll(pair, rank, 1)
    half = held // 2
    packed = jnp.where(iota((half, LANES), 1) < rank, both[:half, :], both[half:, :])
    mine_ref[...] = packed
    sent_ref[...] = packed.astype(jnp.bfloat16)


def down(got, factors, capacity, steps, after):
    resident, rank, width = factors.shape
    held = len(got) * capacity * steps
    return pl.pallas_call(
        functools.partial(down_kernel, capacity, steps),
        out_shape=[
            jax.ShapeDtypeStruct((held // 2, LANES), jnp.float32),
            jax.ShapeDtypeStruct((held // 2, LANES), jnp.bfloat16),
            jax.ShapeDtypeStruct((held, resident * rank), jnp.bfloat16),
        ],
        in_specs=[VMEM] * (len(got) + 1) + [ANY],
        out_specs=[VMEM] * 3,
        compiler_params=pltpu.CompilerParams(vmem_limit_bytes=12 * MIB),
        cost_estimate=pl.CostEstimate(
            flops=200 * held * resident * rank * width,
            bytes_accessed=2 * resident * rank * width,
            transcendentals=0,
        ),
        name="down",
    )(*got, factors, after)


def up_kernel(peers, mine_ref, *refs):
    got_refs, (mask_ref, up_ref, _, *delta_refs) = refs[:peers], refs[peers:]
    resident, rank, columns = up_ref.shape
    wide = resident * rank
    total = mine_ref[...]
    for ref in got_refs:
        total = total + ref[...].astype(jnp.float32)
    other = pltpu.roll(total, rank, 1)
    first = iota(total.shape, 1) < rank
    both = jnp.concatenate(
        [jnp.where(first, total, other), jnp.where(first, other, total)], axis=0
    )
    both = jnp.concatenate([both] * (wide // LANES), axis=1)
    low = jnp.where(mask_ref[...].astype(jnp.float32) > 0.5, both, 0.0).astype(jnp.bfloat16)
    delta = jnp.dot(
        low, up_ref[...].reshape(wide, columns), preferred_element_type=jnp.float32
    ).astype(jnp.bfloat16)
    size = delta.shape[0] // len(delta_refs)
    for d, ref in enumerate(delta_refs):
        ref[...] = delta[d * size : (d + 1) * size, :]


def up(mine, got, mask, factors, owners, after):
    resident, rank, columns = factors.shape
    held = mask.shape[0]
    return pl.pallas_call(
        functools.partial(up_kernel, len(got)),
        out_shape=[jax.ShapeDtypeStruct((held // owners, columns), jnp.bfloat16)] * owners,
        in_specs=[VMEM] * (len(got) + 3) + [ANY],
        out_specs=[VMEM] * owners,
        compiler_params=pltpu.CompilerParams(vmem_limit_bytes=16 * MIB),
        cost_estimate=pl.CostEstimate(
            flops=200 * held * resident * rank * columns,
            bytes_accessed=2 * resident * rank * columns,
            transcendentals=0,
        ),
        name="up",
    )(mine, *got, mask, factors, after)


def finish_kernel(owners, pick_ref, *refs):
    delta_refs, (*near_refs, base_ref, out_hbm, out_ref, sems) = refs[:owners], refs[owners:]
    width = near_refs[0].shape[1]
    pick = pick_ref[...]
    copies = []
    for n, near_ref in enumerate(near_refs):
        cols = slice(n * width, (n + 1) * width)
        mixed = base_ref[:, cols] + near_ref[...].astype(jnp.float32)
        delta = jnp.concatenate([ref[:, cols] for ref in delta_refs], axis=0)
        mixed = mixed + lax.dot_general(
            pick, delta, (((0,), (0,)), ((), ())), preferred_element_type=jnp.float32
        )
        out_ref[:, :, cols] = mixed.astype(jnp.bfloat16).reshape(*out_ref.shape[:2], width)
        copies.append(
            pltpu.make_async_copy(out_ref.at[:, :, cols], out_hbm.at[:, :, cols], sems.at[n])
        )
        copies[n].start()
    for copy in copies:
        copy.wait()


def finish(base, pick, delta, near, steps):
    tokens, columns = base.shape
    shape = (steps, tokens // steps, columns)
    operands = [pick, *delta, *near, base]
    return pl.pallas_call(
        functools.partial(finish_kernel, len(delta)),
        out_shape=jax.ShapeDtypeStruct(shape, jnp.bfloat16),
        in_specs=[VMEM] * len(operands),
        out_specs=HBM,
        scratch_shapes=[
            pltpu.VMEM(shape, jnp.bfloat16),
            pltpu.SemaphoreType.DMA((len(near),)),
        ],
        compiler_params=pltpu.CompilerParams(vmem_limit_bytes=12 * MIB),
        cost_estimate=pl.CostEstimate(
            flops=2 * tokens * pick.shape[0] * columns,
            bytes_accessed=10 * tokens * columns,
            transcendentals=0,
        ),
        name="finish",
    )(*operands)


def body(
    queries,
    fresh_token_keys,
    fresh_token_values,
    cached_key_rows,
    cached_value_rows,
    cache_live_lengths,
    output_projection_weight,
    adapter_down_factors,
    adapter_up_factors,
    adapter_of_row,
    adapter_storage_slot,
):
    step_count, row_count, _ = queries.shape
    resident = adapter_down_factors.shape[0]
    owners = lax.axis_size("replica")
    tensors = lax.axis_size("tensor")
    capacity = max(2, 2 * row_count // owners)
    columns = adapter_up_factors.shape[2]
    far_sent, far_kept = list(range(3, tensors, 2)), list(range(2, tensors, 2))

    attn, pick, w_here, sent = attend_and_pick(
        cache_live_lengths,
        adapter_of_row,
        adapter_storage_slot,
        queries,
        fresh_token_keys,
        fresh_token_values,
        cached_key_rows,
        cached_value_rows,
        output_projection_weight,
        owners,
        capacity,
        resident,
        columns,
        far_sent,
    )
    early, late = partner_order(owners)
    got_early = exchange_all(sent[: len(early)], early, "replica")
    got_late = exchange_all(sent[len(early) :], late, "replica")

    weight = output_projection_weight
    *parts, w_here = project(attn, weight, columns, far_sent, here=w_here, bring=far_kept)
    far_got = [xor_exchange(part, "tensor", 1) for part in parts]
    kept = project(
        attn, weight, columns, far_kept, here=w_here, dtype=jnp.float32, after=[parts[0]]
    )

    def low_rank(got, after):
        mine, sent_low, mask = down(got, adapter_down_factors, capacity, step_count, after)
        others = [xor_exchange(sent_low, "tensor", d) for d in range(1, tensors)]
        return mine, others, mask, sent_low

    *low_early, sent_early = low_rank(got_early, kept[0])
    *low_late, sent_late = low_rank(got_late, sent_early)
    delta_early = up(*low_early, adapter_up_factors, len(early), sent_late)
    back_early = exchange_all(delta_early, early, "replica")
    halves_sent = [merge(*pair, delta_early[0]) for pair in zip(kept, far_got, strict=True)]
    others = [xor_exchange(half, "tensor", d) for half, d in zip(halves_sent, far_kept, strict=True)]
    delta_late = up(*low_late, adapter_up_factors, len(late), halves_sent[0])
    back_late = exchange_all(delta_late, late, "replica")

    near, w_here = project(attn, weight, columns, [1], bring=[0], after=[delta_late[0]])
    width = columns // PIECES
    near_got = [
        xor_exchange(near[:, n * width : (n + 1) * width], "tensor", 1) for n in range(PIECES)
    ]
    (own,) = project(
        attn, weight, columns, [0], here=w_here, add=others, dtype=jnp.float32, after=[near]
    )
    return finish(own, pick, [*back_early, *back_late], near_got, step_count)


def solution(mesh):
    in_specs = (
        P(None, ("groups", "replica"), "tensor"),
        P(None, ("groups", "replica"), "tensor"),
        P(None, ("groups", "replica"), "tensor"),
        P(("groups", "replica"), None, "tensor"),
        P(("groups", "replica"), None, "tensor"),
        P(("groups", "replica")),
        P("tensor", None),
        P(("groups", "replica"), None, "tensor"),
        P(("groups", "replica"), None, "tensor"),
        P(("groups", "replica")),
        P("groups"),
    )
    out_specs = P(None, ("groups", "replica"), "tensor")
    return jax.shard_map(body, mesh=mesh, in_specs=in_specs, out_specs=out_specs, check_vma=False)
```

```python
import functools
import math

import jax
import jax.numpy as jnp
import numpy as np
from jax import lax
from jax.experimental import pallas as pl
from jax.experimental.pallas import tpu as pltpu
from jax.sharding import PartitionSpec as P

HEAD_WIDTH = 128
LANES = 128
META_ROWS = 16
TILE = 512
TOGETHER = 4
PIECES = 2
MIB = 1024 * 1024
VMEM = pl.BlockSpec(memory_space=pltpu.VMEM)
ANY = pl.BlockSpec(memory_space=pl.ANY)
HBM = pl.BlockSpec(memory_space=pltpu.HBM)


def iota(shape, dim):
    return lax.broadcasted_iota(jnp.int32, shape, dim)


def halves(n):
    if n & (n - 1):
        raise ValueError(n)
    return n.bit_length() - 1


def div(x, n):
    return lax.shift_right_logical(x, jnp.int32(halves(n)))


def mod(x, n):
    return x & ((1 << halves(n)) - 1)


def in_hbm(*arrays):
    return [pltpu.with_memory_space_constraint(a, pltpu.HBM) for a in arrays]


def xor_exchange(value, axis, distance):
    size = lax.axis_size(axis)
    return lax.ppermute(value, axis, [(i, i ^ distance) for i in range(size)])


def partner_order(size):
    return [0, *range(size // 2, size), *range(1, size // 2)]


def exchange_all(blocks, axis):
    order = partner_order(lax.axis_size(axis))
    return [blocks[0]] + [
        xor_exchange(block, axis, distance)
        for block, distance in zip(blocks[1:], order[1:], strict=True)
    ]


def block_copy(w_hbm, dst, sem, distance):
    me = lax.axis_index("tensor")
    columns = dst.shape[-1]
    at = pl.multiple_of(lax.bitwise_xor(me, jnp.int32(distance)) * columns, LANES)
    return pltpu.make_async_copy(w_hbm.at[:, pl.ds(at, columns)], dst, sem)


def attend_kernel(
    owners,
    capacity,
    resident,
    lengths_hbm,
    adapter_hbm,
    slot_hbm,
    q_hbm,
    order_hbm,
    kf_hbm,
    vf_hbm,
    k_hbm,
    v_hbm,
    attn_ref,
    pick_ref,
    *rest,
):
    send_refs, rest = rest[:owners], rest[owners:]
    lengths_ref, adapter_ref, slot_ref, q_ref, kf_ref, vf_ref, k_ref, v_ref = rest[:8]
    order_ref, q_cols_ref, o_ref, sems, small_sems = rest[8:]
    steps, rows, width = q_ref.shape
    cache, kv_width = k_ref.shape[1:]
    heads = width // HEAD_WIDTH
    kv_here = kv_width // HEAD_WIDTH
    group = heads // kv_here
    per_row = heads * steps
    total = rows * per_row
    tokens = steps * rows
    chunks = sems.shape[1]
    chunk_rows = rows // chunks
    scale = 1.0 / math.sqrt(HEAD_WIDTH)

    def kv_copies(c):
        at = pl.ds(c * chunk_rows, chunk_rows)
        return [
            pltpu.make_async_copy(src.at[at], dst.at[at], sems.at[which, c])
            for which, (src, dst) in enumerate([(k_hbm, k_ref), (v_hbm, v_ref)])
        ]

    small = [
        pltpu.make_async_copy(src, dst, small_sems.at[n])
        for n, (src, dst) in enumerate(
            [
                (q_hbm, q_ref),
                (order_hbm, order_ref),
                (kf_hbm, kf_ref),
                (lengths_hbm, lengths_ref),
                (adapter_hbm, adapter_ref),
                (slot_hbm, slot_ref),
                (vf_hbm, vf_ref),
            ]
        )
    ]
    q_copy, order_copy, kf_copy, lengths_copy, adapter_copy, slot_copy, vf_copy = small
    first, *others = [kv_copies(c) for c in range(chunks)]
    for copy in [*small[:2], *first, *small[2:], *sum(others, [])]:
        copy.start()

    adapter_copy.wait()
    slot_copy.wait()
    me = lax.axis_index("replica")
    positions = partner_order(owners)
    row_at = mod(iota((8, tokens), 1), rows)
    row_down = iota((rows, LANES), 0)
    first_slot = jnp.zeros((8, tokens), jnp.int32)
    local_of = jnp.zeros((rows, LANES), jnp.int32)
    firsts = []
    for r in range(rows):
        slot = slot_ref[adapter_ref[r]]
        owner = jnp.int32(0)
        for d in range(1, owners):
            owner = owner + (slot >= d * resident).astype(jnp.int32)
        partner = lax.bitwise_xor(owner, me)
        first = jnp.int32(0)
        for d in range(1, owners):
            first = jnp.where(partner == positions[d], d * capacity, first)
        firsts.append(first)
        first_slot = jnp.where(row_at == r, first, first_slot)
        local_of = jnp.where(row_down == r, slot - owner * resident, local_of)
    place = first_slot
    for r in range(rows - 1):
        place = place + ((first_slot == firsts[r]) & (row_at > r)).astype(jnp.int32)
    held = owners * capacity * steps
    slot_at = iota((held, tokens), 0)
    token_at = iota((held, tokens), 1)
    pick = (
        (jnp.concatenate([place] * (held // 8), axis=0) == div(slot_at, steps))
        & (mod(slot_at, steps) == div(token_at, rows))
    ).astype(jnp.bfloat16)
    pick_ref[...] = pick
    local_hot = (local_of == iota((rows, LANES), 1)).astype(jnp.bfloat16)
    entry = iota((owners * META_ROWS, rows), 0)
    entry_place = mod(entry, META_ROWS)
    entry_slot = div(entry, META_ROWS) * capacity + entry_place
    entry_pick = (
        (jnp.concatenate([place[:, :rows]] * (owners * META_ROWS // 8), axis=0) == entry_slot)
        & (entry_place < capacity)
    ).astype(jnp.bfloat16)
    meta = jnp.dot(entry_pick, local_hot, preferred_element_type=jnp.float32)

    q_copy.wait()
    by_head = jnp.concatenate(
        [
            q_ref[:, :, h * HEAD_WIDTH : (h + 1) * HEAD_WIDTH].reshape(tokens, HEAD_WIDTH)
            for h in range(heads)
        ],
        axis=0,
    )
    order_copy.wait()
    q_cols_ref[...] = jnp.dot(
        by_head.astype(jnp.float32).T.astype(jnp.bfloat16),
        order_ref[...],
        preferred_element_type=jnp.float32,
    )
    lane = iota((HEAD_WIDTH, LANES), 1)
    row_of = div(lane, per_row)
    kv_of = mod(div(lane, steps * group), kv_here)

    kf_copy.wait()
    kf = kf_ref[...].reshape(tokens, kv_width)
    token, query = iota((tokens, LANES), 0), iota((tokens, LANES), 1)
    position = iota((cache, LANES), 0)

    def scores(c):
        cols = q_cols_ref[:, pl.ds(pl.multiple_of(c * LANES, LANES), LANES)]
        by_kv = [jnp.where(kv_of == g, cols, 0.0) for g in range(kv_here)]
        fresh = jnp.dot(
            kf,
            jnp.concatenate(by_kv, axis=0).astype(jnp.bfloat16),
            preferred_element_type=jnp.float32,
        )
        live = (mod(token, rows) == div(query, per_row) + c * chunk_rows) & (
            div(token, rows) <= mod(query, steps)
        )
        fresh = jnp.where(live, fresh * scale, -jnp.inf)
        weights = jnp.concatenate(
            [jnp.where(row_of == j, q, 0.0) for j in range(chunk_rows) for q in by_kv], axis=0
        ).astype(jnp.bfloat16)
        keys = jnp.concatenate([k_ref[c * chunk_rows + j] for j in range(chunk_rows)], axis=1)
        cached = jnp.dot(keys, weights, preferred_element_type=jnp.float32)
        return cached * scale, fresh

    def softmax(c, cached, fresh):
        length = jnp.zeros((1, LANES), jnp.int32)
        for j in range(chunk_rows):
            length = jnp.where(
                div(iota((1, LANES), 1), per_row) == j, lengths_ref[c * chunk_rows + j], length
            )
        cached = jnp.where(position < length, cached, -jnp.inf)
        top = jnp.maximum(
            jnp.max(cached, axis=0, keepdims=True), jnp.max(fresh, axis=0, keepdims=True)
        )
        wc, wf = jnp.exp(cached - top), jnp.exp(fresh - top)
        share = 1.0 / (
            jnp.sum(wc, axis=0, keepdims=True) + jnp.sum(wf, axis=0, keepdims=True)
        )
        return (wc * share).T.astype(jnp.bfloat16), (wf * share).T.astype(jnp.bfloat16)

    kv_down = mod(div(iota((LANES, HEAD_WIDTH), 0), steps * group), kv_here)

    def values(c, cached, fresh):
        out = jnp.concatenate(
            [
                jnp.dot(
                    cached[j * per_row : (j + 1) * per_row, :],
                    v_ref[c * chunk_rows + j],
                    preferred_element_type=jnp.float32,
                )
                for j in range(chunk_rows)
            ],
            axis=0,
        ) + jnp.dot(fresh, vf, preferred_element_type=jnp.float32)
        own = out[:, :HEAD_WIDTH]
        for g in range(1, kv_here):
            own = jnp.where(kv_down == g, out[:, g * HEAD_WIDTH : (g + 1) * HEAD_WIDTH], own)
        return own.astype(jnp.bfloat16)

    lengths_copy.wait()
    vf_copy.wait()
    vf = vf_ref[...].reshape(tokens, kv_width)

    together = min(TOGETHER, chunks)

    @pl.loop(0, chunks // together)
    def _(i):
        groups = [i * together + n for n in range(together)]
        for c in groups:
            for copy in kv_copies(c):
                copy.wait()

        scored = [scores(c) for c in groups]
        probs = [softmax(c, *part) for c, part in zip(groups, scored, strict=True)]
        for c, part in zip(groups, probs, strict=True):
            o_ref[pl.ds(pl.multiple_of(c * LANES, LANES), LANES), :] = values(c, *part)

    out = jnp.dot(
        order_ref[...], o_ref[...], preferred_element_type=jnp.float32
    ).astype(jnp.bfloat16)
    attn = jnp.concatenate(
        [out[h * tokens : (h + 1) * tokens, :] for h in range(heads)], axis=1
    )
    attn_ref[...] = attn
    sent = jnp.dot(pick, attn, preferred_element_type=jnp.float32)
    size = capacity * steps
    for d in range(owners):
        mine = sent[d * size : (d + 1) * size, :]
        send_refs[d][...] = jnp.concatenate(
            [mine[:, h * HEAD_WIDTH : (h + 1) * HEAD_WIDTH] for h in range(heads)]
            + [meta[d * META_ROWS : (d + 1) * META_ROWS, :]],
            axis=0,
        ).astype(jnp.bfloat16)


def row_order(heads, steps, rows):
    head, step, row = np.indices((heads, steps, rows)).reshape(3, -1)
    return np.eye(heads * steps * rows)[(row * heads + head) * steps + step]


def attend_and_pick(
    lengths,
    adapter_of_row,
    storage_slot,
    queries,
    fresh_keys,
    fresh_values,
    cached_keys,
    cached_values,
    owners,
    capacity,
    resident,
):
    steps, rows, width = queries.shape
    cache, kv_width = cached_keys.shape[1:]
    heads = width // HEAD_WIDTH
    total = rows * heads * steps
    tokens = steps * rows
    size = capacity * steps
    chunks = total // LANES
    outs = pl.pallas_call(
        functools.partial(attend_kernel, owners, capacity, resident),
        out_shape=[
            jax.ShapeDtypeStruct((tokens, width), jnp.bfloat16),
            jax.ShapeDtypeStruct((owners * size, tokens), jnp.bfloat16),
        ]
        + [jax.ShapeDtypeStruct((heads * size + META_ROWS, HEAD_WIDTH), jnp.bfloat16)] * owners,
        in_specs=[HBM] * 9,
        out_specs=[VMEM] * (2 + owners),
        scratch_shapes=[
            pltpu.SMEM(lengths.shape, jnp.int32),
            pltpu.SMEM(adapter_of_row.shape, jnp.int32),
            pltpu.SMEM(storage_slot.shape, jnp.int32),
            pltpu.VMEM(queries.shape, jnp.bfloat16),
            pltpu.VMEM(fresh_keys.shape, jnp.bfloat16),
            pltpu.VMEM(fresh_values.shape, jnp.bfloat16),
            pltpu.VMEM((rows, cache, kv_width), jnp.bfloat16),
            pltpu.VMEM((rows, cache, kv_width), jnp.bfloat16),
            pltpu.VMEM((total, total), jnp.bfloat16),
            pltpu.VMEM((HEAD_WIDTH, total), jnp.float32),
            pltpu.VMEM((total, HEAD_WIDTH), jnp.bfloat16),
            pltpu.SemaphoreType.DMA((2, chunks)),
            pltpu.SemaphoreType.DMA((7,)),
        ],
        compiler_params=pltpu.CompilerParams(vmem_limit_bytes=24 * MIB),
        cost_estimate=pl.CostEstimate(
            flops=8 * total * cache * kv_width,
            bytes_accessed=4 * rows * cache * kv_width,
            transcendentals=total * cache,
        ),
        name="attend",
    )(
        *in_hbm(
            lengths,
            adapter_of_row,
            storage_slot,
            queries,
            jnp.asarray(row_order(heads, steps, rows), jnp.bfloat16),
            fresh_keys,
            fresh_values,
            cached_keys,
            cached_values,
        ),
    )
    return outs[0], outs[1], outs[2:]


def project_kernel(blocks, here, bring, added, attn_ref, w_hbm, *refs):
    here_ref = refs[0] if here else None
    add_refs = refs[bool(here) :][:added]
    refs = refs[len(refs) - len(blocks) - bool(bring) - 2 :]
    outs, w_ref, sems = refs[: len(blocks)], refs[-2], refs[-1]
    fetched = blocks[here:]
    copies = [
        block_copy(w_hbm, w_ref.at[n], sems.at[n], d) for n, d in enumerate(fetched)
    ] + [
        block_copy(w_hbm, refs[len(blocks)].at[n], sems.at[len(fetched) + n], d)
        for n, d in enumerate(bring)
    ]
    for copy in copies:
        copy.start()
    attn = attn_ref[...]
    for n in range(len(blocks)):
        if n >= here:
            copies[n - here].wait()
        block = here_ref.at[n] if n < here else w_ref.at[n - here]

        @pl.loop(0, block.shape[-1] // TILE)
        def _(i, n=n, block=block, out_ref=outs[n]):
            cols = pl.ds(pl.multiple_of(i * TILE, TILE), TILE)
            out = jnp.dot(attn, block[:, cols], preferred_element_type=jnp.float32)
            for add_ref in add_refs[n :: len(blocks)]:
                out = out + add_ref[:, cols].astype(jnp.float32)
            out_ref[:, cols] = out.astype(out_ref.dtype)

    for copy in copies[len(fetched) :]:
        copy.wait()


def project(attn, weight, columns, blocks, here=None, bring=(), add=(), dtype=jnp.bfloat16, after=()):
    tokens, width = attn.shape
    held = 0 if here is None else here.shape[0]
    fetched = len(blocks) - held
    extra = [*([here] if held else []), *add]
    outs = [jax.ShapeDtypeStruct((tokens, columns), dtype)] * len(blocks)
    if bring:
        outs.append(pltpu.VMEM((len(bring), width, columns), jnp.bfloat16))
    return pl.pallas_call(
        functools.partial(project_kernel, blocks, held, bring, len(add)),
        out_shape=outs,
        in_specs=[VMEM, HBM] + [VMEM] * len(extra) + [ANY] * len(after),
        out_specs=[VMEM] * len(outs),
        scratch_shapes=[
            pltpu.VMEM((max(fetched, 1), width if fetched else 16, columns), jnp.bfloat16),
            pltpu.SemaphoreType.DMA((fetched + len(bring),)),
        ],
        compiler_params=pltpu.CompilerParams(vmem_limit_bytes=16 * MIB),
        cost_estimate=pl.CostEstimate(
            flops=2 * tokens * width * columns * len(blocks),
            bytes_accessed=2 * width * columns * len(blocks),
            transcendentals=0,
        ),
        name="project",
    )(attn, *in_hbm(weight), *extra, *after)


def merge_kernel(mine_ref, got_ref, _, out_ref):
    out_ref[...] = (mine_ref[...] + got_ref[...].astype(jnp.float32)).astype(jnp.bfloat16)


def merge(mine, got, after):
    return pl.pallas_call(
        merge_kernel,
        out_shape=jax.ShapeDtypeStruct(mine.shape, jnp.bfloat16),
        in_specs=[VMEM, VMEM, ANY],
        out_specs=VMEM,
        compiler_params=pltpu.CompilerParams(vmem_limit_bytes=4 * MIB),
        name="merge",
    )(mine, got, after)


def down_kernel(capacity, steps, *refs):
    (*got_refs, down_ref, _, mine_ref, sent_ref, mask_ref) = refs
    resident, rank, width = down_ref.shape
    wide = resident * rank
    heads = width // HEAD_WIDTH
    size = capacity * steps
    held = size * len(got_refs)
    got = [ref[...].astype(jnp.float32) for ref in got_refs]
    rows = jnp.concatenate(
        [
            jnp.concatenate([part[h * size : (h + 1) * size, :] for part in got], axis=0)
            for h in range(heads)
        ],
        axis=1,
    ).astype(jnp.bfloat16)
    meta = jnp.concatenate([part[heads * size :, :] for part in got], axis=0)
    spread = div(iota((LANES, wide), 1), rank) == iota((LANES, wide), 0)
    entries = meta.shape[0]
    slot, entry = iota((held, entries), 0), iota((held, entries), 1)
    of_slot = entry == div(slot, size) * META_ROWS + div(mod(slot, size), steps)
    local = jnp.dot(
        of_slot.astype(jnp.bfloat16),
        meta.astype(jnp.bfloat16),
        preferred_element_type=jnp.float32,
    )
    mask = jnp.dot(
        local.astype(jnp.bfloat16),
        spread.astype(jnp.bfloat16),
        preferred_element_type=jnp.float32,
    )
    mask_ref[...] = mask.astype(jnp.bfloat16)
    low = lax.dot_general(
        rows,
        down_ref[...].reshape(wide, width),
        (((1,), (1,)), ((), ())),
        preferred_element_type=jnp.float32,
    )
    low = low * mask
    pair = low[:, :LANES]
    for n in range(1, wide // LANES):
        pair = pair + low[:, n * LANES : (n + 1) * LANES]
    both = pair + pltpu.roll(pair, rank, 1)
    half = held // 2
    packed = jnp.where(iota((half, LANES), 1) < rank, both[:half, :], both[half:, :])
    mine_ref[...] = packed
    sent_ref[...] = packed.astype(jnp.bfloat16)


def down(got, factors, capacity, steps, after):
    resident, rank, width = factors.shape
    held = len(got) * capacity * steps
    return pl.pallas_call(
        functools.partial(down_kernel, capacity, steps),
        out_shape=[
            jax.ShapeDtypeStruct((held // 2, LANES), jnp.float32),
            jax.ShapeDtypeStruct((held // 2, LANES), jnp.bfloat16),
            jax.ShapeDtypeStruct((held, resident * rank), jnp.bfloat16),
        ],
        in_specs=[VMEM] * (len(got) + 1) + [ANY],
        out_specs=[VMEM] * 3,
        compiler_params=pltpu.CompilerParams(vmem_limit_bytes=12 * MIB),
        cost_estimate=pl.CostEstimate(
            flops=200 * held * resident * rank * width,
            bytes_accessed=2 * resident * rank * width,
            transcendentals=0,
        ),
        name="down",
    )(*got, factors, after)


def up_kernel(peers, mine_ref, *refs):
    got_refs, (mask_ref, up_ref, _, *delta_refs) = refs[:peers], refs[peers:]
    resident, rank, columns = up_ref.shape
    wide = resident * rank
    total = mine_ref[...]
    for ref in got_refs:
        total = total + ref[...].astype(jnp.float32)
    other = pltpu.roll(total, rank, 1)
    first = iota(total.shape, 1) < rank
    both = jnp.concatenate(
        [jnp.where(first, total, other), jnp.where(first, other, total)], axis=0
    )
    both = jnp.concatenate([both] * (wide // LANES), axis=1)
    low = jnp.where(mask_ref[...].astype(jnp.float32) > 0.5, both, 0.0).astype(jnp.bfloat16)
    delta = jnp.dot(
        low, up_ref[...].reshape(wide, columns), preferred_element_type=jnp.float32
    ).astype(jnp.bfloat16)
    size = delta.shape[0] // len(delta_refs)
    for d, ref in enumerate(delta_refs):
        ref[...] = delta[d * size : (d + 1) * size, :]


def up(mine, got, mask, factors, owners, after):
    resident, rank, columns = factors.shape
    held = mask.shape[0]
    return pl.pallas_call(
        functools.partial(up_kernel, len(got)),
        out_shape=[jax.ShapeDtypeStruct((held // owners, columns), jnp.bfloat16)] * owners,
        in_specs=[VMEM] * (len(got) + 3) + [ANY],
        out_specs=[VMEM] * owners,
        compiler_params=pltpu.CompilerParams(vmem_limit_bytes=16 * MIB),
        cost_estimate=pl.CostEstimate(
            flops=200 * held * resident * rank * columns,
            bytes_accessed=2 * resident * rank * columns,
            transcendentals=0,
        ),
        name="up",
    )(mine, *got, mask, factors, after)


def finish_kernel(owners, pick_ref, *refs):
    delta_refs, (*near_refs, base_ref, out_hbm, out_ref, sems) = refs[:owners], refs[owners:]
    width = near_refs[0].shape[1]
    pick = pick_ref[...]
    copies = []
    for n, near_ref in enumerate(near_refs):
        cols = slice(n * width, (n + 1) * width)
        mixed = base_ref[:, cols] + near_ref[...].astype(jnp.float32)
        delta = jnp.concatenate([ref[:, cols] for ref in delta_refs], axis=0)
        mixed = mixed + lax.dot_general(
            pick, delta, (((0,), (0,)), ((), ())), preferred_element_type=jnp.float32
        )
        out_ref[:, :, cols] = mixed.astype(jnp.bfloat16).reshape(*out_ref.shape[:2], width)
        copies.append(
            pltpu.make_async_copy(out_ref.at[:, :, cols], out_hbm.at[:, :, cols], sems.at[n])
        )
        copies[n].start()
    for copy in copies:
        copy.wait()


def finish(base, pick, delta, near, steps):
    tokens, columns = base.shape
    shape = (steps, tokens // steps, columns)
    operands = [pick, *delta, *near, base]
    return pl.pallas_call(
        functools.partial(finish_kernel, len(delta)),
        out_shape=jax.ShapeDtypeStruct(shape, jnp.bfloat16),
        in_specs=[VMEM] * len(operands),
        out_specs=HBM,
        scratch_shapes=[
            pltpu.VMEM(shape, jnp.bfloat16),
            pltpu.SemaphoreType.DMA((len(near),)),
        ],
        compiler_params=pltpu.CompilerParams(vmem_limit_bytes=12 * MIB),
        cost_estimate=pl.CostEstimate(
            flops=2 * tokens * pick.shape[0] * columns,
            bytes_accessed=10 * tokens * columns,
            transcendentals=0,
        ),
        name="finish",
    )(*operands)


def body(
    queries,
    fresh_token_keys,
    fresh_token_values,
    cached_key_rows,
    cached_value_rows,
    cache_live_lengths,
    output_projection_weight,
    adapter_down_factors,
    adapter_up_factors,
    adapter_of_row,
    adapter_storage_slot,
):
    step_count, row_count, _ = queries.shape
    resident = adapter_down_factors.shape[0]
    owners = lax.axis_size("replica")
    tensors = lax.axis_size("tensor")
    capacity = max(2, 2 * row_count // owners)
    columns = adapter_up_factors.shape[2]
    far_sent, far_kept = list(range(3, tensors, 2)), list(range(2, tensors, 2))

    attn, pick, sent = attend_and_pick(
        cache_live_lengths,
        adapter_of_row,
        adapter_storage_slot,
        queries,
        fresh_token_keys,
        fresh_token_values,
        cached_key_rows,
        cached_value_rows,
        owners,
        capacity,
        resident,
    )
    got = exchange_all(sent, "replica")

    weight = output_projection_weight
    *parts, w_here = project(attn, weight, columns, far_sent, bring=far_kept)
    far_got = [xor_exchange(part, "tensor", 1) for part in parts]

    kept = project(
        attn, weight, columns, far_kept, here=w_here, dtype=jnp.float32, after=[parts[0]]
    )
    mine, low_sent, mask = down(got, adapter_down_factors, capacity, step_count, kept[0])
    low_got = [xor_exchange(low_sent, "tensor", d) for d in range(1, tensors)]
    halves_sent = [merge(*pair, low_sent) for pair in zip(kept, far_got, strict=True)]
    others = [xor_exchange(half, "tensor", d) for half, d in zip(halves_sent, far_kept, strict=True)]
    delta = up(mine, low_got, mask, adapter_up_factors, owners, halves_sent[0])
    delta_got = exchange_all(delta, "replica")

    (near,) = project(attn, weight, columns, [1], after=[delta[0]])
    width = columns // PIECES
    near_got = [
        xor_exchange(near[:, n * width : (n + 1) * width], "tensor", 1) for n in range(PIECES)
    ]
    (own,) = project(
        attn, weight, columns, [0], add=others, dtype=jnp.float32, after=[near]
    )
    return finish(own, pick, delta_got, near_got, step_count)


def solution(mesh):
    in_specs = (
        P(None, ("groups", "replica"), "tensor"),
        P(None, ("groups", "replica"), "tensor"),
        P(None, ("groups", "replica"), "tensor"),
        P(("groups", "replica"), None, "tensor"),
        P(("groups", "replica"), None, "tensor"),
        P(("groups", "replica")),
        P("tensor", None),
        P(("groups", "replica"), None, "tensor"),
        P(("groups", "replica"), None, "tensor"),
        P(("groups", "replica")),
        P("groups"),
    )
    out_specs = P(None, ("groups", "replica"), "tensor")
    return jax.shard_map(body, mesh=mesh, in_specs=in_specs, out_specs=out_specs, check_vma=False)
```

```python
import functools
import math

import jax
import jax.numpy as jnp
import numpy as np
from jax import lax
from jax.experimental import pallas as pl
from jax.experimental.pallas import tpu as pltpu
from jax.sharding import PartitionSpec as P

HEAD_WIDTH = 128
LANES = 128
META_ROWS = 16
TILE = 512
TOGETHER = 4
PIECES = 2
MIB = 1024 * 1024
VMEM = pl.BlockSpec(memory_space=pltpu.VMEM)
ANY = pl.BlockSpec(memory_space=pl.ANY)
HBM = pl.BlockSpec(memory_space=pltpu.HBM)


def iota(shape, dim):
    return lax.broadcasted_iota(jnp.int32, shape, dim)


def halves(n):
    if n & (n - 1):
        raise ValueError(n)
    return n.bit_length() - 1


def div(x, n):
    return lax.shift_right_logical(x, jnp.int32(halves(n)))


def mod(x, n):
    return x & ((1 << halves(n)) - 1)


def in_hbm(*arrays):
    return [pltpu.with_memory_space_constraint(a, pltpu.HBM) for a in arrays]


def xor_exchange(value, axis, distance):
    size = lax.axis_size(axis)
    return lax.ppermute(value, axis, [(i, i ^ distance) for i in range(size)])


def partner_order(size):
    return [0, *range(size // 2, size), *range(1, size // 2)]


def exchange_all(blocks, axis):
    order = partner_order(lax.axis_size(axis))
    return [blocks[0]] + [
        xor_exchange(block, axis, distance)
        for block, distance in zip(blocks[1:], order[1:], strict=True)
    ]


def block_copy(w_hbm, dst, sem, distance):
    me = lax.axis_index("tensor")
    columns = dst.shape[-1]
    at = pl.multiple_of(lax.bitwise_xor(me, jnp.int32(distance)) * columns, LANES)
    return pltpu.make_async_copy(w_hbm.at[:, pl.ds(at, columns)], dst, sem)


def attend_kernel(
    owners,
    capacity,
    resident,
    ahead,
    lengths_hbm,
    adapter_hbm,
    slot_hbm,
    q_hbm,
    order_hbm,
    kf_hbm,
    vf_hbm,
    k_hbm,
    v_hbm,
    w_hbm,
    attn_ref,
    pick_ref,
    w_ref,
    *rest,
):
    send_refs, rest = rest[:owners], rest[owners:]
    lengths_ref, adapter_ref, slot_ref, q_ref, kf_ref, vf_ref, k_ref, v_ref = rest[:8]
    order_ref, q_cols_ref, o_ref, sems, small_sems, w_sems = rest[8:]
    steps, rows, width = q_ref.shape
    cache, kv_width = k_ref.shape[1:]
    heads = width // HEAD_WIDTH
    kv_here = kv_width // HEAD_WIDTH
    group = heads // kv_here
    per_row = heads * steps
    total = rows * per_row
    tokens = steps * rows
    chunks = sems.shape[1]
    chunk_rows = rows // chunks
    scale = 1.0 / math.sqrt(HEAD_WIDTH)

    def kv_copies(c):
        at = pl.ds(c * chunk_rows, chunk_rows)
        return [
            pltpu.make_async_copy(src.at[at], dst.at[at], sems.at[which, c])
            for which, (src, dst) in enumerate([(k_hbm, k_ref), (v_hbm, v_ref)])
        ]

    small = [
        pltpu.make_async_copy(src, dst, small_sems.at[n])
        for n, (src, dst) in enumerate(
            [
                (q_hbm, q_ref),
                (order_hbm, order_ref),
                (kf_hbm, kf_ref),
                (lengths_hbm, lengths_ref),
                (adapter_hbm, adapter_ref),
                (slot_hbm, slot_ref),
                (vf_hbm, vf_ref),
            ]
        )
    ]
    q_copy, order_copy, kf_copy, lengths_copy, adapter_copy, slot_copy, vf_copy = small
    first, *others = [kv_copies(c) for c in range(chunks)]
    for copy in [*small[:2], *first, *small[2:], *sum(others, [])]:
        copy.start()

    adapter_copy.wait()
    slot_copy.wait()
    me = lax.axis_index("replica")
    positions = partner_order(owners)
    row_at = mod(iota((8, tokens), 1), rows)
    row_down = iota((rows, LANES), 0)
    first_slot = jnp.zeros((8, tokens), jnp.int32)
    local_of = jnp.zeros((rows, LANES), jnp.int32)
    firsts = []
    for r in range(rows):
        slot = slot_ref[adapter_ref[r]]
        owner = jnp.int32(0)
        for d in range(1, owners):
            owner = owner + (slot >= d * resident).astype(jnp.int32)
        partner = lax.bitwise_xor(owner, me)
        first = jnp.int32(0)
        for d in range(1, owners):
            first = jnp.where(partner == positions[d], d * capacity, first)
        firsts.append(first)
        first_slot = jnp.where(row_at == r, first, first_slot)
        local_of = jnp.where(row_down == r, slot - owner * resident, local_of)
    place = first_slot
    for r in range(rows - 1):
        place = place + ((first_slot == firsts[r]) & (row_at > r)).astype(jnp.int32)
    held = owners * capacity * steps
    slot_at = iota((held, tokens), 0)
    token_at = iota((held, tokens), 1)
    pick = (
        (jnp.concatenate([place] * (held // 8), axis=0) == div(slot_at, steps))
        & (mod(slot_at, steps) == div(token_at, rows))
    ).astype(jnp.bfloat16)
    pick_ref[...] = pick
    local_hot = (local_of == iota((rows, LANES), 1)).astype(jnp.bfloat16)
    entry = iota((owners * META_ROWS, rows), 0)
    entry_place = mod(entry, META_ROWS)
    entry_slot = div(entry, META_ROWS) * capacity + entry_place
    entry_pick = (
        (jnp.concatenate([place[:, :rows]] * (owners * META_ROWS // 8), axis=0) == entry_slot)
        & (entry_place < capacity)
    ).astype(jnp.bfloat16)
    meta = jnp.dot(entry_pick, local_hot, preferred_element_type=jnp.float32)

    q_copy.wait()
    by_head = jnp.concatenate(
        [
            q_ref[:, :, h * HEAD_WIDTH : (h + 1) * HEAD_WIDTH].reshape(tokens, HEAD_WIDTH)
            for h in range(heads)
        ],
        axis=0,
    )
    order_copy.wait()
    q_cols_ref[...] = jnp.dot(
        by_head.astype(jnp.float32).T.astype(jnp.bfloat16),
        order_ref[...],
        preferred_element_type=jnp.float32,
    )
    lane = iota((HEAD_WIDTH, LANES), 1)
    row_of = div(lane, per_row)
    kv_of = mod(div(lane, steps * group), kv_here)

    kf_copy.wait()
    kf = kf_ref[...].reshape(tokens, kv_width)
    token, query = iota((tokens, LANES), 0), iota((tokens, LANES), 1)
    position = iota((cache, LANES), 0)

    def scores(c):
        cols = q_cols_ref[:, pl.ds(pl.multiple_of(c * LANES, LANES), LANES)]
        by_kv = [jnp.where(kv_of == g, cols, 0.0) for g in range(kv_here)]
        fresh = jnp.dot(
            kf,
            jnp.concatenate(by_kv, axis=0).astype(jnp.bfloat16),
            preferred_element_type=jnp.float32,
        )
        live = (mod(token, rows) == div(query, per_row) + c * chunk_rows) & (
            div(token, rows) <= mod(query, steps)
        )
        fresh = jnp.where(live, fresh * scale, -jnp.inf)
        weights = jnp.concatenate(
            [jnp.where(row_of == j, q, 0.0) for j in range(chunk_rows) for q in by_kv], axis=0
        ).astype(jnp.bfloat16)
        keys = jnp.concatenate([k_ref[c * chunk_rows + j] for j in range(chunk_rows)], axis=1)
        cached = jnp.dot(keys, weights, preferred_element_type=jnp.float32)
        return cached * scale, fresh

    def softmax(c, cached, fresh):
        length = jnp.zeros((1, LANES), jnp.int32)
        for j in range(chunk_rows):
            length = jnp.where(
                div(iota((1, LANES), 1), per_row) == j, lengths_ref[c * chunk_rows + j], length
            )
        cached = jnp.where(position < length, cached, -jnp.inf)
        top = jnp.maximum(
            jnp.max(cached, axis=0, keepdims=True), jnp.max(fresh, axis=0, keepdims=True)
        )
        wc, wf = jnp.exp(cached - top), jnp.exp(fresh - top)
        share = 1.0 / (
            jnp.sum(wc, axis=0, keepdims=True) + jnp.sum(wf, axis=0, keepdims=True)
        )
        return (wc * share).T.astype(jnp.bfloat16), (wf * share).T.astype(jnp.bfloat16)

    kv_down = mod(div(iota((LANES, HEAD_WIDTH), 0), steps * group), kv_here)

    def values(c, cached, fresh):
        out = jnp.concatenate(
            [
                jnp.dot(
                    cached[j * per_row : (j + 1) * per_row, :],
                    v_ref[c * chunk_rows + j],
                    preferred_element_type=jnp.float32,
                )
                for j in range(chunk_rows)
            ],
            axis=0,
        ) + jnp.dot(fresh, vf, preferred_element_type=jnp.float32)
        own = out[:, :HEAD_WIDTH]
        for g in range(1, kv_here):
            own = jnp.where(kv_down == g, out[:, g * HEAD_WIDTH : (g + 1) * HEAD_WIDTH], own)
        return own.astype(jnp.bfloat16)

    lengths_copy.wait()
    vf_copy.wait()
    vf = vf_ref[...].reshape(tokens, kv_width)

    w_copies = [block_copy(w_hbm, w_ref.at[n], w_sems.at[n], d) for n, d in enumerate(ahead)]
    for copy in w_copies:
        copy.start()
    together = min(TOGETHER, chunks)

    @pl.loop(0, chunks // together)
    def _(i):
        groups = [i * together + n for n in range(together)]
        for c in groups:
            for copy in kv_copies(c):
                copy.wait()

        scored = [scores(c) for c in groups]
        probs = [softmax(c, *part) for c, part in zip(groups, scored, strict=True)]
        for c, part in zip(groups, probs, strict=True):
            o_ref[pl.ds(pl.multiple_of(c * LANES, LANES), LANES), :] = values(c, *part)

    out = jnp.dot(
        order_ref[...], o_ref[...], preferred_element_type=jnp.float32
    ).astype(jnp.bfloat16)
    attn = jnp.concatenate(
        [out[h * tokens : (h + 1) * tokens, :] for h in range(heads)], axis=1
    )
    attn_ref[...] = attn
    sent = jnp.dot(pick, attn, preferred_element_type=jnp.float32)
    size = capacity * steps
    for d in range(owners):
        mine = sent[d * size : (d + 1) * size, :]
        send_refs[d][...] = jnp.concatenate(
            [mine[:, h * HEAD_WIDTH : (h + 1) * HEAD_WIDTH] for h in range(heads)]
            + [meta[d * META_ROWS : (d + 1) * META_ROWS, :]],
            axis=0,
        ).astype(jnp.bfloat16)
    for copy in w_copies:
        copy.wait()


def row_order(heads, steps, rows):
    head, step, row = np.indices((heads, steps, rows)).reshape(3, -1)
    return np.eye(heads * steps * rows)[(row * heads + head) * steps + step]


def attend_and_pick(
    lengths,
    adapter_of_row,
    storage_slot,
    queries,
    fresh_keys,
    fresh_values,
    cached_keys,
    cached_values,
    weight,
    owners,
    capacity,
    resident,
    columns,
    ahead,
):
    steps, rows, width = queries.shape
    cache, kv_width = cached_keys.shape[1:]
    heads = width // HEAD_WIDTH
    total = rows * heads * steps
    tokens = steps * rows
    size = capacity * steps
    chunks = total // LANES
    outs = pl.pallas_call(
        functools.partial(attend_kernel, owners, capacity, resident, ahead),
        out_shape=[
            jax.ShapeDtypeStruct((tokens, width), jnp.bfloat16),
            jax.ShapeDtypeStruct((owners * size, tokens), jnp.bfloat16),
            pltpu.VMEM((len(ahead), width, columns), jnp.bfloat16),
        ]
        + [jax.ShapeDtypeStruct((heads * size + META_ROWS, HEAD_WIDTH), jnp.bfloat16)] * owners,
        in_specs=[HBM] * 10,
        out_specs=[VMEM] * (3 + owners),
        scratch_shapes=[
            pltpu.SMEM(lengths.shape, jnp.int32),
            pltpu.SMEM(adapter_of_row.shape, jnp.int32),
            pltpu.SMEM(storage_slot.shape, jnp.int32),
            pltpu.VMEM(queries.shape, jnp.bfloat16),
            pltpu.VMEM(fresh_keys.shape, jnp.bfloat16),
            pltpu.VMEM(fresh_values.shape, jnp.bfloat16),
            pltpu.VMEM((rows, cache, kv_width), jnp.bfloat16),
            pltpu.VMEM((rows, cache, kv_width), jnp.bfloat16),
            pltpu.VMEM((total, total), jnp.bfloat16),
            pltpu.VMEM((HEAD_WIDTH, total), jnp.float32),
            pltpu.VMEM((total, HEAD_WIDTH), jnp.bfloat16),
            pltpu.SemaphoreType.DMA((2, chunks)),
            pltpu.SemaphoreType.DMA((7,)),
            pltpu.SemaphoreType.DMA((len(ahead),)),
        ],
        compiler_params=pltpu.CompilerParams(vmem_limit_bytes=24 * MIB),
        cost_estimate=pl.CostEstimate(
            flops=8 * total * cache * kv_width,
            bytes_accessed=4 * rows * cache * kv_width,
            transcendentals=total * cache,
        ),
        name="attend",
    )(
        *in_hbm(
            lengths,
            adapter_of_row,
            storage_slot,
            queries,
            jnp.asarray(row_order(heads, steps, rows), jnp.bfloat16),
            fresh_keys,
            fresh_values,
            cached_keys,
            cached_values,
            weight,
        ),
    )
    return outs[0], outs[1], outs[2], outs[3:]


def project_kernel(blocks, here, bring, added, attn_ref, w_hbm, *refs):
    here_ref = refs[0] if here else None
    add_refs = refs[bool(here) :][:added]
    refs = refs[len(refs) - len(blocks) - bool(bring) - 2 :]
    outs, w_ref, sems = refs[: len(blocks)], refs[-2], refs[-1]
    fetched = blocks[here:]
    copies = [
        block_copy(w_hbm, w_ref.at[n], sems.at[n], d) for n, d in enumerate(fetched)
    ] + [
        block_copy(w_hbm, refs[len(blocks)].at[n], sems.at[len(fetched) + n], d)
        for n, d in enumerate(bring)
    ]
    for copy in copies:
        copy.start()
    attn = attn_ref[...]
    for n in range(len(blocks)):
        if n >= here:
            copies[n - here].wait()
        block = here_ref.at[n] if n < here else w_ref.at[n - here]

        @pl.loop(0, block.shape[-1] // TILE)
        def _(i, n=n, block=block, out_ref=outs[n]):
            cols = pl.ds(pl.multiple_of(i * TILE, TILE), TILE)
            out = jnp.dot(attn, block[:, cols], preferred_element_type=jnp.float32)
            for add_ref in add_refs[n :: len(blocks)]:
                out = out + add_ref[:, cols].astype(jnp.float32)
            out_ref[:, cols] = out.astype(out_ref.dtype)

    for copy in copies[len(fetched) :]:
        copy.wait()


def project(attn, weight, columns, blocks, here=None, bring=(), add=(), dtype=jnp.bfloat16, after=()):
    tokens, width = attn.shape
    held = 0 if here is None else here.shape[0]
    fetched = len(blocks) - held
    extra = [*([here] if held else []), *add]
    outs = [jax.ShapeDtypeStruct((tokens, columns), dtype)] * len(blocks)
    if bring:
        outs.append(pltpu.VMEM((len(bring), width, columns), jnp.bfloat16))
    return pl.pallas_call(
        functools.partial(project_kernel, blocks, held, bring, len(add)),
        out_shape=outs,
        in_specs=[VMEM, HBM] + [VMEM] * len(extra) + [ANY] * len(after),
        out_specs=[VMEM] * len(outs),
        scratch_shapes=[
            pltpu.VMEM((max(fetched, 1), width if fetched else 16, columns), jnp.bfloat16),
            pltpu.SemaphoreType.DMA((fetched + len(bring),)),
        ],
        compiler_params=pltpu.CompilerParams(vmem_limit_bytes=16 * MIB),
        cost_estimate=pl.CostEstimate(
            flops=2 * tokens * width * columns * len(blocks),
            bytes_accessed=2 * width * columns * len(blocks),
            transcendentals=0,
        ),
        name="project",
    )(attn, *in_hbm(weight), *extra, *after)


def merge_kernel(mine_ref, got_ref, _, out_ref):
    out_ref[...] = (mine_ref[...] + got_ref[...].astype(jnp.float32)).astype(jnp.bfloat16)


def merge(mine, got, after):
    return pl.pallas_call(
        merge_kernel,
        out_shape=jax.ShapeDtypeStruct(mine.shape, jnp.bfloat16),
        in_specs=[VMEM, VMEM, ANY],
        out_specs=VMEM,
        compiler_params=pltpu.CompilerParams(vmem_limit_bytes=4 * MIB),
        name="merge",
    )(mine, got, after)


def down_kernel(capacity, steps, *refs):
    (*got_refs, down_ref, _, mine_ref, sent_ref, mask_ref) = refs
    resident, rank, width = down_ref.shape
    wide = resident * rank
    heads = width // HEAD_WIDTH
    size = capacity * steps
    held = size * len(got_refs)
    got = [ref[...].astype(jnp.float32) for ref in got_refs]
    rows = jnp.concatenate(
        [
            jnp.concatenate([part[h * size : (h + 1) * size, :] for part in got], axis=0)
            for h in range(heads)
        ],
        axis=1,
    ).astype(jnp.bfloat16)
    meta = jnp.concatenate([part[heads * size :, :] for part in got], axis=0)
    spread = div(iota((LANES, wide), 1), rank) == iota((LANES, wide), 0)
    entries = meta.shape[0]
    slot, entry = iota((held, entries), 0), iota((held, entries), 1)
    of_slot = entry == div(slot, size) * META_ROWS + div(mod(slot, size), steps)
    local = jnp.dot(
        of_slot.astype(jnp.bfloat16),
        meta.astype(jnp.bfloat16),
        preferred_element_type=jnp.float32,
    )
    mask = jnp.dot(
        local.astype(jnp.bfloat16),
        spread.astype(jnp.bfloat16),
        preferred_element_type=jnp.float32,
    )
    mask_ref[...] = mask.astype(jnp.bfloat16)
    low = lax.dot_general(
        rows,
        down_ref[...].reshape(wide, width),
        (((1,), (1,)), ((), ())),
        preferred_element_type=jnp.float32,
    )
    low = low * mask
    pair = low[:, :LANES]
    for n in range(1, wide // LANES):
        pair = pair + low[:, n * LANES : (n + 1) * LANES]
    both = pair + pltpu.roll(pair, rank, 1)
    half = held // 2
    packed = jnp.where(iota((half, LANES), 1) < rank, both[:half, :], both[half:, :])
    mine_ref[...] = packed
    sent_ref[...] = packed.astype(jnp.bfloat16)


def down(got, factors, capacity, steps, after):
    resident, rank, width = factors.shape
    held = len(got) * capacity * steps
    return pl.pallas_call(
        functools.partial(down_kernel, capacity, steps),
        out_shape=[
            jax.ShapeDtypeStruct((held // 2, LANES), jnp.float32),
            jax.ShapeDtypeStruct((held // 2, LANES), jnp.bfloat16),
            jax.ShapeDtypeStruct((held, resident * rank), jnp.bfloat16),
        ],
        in_specs=[VMEM] * (len(got) + 1) + [ANY],
        out_specs=[VMEM] * 3,
        compiler_params=pltpu.CompilerParams(vmem_limit_bytes=12 * MIB),
        cost_estimate=pl.CostEstimate(
            flops=200 * held * resident * rank * width,
            bytes_accessed=2 * resident * rank * width,
            transcendentals=0,
        ),
        name="down",
    )(*got, factors, after)


def up_kernel(peers, mine_ref, *refs):
    got_refs, (mask_ref, up_ref, _, *delta_refs) = refs[:peers], refs[peers:]
    resident, rank, columns = up_ref.shape
    wide = resident * rank
    total = mine_ref[...]
    for ref in got_refs:
        total = total + ref[...].astype(jnp.float32)
    other = pltpu.roll(total, rank, 1)
    first = iota(total.shape, 1) < rank
    both = jnp.concatenate(
        [jnp.where(first, total, other), jnp.where(first, other, total)], axis=0
    )
    both = jnp.concatenate([both] * (wide // LANES), axis=1)
    low = jnp.where(mask_ref[...].astype(jnp.float32) > 0.5, both, 0.0).astype(jnp.bfloat16)
    delta = jnp.dot(
        low, up_ref[...].reshape(wide, columns), preferred_element_type=jnp.float32
    ).astype(jnp.bfloat16)
    size = delta.shape[0] // len(delta_refs)
    for d, ref in enumerate(delta_refs):
        ref[...] = delta[d * size : (d + 1) * size, :]


def up(mine, got, mask, factors, owners, after):
    resident, rank, columns = factors.shape
    held = mask.shape[0]
    return pl.pallas_call(
        functools.partial(up_kernel, len(got)),
        out_shape=[jax.ShapeDtypeStruct((held // owners, columns), jnp.bfloat16)] * owners,
        in_specs=[VMEM] * (len(got) + 3) + [ANY],
        out_specs=[VMEM] * owners,
        compiler_params=pltpu.CompilerParams(vmem_limit_bytes=16 * MIB),
        cost_estimate=pl.CostEstimate(
            flops=200 * held * resident * rank * columns,
            bytes_accessed=2 * resident * rank * columns,
            transcendentals=0,
        ),
        name="up",
    )(mine, *got, mask, factors, after)


def finish_kernel(owners, pick_ref, *refs):
    delta_refs, (*near_refs, base_ref, out_hbm, out_ref, sems) = refs[:owners], refs[owners:]
    width = near_refs[0].shape[1]
    pick = pick_ref[...]
    copies = []
    for n, near_ref in enumerate(near_refs):
        cols = slice(n * width, (n + 1) * width)
        mixed = base_ref[:, cols] + near_ref[...].astype(jnp.float32)
        delta = jnp.concatenate([ref[:, cols] for ref in delta_refs], axis=0)
        mixed = mixed + lax.dot_general(
            pick, delta, (((0,), (0,)), ((), ())), preferred_element_type=jnp.float32
        )
        out_ref[:, :, cols] = mixed.astype(jnp.bfloat16).reshape(*out_ref.shape[:2], width)
        copies.append(
            pltpu.make_async_copy(out_ref.at[:, :, cols], out_hbm.at[:, :, cols], sems.at[n])
        )
        copies[n].start()
    for copy in copies:
        copy.wait()


def finish(base, pick, delta, near, steps):
    tokens, columns = base.shape
    shape = (steps, tokens // steps, columns)
    operands = [pick, *delta, *near, base]
    return pl.pallas_call(
        functools.partial(finish_kernel, len(delta)),
        out_shape=jax.ShapeDtypeStruct(shape, jnp.bfloat16),
        in_specs=[VMEM] * len(operands),
        out_specs=HBM,
        scratch_shapes=[
            pltpu.VMEM(shape, jnp.bfloat16),
            pltpu.SemaphoreType.DMA((len(near),)),
        ],
        compiler_params=pltpu.CompilerParams(vmem_limit_bytes=12 * MIB),
        cost_estimate=pl.CostEstimate(
            flops=2 * tokens * pick.shape[0] * columns,
            bytes_accessed=10 * tokens * columns,
            transcendentals=0,
        ),
        name="finish",
    )(*operands)


def body(
    queries,
    fresh_token_keys,
    fresh_token_values,
    cached_key_rows,
    cached_value_rows,
    cache_live_lengths,
    output_projection_weight,
    adapter_down_factors,
    adapter_up_factors,
    adapter_of_row,
    adapter_storage_slot,
):
    step_count, row_count, _ = queries.shape
    resident = adapter_down_factors.shape[0]
    owners = lax.axis_size("replica")
    tensors = lax.axis_size("tensor")
    capacity = max(2, 2 * row_count // owners)
    columns = adapter_up_factors.shape[2]
    far_sent, far_kept = list(range(3, tensors, 2)), list(range(2, tensors, 2))

    attn, pick, w_here, sent = attend_and_pick(
        cache_live_lengths,
        adapter_of_row,
        adapter_storage_slot,
        queries,
        fresh_token_keys,
        fresh_token_values,
        cached_key_rows,
        cached_value_rows,
        output_projection_weight,
        owners,
        capacity,
        resident,
        columns,
        far_sent,
    )
    got = exchange_all(sent, "replica")

    weight = output_projection_weight
    *parts, w_here = project(attn, weight, columns, far_sent, here=w_here, bring=far_kept)
    far_got = [xor_exchange(part, "tensor", 1) for part in parts]

    kept = project(
        attn, weight, columns, far_kept, here=w_here, dtype=jnp.float32, after=[parts[0]]
    )
    mine, low_sent, mask = down(got, adapter_down_factors, capacity, step_count, kept[0])
    low_got = [xor_exchange(low_sent, "tensor", d) for d in range(1, tensors)]
    halves_sent = [merge(*pair, low_sent) for pair in zip(kept, far_got, strict=True)]
    others = [xor_exchange(half, "tensor", d) for half, d in zip(halves_sent, far_kept, strict=True)]
    delta = up(mine, low_got, mask, adapter_up_factors, owners, halves_sent[0])
    delta_got = exchange_all(delta, "replica")

    (near,) = project(attn, weight, columns, [1], after=[delta[0]])
    width = columns // PIECES
    near_got = [
        xor_exchange(near[:, n * width : (n + 1) * width], "tensor", 1) for n in range(PIECES)
    ]
    (own,) = project(
        attn, weight, columns, [0], add=others, dtype=jnp.float32, after=[near]
    )
    return finish(own, pick, delta_got, near_got, step_count)


def solution(mesh):
    in_specs = (
        P(None, ("groups", "replica"), "tensor"),
        P(None, ("groups", "replica"), "tensor"),
        P(None, ("groups", "replica"), "tensor"),
        P(("groups", "replica"), None, "tensor"),
        P(("groups", "replica"), None, "tensor"),
        P(("groups", "replica")),
        P("tensor", None),
        P(("groups", "replica"), None, "tensor"),
        P(("groups", "replica"), None, "tensor"),
        P(("groups", "replica")),
        P("groups"),
    )
    out_specs = P(None, ("groups", "replica"), "tensor")
    return jax.shard_map(body, mesh=mesh, in_specs=in_specs, out_specs=out_specs, check_vma=False)
```

```python
import functools
import math

import jax
import jax.numpy as jnp
import numpy as np
from jax import lax
from jax.experimental import pallas as pl
from jax.experimental.pallas import tpu as pltpu
from jax.sharding import PartitionSpec as P

HEAD_WIDTH = 128
LANES = 128
META_ROWS = 16
TILE = 512
TOGETHER = 2
PIECES = 2
MIB = 1024 * 1024
VMEM = pl.BlockSpec(memory_space=pltpu.VMEM)
ANY = pl.BlockSpec(memory_space=pl.ANY)
HBM = pl.BlockSpec(memory_space=pltpu.HBM)


def iota(shape, dim):
    return lax.broadcasted_iota(jnp.int32, shape, dim)


def halves(n):
    if n & (n - 1):
        raise ValueError(n)
    return n.bit_length() - 1


def div(x, n):
    return lax.shift_right_logical(x, jnp.int32(halves(n)))


def mod(x, n):
    return x & ((1 << halves(n)) - 1)


def in_hbm(*arrays):
    return [pltpu.with_memory_space_constraint(a, pltpu.HBM) for a in arrays]


def xor_exchange(value, axis, distance):
    size = lax.axis_size(axis)
    return lax.ppermute(value, axis, [(i, i ^ distance) for i in range(size)])


def partner_order(size):
    return [0, *range(size // 2, size), *range(1, size // 2)]


def exchange_all(blocks, axis):
    order = partner_order(lax.axis_size(axis))
    return [blocks[0]] + [
        xor_exchange(block, axis, distance)
        for block, distance in zip(blocks[1:], order[1:], strict=True)
    ]


def block_copy(w_hbm, dst, sem, distance):
    me = lax.axis_index("tensor")
    columns = dst.shape[-1]
    at = pl.multiple_of(lax.bitwise_xor(me, jnp.int32(distance)) * columns, LANES)
    return pltpu.make_async_copy(w_hbm.at[:, pl.ds(at, columns)], dst, sem)


def attend_kernel(
    owners,
    capacity,
    resident,
    lengths_hbm,
    adapter_hbm,
    slot_hbm,
    q_hbm,
    order_hbm,
    kf_hbm,
    vf_hbm,
    k_hbm,
    v_hbm,
    attn_ref,
    pick_ref,
    *rest,
):
    send_refs, rest = rest[:owners], rest[owners:]
    lengths_ref, adapter_ref, slot_ref, q_ref, kf_ref, vf_ref, k_ref, v_ref = rest[:8]
    order_ref, q_cols_ref, o_ref, sems, small_sems = rest[8:]
    steps, rows, width = q_ref.shape
    cache, kv_width = k_ref.shape[1:]
    heads = width // HEAD_WIDTH
    kv_here = kv_width // HEAD_WIDTH
    group = heads // kv_here
    per_row = heads * steps
    total = rows * per_row
    tokens = steps * rows
    chunks = sems.shape[1]
    chunk_rows = rows // chunks
    scale = 1.0 / math.sqrt(HEAD_WIDTH)

    def kv_copies(c):
        at = pl.ds(c * chunk_rows, chunk_rows)
        return [
            pltpu.make_async_copy(src.at[at], dst.at[at], sems.at[which, c])
            for which, (src, dst) in enumerate([(k_hbm, k_ref), (v_hbm, v_ref)])
        ]

    small = [
        pltpu.make_async_copy(src, dst, small_sems.at[n])
        for n, (src, dst) in enumerate(
            [
                (q_hbm, q_ref),
                (order_hbm, order_ref),
                (kf_hbm, kf_ref),
                (lengths_hbm, lengths_ref),
                (adapter_hbm, adapter_ref),
                (slot_hbm, slot_ref),
                (vf_hbm, vf_ref),
            ]
        )
    ]
    q_copy, order_copy, kf_copy, lengths_copy, adapter_copy, slot_copy, vf_copy = small
    first, *others = [kv_copies(c) for c in range(chunks)]
    for copy in [*small[:2], *first, *small[2:], *sum(others, [])]:
        copy.start()

    adapter_copy.wait()
    slot_copy.wait()
    me = lax.axis_index("replica")
    positions = partner_order(owners)
    row_at = mod(iota((8, tokens), 1), rows)
    row_down = iota((rows, LANES), 0)
    first_slot = jnp.zeros((8, tokens), jnp.int32)
    local_of = jnp.zeros((rows, LANES), jnp.int32)
    firsts = []
    for r in range(rows):
        slot = slot_ref[adapter_ref[r]]
        owner = jnp.int32(0)
        for d in range(1, owners):
            owner = owner + (slot >= d * resident).astype(jnp.int32)
        partner = lax.bitwise_xor(owner, me)
        first = jnp.int32(0)
        for d in range(1, owners):
            first = jnp.where(partner == positions[d], d * capacity, first)
        firsts.append(first)
        first_slot = jnp.where(row_at == r, first, first_slot)
        local_of = jnp.where(row_down == r, slot - owner * resident, local_of)
    place = first_slot
    for r in range(rows - 1):
        place = place + ((first_slot == firsts[r]) & (row_at > r)).astype(jnp.int32)
    held = owners * capacity * steps
    slot_at = iota((held, tokens), 0)
    token_at = iota((held, tokens), 1)
    pick = (
        (jnp.concatenate([place] * (held // 8), axis=0) == div(slot_at, steps))
        & (mod(slot_at, steps) == div(token_at, rows))
    ).astype(jnp.bfloat16)
    pick_ref[...] = pick
    local_hot = (local_of == iota((rows, LANES), 1)).astype(jnp.bfloat16)
    entry = iota((owners * META_ROWS, rows), 0)
    entry_place = mod(entry, META_ROWS)
    entry_slot = div(entry, META_ROWS) * capacity + entry_place
    entry_pick = (
        (jnp.concatenate([place[:, :rows]] * (owners * META_ROWS // 8), axis=0) == entry_slot)
        & (entry_place < capacity)
    ).astype(jnp.bfloat16)
    meta = jnp.dot(entry_pick, local_hot, preferred_element_type=jnp.float32)

    q_copy.wait()
    by_head = jnp.concatenate(
        [
            q_ref[:, :, h * HEAD_WIDTH : (h + 1) * HEAD_WIDTH].reshape(tokens, HEAD_WIDTH)
            for h in range(heads)
        ],
        axis=0,
    )
    order_copy.wait()
    q_cols_ref[...] = jnp.dot(
        by_head.astype(jnp.float32).T.astype(jnp.bfloat16),
        order_ref[...],
        preferred_element_type=jnp.float32,
    )
    lane = iota((HEAD_WIDTH, LANES), 1)
    row_of = div(lane, per_row)
    kv_of = mod(div(lane, steps * group), kv_here)

    kf_copy.wait()
    kf = kf_ref[...].reshape(tokens, kv_width)
    token, query = iota((tokens, LANES), 0), iota((tokens, LANES), 1)
    position = iota((cache, LANES), 0)

    def scores(c):
        cols = q_cols_ref[:, pl.ds(pl.multiple_of(c * LANES, LANES), LANES)]
        by_kv = [jnp.where(kv_of == g, cols, 0.0) for g in range(kv_here)]
        fresh = jnp.dot(
            kf,
            jnp.concatenate(by_kv, axis=0).astype(jnp.bfloat16),
            preferred_element_type=jnp.float32,
        )
        live = (mod(token, rows) == div(query, per_row) + c * chunk_rows) & (
            div(token, rows) <= mod(query, steps)
        )
        fresh = jnp.where(live, fresh * scale, -jnp.inf)
        weights = jnp.concatenate(
            [jnp.where(row_of == j, q, 0.0) for j in range(chunk_rows) for q in by_kv], axis=0
        ).astype(jnp.bfloat16)
        keys = jnp.concatenate([k_ref[c * chunk_rows + j] for j in range(chunk_rows)], axis=1)
        cached = jnp.dot(keys, weights, preferred_element_type=jnp.float32)
        return cached * scale, fresh

    def softmax(c, cached, fresh):
        length = jnp.zeros((1, LANES), jnp.int32)
        for j in range(chunk_rows):
            length = jnp.where(
                div(iota((1, LANES), 1), per_row) == j, lengths_ref[c * chunk_rows + j], length
            )
        cached = jnp.where(position < length, cached, -jnp.inf)
        top = jnp.maximum(
            jnp.max(cached, axis=0, keepdims=True), jnp.max(fresh, axis=0, keepdims=True)
        )
        wc, wf = jnp.exp(cached - top), jnp.exp(fresh - top)
        share = 1.0 / (
            jnp.sum(wc, axis=0, keepdims=True) + jnp.sum(wf, axis=0, keepdims=True)
        )
        return (wc * share).T.astype(jnp.bfloat16), (wf * share).T.astype(jnp.bfloat16)

    kv_down = mod(div(iota((LANES, HEAD_WIDTH), 0), steps * group), kv_here)

    def values(c, cached, fresh):
        out = jnp.concatenate(
            [
                jnp.dot(
                    cached[j * per_row : (j + 1) * per_row, :],
                    v_ref[c * chunk_rows + j],
                    preferred_element_type=jnp.float32,
                )
                for j in range(chunk_rows)
            ],
            axis=0,
        ) + jnp.dot(fresh, vf, preferred_element_type=jnp.float32)
        own = out[:, :HEAD_WIDTH]
        for g in range(1, kv_here):
            own = jnp.where(kv_down == g, out[:, g * HEAD_WIDTH : (g + 1) * HEAD_WIDTH], own)
        return own.astype(jnp.bfloat16)

    lengths_copy.wait()
    vf_copy.wait()
    vf = vf_ref[...].reshape(tokens, kv_width)

    together = min(TOGETHER, chunks)

    @pl.loop(0, chunks // together)
    def _(i):
        groups = [i * together + n for n in range(together)]
        for c in groups:
            for copy in kv_copies(c):
                copy.wait()

        scored = [scores(c) for c in groups]
        probs = [softmax(c, *part) for c, part in zip(groups, scored, strict=True)]
        for c, part in zip(groups, probs, strict=True):
            o_ref[pl.ds(pl.multiple_of(c * LANES, LANES), LANES), :] = values(c, *part)

    out = jnp.dot(
        order_ref[...], o_ref[...], preferred_element_type=jnp.float32
    ).astype(jnp.bfloat16)
    attn = jnp.concatenate(
        [out[h * tokens : (h + 1) * tokens, :] for h in range(heads)], axis=1
    )
    attn_ref[...] = attn
    sent = jnp.dot(pick, attn, preferred_element_type=jnp.float32)
    size = capacity * steps
    for d in range(owners):
        mine = sent[d * size : (d + 1) * size, :]
        send_refs[d][...] = jnp.concatenate(
            [mine[:, h * HEAD_WIDTH : (h + 1) * HEAD_WIDTH] for h in range(heads)]
            + [meta[d * META_ROWS : (d + 1) * META_ROWS, :]],
            axis=0,
        ).astype(jnp.bfloat16)


def row_order(heads, steps, rows):
    head, step, row = np.indices((heads, steps, rows)).reshape(3, -1)
    return np.eye(heads * steps * rows)[(row * heads + head) * steps + step]


def attend_and_pick(
    lengths,
    adapter_of_row,
    storage_slot,
    queries,
    fresh_keys,
    fresh_values,
    cached_keys,
    cached_values,
    owners,
    capacity,
    resident,
):
    steps, rows, width = queries.shape
    cache, kv_width = cached_keys.shape[1:]
    heads = width // HEAD_WIDTH
    total = rows * heads * steps
    tokens = steps * rows
    size = capacity * steps
    chunks = total // LANES
    outs = pl.pallas_call(
        functools.partial(attend_kernel, owners, capacity, resident),
        out_shape=[
            jax.ShapeDtypeStruct((tokens, width), jnp.bfloat16),
            jax.ShapeDtypeStruct((owners * size, tokens), jnp.bfloat16),
        ]
        + [jax.ShapeDtypeStruct((heads * size + META_ROWS, HEAD_WIDTH), jnp.bfloat16)] * owners,
        in_specs=[HBM] * 9,
        out_specs=[VMEM] * (2 + owners),
        scratch_shapes=[
            pltpu.SMEM(lengths.shape, jnp.int32),
            pltpu.SMEM(adapter_of_row.shape, jnp.int32),
            pltpu.SMEM(storage_slot.shape, jnp.int32),
            pltpu.VMEM(queries.shape, jnp.bfloat16),
            pltpu.VMEM(fresh_keys.shape, jnp.bfloat16),
            pltpu.VMEM(fresh_values.shape, jnp.bfloat16),
            pltpu.VMEM((rows, cache, kv_width), jnp.bfloat16),
            pltpu.VMEM((rows, cache, kv_width), jnp.bfloat16),
            pltpu.VMEM((total, total), jnp.bfloat16),
            pltpu.VMEM((HEAD_WIDTH, total), jnp.float32),
            pltpu.VMEM((total, HEAD_WIDTH), jnp.bfloat16),
            pltpu.SemaphoreType.DMA((2, chunks)),
            pltpu.SemaphoreType.DMA((7,)),
        ],
        compiler_params=pltpu.CompilerParams(vmem_limit_bytes=24 * MIB),
        cost_estimate=pl.CostEstimate(
            flops=8 * total * cache * kv_width,
            bytes_accessed=4 * rows * cache * kv_width,
            transcendentals=total * cache,
        ),
        name="attend",
    )(
        *in_hbm(
            lengths,
            adapter_of_row,
            storage_slot,
            queries,
            jnp.asarray(row_order(heads, steps, rows), jnp.bfloat16),
            fresh_keys,
            fresh_values,
            cached_keys,
            cached_values,
        ),
    )
    return outs[0], outs[1], outs[2:]


def project_kernel(blocks, here, bring, added, attn_ref, w_hbm, *refs):
    here_ref = refs[0] if here else None
    add_refs = refs[bool(here) :][:added]
    refs = refs[len(refs) - len(blocks) - bool(bring) - 2 :]
    outs, w_ref, sems = refs[: len(blocks)], refs[-2], refs[-1]
    fetched = blocks[here:]
    copies = [
        block_copy(w_hbm, w_ref.at[n], sems.at[n], d) for n, d in enumerate(fetched)
    ] + [
        block_copy(w_hbm, refs[len(blocks)].at[n], sems.at[len(fetched) + n], d)
        for n, d in enumerate(bring)
    ]
    for copy in copies:
        copy.start()
    attn = attn_ref[...]
    for n in range(len(blocks)):
        if n >= here:
            copies[n - here].wait()
        block = here_ref.at[n] if n < here else w_ref.at[n - here]

        @pl.loop(0, block.shape[-1] // TILE)
        def _(i, n=n, block=block, out_ref=outs[n]):
            cols = pl.ds(pl.multiple_of(i * TILE, TILE), TILE)
            out = jnp.dot(attn, block[:, cols], preferred_element_type=jnp.float32)
            for add_ref in add_refs[n :: len(blocks)]:
                out = out + add_ref[:, cols].astype(jnp.float32)
            out_ref[:, cols] = out.astype(out_ref.dtype)

    for copy in copies[len(fetched) :]:
        copy.wait()


def project(attn, weight, columns, blocks, here=None, bring=(), add=(), dtype=jnp.bfloat16, after=()):
    tokens, width = attn.shape
    held = 0 if here is None else here.shape[0]
    fetched = len(blocks) - held
    extra = [*([here] if held else []), *add]
    outs = [jax.ShapeDtypeStruct((tokens, columns), dtype)] * len(blocks)
    if bring:
        outs.append(pltpu.VMEM((len(bring), width, columns), jnp.bfloat16))
    return pl.pallas_call(
        functools.partial(project_kernel, blocks, held, bring, len(add)),
        out_shape=outs,
        in_specs=[VMEM, HBM] + [VMEM] * len(extra) + [ANY] * len(after),
        out_specs=[VMEM] * len(outs),
        scratch_shapes=[
            pltpu.VMEM((max(fetched, 1), width if fetched else 16, columns), jnp.bfloat16),
            pltpu.SemaphoreType.DMA((fetched + len(bring),)),
        ],
        compiler_params=pltpu.CompilerParams(vmem_limit_bytes=16 * MIB),
        cost_estimate=pl.CostEstimate(
            flops=2 * tokens * width * columns * len(blocks),
            bytes_accessed=2 * width * columns * len(blocks),
            transcendentals=0,
        ),
        name="project",
    )(attn, *in_hbm(weight), *extra, *after)


def down_kernel(capacity, steps, *refs):
    (*got_refs, down_ref, _, mine_ref, sent_ref, mask_ref) = refs
    resident, rank, width = down_ref.shape
    wide = resident * rank
    heads = width // HEAD_WIDTH
    size = capacity * steps
    held = size * len(got_refs)
    got = [ref[...].astype(jnp.float32) for ref in got_refs]
    rows = jnp.concatenate(
        [
            jnp.concatenate([part[h * size : (h + 1) * size, :] for part in got], axis=0)
            for h in range(heads)
        ],
        axis=1,
    ).astype(jnp.bfloat16)
    meta = jnp.concatenate([part[heads * size :, :] for part in got], axis=0)
    spread = div(iota((LANES, wide), 1), rank) == iota((LANES, wide), 0)
    entries = meta.shape[0]
    slot, entry = iota((held, entries), 0), iota((held, entries), 1)
    of_slot = entry == div(slot, size) * META_ROWS + div(mod(slot, size), steps)
    local = jnp.dot(
        of_slot.astype(jnp.bfloat16),
        meta.astype(jnp.bfloat16),
        preferred_element_type=jnp.float32,
    )
    mask = jnp.dot(
        local.astype(jnp.bfloat16),
        spread.astype(jnp.bfloat16),
        preferred_element_type=jnp.float32,
    )
    mask_ref[...] = mask.astype(jnp.bfloat16)
    low = lax.dot_general(
        rows,
        down_ref[...].reshape(wide, width),
        (((1,), (1,)), ((), ())),
        preferred_element_type=jnp.float32,
    )
    low = low * mask
    pair = low[:, :LANES]
    for n in range(1, wide // LANES):
        pair = pair + low[:, n * LANES : (n + 1) * LANES]
    both = pair + pltpu.roll(pair, rank, 1)
    half = held // 2
    packed = jnp.where(iota((half, LANES), 1) < rank, both[:half, :], both[half:, :])
    mine_ref[...] = packed
    sent_ref[...] = packed.astype(jnp.bfloat16)


def down(got, factors, capacity, steps, after):
    resident, rank, width = factors.shape
    held = len(got) * capacity * steps
    return pl.pallas_call(
        functools.partial(down_kernel, capacity, steps),
        out_shape=[
            jax.ShapeDtypeStruct((held // 2, LANES), jnp.float32),
            jax.ShapeDtypeStruct((held // 2, LANES), jnp.bfloat16),
            jax.ShapeDtypeStruct((held, resident * rank), jnp.bfloat16),
        ],
        in_specs=[VMEM] * (len(got) + 1) + [ANY],
        out_specs=[VMEM] * 3,
        compiler_params=pltpu.CompilerParams(vmem_limit_bytes=12 * MIB),
        cost_estimate=pl.CostEstimate(
            flops=200 * held * resident * rank * width,
            bytes_accessed=2 * resident * rank * width,
            transcendentals=0,
        ),
        name="down",
    )(*got, factors, after)


def up_kernel(peers, mine_ref, *refs):
    got_refs, (mask_ref, up_ref, _, *delta_refs) = refs[:peers], refs[peers:]
    resident, rank, columns = up_ref.shape
    wide = resident * rank
    total = mine_ref[...]
    for ref in got_refs:
        total = total + ref[...].astype(jnp.float32)
    other = pltpu.roll(total, rank, 1)
    first = iota(total.shape, 1) < rank
    both = jnp.concatenate(
        [jnp.where(first, total, other), jnp.where(first, other, total)], axis=0
    )
    both = jnp.concatenate([both] * (wide // LANES), axis=1)
    low = jnp.where(mask_ref[...].astype(jnp.float32) > 0.5, both, 0.0).astype(jnp.bfloat16)
    delta = jnp.dot(
        low, up_ref[...].reshape(wide, columns), preferred_element_type=jnp.float32
    ).astype(jnp.bfloat16)
    size = delta.shape[0] // len(delta_refs)
    for d, ref in enumerate(delta_refs):
        ref[...] = delta[d * size : (d + 1) * size, :]


def up(mine, got, mask, factors, owners, after):
    resident, rank, columns = factors.shape
    held = mask.shape[0]
    return pl.pallas_call(
        functools.partial(up_kernel, len(got)),
        out_shape=[jax.ShapeDtypeStruct((held // owners, columns), jnp.bfloat16)] * owners,
        in_specs=[VMEM] * (len(got) + 3) + [ANY],
        out_specs=[VMEM] * owners,
        compiler_params=pltpu.CompilerParams(vmem_limit_bytes=16 * MIB),
        cost_estimate=pl.CostEstimate(
            flops=200 * held * resident * rank * columns,
            bytes_accessed=2 * resident * rank * columns,
            transcendentals=0,
        ),
        name="up",
    )(mine, *got, mask, factors, after)


def finish_kernel(owners, pick_ref, *refs):
    delta_refs, (*near_refs, base_ref, out_hbm, out_ref, sems) = refs[:owners], refs[owners:]
    width = near_refs[0].shape[1]
    pick = pick_ref[...]
    copies = []
    for n, near_ref in enumerate(near_refs):
        cols = slice(n * width, (n + 1) * width)
        mixed = base_ref[:, cols] + near_ref[...].astype(jnp.float32)
        delta = jnp.concatenate([ref[:, cols] for ref in delta_refs], axis=0)
        mixed = mixed + lax.dot_general(
            pick, delta, (((0,), (0,)), ((), ())), preferred_element_type=jnp.float32
        )
        out_ref[:, :, cols] = mixed.astype(jnp.bfloat16).reshape(*out_ref.shape[:2], width)
        copies.append(
            pltpu.make_async_copy(out_ref.at[:, :, cols], out_hbm.at[:, :, cols], sems.at[n])
        )
        copies[n].start()
    for copy in copies:
        copy.wait()


def finish(base, pick, delta, near, steps):
    tokens, columns = base.shape
    shape = (steps, tokens // steps, columns)
    operands = [pick, *delta, *near, base]
    return pl.pallas_call(
        functools.partial(finish_kernel, len(delta)),
        out_shape=jax.ShapeDtypeStruct(shape, jnp.bfloat16),
        in_specs=[VMEM] * len(operands),
        out_specs=HBM,
        scratch_shapes=[
            pltpu.VMEM(shape, jnp.bfloat16),
            pltpu.SemaphoreType.DMA((len(near),)),
        ],
        compiler_params=pltpu.CompilerParams(vmem_limit_bytes=12 * MIB),
        cost_estimate=pl.CostEstimate(
            flops=2 * tokens * pick.shape[0] * columns,
            bytes_accessed=10 * tokens * columns,
            transcendentals=0,
        ),
        name="finish",
    )(*operands)


def body(
    queries,
    fresh_token_keys,
    fresh_token_values,
    cached_key_rows,
    cached_value_rows,
    cache_live_lengths,
    output_projection_weight,
    adapter_down_factors,
    adapter_up_factors,
    adapter_of_row,
    adapter_storage_slot,
):
    step_count, row_count, _ = queries.shape
    resident = adapter_down_factors.shape[0]
    owners = lax.axis_size("replica")
    tensors = lax.axis_size("tensor")
    capacity = max(2, 2 * row_count // owners)
    columns = adapter_up_factors.shape[2]
    far_sent, far_kept = list(range(3, tensors, 2)), list(range(2, tensors, 2))

    attn, pick, sent = attend_and_pick(
        cache_live_lengths,
        adapter_of_row,
        adapter_storage_slot,
        queries,
        fresh_token_keys,
        fresh_token_values,
        cached_key_rows,
        cached_value_rows,
        owners,
        capacity,
        resident,
    )
    got = exchange_all(sent, "replica")

    weight = output_projection_weight
    *parts, w_here = project(attn, weight, columns, far_sent, bring=far_kept)
    far_got = [xor_exchange(part, "tensor", 1) for part in parts]

    mine, low_sent, mask = down(got, adapter_down_factors, capacity, step_count, parts[0])
    low_got = [xor_exchange(low_sent, "tensor", d) for d in range(1, tensors)]
    halves_sent = project(
        attn, weight, columns, far_kept, here=w_here, add=far_got, after=[low_sent]
    )
    others = [xor_exchange(half, "tensor", d) for half, d in zip(halves_sent, far_kept, strict=True)]
    delta = up(mine, low_got, mask, adapter_up_factors, owners, halves_sent[0])
    delta_got = exchange_all(delta, "replica")

    (near,) = project(attn, weight, columns, [1], after=[delta[0]])
    width = columns // PIECES
    near_got = [
        xor_exchange(near[:, n * width : (n + 1) * width], "tensor", 1) for n in range(PIECES)
    ]
    (own,) = project(
        attn, weight, columns, [0], add=others, dtype=jnp.float32, after=[near]
    )
    return finish(own, pick, delta_got, near_got, step_count)


def solution(mesh):
    in_specs = (
        P(None, ("groups", "replica"), "tensor"),
        P(None, ("groups", "replica"), "tensor"),
        P(None, ("groups", "replica"), "tensor"),
        P(("groups", "replica"), None, "tensor"),
        P(("groups", "replica"), None, "tensor"),
        P(("groups", "replica")),
        P("tensor", None),
        P(("groups", "replica"), None, "tensor"),
        P(("groups", "replica"), None, "tensor"),
        P(("groups", "replica")),
        P("groups"),
    )
    out_specs = P(None, ("groups", "replica"), "tensor")
    return jax.shard_map(body, mesh=mesh, in_specs=in_specs, out_specs=out_specs, check_vma=False)
```

```python
import functools
import math

import jax
import jax.numpy as jnp
import numpy as np
from jax import lax
from jax.experimental import pallas as pl
from jax.experimental.pallas import tpu as pltpu
from jax.sharding import PartitionSpec as P

HEAD_WIDTH = 128
LANES = 128
META_ROWS = 16
TILE = 512
TOGETHER = 4
PIECES = 2
MIB = 1024 * 1024
VMEM = pl.BlockSpec(memory_space=pltpu.VMEM)
ANY = pl.BlockSpec(memory_space=pl.ANY)
HBM = pl.BlockSpec(memory_space=pltpu.HBM)


def iota(shape, dim):
    return lax.broadcasted_iota(jnp.int32, shape, dim)


def halves(n):
    if n & (n - 1):
        raise ValueError(n)
    return n.bit_length() - 1


def div(x, n):
    return lax.shift_right_logical(x, jnp.int32(halves(n)))


def mod(x, n):
    return x & ((1 << halves(n)) - 1)


def in_hbm(*arrays):
    return [pltpu.with_memory_space_constraint(a, pltpu.HBM) for a in arrays]


def xor_exchange(value, axis, distance):
    size = lax.axis_size(axis)
    return lax.ppermute(value, axis, [(i, i ^ distance) for i in range(size)])


def partner_order(size):
    return [0, *range(size // 2, size), *range(1, size // 2)]


def exchange_all(blocks, axis):
    order = partner_order(lax.axis_size(axis))
    return [blocks[0]] + [
        xor_exchange(block, axis, distance)
        for block, distance in zip(blocks[1:], order[1:], strict=True)
    ]


def block_copy(w_hbm, dst, sem, distance):
    me = lax.axis_index("tensor")
    columns = dst.shape[-1]
    at = pl.multiple_of(lax.bitwise_xor(me, jnp.int32(distance)) * columns, LANES)
    return pltpu.make_async_copy(w_hbm.at[:, pl.ds(at, columns)], dst, sem)


def attend_kernel(
    owners,
    capacity,
    resident,
    lengths_hbm,
    adapter_hbm,
    slot_hbm,
    q_hbm,
    order_hbm,
    kf_hbm,
    vf_hbm,
    k_hbm,
    v_hbm,
    attn_ref,
    pick_ref,
    *rest,
):
    send_refs, rest = rest[:owners], rest[owners:]
    lengths_ref, adapter_ref, slot_ref, q_ref, kf_ref, vf_ref, k_ref, v_ref = rest[:8]
    order_ref, q_cols_ref, o_ref, sems, small_sems = rest[8:]
    steps, rows, width = q_ref.shape
    cache, kv_width = k_ref.shape[1:]
    heads = width // HEAD_WIDTH
    kv_here = kv_width // HEAD_WIDTH
    group = heads // kv_here
    per_row = heads * steps
    total = rows * per_row
    tokens = steps * rows
    chunks = sems.shape[1]
    chunk_rows = rows // chunks
    scale = 1.0 / math.sqrt(HEAD_WIDTH)

    def kv_copies(c):
        at = pl.ds(c * chunk_rows, chunk_rows)
        return [
            pltpu.make_async_copy(src.at[at], dst.at[at], sems.at[which, c])
            for which, (src, dst) in enumerate([(k_hbm, k_ref), (v_hbm, v_ref)])
        ]

    small = [
        pltpu.make_async_copy(src, dst, small_sems.at[n])
        for n, (src, dst) in enumerate(
            [
                (q_hbm, q_ref),
                (order_hbm, order_ref),
                (kf_hbm, kf_ref),
                (lengths_hbm, lengths_ref),
                (adapter_hbm, adapter_ref),
                (slot_hbm, slot_ref),
                (vf_hbm, vf_ref),
            ]
        )
    ]
    q_copy, order_copy, kf_copy, lengths_copy, adapter_copy, slot_copy, vf_copy = small
    first, *others = [kv_copies(c) for c in range(chunks)]
    for copy in [*small[:2], *first, *small[2:], *sum(others, [])]:
        copy.start()

    adapter_copy.wait()
    slot_copy.wait()
    me = lax.axis_index("replica")
    positions = partner_order(owners)
    row_at = mod(iota((8, tokens), 1), rows)
    row_down = iota((rows, LANES), 0)
    first_slot = jnp.zeros((8, tokens), jnp.int32)
    local_of = jnp.zeros((rows, LANES), jnp.int32)
    firsts = []
    for r in range(rows):
        slot = slot_ref[adapter_ref[r]]
        owner = jnp.int32(0)
        for d in range(1, owners):
            owner = owner + (slot >= d * resident).astype(jnp.int32)
        partner = lax.bitwise_xor(owner, me)
        first = jnp.int32(0)
        for d in range(1, owners):
            first = jnp.where(partner == positions[d], d * capacity, first)
        firsts.append(first)
        first_slot = jnp.where(row_at == r, first, first_slot)
        local_of = jnp.where(row_down == r, slot - owner * resident, local_of)
    place = first_slot
    for r in range(rows - 1):
        place = place + ((first_slot == firsts[r]) & (row_at > r)).astype(jnp.int32)
    held = owners * capacity * steps
    slot_at = iota((held, tokens), 0)
    token_at = iota((held, tokens), 1)
    pick = (
        (jnp.concatenate([place] * (held // 8), axis=0) == div(slot_at, steps))
        & (mod(slot_at, steps) == div(token_at, rows))
    ).astype(jnp.bfloat16)
    pick_ref[...] = pick
    local_hot = (local_of == iota((rows, LANES), 1)).astype(jnp.bfloat16)
    entry = iota((owners * META_ROWS, rows), 0)
    entry_place = mod(entry, META_ROWS)
    entry_slot = div(entry, META_ROWS) * capacity + entry_place
    entry_pick = (
        (jnp.concatenate([place[:, :rows]] * (owners * META_ROWS // 8), axis=0) == entry_slot)
        & (entry_place < capacity)
    ).astype(jnp.bfloat16)
    meta = jnp.dot(entry_pick, local_hot, preferred_element_type=jnp.float32)

    q_copy.wait()
    by_head = jnp.concatenate(
        [
            q_ref[:, :, h * HEAD_WIDTH : (h + 1) * HEAD_WIDTH].reshape(tokens, HEAD_WIDTH)
            for h in range(heads)
        ],
        axis=0,
    )
    order_copy.wait()
    q_cols_ref[...] = jnp.dot(
        by_head.astype(jnp.float32).T.astype(jnp.bfloat16),
        order_ref[...],
        preferred_element_type=jnp.float32,
    )
    lane = iota((HEAD_WIDTH, LANES), 1)
    row_of = div(lane, per_row)
    kv_of = mod(div(lane, steps * group), kv_here)

    kf_copy.wait()
    kf = kf_ref[...].reshape(tokens, kv_width)
    token, query = iota((tokens, LANES), 0), iota((tokens, LANES), 1)
    position = iota((cache, LANES), 0)

    def scores(c):
        cols = q_cols_ref[:, pl.ds(pl.multiple_of(c * LANES, LANES), LANES)]
        by_kv = [jnp.where(kv_of == g, cols, 0.0) for g in range(kv_here)]
        fresh = jnp.dot(
            kf,
            jnp.concatenate(by_kv, axis=0).astype(jnp.bfloat16),
            preferred_element_type=jnp.float32,
        )
        live = (mod(token, rows) == div(query, per_row) + c * chunk_rows) & (
            div(token, rows) <= mod(query, steps)
        )
        fresh = jnp.where(live, fresh * scale, -jnp.inf)
        weights = jnp.concatenate(
            [jnp.where(row_of == j, q, 0.0) for j in range(chunk_rows) for q in by_kv], axis=0
        ).astype(jnp.bfloat16)
        keys = jnp.concatenate([k_ref[c * chunk_rows + j] for j in range(chunk_rows)], axis=1)
        cached = jnp.dot(keys, weights, preferred_element_type=jnp.float32)
        return cached * scale, fresh

    def softmax(c, cached, fresh):
        length = jnp.zeros((1, LANES), jnp.int32)
        for j in range(chunk_rows):
            length = jnp.where(
                div(iota((1, LANES), 1), per_row) == j, lengths_ref[c * chunk_rows + j], length
            )
        cached = jnp.where(position < length, cached, -jnp.inf)
        top = jnp.maximum(
            jnp.max(cached, axis=0, keepdims=True), jnp.max(fresh, axis=0, keepdims=True)
        )
        wc, wf = jnp.exp(cached - top), jnp.exp(fresh - top)
        share = 1.0 / (
            jnp.sum(wc, axis=0, keepdims=True) + jnp.sum(wf, axis=0, keepdims=True)
        )
        return (wc * share).T.astype(jnp.bfloat16), (wf * share).T.astype(jnp.bfloat16)

    kv_down = mod(div(iota((LANES, HEAD_WIDTH), 0), steps * group), kv_here)

    def values(c, cached, fresh):
        out = jnp.concatenate(
            [
                jnp.dot(
                    cached[j * per_row : (j + 1) * per_row, :],
                    v_ref[c * chunk_rows + j],
                    preferred_element_type=jnp.float32,
                )
                for j in range(chunk_rows)
            ],
            axis=0,
        ) + jnp.dot(fresh, vf, preferred_element_type=jnp.float32)
        own = out[:, :HEAD_WIDTH]
        for g in range(1, kv_here):
            own = jnp.where(kv_down == g, out[:, g * HEAD_WIDTH : (g + 1) * HEAD_WIDTH], own)
        return own.astype(jnp.bfloat16)

    lengths_copy.wait()
    vf_copy.wait()
    vf = vf_ref[...].reshape(tokens, kv_width)

    together = min(TOGETHER, chunks)

    @pl.loop(0, chunks // together)
    def _(i):
        groups = [i * together + n for n in range(together)]
        for c in groups:
            for copy in kv_copies(c):
                copy.wait()

        scored = [scores(c) for c in groups]
        probs = [softmax(c, *part) for c, part in zip(groups, scored, strict=True)]
        for c, part in zip(groups, probs, strict=True):
            o_ref[pl.ds(pl.multiple_of(c * LANES, LANES), LANES), :] = values(c, *part)

    out = jnp.dot(
        order_ref[...], o_ref[...], preferred_element_type=jnp.float32
    ).astype(jnp.bfloat16)
    attn = jnp.concatenate(
        [out[h * tokens : (h + 1) * tokens, :] for h in range(heads)], axis=1
    )
    attn_ref[...] = attn
    sent = jnp.dot(pick, attn, preferred_element_type=jnp.float32)
    size = capacity * steps
    for d in range(owners):
        mine = sent[d * size : (d + 1) * size, :]
        send_refs[d][...] = jnp.concatenate(
            [mine[:, h * HEAD_WIDTH : (h + 1) * HEAD_WIDTH] for h in range(heads)]
            + [meta[d * META_ROWS : (d + 1) * META_ROWS, :]],
            axis=0,
        ).astype(jnp.bfloat16)


def row_order(heads, steps, rows):
    head, step, row = np.indices((heads, steps, rows)).reshape(3, -1)
    return np.eye(heads * steps * rows)[(row * heads + head) * steps + step]


def attend_and_pick(
    lengths,
    adapter_of_row,
    storage_slot,
    queries,
    fresh_keys,
    fresh_values,
    cached_keys,
    cached_values,
    owners,
    capacity,
    resident,
):
    steps, rows, width = queries.shape
    cache, kv_width = cached_keys.shape[1:]
    heads = width // HEAD_WIDTH
    total = rows * heads * steps
    tokens = steps * rows
    size = capacity * steps
    chunks = total // LANES
    outs = pl.pallas_call(
        functools.partial(attend_kernel, owners, capacity, resident),
        out_shape=[
            jax.ShapeDtypeStruct((tokens, width), jnp.bfloat16),
            jax.ShapeDtypeStruct((owners * size, tokens), jnp.bfloat16),
        ]
        + [jax.ShapeDtypeStruct((heads * size + META_ROWS, HEAD_WIDTH), jnp.bfloat16)] * owners,
        in_specs=[HBM] * 9,
        out_specs=[VMEM] * (2 + owners),
        scratch_shapes=[
            pltpu.SMEM(lengths.shape, jnp.int32),
            pltpu.SMEM(adapter_of_row.shape, jnp.int32),
            pltpu.SMEM(storage_slot.shape, jnp.int32),
            pltpu.VMEM(queries.shape, jnp.bfloat16),
            pltpu.VMEM(fresh_keys.shape, jnp.bfloat16),
            pltpu.VMEM(fresh_values.shape, jnp.bfloat16),
            pltpu.VMEM((rows, cache, kv_width), jnp.bfloat16),
            pltpu.VMEM((rows, cache, kv_width), jnp.bfloat16),
            pltpu.VMEM((total, total), jnp.bfloat16),
            pltpu.VMEM((HEAD_WIDTH, total), jnp.float32),
            pltpu.VMEM((total, HEAD_WIDTH), jnp.bfloat16),
            pltpu.SemaphoreType.DMA((2, chunks)),
            pltpu.SemaphoreType.DMA((7,)),
        ],
        compiler_params=pltpu.CompilerParams(vmem_limit_bytes=24 * MIB),
        cost_estimate=pl.CostEstimate(
            flops=8 * total * cache * kv_width,
            bytes_accessed=4 * rows * cache * kv_width,
            transcendentals=total * cache,
        ),
        name="attend",
    )(
        *in_hbm(
            lengths,
            adapter_of_row,
            storage_slot,
            queries,
            jnp.asarray(row_order(heads, steps, rows), jnp.bfloat16),
            fresh_keys,
            fresh_values,
            cached_keys,
            cached_values,
        ),
    )
    return outs[0], outs[1], outs[2:]


def project_kernel(blocks, here, bring, added, attn_ref, w_hbm, *refs):
    here_ref = refs[0] if here else None
    add_refs = refs[bool(here) :][:added]
    refs = refs[len(refs) - len(blocks) - bool(bring) - 2 :]
    outs, w_ref, sems = refs[: len(blocks)], refs[-2], refs[-1]
    fetched = blocks[here:]
    copies = [
        block_copy(w_hbm, w_ref.at[n], sems.at[n], d) for n, d in enumerate(fetched)
    ] + [
        block_copy(w_hbm, refs[len(blocks)].at[n], sems.at[len(fetched) + n], d)
        for n, d in enumerate(bring)
    ]
    for copy in copies:
        copy.start()
    attn = attn_ref[...]
    for n in range(len(blocks)):
        if n >= here:
            copies[n - here].wait()
        block = here_ref.at[n] if n < here else w_ref.at[n - here]

        @pl.loop(0, block.shape[-1] // TILE)
        def _(i, n=n, block=block, out_ref=outs[n]):
            cols = pl.ds(pl.multiple_of(i * TILE, TILE), TILE)
            out = jnp.dot(attn, block[:, cols], preferred_element_type=jnp.float32)
            for add_ref in add_refs[n :: len(blocks)]:
                out = out + add_ref[:, cols].astype(jnp.float32)
            out_ref[:, cols] = out.astype(out_ref.dtype)

    for copy in copies[len(fetched) :]:
        copy.wait()


def project(attn, weight, columns, blocks, here=None, bring=(), add=(), dtype=jnp.bfloat16, after=()):
    tokens, width = attn.shape
    held = 0 if here is None else here.shape[0]
    fetched = len(blocks) - held
    extra = [*([here] if held else []), *add]
    outs = [jax.ShapeDtypeStruct((tokens, columns), dtype)] * len(blocks)
    if bring:
        outs.append(pltpu.VMEM((len(bring), width, columns), jnp.bfloat16))
    return pl.pallas_call(
        functools.partial(project_kernel, blocks, held, bring, len(add)),
        out_shape=outs,
        in_specs=[VMEM, HBM] + [VMEM] * len(extra) + [ANY] * len(after),
        out_specs=[VMEM] * len(outs),
        scratch_shapes=[
            pltpu.VMEM((max(fetched, 1), width if fetched else 16, columns), jnp.bfloat16),
            pltpu.SemaphoreType.DMA((fetched + len(bring),)),
        ],
        compiler_params=pltpu.CompilerParams(vmem_limit_bytes=16 * MIB),
        cost_estimate=pl.CostEstimate(
            flops=2 * tokens * width * columns * len(blocks),
            bytes_accessed=2 * width * columns * len(blocks),
            transcendentals=0,
        ),
        name="project",
    )(attn, *in_hbm(weight), *extra, *after)


def merge_kernel(mine_ref, got_ref, _, out_ref):
    out_ref[...] = (mine_ref[...] + got_ref[...].astype(jnp.float32)).astype(jnp.bfloat16)


def merge(mine, got, after):
    return pl.pallas_call(
        merge_kernel,
        out_shape=jax.ShapeDtypeStruct(mine.shape, jnp.bfloat16),
        in_specs=[VMEM, VMEM, ANY],
        out_specs=VMEM,
        compiler_params=pltpu.CompilerParams(vmem_limit_bytes=4 * MIB),
        name="merge",
    )(mine, got, after)


def down_kernel(capacity, steps, *refs):
    (*got_refs, down_ref, _, mine_ref, sent_ref, mask_ref) = refs
    resident, rank, width = down_ref.shape
    wide = resident * rank
    heads = width // HEAD_WIDTH
    size = capacity * steps
    held = size * len(got_refs)
    got = [ref[...].astype(jnp.float32) for ref in got_refs]
    rows = jnp.concatenate(
        [
            jnp.concatenate([part[h * size : (h + 1) * size, :] for part in got], axis=0)
            for h in range(heads)
        ],
        axis=1,
    ).astype(jnp.bfloat16)
    meta = jnp.concatenate([part[heads * size :, :] for part in got], axis=0)
    spread = div(iota((LANES, wide), 1), rank) == iota((LANES, wide), 0)
    entries = meta.shape[0]
    slot, entry = iota((held, entries), 0), iota((held, entries), 1)
    of_slot = entry == div(slot, size) * META_ROWS + div(mod(slot, size), steps)
    local = jnp.dot(
        of_slot.astype(jnp.bfloat16),
        meta.astype(jnp.bfloat16),
        preferred_element_type=jnp.float32,
    )
    mask = jnp.dot(
        local.astype(jnp.bfloat16),
        spread.astype(jnp.bfloat16),
        preferred_element_type=jnp.float32,
    )
    mask_ref[...] = mask.astype(jnp.bfloat16)
    low = lax.dot_general(
        rows,
        down_ref[...].reshape(wide, width),
        (((1,), (1,)), ((), ())),
        preferred_element_type=jnp.float32,
    )
    low = low * mask
    pair = low[:, :LANES]
    for n in range(1, wide // LANES):
        pair = pair + low[:, n * LANES : (n + 1) * LANES]
    both = pair + pltpu.roll(pair, rank, 1)
    half = held // 2
    packed = jnp.where(iota((half, LANES), 1) < rank, both[:half, :], both[half:, :])
    mine_ref[...] = packed
    sent_ref[...] = packed.astype(jnp.bfloat16)


def down(got, factors, capacity, steps, after):
    resident, rank, width = factors.shape
    held = len(got) * capacity * steps
    return pl.pallas_call(
        functools.partial(down_kernel, capacity, steps),
        out_shape=[
            jax.ShapeDtypeStruct((held // 2, LANES), jnp.float32),
            jax.ShapeDtypeStruct((held // 2, LANES), jnp.bfloat16),
            jax.ShapeDtypeStruct((held, resident * rank), jnp.bfloat16),
        ],
        in_specs=[VMEM] * (len(got) + 1) + [ANY],
        out_specs=[VMEM] * 3,
        compiler_params=pltpu.CompilerParams(vmem_limit_bytes=12 * MIB),
        cost_estimate=pl.CostEstimate(
            flops=200 * held * resident * rank * width,
            bytes_accessed=2 * resident * rank * width,
            transcendentals=0,
        ),
        name="down",
    )(*got, factors, after)


def up_kernel(peers, mine_ref, *refs):
    got_refs, (mask_ref, up_ref, _, *delta_refs) = refs[:peers], refs[peers:]
    resident, rank, columns = up_ref.shape
    wide = resident * rank
    total = mine_ref[...]
    for ref in got_refs:
        total = total + ref[...].astype(jnp.float32)
    other = pltpu.roll(total, rank, 1)
    first = iota(total.shape, 1) < rank
    both = jnp.concatenate(
        [jnp.where(first, total, other), jnp.where(first, other, total)], axis=0
    )
    both = jnp.concatenate([both] * (wide // LANES), axis=1)
    low = jnp.where(mask_ref[...].astype(jnp.float32) > 0.5, both, 0.0).astype(jnp.bfloat16)
    delta = jnp.dot(
        low, up_ref[...].reshape(wide, columns), preferred_element_type=jnp.float32
    ).astype(jnp.bfloat16)
    size = delta.shape[0] // len(delta_refs)
    for d, ref in enumerate(delta_refs):
        ref[...] = delta[d * size : (d + 1) * size, :]


def up(mine, got, mask, factors, owners, after):
    resident, rank, columns = factors.shape
    held = mask.shape[0]
    return pl.pallas_call(
        functools.partial(up_kernel, len(got)),
        out_shape=[jax.ShapeDtypeStruct((held // owners, columns), jnp.bfloat16)] * owners,
        in_specs=[VMEM] * (len(got) + 3) + [ANY],
        out_specs=[VMEM] * owners,
        compiler_params=pltpu.CompilerParams(vmem_limit_bytes=16 * MIB),
        cost_estimate=pl.CostEstimate(
            flops=200 * held * resident * rank * columns,
            bytes_accessed=2 * resident * rank * columns,
            transcendentals=0,
        ),
        name="up",
    )(mine, *got, mask, factors, after)


def finish_kernel(owners, pick_ref, *refs):
    delta_refs, (*near_refs, base_ref, out_hbm, out_ref, sems) = refs[:owners], refs[owners:]
    width = near_refs[0].shape[1]
    pick = pick_ref[...]
    copies = []
    for n, near_ref in enumerate(near_refs):
        cols = slice(n * width, (n + 1) * width)
        mixed = base_ref[:, cols] + near_ref[...].astype(jnp.float32)
        delta = jnp.concatenate([ref[:, cols] for ref in delta_refs], axis=0)
        mixed = mixed + lax.dot_general(
            pick, delta, (((0,), (0,)), ((), ())), preferred_element_type=jnp.float32
        )
        out_ref[:, :, cols] = mixed.astype(jnp.bfloat16).reshape(*out_ref.shape[:2], width)
        copies.append(
            pltpu.make_async_copy(out_ref.at[:, :, cols], out_hbm.at[:, :, cols], sems.at[n])
        )
        copies[n].start()
    for copy in copies:
        copy.wait()


def finish(base, pick, delta, near, steps):
    tokens, columns = base.shape
    shape = (steps, tokens // steps, columns)
    operands = [pick, *delta, *near, base]
    return pl.pallas_call(
        functools.partial(finish_kernel, len(delta)),
        out_shape=jax.ShapeDtypeStruct(shape, jnp.bfloat16),
        in_specs=[VMEM] * len(operands),
        out_specs=HBM,
        scratch_shapes=[
            pltpu.VMEM(shape, jnp.bfloat16),
            pltpu.SemaphoreType.DMA((len(near),)),
        ],
        compiler_params=pltpu.CompilerParams(vmem_limit_bytes=12 * MIB),
        cost_estimate=pl.CostEstimate(
            flops=2 * tokens * pick.shape[0] * columns,
            bytes_accessed=10 * tokens * columns,
            transcendentals=0,
        ),
        name="finish",
    )(*operands)


def body(
    queries,
    fresh_token_keys,
    fresh_token_values,
    cached_key_rows,
    cached_value_rows,
    cache_live_lengths,
    output_projection_weight,
    adapter_down_factors,
    adapter_up_factors,
    adapter_of_row,
    adapter_storage_slot,
):
    step_count, row_count, _ = queries.shape
    resident = adapter_down_factors.shape[0]
    owners = lax.axis_size("replica")
    tensors = lax.axis_size("tensor")
    capacity = max(2, 2 * row_count // owners)
    columns = adapter_up_factors.shape[2]
    far_sent, far_kept = list(range(3, tensors, 2)), list(range(2, tensors, 2))

    attn, pick, sent = attend_and_pick(
        cache_live_lengths,
        adapter_of_row,
        adapter_storage_slot,
        queries,
        fresh_token_keys,
        fresh_token_values,
        cached_key_rows,
        cached_value_rows,
        owners,
        capacity,
        resident,
    )
    got = exchange_all(sent, "replica")

    weight = output_projection_weight
    *parts, w_here = project(attn, weight, columns, far_sent, bring=far_kept)
    far_got = [xor_exchange(part, "tensor", 1) for part in parts]

    mine, low_sent, mask = down(got, adapter_down_factors, capacity, step_count, parts[0])
    low_got = [xor_exchange(low_sent, "tensor", d) for d in range(1, tensors)]
    kept = project(
        attn, weight, columns, far_kept, here=w_here, dtype=jnp.float32, after=[low_sent]
    )
    halves_sent = [merge(*pair, low_sent) for pair in zip(kept, far_got, strict=True)]
    others = [xor_exchange(half, "tensor", d) for half, d in zip(halves_sent, far_kept, strict=True)]
    delta = up(mine, low_got, mask, adapter_up_factors, owners, halves_sent[0])
    delta_got = exchange_all(delta, "replica")

    (near,) = project(attn, weight, columns, [1], after=[delta[0]])
    width = columns // PIECES
    near_got = [
        xor_exchange(near[:, n * width : (n + 1) * width], "tensor", 1) for n in range(PIECES)
    ]
    (own,) = project(
        attn, weight, columns, [0], add=others, dtype=jnp.float32, after=[near]
    )
    return finish(own, pick, delta_got, near_got, step_count)


def solution(mesh):
    in_specs = (
        P(None, ("groups", "replica"), "tensor"),
        P(None, ("groups", "replica"), "tensor"),
        P(None, ("groups", "replica"), "tensor"),
        P(("groups", "replica"), None, "tensor"),
        P(("groups", "replica"), None, "tensor"),
        P(("groups", "replica")),
        P("tensor", None),
        P(("groups", "replica"), None, "tensor"),
        P(("groups", "replica"), None, "tensor"),
        P(("groups", "replica")),
        P("groups"),
    )
    out_specs = P(None, ("groups", "replica"), "tensor")
    return jax.shard_map(body, mesh=mesh, in_specs=in_specs, out_specs=out_specs, check_vma=False)
```

```python
import functools
import math

import jax
import jax.numpy as jnp
import numpy as np
from jax import lax
from jax.experimental import pallas as pl
from jax.experimental.pallas import tpu as pltpu
from jax.sharding import PartitionSpec as P

HEAD_WIDTH = 128
LANES = 128
META_ROWS = 16
TILE = 512
TOGETHER = 4
PIECES = 2
MIB = 1024 * 1024
VMEM = pl.BlockSpec(memory_space=pltpu.VMEM)
ANY = pl.BlockSpec(memory_space=pl.ANY)
HBM = pl.BlockSpec(memory_space=pltpu.HBM)


def iota(shape, dim):
    return lax.broadcasted_iota(jnp.int32, shape, dim)


def halves(n):
    if n & (n - 1):
        raise ValueError(n)
    return n.bit_length() - 1


def div(x, n):
    return lax.shift_right_logical(x, jnp.int32(halves(n)))


def mod(x, n):
    return x & ((1 << halves(n)) - 1)


def in_hbm(*arrays):
    return [pltpu.with_memory_space_constraint(a, pltpu.HBM) for a in arrays]


def xor_exchange(value, axis, distance):
    size = lax.axis_size(axis)
    return lax.ppermute(value, axis, [(i, i ^ distance) for i in range(size)])


def partner_order(size):
    return [0, *range(size // 2, size), *range(1, size // 2)]


def exchange_all(blocks, axis):
    order = partner_order(lax.axis_size(axis))
    return [blocks[0]] + [
        xor_exchange(block, axis, distance)
        for block, distance in zip(blocks[1:], order[1:], strict=True)
    ]


def block_copy(w_hbm, dst, sem, distance):
    me = lax.axis_index("tensor")
    columns = dst.shape[-1]
    at = pl.multiple_of(lax.bitwise_xor(me, jnp.int32(distance)) * columns, LANES)
    return pltpu.make_async_copy(w_hbm.at[:, pl.ds(at, columns)], dst, sem)


def attend_kernel(
    owners,
    capacity,
    resident,
    lengths_hbm,
    adapter_hbm,
    slot_hbm,
    q_hbm,
    order_hbm,
    kf_hbm,
    vf_hbm,
    k_hbm,
    v_hbm,
    attn_ref,
    pick_ref,
    *rest,
):
    send_refs, rest = rest[:owners], rest[owners:]
    lengths_ref, adapter_ref, slot_ref, q_ref, kf_ref, vf_ref, k_ref, v_ref = rest[:8]
    order_ref, q_cols_ref, o_ref, sems, small_sems = rest[8:]
    steps, rows, width = q_ref.shape
    cache, kv_width = k_ref.shape[1:]
    heads = width // HEAD_WIDTH
    kv_here = kv_width // HEAD_WIDTH
    group = heads // kv_here
    per_row = heads * steps
    total = rows * per_row
    tokens = steps * rows
    chunks = sems.shape[1]
    chunk_rows = rows // chunks
    scale = 1.0 / math.sqrt(HEAD_WIDTH)

    def kv_copies(c):
        at = pl.ds(c * chunk_rows, chunk_rows)
        return [
            pltpu.make_async_copy(src.at[at], dst.at[at], sems.at[which, c])
            for which, (src, dst) in enumerate([(k_hbm, k_ref), (v_hbm, v_ref)])
        ]

    small = [
        pltpu.make_async_copy(src, dst, small_sems.at[n])
        for n, (src, dst) in enumerate(
            [
                (q_hbm, q_ref),
                (order_hbm, order_ref),
                (kf_hbm, kf_ref),
                (lengths_hbm, lengths_ref),
                (adapter_hbm, adapter_ref),
                (slot_hbm, slot_ref),
                (vf_hbm, vf_ref),
            ]
        )
    ]
    q_copy, order_copy, kf_copy, lengths_copy, adapter_copy, slot_copy, vf_copy = small
    keys, values_ = zip(*[kv_copies(c) for c in range(chunks)], strict=True)
    for copy in [*small[:2], *keys, *small[2:], *values_]:
        copy.start()

    adapter_copy.wait()
    slot_copy.wait()
    me = lax.axis_index("replica")
    positions = partner_order(owners)
    row_at = mod(iota((8, tokens), 1), rows)
    row_down = iota((rows, LANES), 0)
    first_slot = jnp.zeros((8, tokens), jnp.int32)
    local_of = jnp.zeros((rows, LANES), jnp.int32)
    firsts = []
    for r in range(rows):
        slot = slot_ref[adapter_ref[r]]
        owner = jnp.int32(0)
        for d in range(1, owners):
            owner = owner + (slot >= d * resident).astype(jnp.int32)
        partner = lax.bitwise_xor(owner, me)
        first = jnp.int32(0)
        for d in range(1, owners):
            first = jnp.where(partner == positions[d], d * capacity, first)
        firsts.append(first)
        first_slot = jnp.where(row_at == r, first, first_slot)
        local_of = jnp.where(row_down == r, slot - owner * resident, local_of)
    place = first_slot
    for r in range(rows - 1):
        place = place + ((first_slot == firsts[r]) & (row_at > r)).astype(jnp.int32)
    held = owners * capacity * steps
    slot_at = iota((held, tokens), 0)
    token_at = iota((held, tokens), 1)
    pick = (
        (jnp.concatenate([place] * (held // 8), axis=0) == div(slot_at, steps))
        & (mod(slot_at, steps) == div(token_at, rows))
    ).astype(jnp.bfloat16)
    pick_ref[...] = pick
    local_hot = (local_of == iota((rows, LANES), 1)).astype(jnp.bfloat16)
    entry = iota((owners * META_ROWS, rows), 0)
    entry_place = mod(entry, META_ROWS)
    entry_slot = div(entry, META_ROWS) * capacity + entry_place
    entry_pick = (
        (jnp.concatenate([place[:, :rows]] * (owners * META_ROWS // 8), axis=0) == entry_slot)
        & (entry_place < capacity)
    ).astype(jnp.bfloat16)
    meta = jnp.dot(entry_pick, local_hot, preferred_element_type=jnp.float32)

    q_copy.wait()
    by_head = jnp.concatenate(
        [
            q_ref[:, :, h * HEAD_WIDTH : (h + 1) * HEAD_WIDTH].reshape(tokens, HEAD_WIDTH)
            for h in range(heads)
        ],
        axis=0,
    )
    order_copy.wait()
    q_cols_ref[...] = jnp.dot(
        by_head.astype(jnp.float32).T.astype(jnp.bfloat16),
        order_ref[...],
        preferred_element_type=jnp.float32,
    )
    lane = iota((HEAD_WIDTH, LANES), 1)
    row_of = div(lane, per_row)
    kv_of = mod(div(lane, steps * group), kv_here)

    kf_copy.wait()
    kf = kf_ref[...].reshape(tokens, kv_width)
    token, query = iota((tokens, LANES), 0), iota((tokens, LANES), 1)
    position = iota((cache, LANES), 0)

    def scores(c):
        cols = q_cols_ref[:, pl.ds(pl.multiple_of(c * LANES, LANES), LANES)]
        by_kv = [jnp.where(kv_of == g, cols, 0.0) for g in range(kv_here)]
        fresh = jnp.dot(
            kf,
            jnp.concatenate(by_kv, axis=0).astype(jnp.bfloat16),
            preferred_element_type=jnp.float32,
        )
        live = (mod(token, rows) == div(query, per_row) + c * chunk_rows) & (
            div(token, rows) <= mod(query, steps)
        )
        fresh = jnp.where(live, fresh * scale, -jnp.inf)
        weights = jnp.concatenate(
            [jnp.where(row_of == j, q, 0.0) for j in range(chunk_rows) for q in by_kv], axis=0
        ).astype(jnp.bfloat16)
        keys = jnp.concatenate([k_ref[c * chunk_rows + j] for j in range(chunk_rows)], axis=1)
        cached = jnp.dot(keys, weights, preferred_element_type=jnp.float32)
        return cached * scale, fresh

    def softmax(c, cached, fresh):
        length = jnp.zeros((1, LANES), jnp.int32)
        for j in range(chunk_rows):
            length = jnp.where(
                div(iota((1, LANES), 1), per_row) == j, lengths_ref[c * chunk_rows + j], length
            )
        cached = jnp.where(position < length, cached, -jnp.inf)
        top = jnp.maximum(
            jnp.max(cached, axis=0, keepdims=True), jnp.max(fresh, axis=0, keepdims=True)
        )
        wc, wf = jnp.exp(cached - top), jnp.exp(fresh - top)
        share = 1.0 / (
            jnp.sum(wc, axis=0, keepdims=True) + jnp.sum(wf, axis=0, keepdims=True)
        )
        return (wc * share).T.astype(jnp.bfloat16), (wf * share).T.astype(jnp.bfloat16)

    kv_down = mod(div(iota((LANES, HEAD_WIDTH), 0), steps * group), kv_here)

    def values(c, cached, fresh):
        out = jnp.concatenate(
            [
                jnp.dot(
                    cached[j * per_row : (j + 1) * per_row, :],
                    v_ref[c * chunk_rows + j],
                    preferred_element_type=jnp.float32,
                )
                for j in range(chunk_rows)
            ],
            axis=0,
        ) + jnp.dot(fresh, vf, preferred_element_type=jnp.float32)
        own = out[:, :HEAD_WIDTH]
        for g in range(1, kv_here):
            own = jnp.where(kv_down == g, out[:, g * HEAD_WIDTH : (g + 1) * HEAD_WIDTH], own)
        return own.astype(jnp.bfloat16)

    lengths_copy.wait()
    vf_copy.wait()
    vf = vf_ref[...].reshape(tokens, kv_width)

    together = min(TOGETHER, chunks)

    @pl.loop(0, chunks // together)
    def _(i):
        groups = [i * together + n for n in range(together)]
        for c in groups:
            kv_copies(c)[0].wait()
        scored = [scores(c) for c in groups]
        for c in groups:
            kv_copies(c)[1].wait()
        probs = [softmax(c, *part) for c, part in zip(groups, scored, strict=True)]
        for c, part in zip(groups, probs, strict=True):
            o_ref[pl.ds(pl.multiple_of(c * LANES, LANES), LANES), :] = values(c, *part)

    out = jnp.dot(
        order_ref[...], o_ref[...], preferred_element_type=jnp.float32
    ).astype(jnp.bfloat16)
    attn = jnp.concatenate(
        [out[h * tokens : (h + 1) * tokens, :] for h in range(heads)], axis=1
    )
    attn_ref[...] = attn
    sent = jnp.dot(pick, attn, preferred_element_type=jnp.float32)
    size = capacity * steps
    for d in range(owners):
        mine = sent[d * size : (d + 1) * size, :]
        send_refs[d][...] = jnp.concatenate(
            [mine[:, h * HEAD_WIDTH : (h + 1) * HEAD_WIDTH] for h in range(heads)]
            + [meta[d * META_ROWS : (d + 1) * META_ROWS, :]],
            axis=0,
        ).astype(jnp.bfloat16)


def row_order(heads, steps, rows):
    head, step, row = np.indices((heads, steps, rows)).reshape(3, -1)
    return np.eye(heads * steps * rows)[(row * heads + head) * steps + step]


def attend_and_pick(
    lengths,
    adapter_of_row,
    storage_slot,
    queries,
    fresh_keys,
    fresh_values,
    cached_keys,
    cached_values,
    owners,
    capacity,
    resident,
):
    steps, rows, width = queries.shape
    cache, kv_width = cached_keys.shape[1:]
    heads = width // HEAD_WIDTH
    total = rows * heads * steps
    tokens = steps * rows
    size = capacity * steps
    chunks = total // LANES
    outs = pl.pallas_call(
        functools.partial(attend_kernel, owners, capacity, resident),
        out_shape=[
            jax.ShapeDtypeStruct((tokens, width), jnp.bfloat16),
            jax.ShapeDtypeStruct((owners * size, tokens), jnp.bfloat16),
        ]
        + [jax.ShapeDtypeStruct((heads * size + META_ROWS, HEAD_WIDTH), jnp.bfloat16)] * owners,
        in_specs=[HBM] * 9,
        out_specs=[VMEM] * (2 + owners),
        scratch_shapes=[
            pltpu.SMEM(lengths.shape, jnp.int32),
            pltpu.SMEM(adapter_of_row.shape, jnp.int32),
            pltpu.SMEM(storage_slot.shape, jnp.int32),
            pltpu.VMEM(queries.shape, jnp.bfloat16),
            pltpu.VMEM(fresh_keys.shape, jnp.bfloat16),
            pltpu.VMEM(fresh_values.shape, jnp.bfloat16),
            pltpu.VMEM((rows, cache, kv_width), jnp.bfloat16),
            pltpu.VMEM((rows, cache, kv_width), jnp.bfloat16),
            pltpu.VMEM((total, total), jnp.bfloat16),
            pltpu.VMEM((HEAD_WIDTH, total), jnp.float32),
            pltpu.VMEM((total, HEAD_WIDTH), jnp.bfloat16),
            pltpu.SemaphoreType.DMA((2, chunks)),
            pltpu.SemaphoreType.DMA((7,)),
        ],
        compiler_params=pltpu.CompilerParams(vmem_limit_bytes=24 * MIB),
        cost_estimate=pl.CostEstimate(
            flops=8 * total * cache * kv_width,
            bytes_accessed=4 * rows * cache * kv_width,
            transcendentals=total * cache,
        ),
        name="attend",
    )(
        *in_hbm(
            lengths,
            adapter_of_row,
            storage_slot,
            queries,
            jnp.asarray(row_order(heads, steps, rows), jnp.bfloat16),
            fresh_keys,
            fresh_values,
            cached_keys,
            cached_values,
        ),
    )
    return outs[0], outs[1], outs[2:]


def project_kernel(blocks, here, bring, added, attn_ref, w_hbm, *refs):
    here_ref = refs[0] if here else None
    add_refs = refs[bool(here) :][:added]
    refs = refs[len(refs) - len(blocks) - bool(bring) - 2 :]
    outs, w_ref, sems = refs[: len(blocks)], refs[-2], refs[-1]
    fetched = blocks[here:]
    copies = [
        block_copy(w_hbm, w_ref.at[n], sems.at[n], d) for n, d in enumerate(fetched)
    ] + [
        block_copy(w_hbm, refs[len(blocks)].at[n], sems.at[len(fetched) + n], d)
        for n, d in enumerate(bring)
    ]
    for copy in copies:
        copy.start()
    attn = attn_ref[...]
    for n in range(len(blocks)):
        if n >= here:
            copies[n - here].wait()
        block = here_ref.at[n] if n < here else w_ref.at[n - here]

        @pl.loop(0, block.shape[-1] // TILE)
        def _(i, n=n, block=block, out_ref=outs[n]):
            cols = pl.ds(pl.multiple_of(i * TILE, TILE), TILE)
            out = jnp.dot(attn, block[:, cols], preferred_element_type=jnp.float32)
            for add_ref in add_refs[n :: len(blocks)]:
                out = out + add_ref[:, cols].astype(jnp.float32)
            out_ref[:, cols] = out.astype(out_ref.dtype)

    for copy in copies[len(fetched) :]:
        copy.wait()


def project(attn, weight, columns, blocks, here=None, bring=(), add=(), dtype=jnp.bfloat16, after=()):
    tokens, width = attn.shape
    held = 0 if here is None else here.shape[0]
    fetched = len(blocks) - held
    extra = [*([here] if held else []), *add]
    outs = [jax.ShapeDtypeStruct((tokens, columns), dtype)] * len(blocks)
    if bring:
        outs.append(pltpu.VMEM((len(bring), width, columns), jnp.bfloat16))
    return pl.pallas_call(
        functools.partial(project_kernel, blocks, held, bring, len(add)),
        out_shape=outs,
        in_specs=[VMEM, HBM] + [VMEM] * len(extra) + [ANY] * len(after),
        out_specs=[VMEM] * len(outs),
        scratch_shapes=[
            pltpu.VMEM((max(fetched, 1), width if fetched else 16, columns), jnp.bfloat16),
            pltpu.SemaphoreType.DMA((fetched + len(bring),)),
        ],
        compiler_params=pltpu.CompilerParams(vmem_limit_bytes=16 * MIB),
        cost_estimate=pl.CostEstimate(
            flops=2 * tokens * width * columns * len(blocks),
            bytes_accessed=2 * width * columns * len(blocks),
            transcendentals=0,
        ),
        name="project",
    )(attn, *in_hbm(weight), *extra, *after)


def merge_kernel(mine_ref, got_ref, _, out_ref):
    out_ref[...] = (mine_ref[...] + got_ref[...].astype(jnp.float32)).astype(jnp.bfloat16)


def merge(mine, got, after):
    return pl.pallas_call(
        merge_kernel,
        out_shape=jax.ShapeDtypeStruct(mine.shape, jnp.bfloat16),
        in_specs=[VMEM, VMEM, ANY],
        out_specs=VMEM,
        compiler_params=pltpu.CompilerParams(vmem_limit_bytes=4 * MIB),
        name="merge",
    )(mine, got, after)


def down_kernel(capacity, steps, *refs):
    (*got_refs, down_ref, _, mine_ref, sent_ref, mask_ref) = refs
    resident, rank, width = down_ref.shape
    wide = resident * rank
    heads = width // HEAD_WIDTH
    size = capacity * steps
    held = size * len(got_refs)
    got = [ref[...].astype(jnp.float32) for ref in got_refs]
    rows = jnp.concatenate(
        [
            jnp.concatenate([part[h * size : (h + 1) * size, :] for part in got], axis=0)
            for h in range(heads)
        ],
        axis=1,
    ).astype(jnp.bfloat16)
    meta = jnp.concatenate([part[heads * size :, :] for part in got], axis=0)
    spread = div(iota((LANES, wide), 1), rank) == iota((LANES, wide), 0)
    entries = meta.shape[0]
    slot, entry = iota((held, entries), 0), iota((held, entries), 1)
    of_slot = entry == div(slot, size) * META_ROWS + div(mod(slot, size), steps)
    local = jnp.dot(
        of_slot.astype(jnp.bfloat16),
        meta.astype(jnp.bfloat16),
        preferred_element_type=jnp.float32,
    )
    mask = jnp.dot(
        local.astype(jnp.bfloat16),
        spread.astype(jnp.bfloat16),
        preferred_element_type=jnp.float32,
    )
    mask_ref[...] = mask.astype(jnp.bfloat16)
    low = lax.dot_general(
        rows,
        down_ref[...].reshape(wide, width),
        (((1,), (1,)), ((), ())),
        preferred_element_type=jnp.float32,
    )
    low = low * mask
    pair = low[:, :LANES]
    for n in range(1, wide // LANES):
        pair = pair + low[:, n * LANES : (n + 1) * LANES]
    both = pair + pltpu.roll(pair, rank, 1)
    half = held // 2
    packed = jnp.where(iota((half, LANES), 1) < rank, both[:half, :], both[half:, :])
    mine_ref[...] = packed
    sent_ref[...] = packed.astype(jnp.bfloat16)


def down(got, factors, capacity, steps, after):
    resident, rank, width = factors.shape
    held = len(got) * capacity * steps
    return pl.pallas_call(
        functools.partial(down_kernel, capacity, steps),
        out_shape=[
            jax.ShapeDtypeStruct((held // 2, LANES), jnp.float32),
            jax.ShapeDtypeStruct((held // 2, LANES), jnp.bfloat16),
            jax.ShapeDtypeStruct((held, resident * rank), jnp.bfloat16),
        ],
        in_specs=[VMEM] * (len(got) + 1) + [ANY],
        out_specs=[VMEM] * 3,
        compiler_params=pltpu.CompilerParams(vmem_limit_bytes=12 * MIB),
        cost_estimate=pl.CostEstimate(
            flops=200 * held * resident * rank * width,
            bytes_accessed=2 * resident * rank * width,
            transcendentals=0,
        ),
        name="down",
    )(*got, factors, after)


def up_kernel(peers, mine_ref, *refs):
    got_refs, (mask_ref, up_ref, _, *delta_refs) = refs[:peers], refs[peers:]
    resident, rank, columns = up_ref.shape
    wide = resident * rank
    total = mine_ref[...]
    for ref in got_refs:
        total = total + ref[...].astype(jnp.float32)
    other = pltpu.roll(total, rank, 1)
    first = iota(total.shape, 1) < rank
    both = jnp.concatenate(
        [jnp.where(first, total, other), jnp.where(first, other, total)], axis=0
    )
    both = jnp.concatenate([both] * (wide // LANES), axis=1)
    low = jnp.where(mask_ref[...].astype(jnp.float32) > 0.5, both, 0.0).astype(jnp.bfloat16)
    delta = jnp.dot(
        low, up_ref[...].reshape(wide, columns), preferred_element_type=jnp.float32
    ).astype(jnp.bfloat16)
    size = delta.shape[0] // len(delta_refs)
    for d, ref in enumerate(delta_refs):
        ref[...] = delta[d * size : (d + 1) * size, :]


def up(mine, got, mask, factors, owners, after):
    resident, rank, columns = factors.shape
    held = mask.shape[0]
    return pl.pallas_call(
        functools.partial(up_kernel, len(got)),
        out_shape=[jax.ShapeDtypeStruct((held // owners, columns), jnp.bfloat16)] * owners,
        in_specs=[VMEM] * (len(got) + 3) + [ANY],
        out_specs=[VMEM] * owners,
        compiler_params=pltpu.CompilerParams(vmem_limit_bytes=16 * MIB),
        cost_estimate=pl.CostEstimate(
            flops=200 * held * resident * rank * columns,
            bytes_accessed=2 * resident * rank * columns,
            transcendentals=0,
        ),
        name="up",
    )(mine, *got, mask, factors, after)


def finish_kernel(owners, pick_ref, *refs):
    delta_refs, (*near_refs, base_ref, out_hbm, out_ref, sems) = refs[:owners], refs[owners:]
    width = near_refs[0].shape[1]
    pick = pick_ref[...]
    copies = []
    for n, near_ref in enumerate(near_refs):
        cols = slice(n * width, (n + 1) * width)
        mixed = base_ref[:, cols] + near_ref[...].astype(jnp.float32)
        delta = jnp.concatenate([ref[:, cols] for ref in delta_refs], axis=0)
        mixed = mixed + lax.dot_general(
            pick, delta, (((0,), (0,)), ((), ())), preferred_element_type=jnp.float32
        )
        out_ref[:, :, cols] = mixed.astype(jnp.bfloat16).reshape(*out_ref.shape[:2], width)
        copies.append(
            pltpu.make_async_copy(out_ref.at[:, :, cols], out_hbm.at[:, :, cols], sems.at[n])
        )
        copies[n].start()
    for copy in copies:
        copy.wait()


def finish(base, pick, delta, near, steps):
    tokens, columns = base.shape
    shape = (steps, tokens // steps, columns)
    operands = [pick, *delta, *near, base]
    return pl.pallas_call(
        functools.partial(finish_kernel, len(delta)),
        out_shape=jax.ShapeDtypeStruct(shape, jnp.bfloat16),
        in_specs=[VMEM] * len(operands),
        out_specs=HBM,
        scratch_shapes=[
            pltpu.VMEM(shape, jnp.bfloat16),
            pltpu.SemaphoreType.DMA((len(near),)),
        ],
        compiler_params=pltpu.CompilerParams(vmem_limit_bytes=12 * MIB),
        cost_estimate=pl.CostEstimate(
            flops=2 * tokens * pick.shape[0] * columns,
            bytes_accessed=10 * tokens * columns,
            transcendentals=0,
        ),
        name="finish",
    )(*operands)


def body(
    queries,
    fresh_token_keys,
    fresh_token_values,
    cached_key_rows,
    cached_value_rows,
    cache_live_lengths,
    output_projection_weight,
    adapter_down_factors,
    adapter_up_factors,
    adapter_of_row,
    adapter_storage_slot,
):
    step_count, row_count, _ = queries.shape
    resident = adapter_down_factors.shape[0]
    owners = lax.axis_size("replica")
    tensors = lax.axis_size("tensor")
    capacity = max(2, 2 * row_count // owners)
    columns = adapter_up_factors.shape[2]
    far_sent, far_kept = list(range(3, tensors, 2)), list(range(2, tensors, 2))

    attn, pick, sent = attend_and_pick(
        cache_live_lengths,
        adapter_of_row,
        adapter_storage_slot,
        queries,
        fresh_token_keys,
        fresh_token_values,
        cached_key_rows,
        cached_value_rows,
        owners,
        capacity,
        resident,
    )
    got = exchange_all(sent, "replica")

    weight = output_projection_weight
    *parts, w_here = project(attn, weight, columns, far_sent, bring=far_kept)
    far_got = [xor_exchange(part, "tensor", 1) for part in parts]

    kept = project(
        attn, weight, columns, far_kept, here=w_here, dtype=jnp.float32, after=[parts[0]]
    )
    mine, low_sent, mask = down(got, adapter_down_factors, capacity, step_count, kept[0])
    low_got = [xor_exchange(low_sent, "tensor", d) for d in range(1, tensors)]
    halves_sent = [merge(*pair, low_sent) for pair in zip(kept, far_got, strict=True)]
    others = [xor_exchange(half, "tensor", d) for half, d in zip(halves_sent, far_kept, strict=True)]
    delta = up(mine, low_got, mask, adapter_up_factors, owners, halves_sent[0])
    delta_got = exchange_all(delta, "replica")

    (near,) = project(attn, weight, columns, [1], after=[delta[0]])
    width = columns // PIECES
    near_got = [
        xor_exchange(near[:, n * width : (n + 1) * width], "tensor", 1) for n in range(PIECES)
    ]
    (own,) = project(
        attn, weight, columns, [0], add=others, dtype=jnp.float32, after=[near]
    )
    return finish(own, pick, delta_got, near_got, step_count)


def solution(mesh):
    in_specs = (
        P(None, ("groups", "replica"), "tensor"),
        P(None, ("groups", "replica"), "tensor"),
        P(None, ("groups", "replica"), "tensor"),
        P(("groups", "replica"), None, "tensor"),
        P(("groups", "replica"), None, "tensor"),
        P(("groups", "replica")),
        P("tensor", None),
        P(("groups", "replica"), None, "tensor"),
        P(("groups", "replica"), None, "tensor"),
        P(("groups", "replica")),
        P("groups"),
    )
    out_specs = P(None, ("groups", "replica"), "tensor")
    return jax.shard_map(body, mesh=mesh, in_specs=in_specs, out_specs=out_specs, check_vma=False)
```

```python
import functools
import math

import jax
import jax.numpy as jnp
import numpy as np
from jax import lax
from jax.experimental import pallas as pl
from jax.experimental.pallas import tpu as pltpu
from jax.sharding import PartitionSpec as P

HEAD_WIDTH = 128
LANES = 128
META_ROWS = 16
TILE = 1024
TOGETHER = 4
PIECES = 2
MIB = 1024 * 1024
VMEM = pl.BlockSpec(memory_space=pltpu.VMEM)
ANY = pl.BlockSpec(memory_space=pl.ANY)
HBM = pl.BlockSpec(memory_space=pltpu.HBM)


def iota(shape, dim):
    return lax.broadcasted_iota(jnp.int32, shape, dim)


def halves(n):
    if n & (n - 1):
        raise ValueError(n)
    return n.bit_length() - 1


def div(x, n):
    return lax.shift_right_logical(x, jnp.int32(halves(n)))


def mod(x, n):
    return x & ((1 << halves(n)) - 1)


def in_hbm(*arrays):
    return [pltpu.with_memory_space_constraint(a, pltpu.HBM) for a in arrays]


def xor_exchange(value, axis, distance):
    size = lax.axis_size(axis)
    return lax.ppermute(value, axis, [(i, i ^ distance) for i in range(size)])


def partner_order(size):
    return [0, *range(size // 2, size), *range(1, size // 2)]


def exchange_all(blocks, axis):
    order = partner_order(lax.axis_size(axis))
    return [blocks[0]] + [
        xor_exchange(block, axis, distance)
        for block, distance in zip(blocks[1:], order[1:], strict=True)
    ]


def block_copy(w_hbm, dst, sem, distance):
    me = lax.axis_index("tensor")
    columns = dst.shape[-1]
    at = pl.multiple_of(lax.bitwise_xor(me, jnp.int32(distance)) * columns, LANES)
    return pltpu.make_async_copy(w_hbm.at[:, pl.ds(at, columns)], dst, sem)


def attend_kernel(
    owners,
    capacity,
    resident,
    lengths_hbm,
    adapter_hbm,
    slot_hbm,
    q_hbm,
    order_hbm,
    kf_hbm,
    vf_hbm,
    k_hbm,
    v_hbm,
    attn_ref,
    pick_ref,
    *rest,
):
    send_refs, rest = rest[:owners], rest[owners:]
    lengths_ref, adapter_ref, slot_ref, q_ref, kf_ref, vf_ref, k_ref, v_ref = rest[:8]
    order_ref, q_cols_ref, o_ref, sems, small_sems = rest[8:]
    steps, rows, width = q_ref.shape
    cache, kv_width = k_ref.shape[1:]
    heads = width // HEAD_WIDTH
    kv_here = kv_width // HEAD_WIDTH
    group = heads // kv_here
    per_row = heads * steps
    total = rows * per_row
    tokens = steps * rows
    chunks = sems.shape[1]
    chunk_rows = rows // chunks
    scale = 1.0 / math.sqrt(HEAD_WIDTH)

    def kv_copies(c):
        at = pl.ds(c * chunk_rows, chunk_rows)
        return [
            pltpu.make_async_copy(src.at[at], dst.at[at], sems.at[which, c])
            for which, (src, dst) in enumerate([(k_hbm, k_ref), (v_hbm, v_ref)])
        ]

    small = [
        pltpu.make_async_copy(src, dst, small_sems.at[n])
        for n, (src, dst) in enumerate(
            [
                (q_hbm, q_ref),
                (order_hbm, order_ref),
                (kf_hbm, kf_ref),
                (lengths_hbm, lengths_ref),
                (adapter_hbm, adapter_ref),
                (slot_hbm, slot_ref),
                (vf_hbm, vf_ref),
            ]
        )
    ]
    q_copy, order_copy, kf_copy, lengths_copy, adapter_copy, slot_copy, vf_copy = small
    first, *others = [kv_copies(c) for c in range(chunks)]
    for copy in [*small[:2], *first, *small[2:], *sum(others, [])]:
        copy.start()

    adapter_copy.wait()
    slot_copy.wait()
    me = lax.axis_index("replica")
    positions = partner_order(owners)
    row_at = mod(iota((8, tokens), 1), rows)
    row_down = iota((rows, LANES), 0)
    first_slot = jnp.zeros((8, tokens), jnp.int32)
    local_of = jnp.zeros((rows, LANES), jnp.int32)
    firsts = []
    for r in range(rows):
        slot = slot_ref[adapter_ref[r]]
        owner = jnp.int32(0)
        for d in range(1, owners):
            owner = owner + (slot >= d * resident).astype(jnp.int32)
        partner = lax.bitwise_xor(owner, me)
        first = jnp.int32(0)
        for d in range(1, owners):
            first = jnp.where(partner == positions[d], d * capacity, first)
        firsts.append(first)
        first_slot = jnp.where(row_at == r, first, first_slot)
        local_of = jnp.where(row_down == r, slot - owner * resident, local_of)
    place = first_slot
    for r in range(rows - 1):
        place = place + ((first_slot == firsts[r]) & (row_at > r)).astype(jnp.int32)
    held = owners * capacity * steps
    slot_at = iota((held, tokens), 0)
    token_at = iota((held, tokens), 1)
    pick = (
        (jnp.concatenate([place] * (held // 8), axis=0) == div(slot_at, steps))
        & (mod(slot_at, steps) == div(token_at, rows))
    ).astype(jnp.bfloat16)
    pick_ref[...] = pick
    local_hot = (local_of == iota((rows, LANES), 1)).astype(jnp.bfloat16)
    entry = iota((owners * META_ROWS, rows), 0)
    entry_place = mod(entry, META_ROWS)
    entry_slot = div(entry, META_ROWS) * capacity + entry_place
    entry_pick = (
        (jnp.concatenate([place[:, :rows]] * (owners * META_ROWS // 8), axis=0) == entry_slot)
        & (entry_place < capacity)
    ).astype(jnp.bfloat16)
    meta = jnp.dot(entry_pick, local_hot, preferred_element_type=jnp.float32)

    q_copy.wait()
    by_head = jnp.concatenate(
        [
            q_ref[:, :, h * HEAD_WIDTH : (h + 1) * HEAD_WIDTH].reshape(tokens, HEAD_WIDTH)
            for h in range(heads)
        ],
        axis=0,
    )
    order_copy.wait()
    q_cols_ref[...] = jnp.dot(
        by_head.astype(jnp.float32).T.astype(jnp.bfloat16),
        order_ref[...],
        preferred_element_type=jnp.float32,
    )
    lane = iota((HEAD_WIDTH, LANES), 1)
    row_of = div(lane, per_row)
    kv_of = mod(div(lane, steps * group), kv_here)

    kf_copy.wait()
    kf = kf_ref[...].reshape(tokens, kv_width)
    token, query = iota((tokens, LANES), 0), iota((tokens, LANES), 1)
    position = iota((cache, LANES), 0)

    def scores(c):
        cols = q_cols_ref[:, pl.ds(pl.multiple_of(c * LANES, LANES), LANES)]
        by_kv = [jnp.where(kv_of == g, cols, 0.0) for g in range(kv_here)]
        fresh = jnp.dot(
            kf,
            jnp.concatenate(by_kv, axis=0).astype(jnp.bfloat16),
            preferred_element_type=jnp.float32,
        )
        live = (mod(token, rows) == div(query, per_row) + c * chunk_rows) & (
            div(token, rows) <= mod(query, steps)
        )
        fresh = jnp.where(live, fresh * scale, -jnp.inf)
        weights = jnp.concatenate(
            [jnp.where(row_of == j, q, 0.0) for j in range(chunk_rows) for q in by_kv], axis=0
        ).astype(jnp.bfloat16)
        keys = jnp.concatenate([k_ref[c * chunk_rows + j] for j in range(chunk_rows)], axis=1)
        cached = jnp.dot(keys, weights, preferred_element_type=jnp.float32)
        return cached * scale, fresh

    def softmax(c, cached, fresh):
        length = jnp.zeros((1, LANES), jnp.int32)
        for j in range(chunk_rows):
            length = jnp.where(
                div(iota((1, LANES), 1), per_row) == j, lengths_ref[c * chunk_rows + j], length
            )
        cached = jnp.where(position < length, cached, -jnp.inf)
        top = jnp.maximum(
            jnp.max(cached, axis=0, keepdims=True), jnp.max(fresh, axis=0, keepdims=True)
        )
        wc, wf = jnp.exp(cached - top), jnp.exp(fresh - top)
        share = 1.0 / (
            jnp.sum(wc, axis=0, keepdims=True) + jnp.sum(wf, axis=0, keepdims=True)
        )
        return (wc * share).T.astype(jnp.bfloat16), (wf * share).T.astype(jnp.bfloat16)

    kv_down = mod(div(iota((LANES, HEAD_WIDTH), 0), steps * group), kv_here)

    def values(c, cached, fresh):
        out = jnp.concatenate(
            [
                jnp.dot(
                    cached[j * per_row : (j + 1) * per_row, :],
                    v_ref[c * chunk_rows + j],
                    preferred_element_type=jnp.float32,
                )
                for j in range(chunk_rows)
            ],
            axis=0,
        ) + jnp.dot(fresh, vf, preferred_element_type=jnp.float32)
        own = out[:, :HEAD_WIDTH]
        for g in range(1, kv_here):
            own = jnp.where(kv_down == g, out[:, g * HEAD_WIDTH : (g + 1) * HEAD_WIDTH], own)
        return own.astype(jnp.bfloat16)

    lengths_copy.wait()
    vf_copy.wait()
    vf = vf_ref[...].reshape(tokens, kv_width)

    together = min(TOGETHER, chunks)

    @pl.loop(0, chunks // together)
    def _(i):
        groups = [i * together + n for n in range(together)]
        for c in groups:
            for copy in kv_copies(c):
                copy.wait()

        scored = [scores(c) for c in groups]
        probs = [softmax(c, *part) for c, part in zip(groups, scored, strict=True)]
        for c, part in zip(groups, probs, strict=True):
            o_ref[pl.ds(pl.multiple_of(c * LANES, LANES), LANES), :] = values(c, *part)

    out = jnp.dot(
        order_ref[...], o_ref[...], preferred_element_type=jnp.float32
    ).astype(jnp.bfloat16)
    attn = jnp.concatenate(
        [out[h * tokens : (h + 1) * tokens, :] for h in range(heads)], axis=1
    )
    attn_ref[...] = attn
    sent = jnp.dot(pick, attn, preferred_element_type=jnp.float32)
    size = capacity * steps
    for d in range(owners):
        mine = sent[d * size : (d + 1) * size, :]
        send_refs[d][...] = jnp.concatenate(
            [mine[:, h * HEAD_WIDTH : (h + 1) * HEAD_WIDTH] for h in range(heads)]
            + [meta[d * META_ROWS : (d + 1) * META_ROWS, :]],
            axis=0,
        ).astype(jnp.bfloat16)


def row_order(heads, steps, rows):
    head, step, row = np.indices((heads, steps, rows)).reshape(3, -1)
    return np.eye(heads * steps * rows)[(row * heads + head) * steps + step]


def attend_and_pick(
    lengths,
    adapter_of_row,
    storage_slot,
    queries,
    fresh_keys,
    fresh_values,
    cached_keys,
    cached_values,
    owners,
    capacity,
    resident,
):
    steps, rows, width = queries.shape
    cache, kv_width = cached_keys.shape[1:]
    heads = width // HEAD_WIDTH
    total = rows * heads * steps
    tokens = steps * rows
    size = capacity * steps
    chunks = total // LANES
    outs = pl.pallas_call(
        functools.partial(attend_kernel, owners, capacity, resident),
        out_shape=[
            jax.ShapeDtypeStruct((tokens, width), jnp.bfloat16),
            jax.ShapeDtypeStruct((owners * size, tokens), jnp.bfloat16),
        ]
        + [jax.ShapeDtypeStruct((heads * size + META_ROWS, HEAD_WIDTH), jnp.bfloat16)] * owners,
        in_specs=[HBM] * 9,
        out_specs=[VMEM] * (2 + owners),
        scratch_shapes=[
            pltpu.SMEM(lengths.shape, jnp.int32),
            pltpu.SMEM(adapter_of_row.shape, jnp.int32),
            pltpu.SMEM(storage_slot.shape, jnp.int32),
            pltpu.VMEM(queries.shape, jnp.bfloat16),
            pltpu.VMEM(fresh_keys.shape, jnp.bfloat16),
            pltpu.VMEM(fresh_values.shape, jnp.bfloat16),
            pltpu.VMEM((rows, cache, kv_width), jnp.bfloat16),
            pltpu.VMEM((rows, cache, kv_width), jnp.bfloat16),
            pltpu.VMEM((total, total), jnp.bfloat16),
            pltpu.VMEM((HEAD_WIDTH, total), jnp.float32),
            pltpu.VMEM((total, HEAD_WIDTH), jnp.bfloat16),
            pltpu.SemaphoreType.DMA((2, chunks)),
            pltpu.SemaphoreType.DMA((7,)),
        ],
        compiler_params=pltpu.CompilerParams(vmem_limit_bytes=24 * MIB),
        cost_estimate=pl.CostEstimate(
            flops=8 * total * cache * kv_width,
            bytes_accessed=4 * rows * cache * kv_width,
            transcendentals=total * cache,
        ),
        name="attend",
    )(
        *in_hbm(
            lengths,
            adapter_of_row,
            storage_slot,
            queries,
            jnp.asarray(row_order(heads, steps, rows), jnp.bfloat16),
            fresh_keys,
            fresh_values,
            cached_keys,
            cached_values,
        ),
    )
    return outs[0], outs[1], outs[2:]


def project_kernel(blocks, here, bring, added, attn_ref, w_hbm, *refs):
    here_ref = refs[0] if here else None
    add_refs = refs[bool(here) :][:added]
    refs = refs[len(refs) - len(blocks) - bool(bring) - 2 :]
    outs, w_ref, sems = refs[: len(blocks)], refs[-2], refs[-1]
    fetched = blocks[here:]
    copies = [
        block_copy(w_hbm, w_ref.at[n], sems.at[n], d) for n, d in enumerate(fetched)
    ] + [
        block_copy(w_hbm, refs[len(blocks)].at[n], sems.at[len(fetched) + n], d)
        for n, d in enumerate(bring)
    ]
    for copy in copies:
        copy.start()
    attn = attn_ref[...]
    for n in range(len(blocks)):
        if n >= here:
            copies[n - here].wait()
        block = here_ref.at[n] if n < here else w_ref.at[n - here]

        @pl.loop(0, block.shape[-1] // TILE)
        def _(i, n=n, block=block, out_ref=outs[n]):
            cols = pl.ds(pl.multiple_of(i * TILE, TILE), TILE)
            out = jnp.dot(attn, block[:, cols], preferred_element_type=jnp.float32)
            for add_ref in add_refs[n :: len(blocks)]:
                out = out + add_ref[:, cols].astype(jnp.float32)
            out_ref[:, cols] = out.astype(out_ref.dtype)

    for copy in copies[len(fetched) :]:
        copy.wait()


def project(attn, weight, columns, blocks, here=None, bring=(), add=(), dtype=jnp.bfloat16, after=()):
    tokens, width = attn.shape
    held = 0 if here is None else here.shape[0]
    fetched = len(blocks) - held
    extra = [*([here] if held else []), *add]
    outs = [jax.ShapeDtypeStruct((tokens, columns), dtype)] * len(blocks)
    if bring:
        outs.append(pltpu.VMEM((len(bring), width, columns), jnp.bfloat16))
    return pl.pallas_call(
        functools.partial(project_kernel, blocks, held, bring, len(add)),
        out_shape=outs,
        in_specs=[VMEM, HBM] + [VMEM] * len(extra) + [ANY] * len(after),
        out_specs=[VMEM] * len(outs),
        scratch_shapes=[
            pltpu.VMEM((max(fetched, 1), width if fetched else 16, columns), jnp.bfloat16),
            pltpu.SemaphoreType.DMA((fetched + len(bring),)),
        ],
        compiler_params=pltpu.CompilerParams(vmem_limit_bytes=16 * MIB),
        cost_estimate=pl.CostEstimate(
            flops=2 * tokens * width * columns * len(blocks),
            bytes_accessed=2 * width * columns * len(blocks),
            transcendentals=0,
        ),
        name="project",
    )(attn, *in_hbm(weight), *extra, *after)


def merge_kernel(mine_ref, got_ref, _, out_ref):
    out_ref[...] = (mine_ref[...] + got_ref[...].astype(jnp.float32)).astype(jnp.bfloat16)


def merge(mine, got, after):
    return pl.pallas_call(
        merge_kernel,
        out_shape=jax.ShapeDtypeStruct(mine.shape, jnp.bfloat16),
        in_specs=[VMEM, VMEM, ANY],
        out_specs=VMEM,
        compiler_params=pltpu.CompilerParams(vmem_limit_bytes=4 * MIB),
        name="merge",
    )(mine, got, after)


def down_kernel(capacity, steps, *refs):
    (*got_refs, down_ref, _, mine_ref, sent_ref, mask_ref) = refs
    resident, rank, width = down_ref.shape
    wide = resident * rank
    heads = width // HEAD_WIDTH
    size = capacity * steps
    held = size * len(got_refs)
    got = [ref[...].astype(jnp.float32) for ref in got_refs]
    rows = jnp.concatenate(
        [
            jnp.concatenate([part[h * size : (h + 1) * size, :] for part in got], axis=0)
            for h in range(heads)
        ],
        axis=1,
    ).astype(jnp.bfloat16)
    meta = jnp.concatenate([part[heads * size :, :] for part in got], axis=0)
    spread = div(iota((LANES, wide), 1), rank) == iota((LANES, wide), 0)
    entries = meta.shape[0]
    slot, entry = iota((held, entries), 0), iota((held, entries), 1)
    of_slot = entry == div(slot, size) * META_ROWS + div(mod(slot, size), steps)
    local = jnp.dot(
        of_slot.astype(jnp.bfloat16),
        meta.astype(jnp.bfloat16),
        preferred_element_type=jnp.float32,
    )
    mask = jnp.dot(
        local.astype(jnp.bfloat16),
        spread.astype(jnp.bfloat16),
        preferred_element_type=jnp.float32,
    )
    mask_ref[...] = mask.astype(jnp.bfloat16)
    low = lax.dot_general(
        rows,
        down_ref[...].reshape(wide, width),
        (((1,), (1,)), ((), ())),
        preferred_element_type=jnp.float32,
    )
    low = low * mask
    pair = low[:, :LANES]
    for n in range(1, wide // LANES):
        pair = pair + low[:, n * LANES : (n + 1) * LANES]
    both = pair + pltpu.roll(pair, rank, 1)
    half = held // 2
    packed = jnp.where(iota((half, LANES), 1) < rank, both[:half, :], both[half:, :])
    mine_ref[...] = packed
    sent_ref[...] = packed.astype(jnp.bfloat16)


def down(got, factors, capacity, steps, after):
    resident, rank, width = factors.shape
    held = len(got) * capacity * steps
    return pl.pallas_call(
        functools.partial(down_kernel, capacity, steps),
        out_shape=[
            jax.ShapeDtypeStruct((held // 2, LANES), jnp.float32),
            jax.ShapeDtypeStruct((held // 2, LANES), jnp.bfloat16),
            jax.ShapeDtypeStruct((held, resident * rank), jnp.bfloat16),
        ],
        in_specs=[VMEM] * (len(got) + 1) + [ANY],
        out_specs=[VMEM] * 3,
        compiler_params=pltpu.CompilerParams(vmem_limit_bytes=12 * MIB),
        cost_estimate=pl.CostEstimate(
            flops=200 * held * resident * rank * width,
            bytes_accessed=2 * resident * rank * width,
            transcendentals=0,
        ),
        name="down",
    )(*got, factors, after)


def up_kernel(peers, mine_ref, *refs):
    got_refs, (mask_ref, up_ref, _, *delta_refs) = refs[:peers], refs[peers:]
    resident, rank, columns = up_ref.shape
    wide = resident * rank
    total = mine_ref[...]
    for ref in got_refs:
        total = total + ref[...].astype(jnp.float32)
    other = pltpu.roll(total, rank, 1)
    first = iota(total.shape, 1) < rank
    both = jnp.concatenate(
        [jnp.where(first, total, other), jnp.where(first, other, total)], axis=0
    )
    both = jnp.concatenate([both] * (wide // LANES), axis=1)
    low = jnp.where(mask_ref[...].astype(jnp.float32) > 0.5, both, 0.0).astype(jnp.bfloat16)
    delta = jnp.dot(
        low, up_ref[...].reshape(wide, columns), preferred_element_type=jnp.float32
    ).astype(jnp.bfloat16)
    size = delta.shape[0] // len(delta_refs)
    for d, ref in enumerate(delta_refs):
        ref[...] = delta[d * size : (d + 1) * size, :]


def up(mine, got, mask, factors, owners, after):
    resident, rank, columns = factors.shape
    held = mask.shape[0]
    return pl.pallas_call(
        functools.partial(up_kernel, len(got)),
        out_shape=[jax.ShapeDtypeStruct((held // owners, columns), jnp.bfloat16)] * owners,
        in_specs=[VMEM] * (len(got) + 3) + [ANY],
        out_specs=[VMEM] * owners,
        compiler_params=pltpu.CompilerParams(vmem_limit_bytes=16 * MIB),
        cost_estimate=pl.CostEstimate(
            flops=200 * held * resident * rank * columns,
            bytes_accessed=2 * resident * rank * columns,
            transcendentals=0,
        ),
        name="up",
    )(mine, *got, mask, factors, after)


def finish_kernel(owners, pick_ref, *refs):
    delta_refs, (*near_refs, base_ref, out_hbm, out_ref, sems) = refs[:owners], refs[owners:]
    width = near_refs[0].shape[1]
    pick = pick_ref[...]
    copies = []
    for n, near_ref in enumerate(near_refs):
        cols = slice(n * width, (n + 1) * width)
        mixed = base_ref[:, cols] + near_ref[...].astype(jnp.float32)
        delta = jnp.concatenate([ref[:, cols] for ref in delta_refs], axis=0)
        mixed = mixed + lax.dot_general(
            pick, delta, (((0,), (0,)), ((), ())), preferred_element_type=jnp.float32
        )
        out_ref[:, :, cols] = mixed.astype(jnp.bfloat16).reshape(*out_ref.shape[:2], width)
        copies.append(
            pltpu.make_async_copy(out_ref.at[:, :, cols], out_hbm.at[:, :, cols], sems.at[n])
        )
        copies[n].start()
    for copy in copies:
        copy.wait()


def finish(base, pick, delta, near, steps):
    tokens, columns = base.shape
    shape = (steps, tokens // steps, columns)
    operands = [pick, *delta, *near, base]
    return pl.pallas_call(
        functools.partial(finish_kernel, len(delta)),
        out_shape=jax.ShapeDtypeStruct(shape, jnp.bfloat16),
        in_specs=[VMEM] * len(operands),
        out_specs=HBM,
        scratch_shapes=[
            pltpu.VMEM(shape, jnp.bfloat16),
            pltpu.SemaphoreType.DMA((len(near),)),
        ],
        compiler_params=pltpu.CompilerParams(vmem_limit_bytes=12 * MIB),
        cost_estimate=pl.CostEstimate(
            flops=2 * tokens * pick.shape[0] * columns,
            bytes_accessed=10 * tokens * columns,
            transcendentals=0,
        ),
        name="finish",
    )(*operands)


def body(
    queries,
    fresh_token_keys,
    fresh_token_values,
    cached_key_rows,
    cached_value_rows,
    cache_live_lengths,
    output_projection_weight,
    adapter_down_factors,
    adapter_up_factors,
    adapter_of_row,
    adapter_storage_slot,
):
    step_count, row_count, _ = queries.shape
    resident = adapter_down_factors.shape[0]
    owners = lax.axis_size("replica")
    tensors = lax.axis_size("tensor")
    capacity = max(2, 2 * row_count // owners)
    columns = adapter_up_factors.shape[2]
    far_sent, far_kept = list(range(3, tensors, 2)), list(range(2, tensors, 2))

    attn, pick, sent = attend_and_pick(
        cache_live_lengths,
        adapter_of_row,
        adapter_storage_slot,
        queries,
        fresh_token_keys,
        fresh_token_values,
        cached_key_rows,
        cached_value_rows,
        owners,
        capacity,
        resident,
    )
    got = exchange_all(sent, "replica")

    weight = output_projection_weight
    *parts, w_here = project(attn, weight, columns, far_sent, bring=far_kept)
    far_got = [xor_exchange(part, "tensor", 1) for part in parts]

    kept = project(
        attn, weight, columns, far_kept, here=w_here, dtype=jnp.float32, after=[parts[0]]
    )
    mine, low_sent, mask = down(got, adapter_down_factors, capacity, step_count, kept[0])
    low_got = [xor_exchange(low_sent, "tensor", d) for d in range(1, tensors)]
    halves_sent = [merge(*pair, low_sent) for pair in zip(kept, far_got, strict=True)]
    others = [xor_exchange(half, "tensor", d) for half, d in zip(halves_sent, far_kept, strict=True)]
    delta = up(mine, low_got, mask, adapter_up_factors, owners, halves_sent[0])
    delta_got = exchange_all(delta, "replica")

    (near,) = project(attn, weight, columns, [1], after=[delta[0]])
    width = columns // PIECES
    near_got = [
        xor_exchange(near[:, n * width : (n + 1) * width], "tensor", 1) for n in range(PIECES)
    ]
    (own,) = project(
        attn, weight, columns, [0], add=others, dtype=jnp.float32, after=[near]
    )
    return finish(own, pick, delta_got, near_got, step_count)


def solution(mesh):
    in_specs = (
        P(None, ("groups", "replica"), "tensor"),
        P(None, ("groups", "replica"), "tensor"),
        P(None, ("groups", "replica"), "tensor"),
        P(("groups", "replica"), None, "tensor"),
        P(("groups", "replica"), None, "tensor"),
        P(("groups", "replica")),
        P("tensor", None),
        P(("groups", "replica"), None, "tensor"),
        P(("groups", "replica"), None, "tensor"),
        P(("groups", "replica")),
        P("groups"),
    )
    out_specs = P(None, ("groups", "replica"), "tensor")
    return jax.shard_map(body, mesh=mesh, in_specs=in_specs, out_specs=out_specs, check_vma=False)
```

```python
import functools
import math

import jax
import jax.numpy as jnp
import numpy as np
from jax import lax
from jax.experimental import pallas as pl
from jax.experimental.pallas import tpu as pltpu
from jax.sharding import PartitionSpec as P

HEAD_WIDTH = 128
LANES = 128
META_ROWS = 16
TILE = 1024
TOGETHER = 4
PIECES = 2
MIB = 1024 * 1024
VMEM = pl.BlockSpec(memory_space=pltpu.VMEM)
ANY = pl.BlockSpec(memory_space=pl.ANY)
HBM = pl.BlockSpec(memory_space=pltpu.HBM)


def iota(shape, dim):
    return lax.broadcasted_iota(jnp.int32, shape, dim)


def halves(n):
    if n & (n - 1):
        raise ValueError(n)
    return n.bit_length() - 1


def div(x, n):
    return lax.shift_right_logical(x, jnp.int32(halves(n)))


def mod(x, n):
    return x & ((1 << halves(n)) - 1)


def in_hbm(*arrays):
    return [pltpu.with_memory_space_constraint(a, pltpu.HBM) for a in arrays]


def xor_exchange(value, axis, distance):
    size = lax.axis_size(axis)
    return lax.ppermute(value, axis, [(i, i ^ distance) for i in range(size)])


def partner_order(size):
    return [0, *range(size // 2, size), *range(1, size // 2)]


def exchange_all(blocks, axis):
    order = partner_order(lax.axis_size(axis))
    return [blocks[0]] + [
        xor_exchange(block, axis, distance)
        for block, distance in zip(blocks[1:], order[1:], strict=True)
    ]


def block_copy(w_hbm, dst, sem, distance):
    me = lax.axis_index("tensor")
    columns = dst.shape[-1]
    at = pl.multiple_of(lax.bitwise_xor(me, jnp.int32(distance)) * columns, LANES)
    return pltpu.make_async_copy(w_hbm.at[:, pl.ds(at, columns)], dst, sem)


def attend_kernel(
    owners,
    capacity,
    resident,
    lengths_hbm,
    adapter_hbm,
    slot_hbm,
    q_hbm,
    order_hbm,
    kf_hbm,
    vf_hbm,
    k_hbm,
    v_hbm,
    attn_ref,
    pick_ref,
    *rest,
):
    send_refs, rest = rest[:owners], rest[owners:]
    lengths_ref, adapter_ref, slot_ref, q_ref, kf_ref, vf_ref, k_ref, v_ref = rest[:8]
    order_ref, q_cols_ref, o_ref, sems, small_sems = rest[8:]
    steps, rows, width = q_ref.shape
    cache, kv_width = k_ref.shape[1:]
    heads = width // HEAD_WIDTH
    kv_here = kv_width // HEAD_WIDTH
    group = heads // kv_here
    per_row = heads * steps
    total = rows * per_row
    tokens = steps * rows
    chunks = sems.shape[1]
    chunk_rows = rows // chunks
    scale = 1.0 / math.sqrt(HEAD_WIDTH)

    def kv_copies(c):
        at = pl.ds(c * chunk_rows, chunk_rows)
        return [
            pltpu.make_async_copy(src.at[at], dst.at[at], sems.at[which, c])
            for which, (src, dst) in enumerate([(k_hbm, k_ref), (v_hbm, v_ref)])
        ]

    small = [
        pltpu.make_async_copy(src, dst, small_sems.at[n])
        for n, (src, dst) in enumerate(
            [
                (q_hbm, q_ref),
                (order_hbm, order_ref),
                (kf_hbm, kf_ref),
                (lengths_hbm, lengths_ref),
                (adapter_hbm, adapter_ref),
                (slot_hbm, slot_ref),
                (vf_hbm, vf_ref),
            ]
        )
    ]
    q_copy, order_copy, kf_copy, lengths_copy, adapter_copy, slot_copy, vf_copy = small
    first, *others = [kv_copies(c) for c in range(chunks)]
    for copy in [*small[:2], *first, *small[2:], *sum(others, [])]:
        copy.start()

    adapter_copy.wait()
    slot_copy.wait()
    me = lax.axis_index("replica")
    positions = partner_order(owners)
    row_at = mod(iota((8, tokens), 1), rows)
    row_down = iota((rows, LANES), 0)
    first_slot = jnp.zeros((8, tokens), jnp.int32)
    local_of = jnp.zeros((rows, LANES), jnp.int32)
    firsts = []
    for r in range(rows):
        slot = slot_ref[adapter_ref[r]]
        owner = jnp.int32(0)
        for d in range(1, owners):
            owner = owner + (slot >= d * resident).astype(jnp.int32)
        partner = lax.bitwise_xor(owner, me)
        first = jnp.int32(0)
        for d in range(1, owners):
            first = jnp.where(partner == positions[d], d * capacity, first)
        firsts.append(first)
        first_slot = jnp.where(row_at == r, first, first_slot)
        local_of = jnp.where(row_down == r, slot - owner * resident, local_of)
    place = first_slot
    for r in range(rows - 1):
        place = place + ((first_slot == firsts[r]) & (row_at > r)).astype(jnp.int32)
    held = owners * capacity * steps
    slot_at = iota((held, tokens), 0)
    token_at = iota((held, tokens), 1)
    pick = (
        (jnp.concatenate([place] * (held // 8), axis=0) == div(slot_at, steps))
        & (mod(slot_at, steps) == div(token_at, rows))
    ).astype(jnp.bfloat16)
    pick_ref[...] = pick
    local_hot = (local_of == iota((rows, LANES), 1)).astype(jnp.bfloat16)
    entry = iota((owners * META_ROWS, rows), 0)
    entry_place = mod(entry, META_ROWS)
    entry_slot = div(entry, META_ROWS) * capacity + entry_place
    entry_pick = (
        (jnp.concatenate([place[:, :rows]] * (owners * META_ROWS // 8), axis=0) == entry_slot)
        & (entry_place < capacity)
    ).astype(jnp.bfloat16)
    meta = jnp.dot(entry_pick, local_hot, preferred_element_type=jnp.float32)

    q_copy.wait()
    by_head = jnp.concatenate(
        [
            q_ref[:, :, h * HEAD_WIDTH : (h + 1) * HEAD_WIDTH].reshape(tokens, HEAD_WIDTH)
            for h in range(heads)
        ],
        axis=0,
    )
    order_copy.wait()
    q_cols_ref[...] = jnp.dot(
        by_head.astype(jnp.float32).T.astype(jnp.bfloat16),
        order_ref[...],
        preferred_element_type=jnp.float32,
    )
    lane = iota((HEAD_WIDTH, LANES), 1)
    row_of = div(lane, per_row)
    kv_of = mod(div(lane, steps * group), kv_here)

    kf_copy.wait()
    kf = kf_ref[...].reshape(tokens, kv_width)
    token, query = iota((tokens, LANES), 0), iota((tokens, LANES), 1)
    position = iota((cache, LANES), 0)

    def scores(c):
        cols = q_cols_ref[:, pl.ds(pl.multiple_of(c * LANES, LANES), LANES)]
        by_kv = [jnp.where(kv_of == g, cols, 0.0) for g in range(kv_here)]
        fresh = jnp.dot(
            kf,
            jnp.concatenate(by_kv, axis=0).astype(jnp.bfloat16),
            preferred_element_type=jnp.float32,
        )
        live = (mod(token, rows) == div(query, per_row) + c * chunk_rows) & (
            div(token, rows) <= mod(query, steps)
        )
        fresh = jnp.where(live, fresh * scale, -jnp.inf)
        weights = jnp.concatenate(
            [jnp.where(row_of == j, q, 0.0) for j in range(chunk_rows) for q in by_kv], axis=0
        ).astype(jnp.bfloat16)
        keys = jnp.concatenate([k_ref[c * chunk_rows + j] for j in range(chunk_rows)], axis=1)
        cached = jnp.dot(keys, weights, preferred_element_type=jnp.float32)
        return cached * scale, fresh

    def softmax(c, cached, fresh):
        length = jnp.zeros((1, LANES), jnp.int32)
        for j in range(chunk_rows):
            length = jnp.where(
                div(iota((1, LANES), 1), per_row) == j, lengths_ref[c * chunk_rows + j], length
            )
        cached = jnp.where(position < length, cached, -jnp.inf)
        top = jnp.maximum(
            jnp.max(cached, axis=0, keepdims=True), jnp.max(fresh, axis=0, keepdims=True)
        )
        wc, wf = jnp.exp(cached - top), jnp.exp(fresh - top)
        share = 1.0 / (
            jnp.sum(wc, axis=0, keepdims=True) + jnp.sum(wf, axis=0, keepdims=True)
        )
        return (wc * share).T.astype(jnp.bfloat16), (wf * share).T.astype(jnp.bfloat16)

    kv_down = mod(div(iota((LANES, HEAD_WIDTH), 0), steps * group), kv_here)

    def values(c, cached, fresh):
        out = jnp.concatenate(
            [
                jnp.dot(
                    cached[j * per_row : (j + 1) * per_row, :],
                    v_ref[c * chunk_rows + j],
                    preferred_element_type=jnp.float32,
                )
                for j in range(chunk_rows)
            ],
            axis=0,
        ) + jnp.dot(fresh, vf, preferred_element_type=jnp.float32)
        own = out[:, :HEAD_WIDTH]
        for g in range(1, kv_here):
            own = jnp.where(kv_down == g, out[:, g * HEAD_WIDTH : (g + 1) * HEAD_WIDTH], own)
        return own.astype(jnp.bfloat16)

    lengths_copy.wait()
    vf_copy.wait()
    vf = vf_ref[...].reshape(tokens, kv_width)

    together = min(TOGETHER, chunks)

    @pl.loop(0, chunks // together)
    def _(i):
        groups = [i * together + n for n in range(together)]
        for c in groups:
            for copy in kv_copies(c):
                copy.wait()

        scored = [scores(c) for c in groups]
        probs = [softmax(c, *part) for c, part in zip(groups, scored, strict=True)]
        for c, part in zip(groups, probs, strict=True):
            o_ref[pl.ds(pl.multiple_of(c * LANES, LANES), LANES), :] = values(c, *part)

    out = jnp.dot(
        order_ref[...], o_ref[...], preferred_element_type=jnp.float32
    ).astype(jnp.bfloat16)
    attn = jnp.concatenate(
        [out[h * tokens : (h + 1) * tokens, :] for h in range(heads)], axis=1
    )
    attn_ref[...] = attn
    sent = jnp.dot(pick, attn, preferred_element_type=jnp.float32)
    size = capacity * steps
    for d in range(owners):
        mine = sent[d * size : (d + 1) * size, :]
        send_refs[d][...] = jnp.concatenate(
            [mine[:, h * HEAD_WIDTH : (h + 1) * HEAD_WIDTH] for h in range(heads)]
            + [meta[d * META_ROWS : (d + 1) * META_ROWS, :]],
            axis=0,
        ).astype(jnp.bfloat16)


def row_order(heads, steps, rows):
    head, step, row = np.indices((heads, steps, rows)).reshape(3, -1)
    return np.eye(heads * steps * rows)[(row * heads + head) * steps + step]


def attend_and_pick(
    lengths,
    adapter_of_row,
    storage_slot,
    queries,
    fresh_keys,
    fresh_values,
    cached_keys,
    cached_values,
    owners,
    capacity,
    resident,
):
    steps, rows, width = queries.shape
    cache, kv_width = cached_keys.shape[1:]
    heads = width // HEAD_WIDTH
    total = rows * heads * steps
    tokens = steps * rows
    size = capacity * steps
    chunks = total // LANES
    outs = pl.pallas_call(
        functools.partial(attend_kernel, owners, capacity, resident),
        out_shape=[
            jax.ShapeDtypeStruct((tokens, width), jnp.bfloat16),
            jax.ShapeDtypeStruct((owners * size, tokens), jnp.bfloat16),
        ]
        + [jax.ShapeDtypeStruct((heads * size + META_ROWS, HEAD_WIDTH), jnp.bfloat16)] * owners,
        in_specs=[HBM] * 9,
        out_specs=[VMEM] * (2 + owners),
        scratch_shapes=[
            pltpu.SMEM(lengths.shape, jnp.int32),
            pltpu.SMEM(adapter_of_row.shape, jnp.int32),
            pltpu.SMEM(storage_slot.shape, jnp.int32),
            pltpu.VMEM(queries.shape, jnp.bfloat16),
            pltpu.VMEM(fresh_keys.shape, jnp.bfloat16),
            pltpu.VMEM(fresh_values.shape, jnp.bfloat16),
            pltpu.VMEM((rows, cache, kv_width), jnp.bfloat16),
            pltpu.VMEM((rows, cache, kv_width), jnp.bfloat16),
            pltpu.VMEM((total, total), jnp.bfloat16),
            pltpu.VMEM((HEAD_WIDTH, total), jnp.float32),
            pltpu.VMEM((total, HEAD_WIDTH), jnp.bfloat16),
            pltpu.SemaphoreType.DMA((2, chunks)),
            pltpu.SemaphoreType.DMA((7,)),
        ],
        compiler_params=pltpu.CompilerParams(vmem_limit_bytes=24 * MIB),
        cost_estimate=pl.CostEstimate(
            flops=8 * total * cache * kv_width,
            bytes_accessed=4 * rows * cache * kv_width,
            transcendentals=total * cache,
        ),
        name="attend",
    )(
        *in_hbm(
            lengths,
            adapter_of_row,
            storage_slot,
            queries,
            jnp.asarray(row_order(heads, steps, rows), jnp.bfloat16),
            fresh_keys,
            fresh_values,
            cached_keys,
            cached_values,
        ),
    )
    return outs[0], outs[1], outs[2:]


def project_kernel(blocks, here, bring, added, attn_ref, w_hbm, *refs):
    here_ref = refs[0] if here else None
    add_refs = refs[bool(here) :][:added]
    refs = refs[len(refs) - len(blocks) - bool(bring) - 2 :]
    outs, w_ref, sems = refs[: len(blocks)], refs[-2], refs[-1]
    fetched = blocks[here:]
    copies = [
        block_copy(w_hbm, w_ref.at[n], sems.at[n], d) for n, d in enumerate(fetched)
    ] + [
        block_copy(w_hbm, refs[len(blocks)].at[n], sems.at[len(fetched) + n], d)
        for n, d in enumerate(bring)
    ]
    for copy in copies:
        copy.start()
    attn = attn_ref[...]
    for n in range(len(blocks)):
        if n >= here:
            copies[n - here].wait()
        block = here_ref.at[n] if n < here else w_ref.at[n - here]

        @pl.loop(0, block.shape[-1] // TILE)
        def _(i, n=n, block=block, out_ref=outs[n]):
            cols = pl.ds(pl.multiple_of(i * TILE, TILE), TILE)
            out = jnp.dot(attn, block[:, cols], preferred_element_type=jnp.float32)
            for add_ref in add_refs[n :: len(blocks)]:
                out = out + add_ref[:, cols].astype(jnp.float32)
            out_ref[:, cols] = out.astype(out_ref.dtype)

    for copy in copies[len(fetched) :]:
        copy.wait()


def project(attn, weight, columns, blocks, here=None, bring=(), add=(), dtype=jnp.bfloat16, after=()):
    tokens, width = attn.shape
    held = 0 if here is None else here.shape[0]
    fetched = len(blocks) - held
    extra = [*([here] if held else []), *add]
    outs = [jax.ShapeDtypeStruct((tokens, columns), dtype)] * len(blocks)
    if bring:
        outs.append(pltpu.VMEM((len(bring), width, columns), jnp.bfloat16))
    return pl.pallas_call(
        functools.partial(project_kernel, blocks, held, bring, len(add)),
        out_shape=outs,
        in_specs=[VMEM, HBM] + [VMEM] * len(extra) + [ANY] * len(after),
        out_specs=[VMEM] * len(outs),
        scratch_shapes=[
            pltpu.VMEM((max(fetched, 1), width if fetched else 16, columns), jnp.bfloat16),
            pltpu.SemaphoreType.DMA((fetched + len(bring),)),
        ],
        compiler_params=pltpu.CompilerParams(vmem_limit_bytes=16 * MIB),
        cost_estimate=pl.CostEstimate(
            flops=2 * tokens * width * columns * len(blocks),
            bytes_accessed=2 * width * columns * len(blocks),
            transcendentals=0,
        ),
        name="project",
    )(attn, *in_hbm(weight), *extra, *after)


def merge_kernel(mine_ref, got_ref, _, out_ref):
    out_ref[...] = (mine_ref[...] + got_ref[...].astype(jnp.float32)).astype(jnp.bfloat16)


def merge(mine, got, after):
    return pl.pallas_call(
        merge_kernel,
        out_shape=jax.ShapeDtypeStruct(mine.shape, jnp.bfloat16),
        in_specs=[VMEM, VMEM, ANY],
        out_specs=VMEM,
        compiler_params=pltpu.CompilerParams(vmem_limit_bytes=4 * MIB),
        name="merge",
    )(mine, got, after)


def down_kernel(capacity, steps, *refs):
    (*got_refs, down_ref, _, mine_ref, sent_ref, mask_ref) = refs
    resident, rank, width = down_ref.shape
    wide = resident * rank
    heads = width // HEAD_WIDTH
    size = capacity * steps
    held = size * len(got_refs)
    kind = jnp.bfloat16 if size % 16 == 0 else jnp.float32
    got = [ref[...].astype(kind) for ref in got_refs]
    rows = jnp.concatenate(
        [
            jnp.concatenate([part[h * size : (h + 1) * size, :] for part in got], axis=0)
            for h in range(heads)
        ],
        axis=1,
    ).astype(jnp.bfloat16)
    meta = jnp.concatenate([part[heads * size :, :] for part in got], axis=0)
    spread = div(iota((LANES, wide), 1), rank) == iota((LANES, wide), 0)
    entries = meta.shape[0]
    slot, entry = iota((held, entries), 0), iota((held, entries), 1)
    of_slot = entry == div(slot, size) * META_ROWS + div(mod(slot, size), steps)
    local = jnp.dot(
        of_slot.astype(jnp.bfloat16),
        meta.astype(jnp.bfloat16),
        preferred_element_type=jnp.float32,
    )
    mask = jnp.dot(
        local.astype(jnp.bfloat16),
        spread.astype(jnp.bfloat16),
        preferred_element_type=jnp.float32,
    )
    mask_ref[...] = mask.astype(jnp.bfloat16)
    low = lax.dot_general(
        rows,
        down_ref[...].reshape(wide, width),
        (((1,), (1,)), ((), ())),
        preferred_element_type=jnp.float32,
    )
    low = low * mask
    pair = low[:, :LANES]
    for n in range(1, wide // LANES):
        pair = pair + low[:, n * LANES : (n + 1) * LANES]
    both = pair + pltpu.roll(pair, rank, 1)
    half = held // 2
    packed = jnp.where(iota((half, LANES), 1) < rank, both[:half, :], both[half:, :])
    mine_ref[...] = packed
    sent_ref[...] = packed.astype(jnp.bfloat16)


def down(got, factors, capacity, steps, after):
    resident, rank, width = factors.shape
    held = len(got) * capacity * steps
    return pl.pallas_call(
        functools.partial(down_kernel, capacity, steps),
        out_shape=[
            jax.ShapeDtypeStruct((held // 2, LANES), jnp.float32),
            jax.ShapeDtypeStruct((held // 2, LANES), jnp.bfloat16),
            jax.ShapeDtypeStruct((held, resident * rank), jnp.bfloat16),
        ],
        in_specs=[VMEM] * (len(got) + 1) + [ANY],
        out_specs=[VMEM] * 3,
        compiler_params=pltpu.CompilerParams(vmem_limit_bytes=12 * MIB),
        cost_estimate=pl.CostEstimate(
            flops=200 * held * resident * rank * width,
            bytes_accessed=2 * resident * rank * width,
            transcendentals=0,
        ),
        name="down",
    )(*got, factors, after)


def up_kernel(peers, mine_ref, *refs):
    got_refs, (mask_ref, up_ref, _, *delta_refs) = refs[:peers], refs[peers:]
    resident, rank, columns = up_ref.shape
    wide = resident * rank
    total = mine_ref[...]
    for ref in got_refs:
        total = total + ref[...].astype(jnp.float32)
    other = pltpu.roll(total, rank, 1)
    first = iota(total.shape, 1) < rank
    both = jnp.concatenate(
        [jnp.where(first, total, other), jnp.where(first, other, total)], axis=0
    )
    both = jnp.concatenate([both] * (wide // LANES), axis=1)
    low = jnp.where(mask_ref[...].astype(jnp.float32) > 0.5, both, 0.0).astype(jnp.bfloat16)
    delta = jnp.dot(
        low, up_ref[...].reshape(wide, columns), preferred_element_type=jnp.float32
    ).astype(jnp.bfloat16)
    size = delta.shape[0] // len(delta_refs)
    for d, ref in enumerate(delta_refs):
        ref[...] = delta[d * size : (d + 1) * size, :]


def up(mine, got, mask, factors, owners, after):
    resident, rank, columns = factors.shape
    held = mask.shape[0]
    return pl.pallas_call(
        functools.partial(up_kernel, len(got)),
        out_shape=[jax.ShapeDtypeStruct((held // owners, columns), jnp.bfloat16)] * owners,
        in_specs=[VMEM] * (len(got) + 3) + [ANY],
        out_specs=[VMEM] * owners,
        compiler_params=pltpu.CompilerParams(vmem_limit_bytes=16 * MIB),
        cost_estimate=pl.CostEstimate(
            flops=200 * held * resident * rank * columns,
            bytes_accessed=2 * resident * rank * columns,
            transcendentals=0,
        ),
        name="up",
    )(mine, *got, mask, factors, after)


def finish_kernel(owners, pick_ref, *refs):
    delta_refs, (*near_refs, base_ref, out_hbm, out_ref, sems) = refs[:owners], refs[owners:]
    width = near_refs[0].shape[1]
    pick = pick_ref[...]
    copies = []
    for n, near_ref in enumerate(near_refs):
        cols = slice(n * width, (n + 1) * width)
        mixed = base_ref[:, cols] + near_ref[...].astype(jnp.float32)
        delta = jnp.concatenate([ref[:, cols] for ref in delta_refs], axis=0)
        mixed = mixed + lax.dot_general(
            pick, delta, (((0,), (0,)), ((), ())), preferred_element_type=jnp.float32
        )
        out_ref[:, :, cols] = mixed.astype(jnp.bfloat16).reshape(*out_ref.shape[:2], width)
        copies.append(
            pltpu.make_async_copy(out_ref.at[:, :, cols], out_hbm.at[:, :, cols], sems.at[n])
        )
        copies[n].start()
    for copy in copies:
        copy.wait()


def finish(base, pick, delta, near, steps):
    tokens, columns = base.shape
    shape = (steps, tokens // steps, columns)
    operands = [pick, *delta, *near, base]
    return pl.pallas_call(
        functools.partial(finish_kernel, len(delta)),
        out_shape=jax.ShapeDtypeStruct(shape, jnp.bfloat16),
        in_specs=[VMEM] * len(operands),
        out_specs=HBM,
        scratch_shapes=[
            pltpu.VMEM(shape, jnp.bfloat16),
            pltpu.SemaphoreType.DMA((len(near),)),
        ],
        compiler_params=pltpu.CompilerParams(vmem_limit_bytes=12 * MIB),
        cost_estimate=pl.CostEstimate(
            flops=2 * tokens * pick.shape[0] * columns,
            bytes_accessed=10 * tokens * columns,
            transcendentals=0,
        ),
        name="finish",
    )(*operands)


def body(
    queries,
    fresh_token_keys,
    fresh_token_values,
    cached_key_rows,
    cached_value_rows,
    cache_live_lengths,
    output_projection_weight,
    adapter_down_factors,
    adapter_up_factors,
    adapter_of_row,
    adapter_storage_slot,
):
    step_count, row_count, _ = queries.shape
    resident = adapter_down_factors.shape[0]
    owners = lax.axis_size("replica")
    tensors = lax.axis_size("tensor")
    capacity = max(2, 2 * row_count // owners)
    columns = adapter_up_factors.shape[2]
    far_sent, far_kept = list(range(3, tensors, 2)), list(range(2, tensors, 2))

    attn, pick, sent = attend_and_pick(
        cache_live_lengths,
        adapter_of_row,
        adapter_storage_slot,
        queries,
        fresh_token_keys,
        fresh_token_values,
        cached_key_rows,
        cached_value_rows,
        owners,
        capacity,
        resident,
    )
    got = exchange_all(sent, "replica")

    weight = output_projection_weight
    *parts, w_here = project(attn, weight, columns, far_sent, bring=far_kept)
    far_got = [xor_exchange(part, "tensor", 1) for part in parts]

    kept = project(
        attn, weight, columns, far_kept, here=w_here, dtype=jnp.float32, after=[parts[0]]
    )
    mine, low_sent, mask = down(got, adapter_down_factors, capacity, step_count, kept[0])
    low_got = [xor_exchange(low_sent, "tensor", d) for d in range(1, tensors)]
    halves_sent = [merge(*pair, low_sent) for pair in zip(kept, far_got, strict=True)]
    others = [xor_exchange(half, "tensor", d) for half, d in zip(halves_sent, far_kept, strict=True)]
    delta = up(mine, low_got, mask, adapter_up_factors, owners, halves_sent[0])
    delta_got = exchange_all(delta, "replica")

    (near,) = project(attn, weight, columns, [1], after=[delta[0]])
    width = columns // PIECES
    near_got = [
        xor_exchange(near[:, n * width : (n + 1) * width], "tensor", 1) for n in range(PIECES)
    ]
    (own,) = project(
        attn, weight, columns, [0], add=others, dtype=jnp.float32, after=[near]
    )
    return finish(own, pick, delta_got, near_got, step_count)


def solution(mesh):
    in_specs = (
        P(None, ("groups", "replica"), "tensor"),
        P(None, ("groups", "replica"), "tensor"),
        P(None, ("groups", "replica"), "tensor"),
        P(("groups", "replica"), None, "tensor"),
        P(("groups", "replica"), None, "tensor"),
        P(("groups", "replica")),
        P("tensor", None),
        P(("groups", "replica"), None, "tensor"),
        P(("groups", "replica"), None, "tensor"),
        P(("groups", "replica")),
        P("groups"),
    )
    out_specs = P(None, ("groups", "replica"), "tensor")
    return jax.shard_map(body, mesh=mesh, in_specs=in_specs, out_specs=out_specs, check_vma=False)
```

```python
import functools
import math

import jax
import jax.numpy as jnp
import numpy as np
from jax import lax
from jax.experimental import pallas as pl
from jax.experimental.pallas import tpu as pltpu
from jax.sharding import PartitionSpec as P

HEAD_WIDTH = 128
LANES = 128
META_ROWS = 16
TILE = 1024
TOGETHER = 4
PIECES = 2
MIB = 1024 * 1024
VMEM = pl.BlockSpec(memory_space=pltpu.VMEM)
ANY = pl.BlockSpec(memory_space=pl.ANY)
HBM = pl.BlockSpec(memory_space=pltpu.HBM)


def iota(shape, dim):
    return lax.broadcasted_iota(jnp.int32, shape, dim)


def halves(n):
    if n & (n - 1):
        raise ValueError(n)
    return n.bit_length() - 1


def div(x, n):
    return lax.shift_right_logical(x, jnp.int32(halves(n)))


def mod(x, n):
    return x & ((1 << halves(n)) - 1)


def in_hbm(*arrays):
    return [pltpu.with_memory_space_constraint(a, pltpu.HBM) for a in arrays]


def xor_exchange(value, axis, distance):
    size = lax.axis_size(axis)
    return lax.ppermute(value, axis, [(i, i ^ distance) for i in range(size)])


def partner_order(size):
    return [0, *range(size // 2, size), *range(1, size // 2)]


def exchange_all(blocks, axis):
    order = partner_order(lax.axis_size(axis))
    return [blocks[0]] + [
        xor_exchange(block, axis, distance)
        for block, distance in zip(blocks[1:], order[1:], strict=True)
    ]


def block_copy(w_hbm, dst, sem, distance):
    me = lax.axis_index("tensor")
    columns = dst.shape[-1]
    at = pl.multiple_of(lax.bitwise_xor(me, jnp.int32(distance)) * columns, LANES)
    return pltpu.make_async_copy(w_hbm.at[:, pl.ds(at, columns)], dst, sem)


def attend_kernel(
    owners,
    capacity,
    resident,
    lengths_hbm,
    adapter_hbm,
    slot_hbm,
    q_hbm,
    order_hbm,
    kf_hbm,
    vf_hbm,
    k_hbm,
    v_hbm,
    attn_ref,
    pick_ref,
    *rest,
):
    send_refs, rest = rest[:owners], rest[owners:]
    lengths_ref, adapter_ref, slot_ref, q_ref, kf_ref, vf_ref, k_ref, v_ref = rest[:8]
    order_ref, q_cols_ref, o_ref, sems, small_sems = rest[8:]
    steps, rows, width = q_ref.shape
    cache, kv_width = k_ref.shape[1:]
    heads = width // HEAD_WIDTH
    kv_here = kv_width // HEAD_WIDTH
    group = heads // kv_here
    per_row = heads * steps
    total = rows * per_row
    tokens = steps * rows
    chunks = sems.shape[1]
    chunk_rows = rows // chunks
    scale = 1.0 / math.sqrt(HEAD_WIDTH)

    def kv_copies(c):
        at = pl.ds(c * chunk_rows, chunk_rows)
        return [
            pltpu.make_async_copy(src.at[at], dst.at[at], sems.at[which, c])
            for which, (src, dst) in enumerate([(k_hbm, k_ref), (v_hbm, v_ref)])
        ]

    small = [
        pltpu.make_async_copy(src, dst, small_sems.at[n])
        for n, (src, dst) in enumerate(
            [
                (q_hbm, q_ref),
                (order_hbm, order_ref),
                (kf_hbm, kf_ref),
                (lengths_hbm, lengths_ref),
                (adapter_hbm, adapter_ref),
                (slot_hbm, slot_ref),
                (vf_hbm, vf_ref),
            ]
        )
    ]
    q_copy, order_copy, kf_copy, lengths_copy, adapter_copy, slot_copy, vf_copy = small
    first, *others = [kv_copies(c) for c in range(chunks)]
    for copy in [*small[:2], *first, *small[2:], *sum(others, [])]:
        copy.start()

    adapter_copy.wait()
    slot_copy.wait()
    me = lax.axis_index("replica")
    positions = partner_order(owners)
    row_at = mod(iota((8, tokens), 1), rows)
    row_down = iota((rows, LANES), 0)
    first_slot = jnp.zeros((8, tokens), jnp.int32)
    local_of = jnp.zeros((rows, LANES), jnp.int32)
    firsts = []
    for r in range(rows):
        slot = slot_ref[adapter_ref[r]]
        owner = jnp.int32(0)
        for d in range(1, owners):
            owner = owner + (slot >= d * resident).astype(jnp.int32)
        partner = lax.bitwise_xor(owner, me)
        first = jnp.int32(0)
        for d in range(1, owners):
            first = jnp.where(partner == positions[d], d * capacity, first)
        firsts.append(first)
        first_slot = jnp.where(row_at == r, first, first_slot)
        local_of = jnp.where(row_down == r, slot - owner * resident, local_of)
    place = first_slot
    for r in range(rows - 1):
        place = place + ((first_slot == firsts[r]) & (row_at > r)).astype(jnp.int32)
    held = owners * capacity * steps
    slot_at = iota((held, tokens), 0)
    token_at = iota((held, tokens), 1)
    pick = (
        (jnp.concatenate([place] * (held // 8), axis=0) == div(slot_at, steps))
        & (mod(slot_at, steps) == div(token_at, rows))
    ).astype(jnp.bfloat16)
    pick_ref[...] = pick
    local_hot = (local_of == iota((rows, LANES), 1)).astype(jnp.bfloat16)
    entry = iota((owners * META_ROWS, rows), 0)
    entry_place = mod(entry, META_ROWS)
    entry_slot = div(entry, META_ROWS) * capacity + entry_place
    entry_pick = (
        (jnp.concatenate([place[:, :rows]] * (owners * META_ROWS // 8), axis=0) == entry_slot)
        & (entry_place < capacity)
    ).astype(jnp.bfloat16)
    meta = jnp.dot(entry_pick, local_hot, preferred_element_type=jnp.float32)

    q_copy.wait()
    by_head = jnp.concatenate(
        [
            q_ref[:, :, h * HEAD_WIDTH : (h + 1) * HEAD_WIDTH].reshape(tokens, HEAD_WIDTH)
            for h in range(heads)
        ],
        axis=0,
    )
    order_copy.wait()
    q_cols_ref[...] = jnp.dot(
        by_head.astype(jnp.float32).T.astype(jnp.bfloat16),
        order_ref[...],
        preferred_element_type=jnp.float32,
    )
    lane = iota((HEAD_WIDTH, LANES), 1)
    row_of = div(lane, per_row)
    kv_of = mod(div(lane, steps * group), kv_here)

    kf_copy.wait()
    kf = kf_ref[...].reshape(tokens, kv_width)
    token, query = iota((tokens, LANES), 0), iota((tokens, LANES), 1)
    position = iota((cache, LANES), 0)

    def scores(c):
        cols = q_cols_ref[:, pl.ds(pl.multiple_of(c * LANES, LANES), LANES)]
        by_kv = [jnp.where(kv_of == g, cols, 0.0) for g in range(kv_here)]
        fresh = jnp.dot(
            kf,
            jnp.concatenate(by_kv, axis=0).astype(jnp.bfloat16),
            preferred_element_type=jnp.float32,
        )
        live = (mod(token, rows) == div(query, per_row) + c * chunk_rows) & (
            div(token, rows) <= mod(query, steps)
        )
        fresh = jnp.where(live, fresh * scale, -jnp.inf)
        weights = jnp.concatenate(
            [jnp.where(row_of == j, q, 0.0) for j in range(chunk_rows) for q in by_kv], axis=0
        ).astype(jnp.bfloat16)
        keys = jnp.concatenate([k_ref[c * chunk_rows + j] for j in range(chunk_rows)], axis=1)
        cached = jnp.dot(keys, weights, preferred_element_type=jnp.float32)
        return cached * scale, fresh

    def softmax(c, cached, fresh):
        length = jnp.zeros((1, LANES), jnp.int32)
        for j in range(chunk_rows):
            length = jnp.where(
                div(iota((1, LANES), 1), per_row) == j, lengths_ref[c * chunk_rows + j], length
            )
        cached = jnp.where(position < length, cached, -jnp.inf)
        top = jnp.maximum(
            jnp.max(cached, axis=0, keepdims=True), jnp.max(fresh, axis=0, keepdims=True)
        )
        wc, wf = jnp.exp(cached - top), jnp.exp(fresh - top)
        share = 1.0 / (
            jnp.sum(wc, axis=0, keepdims=True) + jnp.sum(wf, axis=0, keepdims=True)
        )
        return (wc * share).T.astype(jnp.bfloat16), (wf * share).T.astype(jnp.bfloat16)

    kv_down = mod(div(iota((LANES, HEAD_WIDTH), 0), steps * group), kv_here)

    def values(c, cached, fresh):
        out = jnp.concatenate(
            [
                jnp.dot(
                    cached[j * per_row : (j + 1) * per_row, :],
                    v_ref[c * chunk_rows + j],
                    preferred_element_type=jnp.float32,
                )
                for j in range(chunk_rows)
            ],
            axis=0,
        ) + jnp.dot(fresh, vf, preferred_element_type=jnp.float32)
        own = out[:, :HEAD_WIDTH]
        for g in range(1, kv_here):
            own = jnp.where(kv_down == g, out[:, g * HEAD_WIDTH : (g + 1) * HEAD_WIDTH], own)
        return own.astype(jnp.bfloat16)

    lengths_copy.wait()
    vf_copy.wait()
    vf = vf_ref[...].reshape(tokens, kv_width)

    together = min(TOGETHER, chunks)

    @pl.loop(0, chunks // together)
    def _(i):
        groups = [i * together + n for n in range(together)]
        for c in groups:
            for copy in kv_copies(c):
                copy.wait()

        scored = [scores(c) for c in groups]
        probs = [softmax(c, *part) for c, part in zip(groups, scored, strict=True)]
        for c, part in zip(groups, probs, strict=True):
            o_ref[pl.ds(pl.multiple_of(c * LANES, LANES), LANES), :] = values(c, *part)

    out = jnp.dot(
        order_ref[...], o_ref[...], preferred_element_type=jnp.float32
    ).astype(jnp.bfloat16)
    attn = jnp.concatenate(
        [out[h * tokens : (h + 1) * tokens, :] for h in range(heads)], axis=1
    )
    attn_ref[...] = attn
    sent = jnp.dot(pick, attn, preferred_element_type=jnp.float32)
    size = capacity * steps
    for d in range(owners):
        mine = sent[d * size : (d + 1) * size, :]
        send_refs[d][...] = jnp.concatenate(
            [mine[:, h * HEAD_WIDTH : (h + 1) * HEAD_WIDTH] for h in range(heads)]
            + [meta[d * META_ROWS : (d + 1) * META_ROWS, :]],
            axis=0,
        ).astype(jnp.bfloat16)


def row_order(heads, steps, rows):
    head, step, row = np.indices((heads, steps, rows)).reshape(3, -1)
    return np.eye(heads * steps * rows)[(row * heads + head) * steps + step]


def attend_and_pick(
    lengths,
    adapter_of_row,
    storage_slot,
    queries,
    fresh_keys,
    fresh_values,
    cached_keys,
    cached_values,
    owners,
    capacity,
    resident,
):
    steps, rows, width = queries.shape
    cache, kv_width = cached_keys.shape[1:]
    heads = width // HEAD_WIDTH
    total = rows * heads * steps
    tokens = steps * rows
    size = capacity * steps
    chunks = total // LANES
    outs = pl.pallas_call(
        functools.partial(attend_kernel, owners, capacity, resident),
        out_shape=[
            jax.ShapeDtypeStruct((tokens, width), jnp.bfloat16),
            jax.ShapeDtypeStruct((owners * size, tokens), jnp.bfloat16),
        ]
        + [jax.ShapeDtypeStruct((heads * size + META_ROWS, HEAD_WIDTH), jnp.bfloat16)] * owners,
        in_specs=[HBM] * 9,
        out_specs=[VMEM] * (2 + owners),
        scratch_shapes=[
            pltpu.SMEM(lengths.shape, jnp.int32),
            pltpu.SMEM(adapter_of_row.shape, jnp.int32),
            pltpu.SMEM(storage_slot.shape, jnp.int32),
            pltpu.VMEM(queries.shape, jnp.bfloat16),
            pltpu.VMEM(fresh_keys.shape, jnp.bfloat16),
            pltpu.VMEM(fresh_values.shape, jnp.bfloat16),
            pltpu.VMEM((rows, cache, kv_width), jnp.bfloat16),
            pltpu.VMEM((rows, cache, kv_width), jnp.bfloat16),
            pltpu.VMEM((total, total), jnp.bfloat16),
            pltpu.VMEM((HEAD_WIDTH, total), jnp.float32),
            pltpu.VMEM((total, HEAD_WIDTH), jnp.bfloat16),
            pltpu.SemaphoreType.DMA((2, chunks)),
            pltpu.SemaphoreType.DMA((7,)),
        ],
        compiler_params=pltpu.CompilerParams(vmem_limit_bytes=24 * MIB),
        cost_estimate=pl.CostEstimate(
            flops=8 * total * cache * kv_width,
            bytes_accessed=4 * rows * cache * kv_width,
            transcendentals=total * cache,
        ),
        name="attend",
    )(
        *in_hbm(
            lengths,
            adapter_of_row,
            storage_slot,
            queries,
            jnp.asarray(row_order(heads, steps, rows), jnp.bfloat16),
            fresh_keys,
            fresh_values,
            cached_keys,
            cached_values,
        ),
    )
    return outs[0], outs[1], outs[2:]


def project_kernel(blocks, here, bring, added, attn_ref, w_hbm, *refs):
    here_ref = refs[0] if here else None
    add_refs = refs[bool(here) :][:added]
    refs = refs[len(refs) - len(blocks) - bool(bring) - 2 :]
    outs, w_ref, sems = refs[: len(blocks)], refs[-2], refs[-1]
    fetched = blocks[here:]
    copies = [
        block_copy(w_hbm, w_ref.at[n], sems.at[n], d) for n, d in enumerate(fetched)
    ] + [
        block_copy(w_hbm, refs[len(blocks)].at[n], sems.at[len(fetched) + n], d)
        for n, d in enumerate(bring)
    ]
    for copy in copies:
        copy.start()
    attn = attn_ref[...]
    for n in range(len(blocks)):
        if n >= here:
            copies[n - here].wait()
        block = here_ref.at[n] if n < here else w_ref.at[n - here]

        @pl.loop(0, block.shape[-1] // TILE)
        def _(i, n=n, block=block, out_ref=outs[n]):
            cols = pl.ds(pl.multiple_of(i * TILE, TILE), TILE)
            out = jnp.dot(attn, block[:, cols], preferred_element_type=jnp.float32)
            for add_ref in add_refs[n :: len(blocks)]:
                out = out + add_ref[:, cols].astype(jnp.float32)
            out_ref[:, cols] = out.astype(out_ref.dtype)

    for copy in copies[len(fetched) :]:
        copy.wait()


def project(attn, weight, columns, blocks, here=None, bring=(), add=(), dtype=jnp.bfloat16, after=()):
    tokens, width = attn.shape
    held = 0 if here is None else here.shape[0]
    fetched = len(blocks) - held
    extra = [*([here] if held else []), *add]
    outs = [jax.ShapeDtypeStruct((tokens, columns), dtype)] * len(blocks)
    if bring:
        outs.append(pltpu.VMEM((len(bring), width, columns), jnp.bfloat16))
    return pl.pallas_call(
        functools.partial(project_kernel, blocks, held, bring, len(add)),
        out_shape=outs,
        in_specs=[VMEM, HBM] + [VMEM] * len(extra) + [ANY] * len(after),
        out_specs=[VMEM] * len(outs),
        scratch_shapes=[
            pltpu.VMEM((max(fetched, 1), width if fetched else 16, columns), jnp.bfloat16),
            pltpu.SemaphoreType.DMA((fetched + len(bring),)),
        ],
        compiler_params=pltpu.CompilerParams(vmem_limit_bytes=16 * MIB),
        cost_estimate=pl.CostEstimate(
            flops=2 * tokens * width * columns * len(blocks),
            bytes_accessed=2 * width * columns * len(blocks),
            transcendentals=0,
        ),
        name="project",
    )(attn, *in_hbm(weight), *extra, *after)


def merge_kernel(mine_ref, got_ref, _, out_ref):
    out_ref[...] = (mine_ref[...] + got_ref[...].astype(jnp.float32)).astype(jnp.bfloat16)


def merge(mine, got, after):
    return pl.pallas_call(
        merge_kernel,
        out_shape=jax.ShapeDtypeStruct(mine.shape, jnp.bfloat16),
        in_specs=[VMEM, VMEM, ANY],
        out_specs=VMEM,
        compiler_params=pltpu.CompilerParams(vmem_limit_bytes=4 * MIB),
        name="merge",
    )(mine, got, after)


def down_kernel(capacity, steps, *refs):
    (*got_refs, down_ref, _, mine_ref, sent_ref, mask_ref) = refs
    resident, rank, width = down_ref.shape
    wide = resident * rank
    heads = width // HEAD_WIDTH
    size = capacity * steps
    held = size * len(got_refs)
    kind = jnp.bfloat16 if size % 16 == 0 else jnp.float32
    got = [ref[...].astype(kind) for ref in got_refs]
    rows = jnp.concatenate(
        [
            jnp.concatenate([part[h * size : (h + 1) * size, :] for part in got], axis=0)
            for h in range(heads)
        ],
        axis=1,
    ).astype(jnp.bfloat16)
    meta = jnp.concatenate([part[heads * size :, :] for part in got], axis=0)
    spread = div(iota((LANES, wide), 1), rank) == iota((LANES, wide), 0)
    entries = meta.shape[0]
    slot, entry = iota((held, entries), 0), iota((held, entries), 1)
    of_slot = entry == div(slot, size) * META_ROWS + div(mod(slot, size), steps)
    local = jnp.dot(
        of_slot.astype(jnp.bfloat16),
        meta.astype(jnp.bfloat16),
        preferred_element_type=jnp.float32,
    )
    mask = jnp.dot(
        local.astype(jnp.bfloat16),
        spread.astype(jnp.bfloat16),
        preferred_element_type=jnp.float32,
    )
    mask_ref[...] = mask.astype(jnp.bfloat16)
    low = lax.dot_general(
        rows,
        down_ref[...].reshape(wide, width),
        (((1,), (1,)), ((), ())),
        preferred_element_type=jnp.float32,
    )
    low = low * mask
    pair = low[:, :LANES]
    for n in range(1, wide // LANES):
        pair = pair + low[:, n * LANES : (n + 1) * LANES]
    both = pair + pltpu.roll(pair, rank, 1)
    half = held // 2
    packed = jnp.where(iota((half, LANES), 1) < rank, both[:half, :], both[half:, :])
    mine_ref[...] = packed
    sent_ref[...] = packed.astype(jnp.bfloat16)


def down(got, factors, capacity, steps, after):
    resident, rank, width = factors.shape
    held = len(got) * capacity * steps
    return pl.pallas_call(
        functools.partial(down_kernel, capacity, steps),
        out_shape=[
            jax.ShapeDtypeStruct((held // 2, LANES), jnp.float32),
            jax.ShapeDtypeStruct((held // 2, LANES), jnp.bfloat16),
            jax.ShapeDtypeStruct((held, resident * rank), jnp.bfloat16),
        ],
        in_specs=[VMEM] * (len(got) + 1) + [ANY],
        out_specs=[VMEM] * 3,
        compiler_params=pltpu.CompilerParams(vmem_limit_bytes=12 * MIB),
        cost_estimate=pl.CostEstimate(
            flops=200 * held * resident * rank * width,
            bytes_accessed=2 * resident * rank * width,
            transcendentals=0,
        ),
        name="down",
    )(*got, factors, after)


def up_kernel(peers, mine_ref, *refs):
    got_refs, (mask_ref, up_ref, _, *delta_refs) = refs[:peers], refs[peers:]
    resident, rank, columns = up_ref.shape
    wide = resident * rank
    total = mine_ref[...]
    for ref in got_refs:
        total = total + ref[...].astype(jnp.float32)
    other = pltpu.roll(total, rank, 1)
    first = iota(total.shape, 1) < rank
    both = jnp.concatenate(
        [jnp.where(first, total, other), jnp.where(first, other, total)], axis=0
    )
    both = jnp.concatenate([both] * (wide // LANES), axis=1)
    low = jnp.where(mask_ref[...].astype(jnp.float32) > 0.5, both, 0.0).astype(jnp.bfloat16)
    delta = jnp.dot(
        low, up_ref[...].reshape(wide, columns), preferred_element_type=jnp.float32
    ).astype(jnp.bfloat16)
    size = delta.shape[0] // len(delta_refs)
    for d, ref in enumerate(delta_refs):
        ref[...] = delta[d * size : (d + 1) * size, :]


def up(mine, got, mask, factors, owners, after):
    resident, rank, columns = factors.shape
    held = mask.shape[0]
    return pl.pallas_call(
        functools.partial(up_kernel, len(got)),
        out_shape=[jax.ShapeDtypeStruct((held // owners, columns), jnp.bfloat16)] * owners,
        in_specs=[VMEM] * (len(got) + 3) + [ANY],
        out_specs=[VMEM] * owners,
        compiler_params=pltpu.CompilerParams(vmem_limit_bytes=16 * MIB),
        cost_estimate=pl.CostEstimate(
            flops=200 * held * resident * rank * columns,
            bytes_accessed=2 * resident * rank * columns,
            transcendentals=0,
        ),
        name="up",
    )(mine, *got, mask, factors, after)


def finish_kernel(owners, pick_ref, *refs):
    delta_refs, (*near_refs, base_ref, out_hbm, out_ref, sems) = refs[:owners], refs[owners:]
    pieces = sems.shape[0]
    width = base_ref.shape[1] // pieces
    per_near = pieces // len(near_refs)
    pick = pick_ref[...]
    copies = []
    for n in range(pieces):
        cols = slice(n * width, (n + 1) * width)
        near_cols = slice(n % per_near * width, (n % per_near + 1) * width)
        mixed = base_ref[:, cols] + near_refs[n // per_near][:, near_cols].astype(jnp.float32)
        delta = jnp.concatenate([ref[:, cols] for ref in delta_refs], axis=0)
        mixed = mixed + lax.dot_general(
            pick, delta, (((0,), (0,)), ((), ())), preferred_element_type=jnp.float32
        )
        out_ref[:, :, cols] = mixed.astype(jnp.bfloat16).reshape(*out_ref.shape[:2], width)
        copies.append(
            pltpu.make_async_copy(out_ref.at[:, :, cols], out_hbm.at[:, :, cols], sems.at[n])
        )
        copies[n].start()
    for copy in copies:
        copy.wait()


def finish(base, pick, delta, near, steps):
    tokens, columns = base.shape
    shape = (steps, tokens // steps, columns)
    operands = [pick, *delta, *near, base]
    return pl.pallas_call(
        functools.partial(finish_kernel, len(delta)),
        out_shape=jax.ShapeDtypeStruct(shape, jnp.bfloat16),
        in_specs=[VMEM] * len(operands),
        out_specs=HBM,
        scratch_shapes=[
            pltpu.VMEM(shape, jnp.bfloat16),
            pltpu.SemaphoreType.DMA((2 * len(near),)),
        ],
        compiler_params=pltpu.CompilerParams(vmem_limit_bytes=12 * MIB),
        cost_estimate=pl.CostEstimate(
            flops=2 * tokens * pick.shape[0] * columns,
            bytes_accessed=10 * tokens * columns,
            transcendentals=0,
        ),
        name="finish",
    )(*operands)


def body(
    queries,
    fresh_token_keys,
    fresh_token_values,
    cached_key_rows,
    cached_value_rows,
    cache_live_lengths,
    output_projection_weight,
    adapter_down_factors,
    adapter_up_factors,
    adapter_of_row,
    adapter_storage_slot,
):
    step_count, row_count, _ = queries.shape
    resident = adapter_down_factors.shape[0]
    owners = lax.axis_size("replica")
    tensors = lax.axis_size("tensor")
    capacity = max(2, 2 * row_count // owners)
    columns = adapter_up_factors.shape[2]
    far_sent, far_kept = list(range(3, tensors, 2)), list(range(2, tensors, 2))

    attn, pick, sent = attend_and_pick(
        cache_live_lengths,
        adapter_of_row,
        adapter_storage_slot,
        queries,
        fresh_token_keys,
        fresh_token_values,
        cached_key_rows,
        cached_value_rows,
        owners,
        capacity,
        resident,
    )
    got = exchange_all(sent, "replica")

    weight = output_projection_weight
    *parts, w_here = project(attn, weight, columns, far_sent, bring=far_kept)
    far_got = [xor_exchange(part, "tensor", 1) for part in parts]

    kept = project(
        attn, weight, columns, far_kept, here=w_here, dtype=jnp.float32, after=[parts[0]]
    )
    mine, low_sent, mask = down(got, adapter_down_factors, capacity, step_count, kept[0])
    low_got = [xor_exchange(low_sent, "tensor", d) for d in range(1, tensors)]
    halves_sent = [merge(*pair, low_sent) for pair in zip(kept, far_got, strict=True)]
    others = [xor_exchange(half, "tensor", d) for half, d in zip(halves_sent, far_kept, strict=True)]
    delta = up(mine, low_got, mask, adapter_up_factors, owners, halves_sent[0])
    delta_got = exchange_all(delta, "replica")

    (near,) = project(attn, weight, columns, [1], after=[delta[0]])
    width = columns // PIECES
    near_got = [
        xor_exchange(near[:, n * width : (n + 1) * width], "tensor", 1) for n in range(PIECES)
    ]
    (own,) = project(
        attn, weight, columns, [0], add=others, dtype=jnp.float32, after=[near]
    )
    return finish(own, pick, delta_got, near_got, step_count)


def solution(mesh):
    in_specs = (
        P(None, ("groups", "replica"), "tensor"),
        P(None, ("groups", "replica"), "tensor"),
        P(None, ("groups", "replica"), "tensor"),
        P(("groups", "replica"), None, "tensor"),
        P(("groups", "replica"), None, "tensor"),
        P(("groups", "replica")),
        P("tensor", None),
        P(("groups", "replica"), None, "tensor"),
        P(("groups", "replica"), None, "tensor"),
        P(("groups", "replica")),
        P("groups"),
    )
    out_specs = P(None, ("groups", "replica"), "tensor")
    return jax.shard_map(body, mesh=mesh, in_specs=in_specs, out_specs=out_specs, check_vma=False)
```
